32 devices in a mesh: rows: 8 (over z, core), cols: 4 (over y, x).
Axes of the slice: x: 2, y: 2, z: 4, core: 2. Of those that a mesh axis runs over, the one named last changes fastest.
Arguments:
- jac: bfloat16 [2048, 1024], P(('rows', 'cols')), may hold values from -0.29882812 to 0.29882812
- panel_jac: bfloat16 [2048, 512], P(('rows', 'cols')), may hold values from -6 to 6
- weights: float32 [2048], P(('rows', 'cols')), may hold values from 0.1 to 1
- tile_lists: int32 [64, 4], P(('rows', 'cols')), may hold values from 0 to 95, as said below
- tile_masks: int32 [64, 4], P(('rows', 'cols')), may hold values from 0 to 1
- tile_order: int32 [96], replicated, may hold values from 0 to 95, as said below
- factor_inverse: float32 [512, 512], replicated, as said below
Outputs:
- panel_factor: float32 [96, 256, 512], P('cols', 'rows')
The draws below stay inside these ranges and needn't reach their ends.
Inputs may be any that keep to these rules, and one draw needn't show every extreme that they name: `tile_order`: a permutation of 0 to 95. `tile_lists`: the 4 tiles of one row block are distinct; among the active slots of one device's 2 row blocks, at most 2 name tiles whose positions i share i // 24; in every draw every device has 2 such slots for one and the same position range. `factor_inverse`: lower triangular with a positive diagonal.
All inputs are finite; a program needn't handle non-finite values.
Results may differ from the reference program's by a relative error of at most 0.0029.
Values may be sent and summed in bfloat16 or wider, within the bound.
No kernel may reach another device: no remote copies, remote signals or barrier semaphores. Data moves between devices by JAX's collectives and lax.ppermute only.
A program may use at most 64 MiB of HBM per device.

```python
import math
import jax
import jax.numpy as jnp
from jax import lax

TILE = 256
NT = 96
PANEL = 512
KT = 4
RB = 32
NB_DEV = 2
NBLK = 64
ROWS_ALL = 2048
TPC = 24
SLOTS = 8
CAP = 2
N_COLS = 4


def tile_plan(key):
    base_key = jax.random.fold_in(key, 11)
    tile_perm = jax.random.permutation(jax.random.fold_in(base_key, 1), NT).astype(jnp.int32)
    devices = NBLK // NB_DEV
    bundles = SLOTS // CAP
    owner_ids = jnp.arange(N_COLS, dtype=jnp.int32)
    ranking = jax.random.permutation(jax.random.fold_in(base_key, 2), N_COLS).astype(jnp.int32)
    favored = (ranking == 0).astype(jnp.int32)
    heavy_owner = (ranking < max(1, N_COLS // 4)).astype(jnp.int32)
    scores = jax.random.randint(jax.random.fold_in(base_key, 3), (devices, N_COLS), 0, 1024)
    scores = scores + heavy_owner[None, :] * jax.random.randint(jax.random.fold_in(base_key, 4), (devices, N_COLS), 0, 2048)
    scores = (scores + favored[None, :] * 4096) * N_COLS + owner_ids[None, :]
    unused, groups = lax.top_k(scores, bundles)
    offset_scores = jax.random.randint(jax.random.fold_in(base_key, 5), (devices, bundles, TPC), 0, 65536)
    offset_scores = offset_scores * TPC + jnp.arange(TPC, dtype=jnp.int32)
    unused_too, offsets = lax.top_k(offset_scores, CAP)
    places = (groups[:, :, None].astype(jnp.int32) * TPC + offsets.astype(jnp.int32)).reshape(NBLK, KT)
    return (tile_perm, tile_perm[places].astype(jnp.int32))


def draw_tile_order(key, part):
    return tile_plan(key)[0]


def draw_tile_lists(key, part):
    return tile_plan(key)[1]


def draw_tile_masks(key, part):
    devices = NBLK // NB_DEV
    coins = jax.random.randint(jax.random.fold_in(key, 13), (devices, SLOTS), 0, 8)
    slot_index = jnp.arange(SLOTS, dtype=jnp.int32)[None, :]
    active = jnp.where(slot_index < CAP, 1, jnp.where(coins > 0, 1, 0))
    return active.reshape(NBLK, KT).astype(jnp.int32)


def draw_factor_inverse(key, part):
    row_index = lax.broadcasted_iota(jnp.int32, (PANEL, PANEL), 0)
    col_index = lax.broadcasted_iota(jnp.int32, (PANEL, PANEL), 1)
    diagonal_part = jnp.exp(jax.random.uniform(jax.random.fold_in(key, 21), (PANEL, PANEL), jnp.float32, math.log(0.5), math.log(2.0)))
    spread = jax.random.normal(jax.random.fold_in(key, 22), (PANEL, PANEL), jnp.float32)
    lower_part = spread * (1.0 / math.sqrt(PANEL))
    result = jnp.where(row_index > col_index, lower_part, jnp.where(row_index == col_index, diagonal_part, 0.0))
    return result.astype(jnp.float32)


def block_scale(own_key, extent, shards, smallest, largest):
    loudness, own = 1.0, jax.random.fold_in(own_key, 6)
    for position, shards_of in shards:
        steps = jnp.exp(jax.random.uniform(jax.random.fold_in(own, position), (shards_of,), jnp.float32, smallest / len(shards), largest / len(shards)))
        loudness = loudness * jnp.repeat(steps, extent[position] // shards_of).reshape([-1 if axis == position else 1 for axis in range(len(extent))])
    return loudness


def normal_values(stream_key, dims, width, reach, pieces=(), kind=jnp.bfloat16):
    entries = width * jax.random.normal(stream_key, dims, jnp.float32)
    if pieces:
        entries = entries * block_scale(stream_key, dims, pieces, -0.22, 0.18)
    return jnp.clip(entries, -reach, reach).astype(kind)


def setup_inputs(seed: int = 0) -> dict:
    key_list = jax.random.split(jax.random.key(seed), 8)
    return {
        "jac": normal_values(key_list[0], (ROWS_ALL, KT * TILE), 0.05, 0.29882812, ((0, 32),)),
        "panel_jac": normal_values(key_list[1], (ROWS_ALL, PANEL), 1.0, 6.0, ((0, 32),)),
        "weights": jnp.clip(jnp.exp(math.log(1.0) - 2.3025851 * jax.random.uniform(key_list[2], (ROWS_ALL,), jnp.float32) ** block_scale(key_list[2], (ROWS_ALL,), ((0, 32),), -0.2, 0.2)), 0.1, 1.0),
        "tile_lists": draw_tile_lists(jax.random.fold_in(key_list[7], 71), 0),
        "tile_masks": draw_tile_masks(jax.random.fold_in(key_list[7], 71), 0),
        "tile_order": draw_tile_order(jax.random.fold_in(key_list[7], 71), 0),
        "factor_inverse": draw_factor_inverse(jax.random.fold_in(key_list[7], 71), 0),
    }


def tile_positions(tile_lists, tile_order):
    tile_count = tile_order.shape[0]
    matches = tile_lists[:, :, None] == tile_order[None, None, :]
    return jnp.sum(jnp.where(matches, jnp.arange(tile_count, dtype=jnp.int32), 0), axis=2).astype(jnp.int32)


def reference(jac, panel_jac, weights, tile_lists, tile_masks, tile_order, factor_inverse):
    places = tile_positions(tile_lists, tile_order)
    weighted = (weights[:, None] * panel_jac).astype(jnp.bfloat16)
    group_size = 32
    steps_count = NBLK // group_size
    columns = jac.reshape(steps_count, group_size, RB, KT, TILE)
    panels = weighted.reshape(steps_count, group_size, RB, PANEL)
    place_groups = places.reshape(steps_count, group_size * KT)
    mask_groups = tile_masks.reshape(steps_count, group_size, KT).astype(jnp.float32)

    def add_group(totals, inputs):
        column_group, panel_group, place_group, mask_group = inputs
        terms = jnp.einsum("brkt,brp->bktp", column_group.astype(jnp.float32), panel_group.astype(jnp.float32), precision=lax.Precision.HIGHEST)
        terms = terms * mask_group[:, :, None, None]
        return totals.at[place_group].add(terms.reshape(group_size * KT, TILE, PANEL)), None

    gram_tiles, unused = lax.scan(add_group, jnp.zeros((NT, TILE, PANEL), jnp.float32), (columns, panels, place_groups, mask_groups))
    return jnp.einsum("ntp,qp->ntq", gram_tiles, factor_inverse, precision=lax.Precision.HIGHEST)
```

```python
import jax
import jax.numpy as jnp
from jax import lax
from jax.sharding import PartitionSpec as P

CAP = 2
GATHERED = 1 << 22


def tile_positions(tile_lists, tile_order):
    tile_count = tile_order.shape[0]
    matches = tile_lists[:, :, None] == tile_order[None, None, :]
    return jnp.sum(jnp.where(matches, jnp.arange(tile_count, dtype=jnp.int32), 0), axis=2)


def apply_inverse(tiles, factor_inverse):
    return jnp.einsum("ntp,qp->ntq", tiles, factor_inverse, precision=lax.Precision.HIGHEST)


def local(jac, panel_jac, weights, tile_lists, tile_masks, tile_order, factor_inverse):
    block_count, slot_count = tile_lists.shape
    block_rows = jac.shape[0] // block_count
    tile_width = jac.shape[1] // slot_count
    slabs, owners = lax.axis_size("rows"), lax.axis_size("cols")
    devices = slabs * owners
    per_owner = tile_order.shape[0] // owners
    slab_width = tile_width // slabs
    bf16 = jnp.bfloat16

    weighted = (weights[:, None] * panel_jac).astype(bf16)

    positions = tile_positions(tile_lists, tile_order).reshape(-1)
    active = tile_masks.reshape(-1) == 1
    owner = positions // per_owner
    same = (owner[:, None] == owner[None, :]) & active[None, :]
    earlier = jnp.tril(jnp.ones(same.shape, bool), -1)
    rank = jnp.sum(same & earlier, axis=1)
    code = (
        (owner[None, None, :] == jnp.arange(owners)[:, None, None])
        & (rank[None, None, :] == jnp.arange(CAP)[None, :, None])
        & active[None, None, :]
    )
    block = jnp.arange(block_count * slot_count) // slot_count
    place = positions % per_owner + per_owner * block
    places = jnp.sum(jnp.where(code, place + 1, 0), axis=2) - 1
    columns = jac.reshape(block_count, block_rows, slot_count, slabs, slab_width)
    chosen = code.astype(bf16).reshape(owners, CAP, block_count, slot_count)
    pieces = jnp.einsum("cjbk,bmkrt->rcjmt", chosen, columns, preferred_element_type=jnp.float32).astype(bf16)
    pieces = pieces.reshape(devices, -1)
    note = jnp.broadcast_to(places.astype(bf16)[None], (slabs, owners, CAP)).reshape(devices, CAP)
    note = jnp.pad(note, ((0, 0), (0, 128 - CAP)))
    sent = jnp.concatenate([pieces, note], axis=1)
    got = lax.all_to_all(sent, ("rows", "cols"), split_axis=0, concat_axis=0, tiled=True)
    size = pieces.shape[1]
    data = got[:, :size].reshape(devices, CAP, block_rows, slab_width)
    where = got[:, size : size + CAP].astype(jnp.int32)
    hot = (where[:, :, None] == jnp.arange(block_count * per_owner)).astype(bf16)
    hot = hot.reshape(devices, CAP, block_count, per_owner)
    mixed = jnp.einsum("djbn,djmt->dbmnt", hot, data, preferred_element_type=jnp.float32).astype(bf16)
    strips = max(1, devices * weighted.size * 2 // GATHERED)

    def strip_gram(strip):
        panels = lax.all_gather(strip, ("rows", "cols"), axis=0, tiled=True)
        panels = panels.reshape(devices, block_count, block_rows, -1)
        return jnp.einsum("dbmnt,dbmp->ntp", mixed, panels, preferred_element_type=jnp.float32)

    if strips == 1:
        gram = strip_gram(weighted)
    else:
        narrow = weighted.reshape(weighted.shape[0], strips, -1).swapaxes(0, 1)
        gram = jnp.moveaxis(lax.map(strip_gram, narrow), 0, 2)
        gram = gram.reshape(per_owner, slab_width, -1)
    return apply_inverse(gram, factor_inverse)


def solution(mesh):
    in_specs = (
        P(("rows", "cols"), None),
        P(("rows", "cols"), None),
        P(("rows", "cols")),
        P(("rows", "cols"), None),
        P(("rows", "cols"), None),
        P(),
        P(),
    )
    out_specs = P("cols", "rows", None)
    return jax.shard_map(local, mesh=mesh, in_specs=in_specs, out_specs=out_specs, check_vma=False)
```

```python
import jax
import jax.numpy as jnp
from jax import lax
from jax.sharding import PartitionSpec as P

CAP = 2
GATHERED = 1 << 22


def tile_positions(tile_lists, tile_order):
    tile_count = tile_order.shape[0]
    matches = tile_lists[:, :, None] == tile_order[None, None, :]
    return jnp.sum(jnp.where(matches, jnp.arange(tile_count, dtype=jnp.int32), 0), axis=2)


def apply_inverse(tiles, factor_inverse):
    return jnp.einsum("ntp,qp->ntq", tiles, factor_inverse, precision=lax.Precision.HIGHEST)


def slot_codes(tile_lists, tile_masks, tile_order, owner_ids):
    block_count, slot_count = tile_lists.shape
    per_owner = tile_order.shape[0] // lax.axis_size("cols")
    positions = tile_positions(tile_lists, tile_order).reshape(-1)
    active = tile_masks.reshape(-1) == 1
    owner = positions // per_owner
    same = (owner[:, None] == owner[None, :]) & active[None, :]
    earlier = jnp.tril(jnp.ones(same.shape, bool), -1)
    rank = jnp.sum(same & earlier, axis=1)
    code = (
        (owner[None, None, :] == owner_ids[:, None, None])
        & (rank[None, None, :] == jnp.arange(CAP)[None, :, None])
        & active[None, None, :]
    )
    block = jnp.arange(block_count * slot_count) // slot_count
    place = positions % per_owner + per_owner * block
    return code, jnp.sum(jnp.where(code, place + 1, 0), axis=2) - 1


def local_general(jac, panel_jac, weights, tile_lists, tile_masks, tile_order, factor_inverse):
    block_count, slot_count = tile_lists.shape
    block_rows = jac.shape[0] // block_count
    tile_width = jac.shape[1] // slot_count
    slabs, owners = lax.axis_size("rows"), lax.axis_size("cols")
    devices = slabs * owners
    per_owner = tile_order.shape[0] // owners
    slab_width = tile_width // slabs
    bf16 = jnp.bfloat16
    weighted = (weights[:, None] * panel_jac).astype(bf16)
    code, places = slot_codes(tile_lists, tile_masks, tile_order, jnp.arange(owners))
    columns = jac.reshape(block_count, block_rows, slot_count, slabs, slab_width)
    chosen = code.astype(bf16).reshape(owners, CAP, block_count, slot_count)
    pieces = jnp.einsum("cjbk,bmkrt->rcjmt", chosen, columns, preferred_element_type=jnp.float32).astype(bf16)
    pieces = pieces.reshape(devices, -1)
    note = jnp.broadcast_to(places.astype(bf16)[None], (slabs, owners, CAP)).reshape(devices, CAP)
    note = jnp.pad(note, ((0, 0), (0, 128 - CAP)))
    sent = jnp.concatenate([pieces, note], axis=1)
    got = lax.all_to_all(sent, ("rows", "cols"), split_axis=0, concat_axis=0, tiled=True)
    size = pieces.shape[1]
    data = got[:, :size].reshape(devices, CAP, block_rows, slab_width)
    where = got[:, size : size + CAP].astype(jnp.int32)
    hot = (where[:, :, None] == jnp.arange(block_count * per_owner)).astype(bf16)
    hot = hot.reshape(devices, CAP, block_count, per_owner)
    mixed = jnp.einsum("djbn,djmt->dbmnt", hot, data, preferred_element_type=jnp.float32).astype(bf16)
    strips = max(1, devices * weighted.size * 2 // GATHERED)

    def strip_gram(strip):
        panels = lax.all_gather(strip, ("rows", "cols"), axis=0, tiled=True)
        panels = panels.reshape(devices, block_count, block_rows, -1)
        return jnp.einsum("dbmnt,dbmp->ntp", mixed, panels, preferred_element_type=jnp.float32)

    if strips == 1:
        gram = strip_gram(weighted)
    else:
        narrow = weighted.reshape(weighted.shape[0], strips, -1).swapaxes(0, 1)
        gram = jnp.moveaxis(lax.map(strip_gram, narrow), 0, 2)
        gram = gram.reshape(per_owner, slab_width, -1)
    return apply_inverse(gram, factor_inverse)


def shift(value, steps_z, flip_cols, flip_core=0):
    slabs, owners = lax.axis_size("rows"), lax.axis_size("cols")
    pairs = []
    for r in range(slabs):
        to_r = ((r // 2 + steps_z) % (slabs // 2)) * 2 + ((r % 2) ^ flip_core)
        for c in range(owners):
            pairs.append((r * owners + c, to_r * owners + (c ^ flip_cols)))
    return lax.ppermute(value, ("rows", "cols"), pairs)


def local(jac, panel_jac, weights, tile_lists, tile_masks, tile_order, factor_inverse):
    block_count, slot_count = tile_lists.shape
    block_rows = jac.shape[0] // block_count
    tile_width = jac.shape[1] // slot_count
    slabs, owners = lax.axis_size("rows"), lax.axis_size("cols")
    layers = slabs // 2
    per_owner = tile_order.shape[0] // owners
    slab_width = tile_width // slabs
    bf16 = jnp.bfloat16
    weighted = (weights[:, None] * panel_jac).astype(bf16)

    lines = [weighted] + [shift(weighted, k, 0) for k in range(1, layers)]
    by_x = [shift(w, 0, 1) for w in lines]
    by_y = [shift(w, 0, 2) for w in lines]
    half = layers // 2
    across = [shift(w, 0, 2) for w in by_x[:half]] + [shift(w, 0, 1) for w in by_y[half:]]

    me_r, me_c = lax.axis_index("rows"), lax.axis_index("cols")
    me_z, me_core = me_r // 2, me_r % 2
    code, places = slot_codes(tile_lists, tile_masks, tile_order, me_c ^ jnp.arange(owners))
    columns = jac.reshape(block_count, block_rows, slot_count, layers, 2, slab_width)
    columns = jnp.take(columns, (me_z + jnp.arange(layers)) % layers, axis=3)
    columns = jnp.take(columns, me_core ^ jnp.arange(2), axis=4)
    chosen = code.astype(bf16).reshape(owners, CAP, block_count, slot_count)
    pieces = jnp.einsum("ejbk,bmkzut->zemjut", chosen, columns, preferred_element_type=jnp.float32).astype(bf16)
    pieces = pieces.reshape(layers, owners, block_rows, -1)
    note = jnp.pad(places.astype(bf16), ((0, 0), (0, pieces.shape[3] - CAP)))
    note = jnp.broadcast_to(note[None, :, None], (layers, owners, 1, pieces.shape[3]))
    sent = jnp.concatenate([pieces, note], axis=2)
    got = [
        [sent[k, e] if k == e == 0 else shift(sent[k, e], k, e) for e in range(owners)]
        for k in range(layers)
    ]

    panels = jnp.stack([w for group in (lines, by_x, by_y, across) for w in group])
    got = jnp.stack([got[k][e] for e in range(owners) for k in range(layers)])
    sources = layers * owners
    panels = panels.reshape(sources, block_count, block_rows, -1)
    data = got[:, :block_rows].reshape(sources, block_rows, CAP, 2, slab_width)
    where = got[:, block_rows, :CAP].astype(jnp.int32)
    hot = (where[:, :, None] == jnp.arange(block_count * per_owner)).astype(bf16)
    hot = hot.reshape(sources, CAP, block_count, per_owner)
    mixed = jnp.einsum("djbn,dmjut->dbmunt", hot, data, preferred_element_type=jnp.float32).astype(bf16)
    gram = jnp.einsum("dbmunt,dbmp->untp", mixed, panels, preferred_element_type=jnp.float32)
    other = shift(gram[1].astype(bf16), 0, 0, 1)
    return apply_inverse(gram[0] + other.astype(jnp.float32), factor_inverse)


def solution(mesh):
    in_specs = (
        P(("rows", "cols"), None),
        P(("rows", "cols"), None),
        P(("rows", "cols")),
        P(("rows", "cols"), None),
        P(("rows", "cols"), None),
        P(),
        P(),
    )
    out_specs = P("cols", "rows", None)
    body = local if (mesh.shape["rows"], mesh.shape["cols"]) == (8, 4) else local_general
    return jax.shard_map(body, mesh=mesh, in_specs=in_specs, out_specs=out_specs, check_vma=False)
```

```python
import functools

import jax
import jax.numpy as jnp
from jax import lax
from jax.experimental import pallas as pl
from jax.experimental.pallas import tpu as pltpu
from jax.sharding import PartitionSpec as P

CAP = 2
GATHERED = 1 << 22


def tile_positions(tile_lists, tile_order):
    tile_count = tile_order.shape[0]
    matches = tile_lists[:, :, None] == tile_order[None, None, :]
    return jnp.sum(jnp.where(matches, jnp.arange(tile_count, dtype=jnp.int32), 0), axis=2)


def apply_inverse(tiles, factor_inverse):
    return jnp.einsum("ntp,qp->ntq", tiles, factor_inverse, precision=lax.Precision.HIGHEST)


def slot_codes(tile_lists, tile_masks, tile_order, owner_ids):
    block_count, slot_count = tile_lists.shape
    per_owner = tile_order.shape[0] // lax.axis_size("cols")
    positions = tile_positions(tile_lists, tile_order).reshape(-1)
    active = tile_masks.reshape(-1) == 1
    owner = positions // per_owner
    same = (owner[:, None] == owner[None, :]) & active[None, :]
    earlier = jnp.tril(jnp.ones(same.shape, bool), -1)
    rank = jnp.sum(same & earlier, axis=1)
    code = (
        (owner[None, None, :] == owner_ids[:, None, None])
        & (rank[None, None, :] == jnp.arange(CAP)[None, :, None])
        & active[None, None, :]
    )
    block = jnp.arange(block_count * slot_count) // slot_count
    place = positions % per_owner + per_owner * block
    return code, jnp.sum(jnp.where(code, place + 1, 0), axis=2) - 1


def local_general(jac, panel_jac, weights, tile_lists, tile_masks, tile_order, factor_inverse):
    block_count, slot_count = tile_lists.shape
    block_rows = jac.shape[0] // block_count
    tile_width = jac.shape[1] // slot_count
    slabs, owners = lax.axis_size("rows"), lax.axis_size("cols")
    devices = slabs * owners
    per_owner = tile_order.shape[0] // owners
    slab_width = tile_width // slabs
    bf16 = jnp.bfloat16
    weighted = (weights[:, None] * panel_jac).astype(bf16)
    code, places = slot_codes(tile_lists, tile_masks, tile_order, jnp.arange(owners))
    columns = jac.reshape(block_count, block_rows, slot_count, slabs, slab_width)
    chosen = code.astype(bf16).reshape(owners, CAP, block_count, slot_count)
    pieces = jnp.einsum("cjbk,bmkrt->rcjmt", chosen, columns, preferred_element_type=jnp.float32).astype(bf16)
    pieces = pieces.reshape(devices, -1)
    note = jnp.broadcast_to(places.astype(bf16)[None], (slabs, owners, CAP)).reshape(devices, CAP)
    note = jnp.pad(note, ((0, 0), (0, 128 - CAP)))
    sent = jnp.concatenate([pieces, note], axis=1)
    got = lax.all_to_all(sent, ("rows", "cols"), split_axis=0, concat_axis=0, tiled=True)
    size = pieces.shape[1]
    data = got[:, :size].reshape(devices, CAP, block_rows, slab_width)
    where = got[:, size : size + CAP].astype(jnp.int32)
    hot = (where[:, :, None] == jnp.arange(block_count * per_owner)).astype(bf16)
    hot = hot.reshape(devices, CAP, block_count, per_owner)
    mixed = jnp.einsum("djbn,djmt->dbmnt", hot, data, preferred_element_type=jnp.float32).astype(bf16)
    strips = max(1, devices * weighted.size * 2 // GATHERED)

    def strip_gram(strip):
        panels = lax.all_gather(strip, ("rows", "cols"), axis=0, tiled=True)
        panels = panels.reshape(devices, block_count, block_rows, -1)
        return jnp.einsum("dbmnt,dbmp->ntp", mixed, panels, preferred_element_type=jnp.float32)

    if strips == 1:
        gram = strip_gram(weighted)
    else:
        narrow = weighted.reshape(weighted.shape[0], strips, -1).swapaxes(0, 1)
        gram = jnp.moveaxis(lax.map(strip_gram, narrow), 0, 2)
        gram = gram.reshape(per_owner, slab_width, -1)
    return apply_inverse(gram, factor_inverse)


def shift(value, steps_z, flip_cols, flip_core=0):
    slabs, owners = lax.axis_size("rows"), lax.axis_size("cols")
    pairs = []
    for r in range(slabs):
        to_r = ((r // 2 + steps_z) % (slabs // 2)) * 2 + ((r % 2) ^ flip_core)
        for c in range(owners):
            pairs.append((r * owners + c, to_r * owners + (c ^ flip_cols)))
    return lax.ppermute(value, ("rows", "cols"), pairs)


def pack_kernel(
    sizes, me_ref, lists_ref, masks_ref, order_ref, weights_ref, panel_ref, jac_ref, *rest
):
    layers, owners, per_owner, block_count, slot_count, block_rows, tile_width = sizes
    parcels, (places_ref, turned_ref) = rest[:layers], rest[layers:]
    f32, bf16 = jnp.float32, jnp.bfloat16
    rows, panel_width = panel_ref.shape
    lane_group = CAP * block_rows
    slab = tile_width // layers
    part = slab // 2
    me_z, me_core, me_c = me_ref[0], me_ref[1], me_ref[2]

    for i in range(order_ref.shape[0]):
        places_ref[order_ref[i]] = i

    row_ids = lax.broadcasted_iota(jnp.int32, (rows, rows), 0)
    lane_ids = lax.broadcasted_iota(jnp.int32, (rows, rows), 1)
    column = jnp.sum(jnp.where(row_ids == lane_ids, weights_ref[...], 0.0), axis=1, keepdims=True)
    weighted = (column * panel_ref[...].astype(f32)).astype(bf16)
    for parcel in parcels:
        parcel[:, :panel_width] = weighted

    for b in range(block_count):
        block = jac_ref[b * block_rows : (b + 1) * block_rows, :].astype(f32)
        start = b * slot_count * tile_width
        turned_ref[start : start + slot_count * tile_width, :] = block.T

    slots = []
    for s in range(block_count * slot_count):
        b, k = divmod(s, slot_count)
        place = places_ref[lists_ref[b, k]]
        owner = jnp.int32(0)
        for c in range(1, owners):
            owner += (place >= c * per_owner).astype(jnp.int32)
        slots.append((place - owner * per_owner, jnp.where(masks_ref[b, k] == 1, owner, -1)))

    lane = lax.broadcasted_iota(jnp.int32, (16, CAP * block_count * block_rows), 1)
    for e in range(owners):
        wanted = me_c ^ e
        found = jnp.int32(0)
        chosen = [jnp.int32(0)] * CAP
        codes = [jnp.int32(-1)] * CAP
        for s, (place, owner) in enumerate(slots):
            hit = owner == wanted
            for j in range(CAP):
                take = hit & (found == j)
                chosen[j] = jnp.where(take, s, chosen[j])
                codes[j] = jnp.where(take, place, codes[j])
            found += hit.astype(jnp.int32)
        note = jnp.full(lane.shape, -1, jnp.int32)
        for j in range(CAP):
            for b in range(block_count):
                at = (j * block_count + b) * block_rows
                here = (lane >= at) & (lane < at + block_rows)
                code = jnp.where(chosen[j] // slot_count == b, codes[j], -1)
                note = jnp.where(here, code, note)
        note = note.astype(f32).astype(bf16)
        at = panel_width + owners * lane_group
        for k, parcel in enumerate(parcels):
            parcel[e * 16 : (e + 1) * 16, at : at + note.shape[1]] = note
            z = lax.rem(me_z + k, layers)
            for u in range(2):
                core = me_core ^ u
                for j in range(CAP):
                    first = pl.multiple_of(chosen[j] * tile_width + z * slab + core * part, part)
                    piece = turned_ref[pl.ds(first, part), :].astype(bf16)
                    to = panel_width + e * lane_group + j * block_rows
                    parcel[u * part : (u + 1) * part, to : to + block_rows] = piece


def sort_kernel(sizes, *refs):
    layers, owners, panel_width, lane_group = sizes
    parcels, outs = refs[:layers], refs[layers:]
    halves, posts = outs[: layers // 2], outs[layers // 2 :]
    rows = parcels[0].shape[0]
    codes_at = panel_width + owners * lane_group
    for k, parcel in enumerate(parcels):
        halves[k // 2][(k % 2) * rows : (k % 2 + 1) * rows, :] = parcel[:, :panel_width]
        for e, post in enumerate(posts):
            at = panel_width + e * lane_group
            post[:rows, k * lane_group : (k + 1) * lane_group] = parcel[:, at : at + lane_group]
            note = parcel[e * 16 : (e + 1) * 16, codes_at:]
            wide = note.shape[1]
            low = rows + 16 * (k // 2)
            post[low : low + 16, (k % 2) * wide : (k % 2 + 1) * wide] = note


def gram_kernel(sizes, *refs):
    layers, owners, per_owner, block_rows, block_count = sizes
    pairs = layers // 2
    panels = refs[: owners * pairs]
    posts = refs[owners * pairs : owners * pairs + owners]
    own_ref, other_ref, placed_ref, rows_ref = refs[owners * pairs + owners :]
    f32, bf16 = jnp.float32, jnp.bfloat16
    rows = block_count * block_rows
    group = CAP * block_rows
    height = posts[0].shape[0] - 16 * pairs
    part = height // 2
    depth = 2 * rows
    for i, panel in enumerate(panels):
        rows_ref[i * depth : (i + 1) * depth, :] = panel[...]
    for u, out_ref in ((1, other_ref), (0, own_ref)):
        for e in range(owners):
            for h in range(pairs):
                post = posts[e]
                columns, codes = [], []
                for j in range(CAP):
                    pieces, notes = [], []
                    for d in range(2):
                        at = (h * 2 + d) * group + j * block_rows
                        piece = post[u * part : (u + 1) * part, at : at + block_rows].astype(f32)
                        pieces += [piece] * block_count
                        low = height + 16 * h
                        wide = CAP * rows
                        notes.append(post[low : low + 16, d * wide + j * rows : d * wide + (j + 1) * rows].astype(f32))
                    columns.append(jnp.concatenate(pieces, axis=1).astype(bf16))
                    note = jnp.concatenate(notes, axis=1)
                    codes.append(jnp.concatenate([note] * (part // 16), axis=0).astype(bf16))
                at = (e * pairs + h) * depth
                for n in range(per_owner):
                    placed = jnp.zeros(columns[0].shape, bf16)
                    for j in range(CAP):
                        placed = jnp.where(codes[j] == jnp.asarray(n, bf16), columns[j], placed)
                    placed_ref[n * part : (n + 1) * part, at : at + depth] = placed
        out_ref[...] = jnp.dot(placed_ref[...], rows_ref[...], preferred_element_type=f32).astype(out_ref.dtype)


def inverse_kernel(own_ref, other_ref, factor_ref, out_ref):
    f32, bf16 = jnp.float32, jnp.bfloat16
    factor = factor_ref[...]
    high = factor.astype(bf16)
    low = (factor - high.astype(f32)).astype(bf16)
    gram = own_ref[...] + other_ref[...].astype(f32)
    gram_high = gram.astype(bf16)
    gram_low = (gram - gram_high.astype(f32)).astype(bf16)
    dims = (((1,), (1,)), ((), ()))

    def times(a, b):
        return lax.dot_general(a, b, dims, preferred_element_type=f32)

    out_ref[...] = times(gram_high, high) + (times(gram_high, low) + times(gram_low, high))


def local(jac, panel_jac, weights, tile_lists, tile_masks, tile_order, factor_inverse):
    block_count, slot_count = tile_lists.shape
    rows, panel_width = panel_jac.shape
    block_rows = rows // block_count
    tile_width = jac.shape[1] // slot_count
    slabs, owners = lax.axis_size("rows"), lax.axis_size("cols")
    layers, pairs = slabs // 2, slabs // 4
    per_owner = tile_order.shape[0] // owners
    slab_width = tile_width // slabs
    f32, bf16 = jnp.float32, jnp.bfloat16
    vmem, smem = pl.BlockSpec(memory_space=pltpu.VMEM), pl.BlockSpec(memory_space=pltpu.SMEM)
    params = pltpu.CompilerParams(vmem_limit_bytes=48 << 20)

    me_r, me_c = lax.axis_index("rows"), lax.axis_index("cols")
    me = jnp.stack([me_r // 2, me_r % 2, me_c]).astype(jnp.int32)
    lane_group = CAP * block_rows
    wide = CAP * block_count * block_rows
    parcel = jax.ShapeDtypeStruct((rows, panel_width + owners * lane_group + wide), bf16)
    sizes = (layers, owners, per_owner, block_count, slot_count, block_rows, tile_width)
    parcels = pl.pallas_call(
        functools.partial(pack_kernel, sizes),
        out_shape=[parcel] * layers,
        in_specs=[smem] * 4 + [vmem] * 3,
        out_specs=[vmem] * layers,
        scratch_shapes=[
            pltpu.SMEM((tile_order.shape[0],), jnp.int32),
            pltpu.VMEM((block_count * slot_count * tile_width, block_rows), f32),
        ],
        compiler_params=params,
        name="pack",
    )(me, tile_lists, tile_masks, tile_order, weights.reshape(1, rows), panel_jac, jac)
    parcels = [parcels[0]] + [shift(parcels[k], k, 0) for k in range(1, layers)]

    height = 2 * slab_width
    half = jax.ShapeDtypeStruct((2 * rows, panel_width), bf16)
    post = jax.ShapeDtypeStruct((height + 16 * pairs, max(layers * lane_group, 2 * wide)), bf16)
    outs = pl.pallas_call(
        functools.partial(sort_kernel, (layers, owners, panel_width, lane_group)),
        out_shape=[half] * pairs + [post] * owners,
        in_specs=[vmem] * layers,
        out_specs=[vmem] * (pairs + owners),
        compiler_params=params,
        name="sort",
    )(*parcels)
    mine, posts = outs[:pairs], outs[pairs:]
    by_x = [shift(w, 0, 1) for w in mine]
    by_y = [shift(w, 0, 2) for w in mine]
    across = [shift(by_x[0], 0, 2), shift(by_y[1], 0, 1)]
    posts = [posts[0]] + [shift(posts[e], 0, e) for e in range(1, owners)]

    count = per_owner * slab_width
    depth = layers * owners * rows
    own, other = pl.pallas_call(
        functools.partial(gram_kernel, (layers, owners, per_owner, block_rows, block_count)),
        out_shape=[
            jax.ShapeDtypeStruct((count, panel_width), f32),
            jax.ShapeDtypeStruct((count, panel_width), bf16),
        ],
        in_specs=[vmem] * (owners * pairs + owners),
        out_specs=[vmem] * 2,
        scratch_shapes=[pltpu.VMEM((count, depth), bf16), pltpu.VMEM((depth, panel_width), bf16)],
        compiler_params=params,
        name="gram",
    )(*mine, *by_x, *by_y, *across, *posts)
    other = shift(other, 0, 0, 1)
    out = pl.pallas_call(
        inverse_kernel,
        out_shape=jax.ShapeDtypeStruct((count, panel_width), f32),
        in_specs=[vmem] * 3,
        out_specs=vmem,
        compiler_params=params,
        name="inverse",
    )(own, other, factor_inverse)
    return out.reshape(per_owner, slab_width, panel_width)


def solution(mesh):
    in_specs = (
        P(("rows", "cols"), None),
        P(("rows", "cols"), None),
        P(("rows", "cols")),
        P(("rows", "cols"), None),
        P(("rows", "cols"), None),
        P(),
        P(),
    )
    out_specs = P("cols", "rows", None)
    body = local if (mesh.shape["rows"], mesh.shape["cols"]) == (8, 4) else local_general
    return jax.shard_map(body, mesh=mesh, in_specs=in_specs, out_specs=out_specs, check_vma=False)
```

```python
import functools

import jax
import jax.numpy as jnp
from jax import lax
from jax.experimental import pallas as pl
from jax.experimental.pallas import tpu as pltpu
from jax.sharding import PartitionSpec as P

CAP = 2
GATHERED = 1 << 22


def tile_positions(tile_lists, tile_order):
    tile_count = tile_order.shape[0]
    matches = tile_lists[:, :, None] == tile_order[None, None, :]
    return jnp.sum(jnp.where(matches, jnp.arange(tile_count, dtype=jnp.int32), 0), axis=2)


def apply_inverse(tiles, factor_inverse):
    return jnp.einsum("ntp,qp->ntq", tiles, factor_inverse, precision=lax.Precision.HIGHEST)


def slot_codes(tile_lists, tile_masks, tile_order, owner_ids):
    block_count, slot_count = tile_lists.shape
    per_owner = tile_order.shape[0] // lax.axis_size("cols")
    positions = tile_positions(tile_lists, tile_order).reshape(-1)
    active = tile_masks.reshape(-1) == 1
    owner = positions // per_owner
    same = (owner[:, None] == owner[None, :]) & active[None, :]
    earlier = jnp.tril(jnp.ones(same.shape, bool), -1)
    rank = jnp.sum(same & earlier, axis=1)
    code = (
        (owner[None, None, :] == owner_ids[:, None, None])
        & (rank[None, None, :] == jnp.arange(CAP)[None, :, None])
        & active[None, None, :]
    )
    block = jnp.arange(block_count * slot_count) // slot_count
    place = positions % per_owner + per_owner * block
    return code, jnp.sum(jnp.where(code, place + 1, 0), axis=2) - 1


def local_general(jac, panel_jac, weights, tile_lists, tile_masks, tile_order, factor_inverse):
    block_count, slot_count = tile_lists.shape
    block_rows = jac.shape[0] // block_count
    tile_width = jac.shape[1] // slot_count
    slabs, owners = lax.axis_size("rows"), lax.axis_size("cols")
    devices = slabs * owners
    per_owner = tile_order.shape[0] // owners
    slab_width = tile_width // slabs
    bf16 = jnp.bfloat16
    weighted = (weights[:, None] * panel_jac).astype(bf16)
    code, places = slot_codes(tile_lists, tile_masks, tile_order, jnp.arange(owners))
    columns = jac.reshape(block_count, block_rows, slot_count, slabs, slab_width)
    chosen = code.astype(bf16).reshape(owners, CAP, block_count, slot_count)
    pieces = jnp.einsum("cjbk,bmkrt->rcjmt", chosen, columns, preferred_element_type=jnp.float32).astype(bf16)
    pieces = pieces.reshape(devices, -1)
    note = jnp.broadcast_to(places.astype(bf16)[None], (slabs, owners, CAP)).reshape(devices, CAP)
    note = jnp.pad(note, ((0, 0), (0, 128 - CAP)))
    sent = jnp.concatenate([pieces, note], axis=1)
    got = lax.all_to_all(sent, ("rows", "cols"), split_axis=0, concat_axis=0, tiled=True)
    size = pieces.shape[1]
    data = got[:, :size].reshape(devices, CAP, block_rows, slab_width)
    where = got[:, size : size + CAP].astype(jnp.int32)
    hot = (where[:, :, None] == jnp.arange(block_count * per_owner)).astype(bf16)
    hot = hot.reshape(devices, CAP, block_count, per_owner)
    mixed = jnp.einsum("djbn,djmt->dbmnt", hot, data, preferred_element_type=jnp.float32).astype(bf16)
    strips = max(1, devices * weighted.size * 2 // GATHERED)

    def strip_gram(strip):
        panels = lax.all_gather(strip, ("rows", "cols"), axis=0, tiled=True)
        panels = panels.reshape(devices, block_count, block_rows, -1)
        return jnp.einsum("dbmnt,dbmp->ntp", mixed, panels, preferred_element_type=jnp.float32)

    if strips == 1:
        gram = strip_gram(weighted)
    else:
        narrow = weighted.reshape(weighted.shape[0], strips, -1).swapaxes(0, 1)
        gram = jnp.moveaxis(lax.map(strip_gram, narrow), 0, 2)
        gram = gram.reshape(per_owner, slab_width, -1)
    return apply_inverse(gram, factor_inverse)


def shift(value, steps_z, flip_cols, flip_core=0):
    slabs, owners = lax.axis_size("rows"), lax.axis_size("cols")
    pairs = []
    for r in range(slabs):
        to_r = ((r // 2 + steps_z) % (slabs // 2)) * 2 + ((r % 2) ^ flip_core)
        for c in range(owners):
            pairs.append((r * owners + c, to_r * owners + (c ^ flip_cols)))
    return lax.ppermute(value, ("rows", "cols"), pairs)


def weigh_kernel(weights_hbm, panel_hbm, out_ref, weights_ref, panel_ref, sems):
    copies = [
        pltpu.make_async_copy(weights_hbm, weights_ref, sems.at[0]),
        pltpu.make_async_copy(panel_hbm, panel_ref, sems.at[1]),
    ]
    for copy in copies:
        copy.start()
    for copy in copies:
        copy.wait()
    rows = panel_ref.shape[0]
    row_ids = lax.broadcasted_iota(jnp.int32, (rows, rows), 0)
    lane_ids = lax.broadcasted_iota(jnp.int32, (rows, rows), 1)
    column = jnp.sum(jnp.where(row_ids == lane_ids, weights_ref[...], 0.0), axis=1, keepdims=True)
    out_ref[...] = (column * panel_ref[...].astype(jnp.float32)).astype(jnp.bfloat16)


def pack_kernel(sizes, lists_hbm, masks_hbm, order_hbm, jac_hbm, weighted_ref, *rest):
    layers, owners, per_owner, block_count, slot_count, block_rows, tile_width = sizes
    parcels = rest[:owners]
    lists_ref, masks_ref, order_ref, jac_ref, places_ref, turned_ref, sems = rest[owners:]
    copies = [
        pltpu.make_async_copy(order_hbm, order_ref, sems.at[0]),
        pltpu.make_async_copy(lists_hbm, lists_ref, sems.at[1]),
        pltpu.make_async_copy(masks_hbm, masks_ref, sems.at[2]),
        pltpu.make_async_copy(jac_hbm, jac_ref, sems.at[3]),
    ]
    for copy in copies:
        copy.start()
    f32, bf16 = jnp.float32, jnp.bfloat16
    panel_width = weighted_ref.shape[1]
    lane_group = CAP * block_rows
    slab = tile_width // layers
    part = slab // 2
    me_r, me_c = lax.axis_index("rows"), lax.axis_index("cols")
    me_z, me_core = me_r // 2, lax.rem(me_r, 2)
    for parcel in parcels[1:]:
        parcel[:, :panel_width] = weighted_ref[...]
    spots = [(parcel, panel_width if e else 0) for e, parcel in enumerate(parcels)]
    for copy in copies:
        copy.wait()

    for b in range(block_count):
        block = jac_ref[b * block_rows : (b + 1) * block_rows, :].astype(f32)
        start = b * slot_count * tile_width
        turned_ref[start : start + slot_count * tile_width, :] = block.T

    for i in range(order_ref.shape[0]):
        places_ref[order_ref[i]] = i
    slots = []
    for s in range(block_count * slot_count):
        b, k = divmod(s, slot_count)
        place = places_ref[lists_ref[b, k]]
        owner = jnp.int32(0)
        for c in range(1, owners):
            owner += (place >= c * per_owner).astype(jnp.int32)
        slots.append((place - owner * per_owner, jnp.where(masks_ref[b, k] == 1, owner, -1)))

    lane = lax.broadcasted_iota(jnp.int32, (16, CAP * block_count * block_rows), 1)
    for e, (parcel, start) in enumerate(spots):
        wanted = me_c ^ e
        found = jnp.int32(0)
        chosen = [jnp.int32(0)] * CAP
        codes = [jnp.int32(-1)] * CAP
        for s, (place, owner) in enumerate(slots):
            hit = owner == wanted
            for j in range(CAP):
                take = hit & (found == j)
                chosen[j] = jnp.where(take, s, chosen[j])
                codes[j] = jnp.where(take, place, codes[j])
            found += hit.astype(jnp.int32)
        note = jnp.full(lane.shape, -1, jnp.int32)
        for j in range(CAP):
            for b in range(block_count):
                at = (j * block_count + b) * block_rows
                here = (lane >= at) & (lane < at + block_rows)
                code = jnp.where(chosen[j] // slot_count == b, codes[j], -1)
                note = jnp.where(here, code, note)
        at = start + layers * lane_group
        parcel[:16, at : at + note.shape[1]] = note.astype(f32).astype(bf16)
        for k in range(layers):
            z = lax.rem(me_z + k, layers)
            for u in range(2):
                core = me_core ^ u
                for j in range(CAP):
                    first = pl.multiple_of(chosen[j] * tile_width + z * slab + core * part, part)
                    piece = turned_ref[pl.ds(first, part), :].astype(bf16)
                    to = start + k * lane_group + j * block_rows
                    parcel[u * part : (u + 1) * part, to : to + block_rows] = piece


def sort_kernel(sizes, starts, *refs):
    layers, owners, lane_group, wide = sizes
    parcels, line = refs[:owners], refs[owners : layers - 1 + owners]
    stacked, posts = refs[layers - 1 + owners], refs[layers + owners :]
    rows = parcels[0].shape[0]
    for k, ref in enumerate(line):
        stacked[k * rows : (k + 1) * rows, :] = ref[...]
    for e, (parcel, start) in enumerate(zip(parcels, starts)):
        at = start + layers * lane_group
        note = parcel[:16, at : at + wide]
        for k, post in enumerate(posts):
            piece = parcel[:, start + k * lane_group : start + (k + 1) * lane_group]
            post[:rows, e * lane_group : (e + 1) * lane_group] = piece
            low = rows + 16 * (e // 2)
            post[low : low + 16, (e % 2) * wide : (e % 2 + 1) * wide] = note


def cut_kernel(by_x_ref, by_y_ref, *refs):
    first_ref, second_ref = refs[-2:]
    half = first_ref.shape[0]
    first_ref[...] = by_x_ref[:half, :]
    second_ref[...] = by_y_ref[half:, :]


def place_kernel(sizes, *refs):
    layers, owners, per_owner, block_rows, block_count = sizes
    posts, (factor_ref, own_ref, other_ref, high_ref, low_ref) = refs[:layers], refs[layers:]
    f32, bf16 = jnp.float32, jnp.bfloat16
    high = factor_ref[...].astype(bf16)
    high_ref[...] = high
    low_ref[...] = (factor_ref[...] - high.astype(f32)).astype(bf16)
    rows = block_count * block_rows
    group, wide = CAP * block_rows, CAP * rows
    height = posts[0].shape[0] - 16 * (owners // 2)
    part = height // 2
    for e in range(owners):
        low = height + 16 * (e // 2)
        for h in range(layers // 2):
            pair = posts[2 * h : 2 * h + 2]
            codes = []
            for j in range(CAP):
                at = (e % 2) * wide + j * rows
                notes = [post[low : low + 16, at : at + rows].astype(f32) for post in pair]
                note = jnp.concatenate(notes, axis=1)
                codes.append(jnp.concatenate([note] * (part // 16), axis=0).astype(bf16))
            lanes = slice((e * layers + 2 * h) * rows, (e * layers + 2 * h + 2) * rows)
            for u, out_ref in ((0, own_ref), (1, other_ref)):
                columns = []
                for j in range(CAP):
                    at = e * group + j * block_rows
                    pieces = []
                    for post in pair:
                        piece = post[u * part : (u + 1) * part, at : at + block_rows].astype(f32)
                        pieces += [piece] * block_count
                    columns.append(jnp.concatenate(pieces, axis=1).astype(bf16))
                for n in range(per_owner):
                    placed = jnp.zeros(columns[0].shape, bf16)
                    for j in range(CAP):
                        placed = jnp.where(codes[j] == jnp.asarray(n, bf16), columns[j], placed)
                    out_ref[n * part : (n + 1) * part, lanes] = placed


def gram_kernel(parts, *refs):
    panels = refs[: len(parts)]
    placed_ref, high_ref, low_ref, out_ref, rows_ref = refs[len(parts) :]
    f32, bf16 = jnp.float32, jnp.bfloat16
    width = rows_ref.shape[1]
    at = 0
    for start, panel in zip(parts, panels):
        rows = panel.shape[0]
        rows_ref[at : at + rows, :] = panel[:, start : start + width]
        at += rows
    gram = jnp.dot(placed_ref[...], rows_ref[...], preferred_element_type=f32)
    gram_high = gram.astype(bf16)
    gram_low = (gram - gram_high.astype(f32)).astype(bf16)
    dims = (((1,), (1,)), ((), ()))
    half = width // 2
    for start, stop in ((0, half), (half, width)):
        high, low = high_ref[start:stop, :stop], low_ref[start:stop, :stop]
        a, b = gram_high[:, :stop], gram_low[:, :stop]
        total = lax.dot_general(a, low, dims, preferred_element_type=f32)
        total += lax.dot_general(b, high, dims, preferred_element_type=f32)
        total += lax.dot_general(a, high, dims, preferred_element_type=f32)
        out_ref[:, start:stop] = total.astype(out_ref.dtype)


def local(jac, panel_jac, weights, tile_lists, tile_masks, tile_order, factor_inverse):
    block_count, slot_count = tile_lists.shape
    rows, panel_width = panel_jac.shape
    block_rows = rows // block_count
    tile_width = jac.shape[1] // slot_count
    slabs, owners = lax.axis_size("rows"), lax.axis_size("cols")
    layers = slabs // 2
    per_owner = tile_order.shape[0] // owners
    slab_width = tile_width // slabs
    f32, bf16 = jnp.float32, jnp.bfloat16
    vmem, anywhere = pl.BlockSpec(memory_space=pltpu.VMEM), pl.BlockSpec(memory_space=pl.ANY)
    params = pltpu.CompilerParams(vmem_limit_bytes=48 << 20)
    shaped = jax.ShapeDtypeStruct

    def in_hbm(value):
        return pltpu.with_memory_space_constraint(value, pltpu.HBM)

    weighted = pl.pallas_call(
        weigh_kernel,
        out_shape=shaped((rows, panel_width), bf16),
        in_specs=[anywhere] * 2,
        out_specs=vmem,
        scratch_shapes=[
            pltpu.VMEM((1, rows), f32),
            pltpu.VMEM((rows, panel_width), bf16),
            pltpu.SemaphoreType.DMA((2,)),
        ],
        compiler_params=params,
        name="weigh",
    )(in_hbm(weights.reshape(1, rows)), in_hbm(panel_jac))
    line = [shift(weighted, k, 0) for k in range(1, layers)]

    lane_group = CAP * block_rows
    wide = CAP * rows
    sizes = (layers, owners, per_owner, block_count, slot_count, block_rows, tile_width)
    post = layers * lane_group + wide
    parcels = pl.pallas_call(
        functools.partial(pack_kernel, sizes),
        out_shape=[shaped((rows, post), bf16)] + [shaped((rows, panel_width + post), bf16)] * (owners - 1),
        in_specs=[anywhere] * 4 + [vmem],
        out_specs=[vmem] * owners,
        scratch_shapes=[
            pltpu.SMEM(tile_lists.shape, jnp.int32),
            pltpu.SMEM(tile_masks.shape, jnp.int32),
            pltpu.SMEM(tile_order.shape, jnp.int32),
            pltpu.VMEM(jac.shape, bf16),
            pltpu.SMEM(tile_order.shape, jnp.int32),
            pltpu.VMEM((block_count * slot_count * tile_width, block_rows), f32),
            pltpu.SemaphoreType.DMA((4,)),
        ],
        compiler_params=params,
        name="pack",
    )(in_hbm(tile_lists), in_hbm(tile_masks), in_hbm(tile_order), in_hbm(jac), weighted)
    parcels = [parcels[0]] + [shift(parcels[e], 0, e) for e in range(1, owners)]
    starts = [0] + [panel_width] * (owners - 1)

    height = 2 * slab_width
    letter = shaped((height + 16 * (owners // 2), max(owners * lane_group, 2 * wide)), bf16)
    others, *posts = pl.pallas_call(
        functools.partial(sort_kernel, (layers, owners, lane_group, wide), starts),
        out_shape=[shaped(((layers - 1) * rows, panel_width), bf16)] + [letter] * layers,
        in_specs=[vmem] * (layers - 1 + owners),
        out_specs=[vmem] * (layers + 1),
        compiler_params=params,
        name="sort",
    )(*parcels, *line)
    posts = [posts[0]] + [shift(posts[k], k, 0) for k in range(1, layers)]
    by_x, by_y = shift(others, 0, 1), shift(others, 0, 2)
    half = shaped((others.shape[0] // 2, panel_width), bf16)
    first, second = pl.pallas_call(
        cut_kernel,
        out_shape=[half] * 2,
        in_specs=[vmem] * 2 + [anywhere] * (layers - 1),
        out_specs=[vmem] * 2,
        compiler_params=params,
        name="cut",
    )(by_x, by_y, *posts[1:])
    across = [shift(first, 0, 2), shift(second, 0, 1)]

    count = per_owner * slab_width
    depth = layers * owners * rows
    own_placed, other_placed, high, low = pl.pallas_call(
        functools.partial(place_kernel, (layers, owners, per_owner, block_rows, block_count)),
        out_shape=[shaped((count, depth), bf16)] * 2 + [shaped(factor_inverse.shape, bf16)] * 2,
        in_specs=[vmem] * (layers + 1),
        out_specs=[vmem] * 4,
        compiler_params=params,
        name="place",
    )(*posts, factor_inverse)

    panels = [weighted, others, parcels[1], by_x, parcels[2], by_y, parcels[3], *across]
    parts = [0] * len(panels)

    def gram(placed, kind):
        return pl.pallas_call(
            functools.partial(gram_kernel, parts),
            out_shape=shaped((count, panel_width), kind),
            in_specs=[vmem] * (len(panels) + 3),
            out_specs=vmem,
            scratch_shapes=[pltpu.VMEM((depth, panel_width), bf16)],
            compiler_params=params,
            name="gram",
        )(*panels, placed, high, low)

    other = shift(gram(other_placed, bf16), 0, 0, 1)
    out = gram(own_placed, f32) + other.astype(f32)
    return out.reshape(per_owner, slab_width, panel_width)


def solution(mesh):
    in_specs = (
        P(("rows", "cols"), None),
        P(("rows", "cols"), None),
        P(("rows", "cols")),
        P(("rows", "cols"), None),
        P(("rows", "cols"), None),
        P(),
        P(),
    )
    out_specs = P("cols", "rows", None)
    body = local if (mesh.shape["rows"], mesh.shape["cols"]) == (8, 4) else local_general
    return jax.shard_map(body, mesh=mesh, in_specs=in_specs, out_specs=out_specs, check_vma=False)
```

```python
import functools

import jax
import jax.numpy as jnp
from jax import lax
from jax.experimental import pallas as pl
from jax.experimental.pallas import tpu as pltpu
from jax.sharding import PartitionSpec as P

CAP = 2
GATHERED = 1 << 22


def tile_positions(tile_lists, tile_order):
    tile_count = tile_order.shape[0]
    matches = tile_lists[:, :, None] == tile_order[None, None, :]
    return jnp.sum(jnp.where(matches, jnp.arange(tile_count, dtype=jnp.int32), 0), axis=2)


def apply_inverse(tiles, factor_inverse):
    return jnp.einsum("ntp,qp->ntq", tiles, factor_inverse, precision=lax.Precision.HIGHEST)


def slot_codes(tile_lists, tile_masks, tile_order, owner_ids):
    block_count, slot_count = tile_lists.shape
    per_owner = tile_order.shape[0] // lax.axis_size("cols")
    positions = tile_positions(tile_lists, tile_order).reshape(-1)
    active = tile_masks.reshape(-1) == 1
    owner = positions // per_owner
    same = (owner[:, None] == owner[None, :]) & active[None, :]
    earlier = jnp.tril(jnp.ones(same.shape, bool), -1)
    rank = jnp.sum(same & earlier, axis=1)
    code = (
        (owner[None, None, :] == owner_ids[:, None, None])
        & (rank[None, None, :] == jnp.arange(CAP)[None, :, None])
        & active[None, None, :]
    )
    block = jnp.arange(block_count * slot_count) // slot_count
    place = positions % per_owner + per_owner * block
    return code, jnp.sum(jnp.where(code, place + 1, 0), axis=2) - 1


def local_general(jac, panel_jac, weights, tile_lists, tile_masks, tile_order, factor_inverse):
    block_count, slot_count = tile_lists.shape
    block_rows = jac.shape[0] // block_count
    tile_width = jac.shape[1] // slot_count
    slabs, owners = lax.axis_size("rows"), lax.axis_size("cols")
    devices = slabs * owners
    per_owner = tile_order.shape[0] // owners
    slab_width = tile_width // slabs
    bf16 = jnp.bfloat16
    weighted = (weights[:, None] * panel_jac).astype(bf16)
    code, places = slot_codes(tile_lists, tile_masks, tile_order, jnp.arange(owners))
    columns = jac.reshape(block_count, block_rows, slot_count, slabs, slab_width)
    chosen = code.astype(bf16).reshape(owners, CAP, block_count, slot_count)
    pieces = jnp.einsum("cjbk,bmkrt->rcjmt", chosen, columns, preferred_element_type=jnp.float32).astype(bf16)
    pieces = pieces.reshape(devices, -1)
    note = jnp.broadcast_to(places.astype(bf16)[None], (slabs, owners, CAP)).reshape(devices, CAP)
    note = jnp.pad(note, ((0, 0), (0, 128 - CAP)))
    sent = jnp.concatenate([pieces, note], axis=1)
    got = lax.all_to_all(sent, ("rows", "cols"), split_axis=0, concat_axis=0, tiled=True)
    size = pieces.shape[1]
    data = got[:, :size].reshape(devices, CAP, block_rows, slab_width)
    where = got[:, size : size + CAP].astype(jnp.int32)
    hot = (where[:, :, None] == jnp.arange(block_count * per_owner)).astype(bf16)
    hot = hot.reshape(devices, CAP, block_count, per_owner)
    mixed = jnp.einsum("djbn,djmt->dbmnt", hot, data, preferred_element_type=jnp.float32).astype(bf16)
    strips = max(1, devices * weighted.size * 2 // GATHERED)

    def strip_gram(strip):
        panels = lax.all_gather(strip, ("rows", "cols"), axis=0, tiled=True)
        panels = panels.reshape(devices, block_count, block_rows, -1)
        return jnp.einsum("dbmnt,dbmp->ntp", mixed, panels, preferred_element_type=jnp.float32)

    if strips == 1:
        gram = strip_gram(weighted)
    else:
        narrow = weighted.reshape(weighted.shape[0], strips, -1).swapaxes(0, 1)
        gram = jnp.moveaxis(lax.map(strip_gram, narrow), 0, 2)
        gram = gram.reshape(per_owner, slab_width, -1)
    return apply_inverse(gram, factor_inverse)


def shift(value, steps_z, flip_cols, flip_core=0):
    slabs, owners = lax.axis_size("rows"), lax.axis_size("cols")
    pairs = []
    for r in range(slabs):
        to_r = ((r // 2 + steps_z) % (slabs // 2)) * 2 + ((r % 2) ^ flip_core)
        for c in range(owners):
            pairs.append((r * owners + c, to_r * owners + (c ^ flip_cols)))
    return lax.ppermute(value, ("rows", "cols"), pairs)


def weigh_kernel(weights_hbm, panel_hbm, out_ref, weights_ref, panel_ref, sems):
    copies = [
        pltpu.make_async_copy(weights_hbm, weights_ref, sems.at[0]),
        pltpu.make_async_copy(panel_hbm, panel_ref, sems.at[1]),
    ]
    for copy in copies:
        copy.start()
    for copy in copies:
        copy.wait()
    rows = panel_ref.shape[0]
    row_ids = lax.broadcasted_iota(jnp.int32, (rows, rows), 0)
    lane_ids = lax.broadcasted_iota(jnp.int32, (rows, rows), 1)
    column = jnp.sum(jnp.where(row_ids == lane_ids, weights_ref[...], 0.0), axis=1, keepdims=True)
    out_ref[...] = (column * panel_ref[...].astype(jnp.float32)).astype(jnp.bfloat16)


def pack_kernel(sizes, lists_hbm, masks_hbm, order_hbm, jac_hbm, weighted_ref, *rest):
    layers, owners, per_owner, block_count, slot_count, block_rows, tile_width = sizes
    kept_ref, to_x_ref, to_y_ref, lists_ref, masks_ref, order_ref, jac_ref, places_ref, turned_ref, sems = rest
    copies = [
        pltpu.make_async_copy(order_hbm, order_ref, sems.at[0]),
        pltpu.make_async_copy(lists_hbm, lists_ref, sems.at[1]),
        pltpu.make_async_copy(masks_hbm, masks_ref, sems.at[2]),
        pltpu.make_async_copy(jac_hbm, jac_ref, sems.at[3]),
    ]
    for copy in copies:
        copy.start()
    f32, bf16 = jnp.float32, jnp.bfloat16
    width = weighted_ref.shape[1]
    lane_group = CAP * block_rows
    post = layers * lane_group
    slab = tile_width // layers
    part = slab // 2
    me_r, me_c = lax.axis_index("rows"), lax.axis_index("cols")
    me_z, me_core = me_r // 2, lax.rem(me_r, 2)
    to_x_ref[:, :width] = weighted_ref[...]
    to_y_ref[:, :width] = weighted_ref[...]
    for copy in copies:
        copy.wait()

    for b in range(block_count):
        block = jac_ref[b * block_rows : (b + 1) * block_rows, :].astype(f32)
        start = b * slot_count * tile_width
        turned_ref[start : start + slot_count * tile_width, :] = block.T

    for i in range(order_ref.shape[0]):
        places_ref[order_ref[i]] = i
    slots = []
    for s in range(block_count * slot_count):
        b, k = divmod(s, slot_count)
        place = places_ref[lists_ref[b, k]]
        owner = jnp.int32(0)
        for c in range(1, owners):
            owner += (place >= c * per_owner).astype(jnp.int32)
        slots.append((place - owner * per_owner, jnp.where(masks_ref[b, k] == 1, owner, -1)))

    shape = (16, CAP * block_count * block_rows)
    lane, row = lax.broadcasted_iota(jnp.int32, shape, 1), lax.broadcasted_iota(jnp.int32, shape, 0)
    notes = []
    spots = [(kept_ref, 0), (to_x_ref, width), (to_y_ref, width), (to_x_ref, width + post)]
    for e, (parcel, start) in enumerate(spots):
        wanted = me_c ^ e
        found = jnp.int32(0)
        chosen = [jnp.int32(0)] * CAP
        codes = [jnp.int32(-1)] * CAP
        for s, (place, owner) in enumerate(slots):
            hit = owner == wanted
            for j in range(CAP):
                take = hit & (found == j)
                chosen[j] = jnp.where(take, s, chosen[j])
                codes[j] = jnp.where(take, place, codes[j])
            found += hit.astype(jnp.int32)
        note = jnp.full(shape, -1, jnp.int32)
        for j in range(CAP):
            for b in range(block_count):
                at = (j * block_count + b) * block_rows
                here = (lane >= at) & (lane < at + block_rows)
                code = jnp.where(chosen[j] // slot_count == b, codes[j], -1)
                note = jnp.where(here, code, note)
        notes.append(note)
        for k in range(layers):
            z = lax.rem(me_z + k, layers)
            for u in range(2):
                core = me_core ^ u
                for j in range(CAP):
                    first = pl.multiple_of(chosen[j] * tile_width + z * slab + core * part, part)
                    piece = turned_ref[pl.ds(first, part), :].astype(bf16)
                    to = start + k * lane_group + j * block_rows
                    parcel[u * part : (u + 1) * part, to : to + block_rows] = piece
    kept_ref[:16, post:] = notes[0].astype(f32).astype(bf16)
    to_x_ref[:16, width + 2 * post :] = jnp.where(row == 0, notes[1], notes[3]).astype(f32).astype(bf16)
    to_y_ref[:16, width + post :] = notes[2].astype(f32).astype(bf16)


def row_of(block, i):
    ids = lax.broadcasted_iota(jnp.int32, block.shape, 0)
    return jnp.sum(jnp.where(ids == i, block.astype(jnp.float32), 0.0), axis=0, keepdims=True)


def rows_from(notes):
    ids = lax.broadcasted_iota(jnp.int32, (16, notes[0].shape[1]), 0)
    block = jnp.full(ids.shape, -1.0, jnp.float32)
    for i, note in enumerate(notes):
        block = jnp.where(ids == i, note, block)
    return block.astype(jnp.bfloat16)


def sort_kernel(sizes, kept_ref, from_x_ref, from_y_ref, *refs):
    layers, width, lane_group, wide = sizes
    line, (stacked, *posts) = refs[: layers - 1], refs[layers - 1 :]
    post = layers * lane_group
    rows = kept_ref.shape[0]
    for k, ref in enumerate(line):
        stacked[k * rows : (k + 1) * rows, :] = ref[...]
    spots = [(kept_ref, 0), (from_x_ref, width), (from_y_ref, width), (from_x_ref, width + post)]
    notes = [row_of(ref[:16, ref.shape[1] - wide :], int(e == 3)) for e, (ref, start) in enumerate(spots)]
    block = rows_from(notes)
    for k, out in enumerate(posts):
        for e, (ref, start) in enumerate(spots):
            piece = ref[:, start + k * lane_group : start + (k + 1) * lane_group]
            out[:rows, e * lane_group : (e + 1) * lane_group] = piece
        out[rows:, :wide] = block


def cut_kernel(sizes, from_y_ref, by_x_ref, by_y_ref, *refs):
    layers, width, lane_group, wide = sizes
    posts, (to_y_ref, to_x_ref) = refs[:layers], refs[layers:]
    rows = from_y_ref.shape[0]
    half = by_x_ref.shape[0] // 2
    part = rows // 2
    post = layers * lane_group
    to_y_ref[:half, :] = by_x_ref[:half, :]
    for k, ref in enumerate(posts):
        for u in range(2):
            piece = ref[u * part : (u + 1) * part, 3 * lane_group : 4 * lane_group]
            at = u * post + k * lane_group
            to_y_ref[half : half + part, at : at + lane_group] = piece
    notes = [row_of(ref[rows:, :wide], 3) for ref in posts]
    to_y_ref[half + part :, :wide] = rows_from(notes)
    to_x_ref[:rows, :] = from_y_ref[:, :width]
    to_x_ref[rows:, :] = by_y_ref[half:, :]


def place(out_ref, lanes, per_owner, pieces, notes, sizes):
    block_count, block_rows = sizes
    f32, bf16 = jnp.float32, jnp.bfloat16
    part, rows = pieces[0].shape[0], block_count * block_rows
    columns, codes = [], []
    for j in range(CAP):
        parts = []
        for piece in pieces:
            parts += [piece[:, j * block_rows : (j + 1) * block_rows].astype(f32)] * block_count
        columns.append(jnp.concatenate(parts, axis=1).astype(bf16))
        note = jnp.concatenate([note[:, j * rows : (j + 1) * rows] for note in notes], axis=1)
        codes.append(jnp.broadcast_to(note, columns[j].shape).astype(bf16))
    for n in range(per_owner):
        placed = jnp.zeros(columns[0].shape, bf16)
        for j in range(CAP):
            placed = jnp.where(codes[j] == jnp.asarray(n, bf16), columns[j], placed)
        out_ref[n * part : (n + 1) * part, lanes] = placed


def near_kernel(sizes, *refs):
    layers, owners, per_owner, block_count, block_rows = sizes
    panels, posts, factor_ref = refs[: 2 * (owners - 1)], refs[2 * (owners - 1) :][:layers], refs[2 * owners - 2 + layers]
    own_ref, other_ref, high_ref, low_ref, placed_ref, rows_ref = refs[2 * owners - 1 + layers :]
    f32, bf16 = jnp.float32, jnp.bfloat16
    high = factor_ref[...].astype(bf16)
    high_ref[...] = high
    low_ref[...] = (factor_ref[...] - high.astype(f32)).astype(bf16)
    rows = block_count * block_rows
    group, wide = CAP * block_rows, CAP * rows
    part = rows // 2
    width = rows_ref.shape[1]
    at = 0
    for panel in panels:
        rows_ref[at : at + panel.shape[0], :] = panel[:, :width]
        at += panel.shape[0]
    for u, out_ref in ((1, other_ref), (0, own_ref)):
        for e in range(owners - 1):
            for h in range(layers // 2):
                pair = posts[2 * h : 2 * h + 2]
                pieces = [post[u * part : (u + 1) * part, e * group : (e + 1) * group] for post in pair]
                notes = [row_of(post[rows:, :wide], e) for post in pair]
                start = (e * layers + 2 * h) * rows
                place(placed_ref, slice(start, start + 2 * rows), per_owner, pieces, notes, (block_count, block_rows))
        out_ref[...] = jnp.dot(placed_ref[...], rows_ref[...], preferred_element_type=f32)


def far_kernel(sizes, u, near_ref, by_y_ref, by_x_ref, high_ref, low_ref, out_ref, placed_ref, rows_ref):
    layers, owners, per_owner, block_count, block_rows = sizes
    f32, bf16 = jnp.float32, jnp.bfloat16
    rows = block_count * block_rows
    group, wide = CAP * block_rows, CAP * rows
    part = rows // 2
    width = rows_ref.shape[1]
    half = (layers - 1) * rows // 2
    rows_ref[:rows, :] = by_x_ref[:rows, :]
    rows_ref[rows : rows + half, :] = by_y_ref[:half, :]
    rows_ref[rows + half :, :] = by_x_ref[rows:, :]
    for h in range(layers // 2):
        pieces, notes = [], []
        for k in (2 * h, 2 * h + 1):
            at = (u * layers + k) * group
            pieces.append(by_y_ref[half : half + part, at : at + group])
            notes.append(row_of(by_y_ref[half + part :, :wide], k))
        start = 2 * h * rows
        place(placed_ref, slice(start, start + 2 * rows), per_owner, pieces, notes, (block_count, block_rows))
    gram = near_ref[...] + jnp.dot(placed_ref[...], rows_ref[...], preferred_element_type=f32)
    gram_high = gram.astype(bf16)
    gram_low = (gram - gram_high.astype(f32)).astype(bf16)
    dims = (((1,), (1,)), ((), ()))
    for start, stop in ((0, width // 2), (width // 2, width)):
        high, low = high_ref[start:stop, :stop], low_ref[start:stop, :stop]
        a, b = gram_high[:, :stop], gram_low[:, :stop]
        total = lax.dot_general(a, low, dims, preferred_element_type=f32)
        total += lax.dot_general(b, high, dims, preferred_element_type=f32)
        total += lax.dot_general(a, high, dims, preferred_element_type=f32)
        out_ref[:, start:stop] = total.astype(out_ref.dtype)


def add_kernel(own_ref, other_ref, out_hbm, sum_ref, sems):
    strips = sems.shape[0]
    height = sum_ref.shape[0] // strips
    copies = []
    for i in range(strips):
        here = pl.ds(i * height, height)
        sum_ref[here, :] = own_ref[here, :] + other_ref[here, :].astype(jnp.float32)
        copies.append(pltpu.make_async_copy(sum_ref.at[here, :], out_hbm.at[here, :], sems.at[i]))
        copies[-1].start()
    for copy in copies:
        copy.wait()


def local(jac, panel_jac, weights, tile_lists, tile_masks, tile_order, factor_inverse):
    block_count, slot_count = tile_lists.shape
    rows, panel_width = panel_jac.shape
    block_rows = rows // block_count
    tile_width = jac.shape[1] // slot_count
    slabs, owners = lax.axis_size("rows"), lax.axis_size("cols")
    layers = slabs // 2
    per_owner = tile_order.shape[0] // owners
    slab_width = tile_width // slabs
    f32, bf16 = jnp.float32, jnp.bfloat16
    vmem, anywhere = pl.BlockSpec(memory_space=pltpu.VMEM), pl.BlockSpec(memory_space=pl.ANY)
    params = pltpu.CompilerParams(vmem_limit_bytes=24 << 20)
    shaped = jax.ShapeDtypeStruct

    def in_hbm(value):
        return pltpu.with_memory_space_constraint(value, pltpu.HBM)

    weighted = pl.pallas_call(
        weigh_kernel,
        out_shape=shaped((rows, panel_width), bf16),
        in_specs=[anywhere] * 2,
        out_specs=vmem,
        scratch_shapes=[
            pltpu.VMEM((1, rows), f32),
            pltpu.VMEM((rows, panel_width), bf16),
            pltpu.SemaphoreType.DMA((2,)),
        ],
        compiler_params=params,
        name="weigh",
    )(in_hbm(weights.reshape(1, rows)), in_hbm(panel_jac))
    line = [shift(weighted, k, 0) for k in range(1, layers)]

    lane_group = CAP * block_rows
    post = layers * lane_group
    wide = CAP * rows
    sizes = (layers, owners, per_owner, block_count, slot_count, block_rows, tile_width)
    kept, to_x, to_y = pl.pallas_call(
        functools.partial(pack_kernel, sizes),
        out_shape=[
            shaped((rows, width), bf16)
            for width in (post + wide, panel_width + 2 * post + wide, panel_width + post + wide)
        ],
        in_specs=[anywhere] * 4 + [vmem],
        out_specs=[vmem] * 3,
        scratch_shapes=[
            pltpu.SMEM(tile_lists.shape, jnp.int32),
            pltpu.SMEM(tile_masks.shape, jnp.int32),
            pltpu.SMEM(tile_order.shape, jnp.int32),
            pltpu.VMEM(jac.shape, bf16),
            pltpu.SMEM(tile_order.shape, jnp.int32),
            pltpu.VMEM((block_count * slot_count * tile_width, block_rows), f32),
            pltpu.SemaphoreType.DMA((4,)),
        ],
        compiler_params=params,
        name="pack",
    )(in_hbm(tile_lists), in_hbm(tile_masks), in_hbm(tile_order), in_hbm(jac), weighted)
    from_x, from_y = shift(to_x, 0, 1), shift(to_y, 0, 2)

    sizes = (layers, panel_width, lane_group, wide)
    others, *posts = pl.pallas_call(
        functools.partial(sort_kernel, sizes),
        out_shape=[shaped(((layers - 1) * rows, panel_width), bf16)]
        + [shaped((rows + 16, owners * lane_group), bf16)] * layers,
        in_specs=[vmem] * (layers + 2),
        out_specs=[vmem] * (layers + 1),
        compiler_params=params,
        name="sort",
    )(kept, from_x, from_y, *line)
    posts = [posts[0]] + [shift(posts[k], k, 0) for k in range(1, layers)]
    by_x, by_y = shift(others, 0, 1), shift(others, 0, 2)

    half = others.shape[0] // 2
    to_y, to_x = pl.pallas_call(
        functools.partial(cut_kernel, sizes),
        out_shape=[
            shaped((half + rows // 2 + 16, panel_width), bf16),
            shaped((rows + half, panel_width), bf16),
        ],
        in_specs=[vmem] * (layers + 3),
        out_specs=[vmem] * 2,
        compiler_params=params,
        name="cut",
    )(from_y, by_x, by_y, *posts)
    across_y, across_x = shift(to_y, 0, 2), shift(to_x, 0, 1)

    count = per_owner * slab_width
    depth = layers * rows
    sizes = (layers, owners, per_owner, block_count, block_rows)
    gram = shaped((count, panel_width), f32)
    panels = [weighted, others, from_x, by_x, from_y, by_y]
    own, other, high, low = pl.pallas_call(
        functools.partial(near_kernel, sizes),
        out_shape=[gram] * 2 + [shaped(factor_inverse.shape, bf16)] * 2,
        in_specs=[vmem] * (len(panels) + layers + 1),
        out_specs=[vmem] * 4,
        scratch_shapes=[
            pltpu.VMEM((count, (owners - 1) * depth), bf16),
            pltpu.VMEM(((owners - 1) * depth, panel_width), bf16),
        ],
        compiler_params=params,
        name="near",
    )(*panels, *posts, factor_inverse)

    def far(u, near, kind):
        return pl.pallas_call(
            functools.partial(far_kernel, sizes, u),
            out_shape=shaped((count, panel_width), kind),
            in_specs=[vmem] * 5,
            out_specs=vmem,
            scratch_shapes=[pltpu.VMEM((count, depth), bf16), pltpu.VMEM((depth, panel_width), bf16)],
            compiler_params=params,
            name="far",
        )(near, across_y, across_x, high, low)

    other = shift(far(1, other, bf16), 0, 0, 1)
    out = pl.pallas_call(
        add_kernel,
        out_shape=shaped((count, panel_width), f32),
        in_specs=[vmem] * 2,
        out_specs=anywhere,
        scratch_shapes=[pltpu.VMEM((count, panel_width), f32), pltpu.SemaphoreType.DMA((4,))],
        compiler_params=params,
        name="add",
    )(far(0, own, f32), other)
    return out.reshape(per_owner, slab_width, panel_width)


def solution(mesh):
    in_specs = (
        P(("rows", "cols"), None),
        P(("rows", "cols"), None),
        P(("rows", "cols")),
        P(("rows", "cols"), None),
        P(("rows", "cols"), None),
        P(),
        P(),
    )
    out_specs = P("cols", "rows", None)
    body = local if (mesh.shape["rows"], mesh.shape["cols"]) == (8, 4) else local_general
    return jax.shard_map(body, mesh=mesh, in_specs=in_specs, out_specs=out_specs, check_vma=False)
```

```python
import functools

import jax
import jax.numpy as jnp
from jax import lax
from jax.experimental import pallas as pl
from jax.experimental.pallas import tpu as pltpu
from jax.sharding import PartitionSpec as P

CAP = 2
GATHERED = 1 << 22


def tile_positions(tile_lists, tile_order):
    tile_count = tile_order.shape[0]
    matches = tile_lists[:, :, None] == tile_order[None, None, :]
    return jnp.sum(jnp.where(matches, jnp.arange(tile_count, dtype=jnp.int32), 0), axis=2)


def apply_inverse(tiles, factor_inverse):
    return jnp.einsum("ntp,qp->ntq", tiles, factor_inverse, precision=lax.Precision.HIGHEST)


def slot_codes(tile_lists, tile_masks, tile_order, owner_ids):
    block_count, slot_count = tile_lists.shape
    per_owner = tile_order.shape[0] // lax.axis_size("cols")
    positions = tile_positions(tile_lists, tile_order).reshape(-1)
    active = tile_masks.reshape(-1) == 1
    owner = positions // per_owner
    same = (owner[:, None] == owner[None, :]) & active[None, :]
    earlier = jnp.tril(jnp.ones(same.shape, bool), -1)
    rank = jnp.sum(same & earlier, axis=1)
    code = (
        (owner[None, None, :] == owner_ids[:, None, None])
        & (rank[None, None, :] == jnp.arange(CAP)[None, :, None])
        & active[None, None, :]
    )
    block = jnp.arange(block_count * slot_count) // slot_count
    place = positions % per_owner + per_owner * block
    return code, jnp.sum(jnp.where(code, place + 1, 0), axis=2) - 1


def local_general(jac, panel_jac, weights, tile_lists, tile_masks, tile_order, factor_inverse):
    block_count, slot_count = tile_lists.shape
    block_rows = jac.shape[0] // block_count
    tile_width = jac.shape[1] // slot_count
    slabs, owners = lax.axis_size("rows"), lax.axis_size("cols")
    devices = slabs * owners
    per_owner = tile_order.shape[0] // owners
    slab_width = tile_width // slabs
    bf16 = jnp.bfloat16
    weighted = (weights[:, None] * panel_jac).astype(bf16)
    code, places = slot_codes(tile_lists, tile_masks, tile_order, jnp.arange(owners))
    columns = jac.reshape(block_count, block_rows, slot_count, slabs, slab_width)
    chosen = code.astype(bf16).reshape(owners, CAP, block_count, slot_count)
    pieces = jnp.einsum("cjbk,bmkrt->rcjmt", chosen, columns, preferred_element_type=jnp.float32).astype(bf16)
    pieces = pieces.reshape(devices, -1)
    note = jnp.broadcast_to(places.astype(bf16)[None], (slabs, owners, CAP)).reshape(devices, CAP)
    note = jnp.pad(note, ((0, 0), (0, 128 - CAP)))
    sent = jnp.concatenate([pieces, note], axis=1)
    got = lax.all_to_all(sent, ("rows", "cols"), split_axis=0, concat_axis=0, tiled=True)
    size = pieces.shape[1]
    data = got[:, :size].reshape(devices, CAP, block_rows, slab_width)
    where = got[:, size : size + CAP].astype(jnp.int32)
    hot = (where[:, :, None] == jnp.arange(block_count * per_owner)).astype(bf16)
    hot = hot.reshape(devices, CAP, block_count, per_owner)
    mixed = jnp.einsum("djbn,djmt->dbmnt", hot, data, preferred_element_type=jnp.float32).astype(bf16)
    strips = max(1, devices * weighted.size * 2 // GATHERED)

    def strip_gram(strip):
        panels = lax.all_gather(strip, ("rows", "cols"), axis=0, tiled=True)
        panels = panels.reshape(devices, block_count, block_rows, -1)
        return jnp.einsum("dbmnt,dbmp->ntp", mixed, panels, preferred_element_type=jnp.float32)

    if strips == 1:
        gram = strip_gram(weighted)
    else:
        narrow = weighted.reshape(weighted.shape[0], strips, -1).swapaxes(0, 1)
        gram = jnp.moveaxis(lax.map(strip_gram, narrow), 0, 2)
        gram = gram.reshape(per_owner, slab_width, -1)
    return apply_inverse(gram, factor_inverse)


def shift(value, steps_z, flip_cols, flip_core=0):
    slabs, owners = lax.axis_size("rows"), lax.axis_size("cols")
    pairs = []
    for r in range(slabs):
        to_r = ((r // 2 + steps_z) % (slabs // 2)) * 2 + ((r % 2) ^ flip_core)
        for c in range(owners):
            pairs.append((r * owners + c, to_r * owners + (c ^ flip_cols)))
    return lax.ppermute(value, ("rows", "cols"), pairs)


def pack_kernel(sizes, lists_hbm, masks_hbm, order_hbm, weights_hbm, panel_hbm, jac_hbm, *refs):
    layers, owners, per_owner, block_count, slot_count, block_rows, tile_width = sizes
    weighted_ref, kept_ref, to_x_ref, to_y_ref = refs[:4]
    lists_ref, masks_ref, order_ref, weights_ref, panel_ref, jac_ref, places_ref, turned_ref, sems = refs[4:]
    copies = [
        pltpu.make_async_copy(order_hbm, order_ref, sems.at[0]),
        pltpu.make_async_copy(lists_hbm, lists_ref, sems.at[1]),
        pltpu.make_async_copy(masks_hbm, masks_ref, sems.at[2]),
        pltpu.make_async_copy(weights_hbm, weights_ref, sems.at[3]),
        pltpu.make_async_copy(panel_hbm, panel_ref, sems.at[4]),
        pltpu.make_async_copy(jac_hbm, jac_ref, sems.at[5]),
    ]
    for copy in copies:
        copy.start()
    f32, bf16 = jnp.float32, jnp.bfloat16
    rows, width = panel_ref.shape
    lane_group = CAP * block_rows
    post = layers * lane_group
    slab = tile_width // layers
    part = slab // 2
    me_r, me_c = lax.axis_index("rows"), lax.axis_index("cols")
    me_z, me_core = me_r // 2, lax.rem(me_r, 2)
    for copy in copies:
        copy.wait()

    row_ids = lax.broadcasted_iota(jnp.int32, (rows, rows), 0)
    lane_ids = lax.broadcasted_iota(jnp.int32, (rows, rows), 1)
    column = jnp.sum(jnp.where(row_ids == lane_ids, weights_ref[...], 0.0), axis=1, keepdims=True)
    weighted = (column * panel_ref[...].astype(f32)).astype(bf16)
    weighted_ref[...] = weighted
    to_x_ref[:, :width] = weighted
    to_y_ref[:, :width] = weighted

    for b in range(block_count):
        block = jac_ref[b * block_rows : (b + 1) * block_rows, :].astype(f32)
        start = b * slot_count * tile_width
        turned_ref[start : start + slot_count * tile_width, :] = block.T

    for i in range(order_ref.shape[0]):
        places_ref[order_ref[i]] = i
    slots = []
    for s in range(block_count * slot_count):
        b, k = divmod(s, slot_count)
        place = places_ref[lists_ref[b, k]]
        owner = jnp.int32(0)
        for c in range(1, owners):
            owner += (place >= c * per_owner).astype(jnp.int32)
        slots.append((place - owner * per_owner, jnp.where(masks_ref[b, k] == 1, owner, -1)))

    shape = (16, CAP * block_count * block_rows)
    lane, row = lax.broadcasted_iota(jnp.int32, shape, 1), lax.broadcasted_iota(jnp.int32, shape, 0)
    notes = []
    spots = [(kept_ref, 0), (to_x_ref, width), (to_y_ref, width), (to_x_ref, width + post)]
    for e, (parcel, start) in enumerate(spots):
        wanted = me_c ^ e
        found = jnp.int32(0)
        chosen = [jnp.int32(0)] * CAP
        codes = [jnp.int32(-1)] * CAP
        for s, (place, owner) in enumerate(slots):
            hit = owner == wanted
            for j in range(CAP):
                take = hit & (found == j)
                chosen[j] = jnp.where(take, s, chosen[j])
                codes[j] = jnp.where(take, place, codes[j])
            found += hit.astype(jnp.int32)
        note = jnp.full(shape, -1, jnp.int32)
        for j in range(CAP):
            for b in range(block_count):
                at = (j * block_count + b) * block_rows
                here = (lane >= at) & (lane < at + block_rows)
                code = jnp.where(chosen[j] // slot_count == b, codes[j], -1)
                note = jnp.where(here, code, note)
        notes.append(note)
        for k in range(layers):
            z = lax.rem(me_z + k, layers)
            for u in range(2):
                core = me_core ^ u
                for j in range(CAP):
                    first = pl.multiple_of(chosen[j] * tile_width + z * slab + core * part, part)
                    piece = turned_ref[pl.ds(first, part), :].astype(bf16)
                    to = start + k * lane_group + j * block_rows
                    parcel[u * part : (u + 1) * part, to : to + block_rows] = piece
    kept_ref[:16, post:] = notes[0].astype(f32).astype(bf16)
    to_x_ref[:16, width + 2 * post :] = jnp.where(row == 0, notes[1], notes[3]).astype(f32).astype(bf16)
    to_y_ref[:16, width + post :] = notes[2].astype(f32).astype(bf16)


def row_of(block, i):
    ids = lax.broadcasted_iota(jnp.int32, block.shape, 0)
    return jnp.sum(jnp.where(ids == i, block.astype(jnp.float32), 0.0), axis=0, keepdims=True)


def rows_from(notes):
    ids = lax.broadcasted_iota(jnp.int32, (16, notes[0].shape[1]), 0)
    block = jnp.full(ids.shape, -1.0, jnp.float32)
    for i, note in enumerate(notes):
        block = jnp.where(ids == i, note, block)
    return block.astype(jnp.bfloat16)


def sort_kernel(sizes, kept_ref, from_x_ref, from_y_ref, *refs):
    layers, width, lane_group, wide = sizes
    line, (stacked, *posts) = refs[: layers - 1], refs[layers - 1 :]
    post = layers * lane_group
    rows = kept_ref.shape[0]
    for k, ref in enumerate(line):
        stacked[k * rows : (k + 1) * rows, :] = ref[...]
    spots = [(kept_ref, 0), (from_x_ref, width), (from_y_ref, width), (from_x_ref, width + post)]
    notes = [row_of(ref[:16, ref.shape[1] - wide :], int(e == 3)) for e, (ref, start) in enumerate(spots)]
    block = rows_from(notes)
    for k, out in enumerate(posts):
        for e, (ref, start) in enumerate(spots):
            piece = ref[:, start + k * lane_group : start + (k + 1) * lane_group]
            out[:rows, e * lane_group : (e + 1) * lane_group] = piece
        out[rows:, :wide] = block


def cut_kernel(sizes, from_y_ref, by_x_ref, by_y_ref, *refs):
    layers, width, lane_group, wide = sizes
    posts, (to_y_ref, to_x_ref) = refs[:layers], refs[layers:]
    rows = from_y_ref.shape[0]
    half = by_x_ref.shape[0] // 2
    part = rows // 2
    post = layers * lane_group
    to_y_ref[:half, :] = by_x_ref[:half, :]
    for k, ref in enumerate(posts):
        for u in range(2):
            piece = ref[u * part : (u + 1) * part, 3 * lane_group : 4 * lane_group]
            at = u * post + k * lane_group
            to_y_ref[half : half + part, at : at + lane_group] = piece
    notes = [row_of(ref[rows:, :wide], 3) for ref in posts]
    to_y_ref[half + part :, :wide] = rows_from(notes)
    to_x_ref[:rows, :] = from_y_ref[:, :width]
    to_x_ref[rows:, :] = by_y_ref[half:, :]


def place(out_ref, lanes, per_owner, pieces, notes, sizes):
    block_count, block_rows = sizes
    f32, bf16 = jnp.float32, jnp.bfloat16
    part, rows = pieces[0].shape[0], block_count * block_rows
    columns, codes = [], []
    for j in range(CAP):
        parts = []
        for piece in pieces:
            parts += [piece[:, j * block_rows : (j + 1) * block_rows].astype(f32)] * block_count
        columns.append(jnp.concatenate(parts, axis=1).astype(bf16))
        note = jnp.concatenate([note[:, j * rows : (j + 1) * rows] for note in notes], axis=1)
        codes.append(jnp.broadcast_to(note, columns[j].shape).astype(bf16))
    for n in range(per_owner):
        placed = jnp.zeros(columns[0].shape, bf16)
        for j in range(CAP):
            placed = jnp.where(codes[j] == jnp.asarray(n, bf16), columns[j], placed)
        out_ref[n * part : (n + 1) * part, lanes] = placed


def near_kernel(sizes, *refs):
    layers, owners, per_owner, block_count, block_rows = sizes
    panels, posts, factor_ref = refs[: 2 * (owners - 1)], refs[2 * (owners - 1) :][:layers], refs[2 * owners - 2 + layers]
    own_ref, other_ref, high_ref, low_ref, placed_ref, rows_ref = refs[2 * owners - 1 + layers :]
    f32, bf16 = jnp.float32, jnp.bfloat16
    high = factor_ref[...].astype(bf16)
    high_ref[...] = high
    low_ref[...] = (factor_ref[...] - high.astype(f32)).astype(bf16)
    rows = block_count * block_rows
    group, wide = CAP * block_rows, CAP * rows
    part = rows // 2
    width = rows_ref.shape[1]
    at = 0
    for panel in panels:
        rows_ref[at : at + panel.shape[0], :] = panel[:, :width]
        at += panel.shape[0]
    for u, out_ref in ((1, other_ref), (0, own_ref)):
        for e in range(owners - 1):
            for h in range(layers // 2):
                pair = posts[2 * h : 2 * h + 2]
                pieces = [post[u * part : (u + 1) * part, e * group : (e + 1) * group] for post in pair]
                notes = [row_of(post[rows:, :wide], e) for post in pair]
                start = (e * layers + 2 * h) * rows
                place(placed_ref, slice(start, start + 2 * rows), per_owner, pieces, notes, (block_count, block_rows))
        out_ref[...] = jnp.dot(placed_ref[...], rows_ref[...], preferred_element_type=f32)


def far_kernel(sizes, u, near_ref, by_y_ref, by_x_ref, out_ref, placed_ref, rows_ref):
    layers, owners, per_owner, block_count, block_rows = sizes
    f32, bf16 = jnp.float32, jnp.bfloat16
    rows = block_count * block_rows
    group, wide = CAP * block_rows, CAP * rows
    part = rows // 2
    half = (layers - 1) * rows // 2
    rows_ref[:rows, :] = by_x_ref[:rows, :]
    rows_ref[rows : rows + half, :] = by_y_ref[:half, :]
    rows_ref[rows + half :, :] = by_x_ref[rows:, :]
    for h in range(layers // 2):
        pieces, notes = [], []
        for k in (2 * h, 2 * h + 1):
            at = (u * layers + k) * group
            pieces.append(by_y_ref[half : half + part, at : at + group])
            notes.append(row_of(by_y_ref[half + part :, :wide], k))
        start = 2 * h * rows
        place(placed_ref, slice(start, start + 2 * rows), per_owner, pieces, notes, (block_count, block_rows))
    gram = near_ref[...] + jnp.dot(placed_ref[...], rows_ref[...], preferred_element_type=f32)
    out_ref[...] = gram.astype(out_ref.dtype)


def inverse_kernel(own_ref, other_ref, high_ref, low_ref, out_hbm, out_ref, sems):
    f32, bf16 = jnp.float32, jnp.bfloat16
    width = own_ref.shape[1]
    strips = sems.shape[0]
    height = own_ref.shape[0] // strips
    dims = (((1,), (1,)), ((), ()))
    copies = []
    for i in range(strips):
        here = pl.ds(i * height, height)
        gram = own_ref[here, :] + other_ref[here, :].astype(f32)
        gram_high = gram.astype(bf16)
        gram_low = (gram - gram_high.astype(f32)).astype(bf16)
        for start, stop in ((0, width // 2), (width // 2, width)):
            high, low = high_ref[start:stop, :stop], low_ref[start:stop, :stop]
            a, b = gram_high[:, :stop], gram_low[:, :stop]
            total = lax.dot_general(a, low, dims, preferred_element_type=f32)
            total += lax.dot_general(b, high, dims, preferred_element_type=f32)
            total += lax.dot_general(a, high, dims, preferred_element_type=f32)
            out_ref[here, start:stop] = total
        copies.append(pltpu.make_async_copy(out_ref.at[here, :], out_hbm.at[here, :], sems.at[i]))
        copies[-1].start()
    for copy in copies:
        copy.wait()


def local(jac, panel_jac, weights, tile_lists, tile_masks, tile_order, factor_inverse):
    block_count, slot_count = tile_lists.shape
    rows, panel_width = panel_jac.shape
    block_rows = rows // block_count
    tile_width = jac.shape[1] // slot_count
    slabs, owners = lax.axis_size("rows"), lax.axis_size("cols")
    layers = slabs // 2
    per_owner = tile_order.shape[0] // owners
    slab_width = tile_width // slabs
    f32, bf16 = jnp.float32, jnp.bfloat16
    vmem, anywhere = pl.BlockSpec(memory_space=pltpu.VMEM), pl.BlockSpec(memory_space=pl.ANY)
    params = pltpu.CompilerParams(vmem_limit_bytes=24 << 20)
    shaped = jax.ShapeDtypeStruct

    def in_hbm(value):
        return pltpu.with_memory_space_constraint(value, pltpu.HBM)

    lane_group = CAP * block_rows
    post = layers * lane_group
    wide = CAP * rows
    sizes = (layers, owners, per_owner, block_count, slot_count, block_rows, tile_width)
    weighted, kept, to_x, to_y = pl.pallas_call(
        functools.partial(pack_kernel, sizes),
        out_shape=[
            shaped((rows, width), bf16)
            for width in (panel_width, post + wide, panel_width + 2 * post + wide, panel_width + post + wide)
        ],
        in_specs=[anywhere] * 6,
        out_specs=[vmem] * 4,
        scratch_shapes=[
            pltpu.SMEM(tile_lists.shape, jnp.int32),
            pltpu.SMEM(tile_masks.shape, jnp.int32),
            pltpu.SMEM(tile_order.shape, jnp.int32),
            pltpu.VMEM((1, rows), f32),
            pltpu.VMEM(panel_jac.shape, bf16),
            pltpu.VMEM(jac.shape, bf16),
            pltpu.SMEM(tile_order.shape, jnp.int32),
            pltpu.VMEM((block_count * slot_count * tile_width, block_rows), f32),
            pltpu.SemaphoreType.DMA((6,)),
        ],
        compiler_params=params,
        name="pack",
    )(*map(in_hbm, (tile_lists, tile_masks, tile_order, weights.reshape(1, rows), panel_jac, jac)))
    line = [shift(weighted, k, 0) for k in range(1, layers)]
    from_x, from_y = shift(to_x, 0, 1), shift(to_y, 0, 2)

    sizes = (layers, panel_width, lane_group, wide)
    others, *posts = pl.pallas_call(
        functools.partial(sort_kernel, sizes),
        out_shape=[shaped(((layers - 1) * rows, panel_width), bf16)]
        + [shaped((rows + 16, owners * lane_group), bf16)] * layers,
        in_specs=[vmem] * (layers + 2),
        out_specs=[vmem] * (layers + 1),
        compiler_params=params,
        name="sort",
    )(kept, from_x, from_y, *line)
    posts = [posts[0]] + [shift(posts[k], k, 0) for k in range(1, layers)]
    by_x, by_y = shift(others, 0, 1), shift(others, 0, 2)

    half = others.shape[0] // 2
    to_y, to_x = pl.pallas_call(
        functools.partial(cut_kernel, sizes),
        out_shape=[
            shaped((half + rows // 2 + 16, panel_width), bf16),
            shaped((rows + half, panel_width), bf16),
        ],
        in_specs=[vmem] * (layers + 3),
        out_specs=[vmem] * 2,
        compiler_params=params,
        name="cut",
    )(from_y, by_x, by_y, *posts)
    across_y, across_x = shift(to_y, 0, 2), shift(to_x, 0, 1)

    count = per_owner * slab_width
    depth = layers * rows
    sizes = (layers, owners, per_owner, block_count, block_rows)
    gram = shaped((count, panel_width), f32)
    panels = [weighted, others, from_x, by_x, from_y, by_y]
    own, other, high, low = pl.pallas_call(
        functools.partial(near_kernel, sizes),
        out_shape=[gram] * 2 + [shaped(factor_inverse.shape, bf16)] * 2,
        in_specs=[vmem] * (len(panels) + layers + 1),
        out_specs=[vmem] * 4,
        scratch_shapes=[
            pltpu.VMEM((count, (owners - 1) * depth), bf16),
            pltpu.VMEM(((owners - 1) * depth, panel_width), bf16),
        ],
        compiler_params=params,
        name="near",
    )(*panels, *posts, factor_inverse)

    def far(u, near, kind):
        return pl.pallas_call(
            functools.partial(far_kernel, sizes, u),
            out_shape=shaped((count, panel_width), kind),
            in_specs=[vmem] * 3,
            out_specs=vmem,
            scratch_shapes=[pltpu.VMEM((count, depth), bf16), pltpu.VMEM((depth, panel_width), bf16)],
            compiler_params=params,
            name="far",
        )(near, across_y, across_x)

    other = shift(far(1, other, bf16), 0, 0, 1)
    out = pl.pallas_call(
        inverse_kernel,
        out_shape=shaped((count, panel_width), f32),
        in_specs=[vmem] * 4,
        out_specs=anywhere,
        scratch_shapes=[pltpu.VMEM((count, panel_width), f32), pltpu.SemaphoreType.DMA((4,))],
        compiler_params=params,
        name="inverse",
    )(far(0, own, f32), other, high, low)
    return out.reshape(per_owner, slab_width, panel_width)


def solution(mesh):
    in_specs = (
        P(("rows", "cols"), None),
        P(("rows", "cols"), None),
        P(("rows", "cols")),
        P(("rows", "cols"), None),
        P(("rows", "cols"), None),
        P(),
        P(),
    )
    out_specs = P("cols", "rows", None)
    body = local if (mesh.shape["rows"], mesh.shape["cols"]) == (8, 4) else local_general
    return jax.shard_map(body, mesh=mesh, in_specs=in_specs, out_specs=out_specs, check_vma=False)
```

```python
import functools

import jax
import jax.numpy as jnp
from jax import lax
from jax.experimental import pallas as pl
from jax.experimental.pallas import tpu as pltpu
from jax.sharding import PartitionSpec as P

CAP = 2
GATHERED = 1 << 22


def tile_positions(tile_lists, tile_order):
    tile_count = tile_order.shape[0]
    matches = tile_lists[:, :, None] == tile_order[None, None, :]
    return jnp.sum(jnp.where(matches, jnp.arange(tile_count, dtype=jnp.int32), 0), axis=2)


def apply_inverse(tiles, factor_inverse):
    return jnp.einsum("ntp,qp->ntq", tiles, factor_inverse, precision=lax.Precision.HIGHEST)


def slot_codes(tile_lists, tile_masks, tile_order, owner_ids):
    block_count, slot_count = tile_lists.shape
    per_owner = tile_order.shape[0] // lax.axis_size("cols")
    positions = tile_positions(tile_lists, tile_order).reshape(-1)
    active = tile_masks.reshape(-1) == 1
    owner = positions // per_owner
    same = (owner[:, None] == owner[None, :]) & active[None, :]
    earlier = jnp.tril(jnp.ones(same.shape, bool), -1)
    rank = jnp.sum(same & earlier, axis=1)
    code = (
        (owner[None, None, :] == owner_ids[:, None, None])
        & (rank[None, None, :] == jnp.arange(CAP)[None, :, None])
        & active[None, None, :]
    )
    block = jnp.arange(block_count * slot_count) // slot_count
    place = positions % per_owner + per_owner * block
    return code, jnp.sum(jnp.where(code, place + 1, 0), axis=2) - 1


def local_general(jac, panel_jac, weights, tile_lists, tile_masks, tile_order, factor_inverse):
    block_count, slot_count = tile_lists.shape
    block_rows = jac.shape[0] // block_count
    tile_width = jac.shape[1] // slot_count
    slabs, owners = lax.axis_size("rows"), lax.axis_size("cols")
    devices = slabs * owners
    per_owner = tile_order.shape[0] // owners
    slab_width = tile_width // slabs
    bf16 = jnp.bfloat16
    weighted = (weights[:, None] * panel_jac).astype(bf16)
    code, places = slot_codes(tile_lists, tile_masks, tile_order, jnp.arange(owners))
    columns = jac.reshape(block_count, block_rows, slot_count, slabs, slab_width)
    chosen = code.astype(bf16).reshape(owners, CAP, block_count, slot_count)
    pieces = jnp.einsum("cjbk,bmkrt->rcjmt", chosen, columns, preferred_element_type=jnp.float32).astype(bf16)
    pieces = pieces.reshape(devices, -1)
    note = jnp.broadcast_to(places.astype(bf16)[None], (slabs, owners, CAP)).reshape(devices, CAP)
    note = jnp.pad(note, ((0, 0), (0, 128 - CAP)))
    sent = jnp.concatenate([pieces, note], axis=1)
    got = lax.all_to_all(sent, ("rows", "cols"), split_axis=0, concat_axis=0, tiled=True)
    size = pieces.shape[1]
    data = got[:, :size].reshape(devices, CAP, block_rows, slab_width)
    where = got[:, size : size + CAP].astype(jnp.int32)
    hot = (where[:, :, None] == jnp.arange(block_count * per_owner)).astype(bf16)
    hot = hot.reshape(devices, CAP, block_count, per_owner)
    mixed = jnp.einsum("djbn,djmt->dbmnt", hot, data, preferred_element_type=jnp.float32).astype(bf16)
    strips = max(1, devices * weighted.size * 2 // GATHERED)

    def strip_gram(strip):
        panels = lax.all_gather(strip, ("rows", "cols"), axis=0, tiled=True)
        panels = panels.reshape(devices, block_count, block_rows, -1)
        return jnp.einsum("dbmnt,dbmp->ntp", mixed, panels, preferred_element_type=jnp.float32)

    if strips == 1:
        gram = strip_gram(weighted)
    else:
        narrow = weighted.reshape(weighted.shape[0], strips, -1).swapaxes(0, 1)
        gram = jnp.moveaxis(lax.map(strip_gram, narrow), 0, 2)
        gram = gram.reshape(per_owner, slab_width, -1)
    return apply_inverse(gram, factor_inverse)


def shift(value, steps_z, flip_cols, flip_core=0):
    slabs, owners = lax.axis_size("rows"), lax.axis_size("cols")
    pairs = []
    for r in range(slabs):
        to_r = ((r // 2 + steps_z) % (slabs // 2)) * 2 + ((r % 2) ^ flip_core)
        for c in range(owners):
            pairs.append((r * owners + c, to_r * owners + (c ^ flip_cols)))
    return lax.ppermute(value, ("rows", "cols"), pairs)


def pack_kernel(sizes, lists_hbm, masks_hbm, order_hbm, weights_hbm, panel_hbm, jac_hbm, *refs):
    layers, owners, per_owner, block_count, slot_count, block_rows, tile_width = sizes
    weighted_ref, kept_ref, to_x_ref, to_y_ref = refs[:4]
    lists_ref, masks_ref, order_ref, weights_ref, panel_ref, jac_ref, places_ref, turned_ref, sems = refs[4:]
    copies = [
        pltpu.make_async_copy(order_hbm, order_ref, sems.at[0]),
        pltpu.make_async_copy(lists_hbm, lists_ref, sems.at[1]),
        pltpu.make_async_copy(masks_hbm, masks_ref, sems.at[2]),
        pltpu.make_async_copy(weights_hbm, weights_ref, sems.at[3]),
        pltpu.make_async_copy(panel_hbm, panel_ref, sems.at[4]),
        pltpu.make_async_copy(jac_hbm, jac_ref, sems.at[5]),
    ]
    for copy in copies:
        copy.start()
    f32, bf16 = jnp.float32, jnp.bfloat16
    rows, width = panel_ref.shape
    lane_group = CAP * block_rows
    post = layers * lane_group
    slab = tile_width // layers
    part = slab // 2
    me_r, me_c = lax.axis_index("rows"), lax.axis_index("cols")
    me_z, me_core = me_r // 2, lax.rem(me_r, 2)
    for copy in copies:
        copy.wait()

    row_ids = lax.broadcasted_iota(jnp.int32, (rows, rows), 0)
    lane_ids = lax.broadcasted_iota(jnp.int32, (rows, rows), 1)
    column = jnp.sum(jnp.where(row_ids == lane_ids, weights_ref[...], 0.0), axis=1, keepdims=True)
    weighted = (column * panel_ref[...].astype(f32)).astype(bf16)
    weighted_ref[...] = weighted
    to_x_ref[:, :width] = weighted
    to_y_ref[:, :width] = weighted

    for b in range(block_count):
        block = jac_ref[b * block_rows : (b + 1) * block_rows, :].astype(f32)
        start = b * slot_count * tile_width
        turned_ref[start : start + slot_count * tile_width, :] = block.T

    for i in range(order_ref.shape[0]):
        places_ref[order_ref[i]] = i
    slots = []
    for s in range(block_count * slot_count):
        b, k = divmod(s, slot_count)
        place = places_ref[lists_ref[b, k]]
        owner = jnp.int32(0)
        for c in range(1, owners):
            owner += (place >= c * per_owner).astype(jnp.int32)
        slots.append((place - owner * per_owner, jnp.where(masks_ref[b, k] == 1, owner, -1)))

    shape = (16, CAP * block_count * block_rows)
    lane, row = lax.broadcasted_iota(jnp.int32, shape, 1), lax.broadcasted_iota(jnp.int32, shape, 0)
    notes = []
    spots = [(kept_ref, 0), (to_x_ref, width), (to_y_ref, width), (to_y_ref, width + post)]
    for e, (parcel, start) in enumerate(spots):
        wanted = me_c ^ e
        found = jnp.int32(0)
        chosen = [jnp.int32(0)] * CAP
        codes = [jnp.int32(-1)] * CAP
        for s, (place, owner) in enumerate(slots):
            hit = owner == wanted
            for j in range(CAP):
                take = hit & (found == j)
                chosen[j] = jnp.where(take, s, chosen[j])
                codes[j] = jnp.where(take, place, codes[j])
            found += hit.astype(jnp.int32)
        note = jnp.full(shape, -1, jnp.int32)
        for j in range(CAP):
            for b in range(block_count):
                at = (j * block_count + b) * block_rows
                here = (lane >= at) & (lane < at + block_rows)
                code = jnp.where(chosen[j] // slot_count == b, codes[j], -1)
                note = jnp.where(here, code, note)
        notes.append(note)
        for k in range(layers):
            z = lax.rem(me_z + k, layers)
            for u in range(2):
                core = me_core ^ u
                for j in range(CAP):
                    first = pl.multiple_of(chosen[j] * tile_width + z * slab + core * part, part)
                    piece = turned_ref[pl.ds(first, part), :].astype(bf16)
                    to = start + k * lane_group + j * block_rows
                    parcel[u * part : (u + 1) * part, to : to + block_rows] = piece
    kept_ref[:16, post:] = notes[0].astype(f32).astype(bf16)
    to_x_ref[:16, width + post :] = notes[1].astype(f32).astype(bf16)
    to_y_ref[:16, width + 2 * post :] = jnp.where(row == 0, notes[2], notes[3]).astype(f32).astype(bf16)


def row_of(block, i):
    ids = lax.broadcasted_iota(jnp.int32, block.shape, 0)
    return jnp.sum(jnp.where(ids == i, block.astype(jnp.float32), 0.0), axis=0, keepdims=True)


def rows_from(notes):
    ids = lax.broadcasted_iota(jnp.int32, (16, notes[0].shape[1]), 0)
    block = jnp.full(ids.shape, -1.0, jnp.float32)
    for i, note in enumerate(notes):
        block = jnp.where(ids == i, note, block)
    return block.astype(jnp.bfloat16)


def sort_kernel(sizes, kept_ref, from_x_ref, from_y_ref, *refs):
    layers, width, lane_group, wide = sizes
    line, (stacked, *posts) = refs[: layers - 1], refs[layers - 1 :]
    post = layers * lane_group
    rows = kept_ref.shape[0]
    for k, ref in enumerate(line):
        stacked[k * rows : (k + 1) * rows, :] = ref[...]
    spots = [(kept_ref, 0), (from_x_ref, width), (from_y_ref, width), (from_y_ref, width + post)]
    notes = [row_of(ref[:16, ref.shape[1] - wide :], int(e == 3)) for e, (ref, start) in enumerate(spots)]
    block = rows_from(notes)
    for k, out in enumerate(posts):
        for e, (ref, start) in enumerate(spots):
            piece = ref[:, start + k * lane_group : start + (k + 1) * lane_group]
            out[:rows, e * lane_group : (e + 1) * lane_group] = piece
        out[rows:, :wide] = block


def rows_to_y_kernel(from_x_ref, by_x_ref, *refs):
    out_ref = refs[-1]
    rows = from_x_ref.shape[0]
    out_ref[:rows, :] = from_x_ref[:, : out_ref.shape[1]]
    out_ref[rows:, :] = by_x_ref[: out_ref.shape[0] - rows, :]


def rest_to_x_kernel(sizes, by_y_ref, *refs):
    layers, lane_group, wide = sizes
    posts, out_ref = refs[:layers], refs[layers]
    rows = posts[0].shape[0] - 16
    part = rows // 2
    last = out_ref.shape[0] - part - 16
    out_ref[:last, :] = by_y_ref[by_y_ref.shape[0] - last :, :]
    for k, ref in enumerate(posts):
        for u in range(2):
            piece = ref[u * part : (u + 1) * part, 3 * lane_group : 4 * lane_group]
            at = (u * layers + k) * lane_group
            out_ref[last : last + part, at : at + lane_group] = piece
    out_ref[last + part :, :wide] = rows_from([row_of(ref[rows:, :wide], 3) for ref in posts])


def place(out_ref, lanes, per_owner, pieces, notes, sizes):
    block_count, block_rows = sizes
    f32, bf16 = jnp.float32, jnp.bfloat16
    part, rows = pieces[0].shape[0], block_count * block_rows
    columns, codes = [], []
    for j in range(CAP):
        parts = []
        for piece in pieces:
            parts += [piece[:, j * block_rows : (j + 1) * block_rows].astype(f32)] * block_count
        columns.append(jnp.concatenate(parts, axis=1).astype(bf16))
        note = jnp.concatenate([note[:, j * rows : (j + 1) * rows] for note in notes], axis=1)
        codes.append(jnp.broadcast_to(note, columns[j].shape).astype(bf16))
    for n in range(per_owner):
        placed = jnp.zeros(columns[0].shape, bf16)
        for j in range(CAP):
            placed = jnp.where(codes[j] == jnp.asarray(n, bf16), columns[j], placed)
        out_ref[n * part : (n + 1) * part, lanes] = placed


def near_kernel(sizes, *refs):
    layers, owners, per_owner, block_count, block_rows = sizes
    panels, posts, factor_ref = refs[: 2 * (owners - 1)], refs[2 * (owners - 1) :][:layers], refs[2 * owners - 2 + layers]
    own_ref, other_ref, high_ref, low_ref, placed_ref, rows_ref = refs[2 * owners - 1 + layers :]
    f32, bf16 = jnp.float32, jnp.bfloat16
    turned = factor_ref[...].T
    high = turned.astype(bf16)
    high_ref[...] = high
    low_ref[...] = (turned - high.astype(f32)).astype(bf16)
    rows = block_count * block_rows
    group, wide = CAP * block_rows, CAP * rows
    part = rows // 2
    width = rows_ref.shape[1]
    at = 0
    for panel in panels:
        rows_ref[at : at + panel.shape[0], :] = panel[:, :width]
        at += panel.shape[0]
    for u, out_ref in ((1, other_ref), (0, own_ref)):
        for e in range(owners - 1):
            for h in range(layers // 2):
                pair = posts[2 * h : 2 * h + 2]
                pieces = [post[u * part : (u + 1) * part, e * group : (e + 1) * group] for post in pair]
                notes = [row_of(post[rows:, :wide], e) for post in pair]
                start = (e * layers + 2 * h) * rows
                place(placed_ref, slice(start, start + 2 * rows), per_owner, pieces, notes, (block_count, block_rows))
        out_ref[...] = jnp.dot(placed_ref[...], rows_ref[...], preferred_element_type=f32)


def far_kernel(sizes, u, near_ref, by_y_ref, by_x_ref, out_ref, placed_ref, rows_ref):
    layers, owners, per_owner, block_count, block_rows = sizes
    f32, bf16 = jnp.float32, jnp.bfloat16
    rows = block_count * block_rows
    group, wide = CAP * block_rows, CAP * rows
    part = rows // 2
    first = by_y_ref.shape[0]
    last = rows_ref.shape[0] - first
    rows_ref[:first, :] = by_y_ref[...]
    rows_ref[first:, :] = by_x_ref[:last, :]
    for h in range(layers // 2):
        pieces, notes = [], []
        for k in (2 * h, 2 * h + 1):
            at = (u * layers + k) * group
            pieces.append(by_x_ref[last : last + part, at : at + group])
            notes.append(row_of(by_x_ref[last + part :, :wide], k))
        start = 2 * h * rows
        place(placed_ref, slice(start, start + 2 * rows), per_owner, pieces, notes, (block_count, block_rows))
    gram = near_ref[...] + jnp.dot(placed_ref[...], rows_ref[...], preferred_element_type=f32)
    out_ref[...] = gram.astype(out_ref.dtype)


def inverse_kernel(own_ref, other_ref, high_ref, low_ref, out_hbm, out_ref, sems):
    f32, bf16 = jnp.float32, jnp.bfloat16
    width = own_ref.shape[1]
    strips = sems.shape[0]
    height = own_ref.shape[0] // strips
    copies = []

    def times(a, b):
        return jnp.dot(a, b, preferred_element_type=f32)

    for i in range(strips):
        here = pl.ds(i * height, height)
        gram = own_ref[here, :] + other_ref[here, :].astype(f32)
        gram_high = gram.astype(bf16)
        gram_low = (gram - gram_high.astype(f32)).astype(bf16)
        for start, stop in ((0, width // 2), (width // 2, width)):
            high, low = high_ref[:stop, start:stop], low_ref[:stop, start:stop]
            a, b = gram_high[:, :stop], gram_low[:, :stop]
            out_ref[here, start:stop] = times(a, high) + (times(a, low) + times(b, high))
        copies.append(pltpu.make_async_copy(out_ref.at[here, :], out_hbm.at[here, :], sems.at[i]))
        copies[-1].start()
    for copy in copies:
        copy.wait()


def local(jac, panel_jac, weights, tile_lists, tile_masks, tile_order, factor_inverse):
    block_count, slot_count = tile_lists.shape
    rows, panel_width = panel_jac.shape
    block_rows = rows // block_count
    tile_width = jac.shape[1] // slot_count
    slabs, owners = lax.axis_size("rows"), lax.axis_size("cols")
    layers = slabs // 2
    per_owner = tile_order.shape[0] // owners
    slab_width = tile_width // slabs
    f32, bf16 = jnp.float32, jnp.bfloat16
    vmem, anywhere = pl.BlockSpec(memory_space=pltpu.VMEM), pl.BlockSpec(memory_space=pl.ANY)
    params = pltpu.CompilerParams(vmem_limit_bytes=24 << 20)
    shaped = jax.ShapeDtypeStruct

    def in_hbm(value):
        return pltpu.with_memory_space_constraint(value, pltpu.HBM)

    lane_group = CAP * block_rows
    post = layers * lane_group
    wide = CAP * rows
    sizes = (layers, owners, per_owner, block_count, slot_count, block_rows, tile_width)
    weighted, kept, to_x, to_y = pl.pallas_call(
        functools.partial(pack_kernel, sizes),
        out_shape=[
            shaped((rows, width), bf16)
            for width in (panel_width, post + wide, panel_width + post + wide, panel_width + 2 * post + wide)
        ],
        in_specs=[anywhere] * 6,
        out_specs=[vmem] * 4,
        scratch_shapes=[
            pltpu.SMEM(tile_lists.shape, jnp.int32),
            pltpu.SMEM(tile_masks.shape, jnp.int32),
            pltpu.SMEM(tile_order.shape, jnp.int32),
            pltpu.VMEM((1, rows), f32),
            pltpu.VMEM(panel_jac.shape, bf16),
            pltpu.VMEM(jac.shape, bf16),
            pltpu.SMEM(tile_order.shape, jnp.int32),
            pltpu.VMEM((block_count * slot_count * tile_width, block_rows), f32),
            pltpu.SemaphoreType.DMA((6,)),
        ],
        compiler_params=params,
        name="pack",
    )(*map(in_hbm, (tile_lists, tile_masks, tile_order, weights.reshape(1, rows), panel_jac, jac)))
    line = [shift(weighted, k, 0) for k in range(1, layers)]
    from_x, from_y = shift(to_x, 0, 1), shift(to_y, 0, 2)

    sizes = (layers, panel_width, lane_group, wide)
    others, *posts = pl.pallas_call(
        functools.partial(sort_kernel, sizes),
        out_shape=[shaped(((layers - 1) * rows, panel_width), bf16)]
        + [shaped((rows + 16, owners * lane_group), bf16)] * layers,
        in_specs=[vmem] * (layers + 2),
        out_specs=[vmem] * (layers + 1),
        compiler_params=params,
        name="sort",
    )(kept, from_x, from_y, *line)
    posts = [posts[0]] + [shift(posts[k], k, 0) for k in range(1, layers)]
    by_x, by_y = shift(others, 0, 1), shift(others, 0, 2)

    last = rows // 2
    rows_to_y = pl.pallas_call(
        rows_to_y_kernel,
        out_shape=shaped((rows + others.shape[0] - last, panel_width), bf16),
        in_specs=[vmem] * 2 + [anywhere] * (layers - 1),
        out_specs=vmem,
        compiler_params=params,
        name="rows_to_y",
    )(from_x, by_x, *posts[1:])
    across_y = shift(rows_to_y, 0, 2)
    rest_to_x = pl.pallas_call(
        functools.partial(rest_to_x_kernel, (layers, lane_group, wide)),
        out_shape=shaped((last + rows // 2 + 16, panel_width), bf16),
        in_specs=[vmem] * (layers + 1),
        out_specs=vmem,
        compiler_params=params,
        name="rest_to_x",
    )(by_y, *posts)
    across_x = shift(rest_to_x, 0, 1)

    count = per_owner * slab_width
    depth = layers * rows
    sizes = (layers, owners, per_owner, block_count, block_rows)
    gram = shaped((count, panel_width), f32)
    panels = [weighted, others, from_x, by_x, from_y, by_y]
    own, other, high, low = pl.pallas_call(
        functools.partial(near_kernel, sizes),
        out_shape=[gram] * 2 + [shaped(factor_inverse.shape, bf16)] * 2,
        in_specs=[vmem] * (len(panels) + layers + 1),
        out_specs=[vmem] * 4,
        scratch_shapes=[
            pltpu.VMEM((count, (owners - 1) * depth), bf16),
            pltpu.VMEM(((owners - 1) * depth, panel_width), bf16),
        ],
        compiler_params=params,
        name="near",
    )(*panels, *posts, factor_inverse)

    def far(u, near, kind):
        return pl.pallas_call(
            functools.partial(far_kernel, sizes, u),
            out_shape=shaped((count, panel_width), kind),
            in_specs=[vmem] * 3,
            out_specs=vmem,
            scratch_shapes=[pltpu.VMEM((count, depth), bf16), pltpu.VMEM((depth, panel_width), bf16)],
            compiler_params=params,
            name="far",
        )(near, across_y, across_x)

    other = shift(far(1, other, bf16), 0, 0, 1)
    out = pl.pallas_call(
        inverse_kernel,
        out_shape=shaped((count, panel_width), f32),
        in_specs=[vmem] * 4,
        out_specs=anywhere,
        scratch_shapes=[pltpu.VMEM((count, panel_width), f32), pltpu.SemaphoreType.DMA((3,))],
        compiler_params=params,
        name="inverse",
    )(far(0, own, f32), other, high, low)
    return out.reshape(per_owner, slab_width, panel_width)


def solution(mesh):
    in_specs = (
        P(("rows", "cols"), None),
        P(("rows", "cols"), None),
        P(("rows", "cols")),
        P(("rows", "cols"), None),
        P(("rows", "cols"), None),
        P(),
        P(),
    )
    out_specs = P("cols", "rows", None)
    body = local if (mesh.shape["rows"], mesh.shape["cols"]) == (8, 4) else local_general
    return jax.shard_map(body, mesh=mesh, in_specs=in_specs, out_specs=out_specs, check_vma=False)
```

```python
import functools

import jax
import jax.numpy as jnp
from jax import lax
from jax.experimental import pallas as pl
from jax.experimental.pallas import tpu as pltpu
from jax.sharding import PartitionSpec as P

CAP = 2
GATHERED = 1 << 22


def tile_positions(tile_lists, tile_order):
    tile_count = tile_order.shape[0]
    matches = tile_lists[:, :, None] == tile_order[None, None, :]
    return jnp.sum(jnp.where(matches, jnp.arange(tile_count, dtype=jnp.int32), 0), axis=2)


def apply_inverse(tiles, factor_inverse):
    return jnp.einsum("ntp,qp->ntq", tiles, factor_inverse, precision=lax.Precision.HIGHEST)


def slot_codes(tile_lists, tile_masks, tile_order, owner_ids):
    block_count, slot_count = tile_lists.shape
    per_owner = tile_order.shape[0] // lax.axis_size("cols")
    positions = tile_positions(tile_lists, tile_order).reshape(-1)
    active = tile_masks.reshape(-1) == 1
    owner = positions // per_owner
    same = (owner[:, None] == owner[None, :]) & active[None, :]
    earlier = jnp.tril(jnp.ones(same.shape, bool), -1)
    rank = jnp.sum(same & earlier, axis=1)
    code = (
        (owner[None, None, :] == owner_ids[:, None, None])
        & (rank[None, None, :] == jnp.arange(CAP)[None, :, None])
        & active[None, None, :]
    )
    block = jnp.arange(block_count * slot_count) // slot_count
    place = positions % per_owner + per_owner * block
    return code, jnp.sum(jnp.where(code, place + 1, 0), axis=2) - 1


def local_general(jac, panel_jac, weights, tile_lists, tile_masks, tile_order, factor_inverse):
    block_count, slot_count = tile_lists.shape
    block_rows = jac.shape[0] // block_count
    tile_width = jac.shape[1] // slot_count
    slabs, owners = lax.axis_size("rows"), lax.axis_size("cols")
    devices = slabs * owners
    per_owner = tile_order.shape[0] // owners
    slab_width = tile_width // slabs
    bf16 = jnp.bfloat16
    weighted = (weights[:, None] * panel_jac).astype(bf16)
    code, places = slot_codes(tile_lists, tile_masks, tile_order, jnp.arange(owners))
    columns = jac.reshape(block_count, block_rows, slot_count, slabs, slab_width)
    chosen = code.astype(bf16).reshape(owners, CAP, block_count, slot_count)
    pieces = jnp.einsum("cjbk,bmkrt->rcjmt", chosen, columns, preferred_element_type=jnp.float32).astype(bf16)
    pieces = pieces.reshape(devices, -1)
    note = jnp.broadcast_to(places.astype(bf16)[None], (slabs, owners, CAP)).reshape(devices, CAP)
    note = jnp.pad(note, ((0, 0), (0, 128 - CAP)))
    sent = jnp.concatenate([pieces, note], axis=1)
    got = lax.all_to_all(sent, ("rows", "cols"), split_axis=0, concat_axis=0, tiled=True)
    size = pieces.shape[1]
    data = got[:, :size].reshape(devices, CAP, block_rows, slab_width)
    where = got[:, size : size + CAP].astype(jnp.int32)
    hot = (where[:, :, None] == jnp.arange(block_count * per_owner)).astype(bf16)
    hot = hot.reshape(devices, CAP, block_count, per_owner)
    mixed = jnp.einsum("djbn,djmt->dbmnt", hot, data, preferred_element_type=jnp.float32).astype(bf16)
    strips = max(1, devices * weighted.size * 2 // GATHERED)

    def strip_gram(strip):
        panels = lax.all_gather(strip, ("rows", "cols"), axis=0, tiled=True)
        panels = panels.reshape(devices, block_count, block_rows, -1)
        return jnp.einsum("dbmnt,dbmp->ntp", mixed, panels, preferred_element_type=jnp.float32)

    if strips == 1:
        gram = strip_gram(weighted)
    else:
        narrow = weighted.reshape(weighted.shape[0], strips, -1).swapaxes(0, 1)
        gram = jnp.moveaxis(lax.map(strip_gram, narrow), 0, 2)
        gram = gram.reshape(per_owner, slab_width, -1)
    return apply_inverse(gram, factor_inverse)


def shift(value, steps_z, flip_cols, flip_core=0):
    slabs, owners = lax.axis_size("rows"), lax.axis_size("cols")
    pairs = []
    for r in range(slabs):
        to_r = ((r // 2 + steps_z) % (slabs // 2)) * 2 + ((r % 2) ^ flip_core)
        for c in range(owners):
            pairs.append((r * owners + c, to_r * owners + (c ^ flip_cols)))
    return lax.ppermute(value, ("rows", "cols"), pairs)


def pack_kernel(sizes, lists_hbm, masks_hbm, order_hbm, weights_hbm, panel_hbm, jac_hbm, *refs):
    layers, owners, per_owner, block_count, slot_count, block_rows, tile_width = sizes
    weighted_ref, parcels_ref = refs[:2]
    lists_ref, masks_ref, order_ref, weights_ref, panel_ref, jac_ref, places_ref, turned_ref, sems = refs[2:]
    copies = [
        pltpu.make_async_copy(order_hbm, order_ref, sems.at[0]),
        pltpu.make_async_copy(lists_hbm, lists_ref, sems.at[1]),
        pltpu.make_async_copy(masks_hbm, masks_ref, sems.at[2]),
        pltpu.make_async_copy(weights_hbm, weights_ref, sems.at[3]),
        pltpu.make_async_copy(panel_hbm, panel_ref, sems.at[4]),
        pltpu.make_async_copy(jac_hbm, jac_ref, sems.at[5]),
    ]
    for copy in copies:
        copy.start()
    f32, bf16 = jnp.float32, jnp.bfloat16
    rows, width = panel_ref.shape
    lane_group = CAP * block_rows
    post = layers * lane_group
    slab = tile_width // layers
    part = slab // 2
    me_r = lax.axis_index("rows")
    me_z, me_core = me_r // 2, lax.rem(me_r, 2)
    for copy in copies:
        copy.wait()

    row_ids = lax.broadcasted_iota(jnp.int32, (rows, rows), 0)
    lane_ids = lax.broadcasted_iota(jnp.int32, (rows, rows), 1)
    column = jnp.sum(jnp.where(row_ids == lane_ids, weights_ref[...], 0.0), axis=1, keepdims=True)
    weighted = (column * panel_ref[...].astype(f32)).astype(bf16)
    weighted_ref[...] = weighted
    for c in range(owners):
        parcels_ref[c, :, :width] = weighted

    for b in range(block_count):
        block = jac_ref[b * block_rows : (b + 1) * block_rows, :].astype(f32)
        start = b * slot_count * tile_width
        turned_ref[start : start + slot_count * tile_width, :] = block.T

    for i in range(order_ref.shape[0]):
        places_ref[order_ref[i]] = i
    slots = []
    for s in range(block_count * slot_count):
        b, k = divmod(s, slot_count)
        place = places_ref[lists_ref[b, k]]
        owner = jnp.int32(0)
        for c in range(1, owners):
            owner += (place >= c * per_owner).astype(jnp.int32)
        slots.append((place - owner * per_owner, jnp.where(masks_ref[b, k] == 1, owner, -1)))

    shape = (16, CAP * block_count * block_rows)
    lane = lax.broadcasted_iota(jnp.int32, shape, 1)
    for wanted in range(owners):
        found = jnp.int32(0)
        chosen = [jnp.int32(0)] * CAP
        codes = [jnp.int32(-1)] * CAP
        for s, (place, owner) in enumerate(slots):
            hit = owner == wanted
            for j in range(CAP):
                take = hit & (found == j)
                chosen[j] = jnp.where(take, s, chosen[j])
                codes[j] = jnp.where(take, place, codes[j])
            found += hit.astype(jnp.int32)
        note = jnp.full(shape, -1, jnp.int32)
        for j in range(CAP):
            for b in range(block_count):
                at = (j * block_count + b) * block_rows
                here = (lane >= at) & (lane < at + block_rows)
                code = jnp.where(chosen[j] // slot_count == b, codes[j], -1)
                note = jnp.where(here, code, note)
        parcels_ref[wanted, :16, width + post :] = note.astype(f32).astype(bf16)
        for k in range(layers):
            z = lax.rem(me_z + k, layers)
            for u in range(2):
                core = me_core ^ u
                for j in range(CAP):
                    first = pl.multiple_of(chosen[j] * tile_width + z * slab + core * part, part)
                    piece = turned_ref[pl.ds(first, part), :].astype(bf16)
                    to = width + k * lane_group + j * block_rows
                    parcels_ref[wanted, u * part : (u + 1) * part, to : to + block_rows] = piece


def row_of(block, i):
    ids = lax.broadcasted_iota(jnp.int32, block.shape, 0)
    return jnp.sum(jnp.where(ids == i, block.astype(jnp.float32), 0.0), axis=0, keepdims=True)


def rows_from(notes):
    ids = lax.broadcasted_iota(jnp.int32, (16, notes[0].shape[1]), 0)
    block = jnp.full(ids.shape, -1.0, jnp.float32)
    for i, note in enumerate(notes):
        block = jnp.where(ids == i, note, block)
    return block.astype(jnp.bfloat16)


def sort_kernel(sizes, parcels_ref, *refs):
    layers, owners, width, lane_group, wide = sizes
    line, (stacked, mail_ref) = refs[: layers - 1], refs[layers - 1 :]
    rows = parcels_ref.shape[1]
    me_z, me_c = lax.axis_index("rows") // 2, lax.axis_index("cols")
    for k, ref in enumerate(line):
        stacked[k * rows : (k + 1) * rows, :] = ref[...]
    at = width + layers * lane_group
    block = rows_from([row_of(parcels_ref[me_c ^ e, :16, at : at + wide], 0) for e in range(owners)])
    for k in range(layers):
        z = lax.rem(me_z + k, layers)
        for e in range(owners):
            start = width + k * lane_group
            piece = parcels_ref[me_c ^ e, :, start : start + lane_group]
            mail_ref[z, :rows, e * lane_group : (e + 1) * lane_group] = piece
        mail_ref[z, rows:, :wide] = block


def first_kernel(in_ref, earlier_ref, out_ref):
    out_ref[...] = in_ref[: out_ref.shape[0], :]


def last_kernel(in_ref, earlier_ref, out_ref):
    out_ref[...] = in_ref[in_ref.shape[0] - out_ref.shape[0] :, :]


def place(out_ref, lanes, per_owner, pieces, notes, sizes):
    block_count, block_rows = sizes
    f32, bf16 = jnp.float32, jnp.bfloat16
    part, rows = pieces[0].shape[0], block_count * block_rows
    columns, codes = [], []
    for j in range(CAP):
        parts = []
        for piece in pieces:
            parts += [piece[:, j * block_rows : (j + 1) * block_rows].astype(f32)] * block_count
        columns.append(jnp.concatenate(parts, axis=1).astype(bf16))
        note = jnp.concatenate([note[:, j * rows : (j + 1) * rows] for note in notes], axis=1)
        codes.append(jnp.broadcast_to(note, columns[j].shape).astype(bf16))
    for n in range(per_owner):
        placed = jnp.zeros(columns[0].shape, bf16)
        for j in range(CAP):
            placed = jnp.where(codes[j] == jnp.asarray(n, bf16), columns[j], placed)
        out_ref[n * part : (n + 1) * part, lanes] = placed


def near_kernel(sizes, panel_ref, others_ref, parcels_ref, by_x_ref, by_y_ref, mail_ref, factor_ref, *refs):
    layers, owners, per_owner, block_count, block_rows = sizes
    own_ref, other_ref, own_far_ref, other_far_ref, high_ref, low_ref, placed_ref, rows_ref = refs
    f32, bf16 = jnp.float32, jnp.bfloat16
    turned = factor_ref[...].T
    high = turned.astype(bf16)
    high_ref[...] = high
    low_ref[...] = (turned - high.astype(f32)).astype(bf16)
    rows = block_count * block_rows
    group, wide = CAP * block_rows, CAP * rows
    part = rows // 2
    width = rows_ref.shape[1]
    depth = layers * rows
    me_z, me_c = lax.axis_index("rows") // 2, lax.axis_index("cols")
    for e, (first, rest) in enumerate(((None, others_ref), (1, by_x_ref), (2, by_y_ref))):
        start = e * depth
        rows_ref[start : start + rows, :] = panel_ref[...] if first is None else parcels_ref[me_c ^ e, :, :width]
        rows_ref[start + rows : start + depth, :] = rest[...]
    for u, out_ref, far_ref in ((1, other_ref, other_far_ref), (0, own_ref, own_far_ref)):
        for e in range(owners):
            for h in range(layers // 2):
                pieces, notes = [], []
                for k in (2 * h, 2 * h + 1):
                    z = lax.rem(me_z + layers - k, layers)
                    pieces.append(mail_ref[z, u * part : (u + 1) * part, e * group : (e + 1) * group])
                    notes.append(row_of(mail_ref[z, rows:, :wide], e))
                to_ref, start = (placed_ref, e * depth) if e < owners - 1 else (far_ref, 0)
                lanes = slice(start + 2 * h * rows, start + 2 * (h + 1) * rows)
                place(to_ref, lanes, per_owner, pieces, notes, (block_count, block_rows))
        out_ref[...] = jnp.dot(placed_ref[...], rows_ref[...], preferred_element_type=f32)


def far_kernel(near_ref, placed_ref, parcels_ref, across_y_ref, across_x_ref, out_ref, rows_ref):
    rows, first = parcels_ref.shape[1], across_y_ref.shape[0]
    diagonal = lax.axis_index("cols") ^ (parcels_ref.shape[0] - 1)
    rows_ref[:rows, :] = parcels_ref[diagonal, :, : rows_ref.shape[1]]
    rows_ref[rows : rows + first, :] = across_y_ref[...]
    rows_ref[rows + first :, :] = across_x_ref[...]
    gram = near_ref[...] + jnp.dot(placed_ref[...], rows_ref[...], preferred_element_type=jnp.float32)
    out_ref[...] = gram.astype(out_ref.dtype)


def inverse_kernel(own_ref, other_ref, high_ref, low_ref, out_hbm, out_ref, sems):
    f32, bf16 = jnp.float32, jnp.bfloat16
    width = own_ref.shape[1]
    strips = sems.shape[0]
    height = own_ref.shape[0] // strips
    copies = []

    def times(a, b):
        return jnp.dot(a, b, preferred_element_type=f32)

    for i in range(strips):
        here = pl.ds(i * height, height)
        gram = own_ref[here, :] + other_ref[here, :].astype(f32)
        gram_high = gram.astype(bf16)
        gram_low = (gram - gram_high.astype(f32)).astype(bf16)
        for start, stop in ((0, width // 2), (width // 2, width)):
            high, low = high_ref[:stop, start:stop], low_ref[:stop, start:stop]
            a, b = gram_high[:, :stop], gram_low[:, :stop]
            out_ref[here, start:stop] = times(a, high) + (times(a, low) + times(b, high))
        copies.append(pltpu.make_async_copy(out_ref.at[here, :], out_hbm.at[here, :], sems.at[i]))
        copies[-1].start()
    for copy in copies:
        copy.wait()


def local(jac, panel_jac, weights, tile_lists, tile_masks, tile_order, factor_inverse):
    block_count, slot_count = tile_lists.shape
    rows, panel_width = panel_jac.shape
    block_rows = rows // block_count
    tile_width = jac.shape[1] // slot_count
    slabs, owners = lax.axis_size("rows"), lax.axis_size("cols")
    layers = slabs // 2
    per_owner = tile_order.shape[0] // owners
    slab_width = tile_width // slabs
    f32, bf16 = jnp.float32, jnp.bfloat16
    vmem, anywhere = pl.BlockSpec(memory_space=pltpu.VMEM), pl.BlockSpec(memory_space=pl.ANY)
    params = pltpu.CompilerParams(vmem_limit_bytes=24 << 20)
    shaped = jax.ShapeDtypeStruct

    def in_hbm(value):
        return pltpu.with_memory_space_constraint(value, pltpu.HBM)

    lane_group = CAP * block_rows
    post = layers * lane_group
    wide = CAP * rows
    sizes = (layers, owners, per_owner, block_count, slot_count, block_rows, tile_width)
    weighted, parcels = pl.pallas_call(
        functools.partial(pack_kernel, sizes),
        out_shape=[
            shaped((rows, panel_width), bf16),
            shaped((owners, rows, panel_width + post + wide), bf16),
        ],
        in_specs=[anywhere] * 6,
        out_specs=[vmem] * 2,
        scratch_shapes=[
            pltpu.SMEM(tile_lists.shape, jnp.int32),
            pltpu.SMEM(tile_masks.shape, jnp.int32),
            pltpu.SMEM(tile_order.shape, jnp.int32),
            pltpu.VMEM((1, rows), f32),
            pltpu.VMEM(panel_jac.shape, bf16),
            pltpu.VMEM(jac.shape, bf16),
            pltpu.SMEM(tile_order.shape, jnp.int32),
            pltpu.VMEM((block_count * slot_count * tile_width, block_rows), f32),
            pltpu.SemaphoreType.DMA((6,)),
        ],
        compiler_params=params,
        name="pack",
    )(*map(in_hbm, (tile_lists, tile_masks, tile_order, weights.reshape(1, rows), panel_jac, jac)))
    line = [shift(weighted, k, 0) for k in range(1, layers)]
    parcels = lax.all_to_all(parcels, "cols", split_axis=0, concat_axis=0, tiled=True)

    others, mail = pl.pallas_call(
        functools.partial(sort_kernel, (layers, owners, panel_width, lane_group, wide)),
        out_shape=[
            shaped(((layers - 1) * rows, panel_width), bf16),
            shaped((layers, rows + 16, owners * lane_group), bf16),
        ],
        in_specs=[vmem] * layers,
        out_specs=[vmem] * 2,
        compiler_params=params,
        name="sort",
    )(parcels, *line)
    by_x, by_y = shift(others, 0, 1), shift(others, 0, 2)
    same_core = [[r for r in range(slabs) if r % 2 == core] for core in range(2)]
    mail = lax.all_to_all(mail, "rows", split_axis=0, concat_axis=0, axis_index_groups=same_core, tiled=True)

    def cut(kernel, value, height, name):
        return pl.pallas_call(
            kernel,
            out_shape=shaped((height, panel_width), bf16),
            in_specs=[vmem, anywhere],
            out_specs=vmem,
            compiler_params=params,
            name=name,
        )(value, mail)

    last = others.shape[0] // 4
    across_y = shift(cut(first_kernel, by_x, others.shape[0] - last, "first"), 0, 2)
    across_x = shift(cut(last_kernel, by_y, last, "last"), 0, 1)

    count = per_owner * slab_width
    depth = layers * rows
    sizes = (layers, owners, per_owner, block_count, block_rows)
    gram = shaped((count, panel_width), f32)
    far_placed = shaped((count, depth), bf16)
    own, other, own_far, other_far, high, low = pl.pallas_call(
        functools.partial(near_kernel, sizes),
        out_shape=[gram] * 2 + [far_placed] * 2 + [shaped(factor_inverse.shape, bf16)] * 2,
        in_specs=[vmem] * 7,
        out_specs=[vmem] * 6,
        scratch_shapes=[
            pltpu.VMEM((count, (owners - 1) * depth), bf16),
            pltpu.VMEM(((owners - 1) * depth, panel_width), bf16),
        ],
        compiler_params=params,
        name="near",
    )(weighted, others, parcels, by_x, by_y, mail, factor_inverse)

    def far(near, placed, kind):
        return pl.pallas_call(
            far_kernel,
            out_shape=shaped((count, panel_width), kind),
            in_specs=[vmem] * 5,
            out_specs=vmem,
            scratch_shapes=[pltpu.VMEM((depth, panel_width), bf16)],
            compiler_params=params,
            name="far",
        )(near, placed, parcels, across_y, across_x)

    other = shift(far(other, other_far, bf16), 0, 0, 1)
    out = pl.pallas_call(
        inverse_kernel,
        out_shape=shaped((count, panel_width), f32),
        in_specs=[vmem] * 4,
        out_specs=anywhere,
        scratch_shapes=[pltpu.VMEM((count, panel_width), f32), pltpu.SemaphoreType.DMA((3,))],
        compiler_params=params,
        name="inverse",
    )(far(own, own_far, f32), other, high, low)
    return out.reshape(per_owner, slab_width, panel_width)


def solution(mesh):
    in_specs = (
        P(("rows", "cols"), None),
        P(("rows", "cols"), None),
        P(("rows", "cols")),
        P(("rows", "cols"), None),
        P(("rows", "cols"), None),
        P(),
        P(),
    )
    out_specs = P("cols", "rows", None)
    body = local if (mesh.shape["rows"], mesh.shape["cols"]) == (8, 4) else local_general
    return jax.shard_map(body, mesh=mesh, in_specs=in_specs, out_specs=out_specs, check_vma=False)
```

```python
import functools

import jax
import jax.numpy as jnp
from jax import lax
from jax.experimental import pallas as pl
from jax.experimental.pallas import tpu as pltpu
from jax.sharding import PartitionSpec as P

CAP = 2
GATHERED = 1 << 22


def tile_positions(tile_lists, tile_order):
    tile_count = tile_order.shape[0]
    matches = tile_lists[:, :, None] == tile_order[None, None, :]
    return jnp.sum(jnp.where(matches, jnp.arange(tile_count, dtype=jnp.int32), 0), axis=2)


def apply_inverse(tiles, factor_inverse):
    return jnp.einsum("ntp,qp->ntq", tiles, factor_inverse, precision=lax.Precision.HIGHEST)


def slot_codes(tile_lists, tile_masks, tile_order, owner_ids):
    block_count, slot_count = tile_lists.shape
    per_owner = tile_order.shape[0] // lax.axis_size("cols")
    positions = tile_positions(tile_lists, tile_order).reshape(-1)
    active = tile_masks.reshape(-1) == 1
    owner = positions // per_owner
    same = (owner[:, None] == owner[None, :]) & active[None, :]
    earlier = jnp.tril(jnp.ones(same.shape, bool), -1)
    rank = jnp.sum(same & earlier, axis=1)
    code = (
        (owner[None, None, :] == owner_ids[:, None, None])
        & (rank[None, None, :] == jnp.arange(CAP)[None, :, None])
        & active[None, None, :]
    )
    block = jnp.arange(block_count * slot_count) // slot_count
    place = positions % per_owner + per_owner * block
    return code, jnp.sum(jnp.where(code, place + 1, 0), axis=2) - 1


def local_general(jac, panel_jac, weights, tile_lists, tile_masks, tile_order, factor_inverse):
    block_count, slot_count = tile_lists.shape
    block_rows = jac.shape[0] // block_count
    tile_width = jac.shape[1] // slot_count
    slabs, owners = lax.axis_size("rows"), lax.axis_size("cols")
    devices = slabs * owners
    per_owner = tile_order.shape[0] // owners
    slab_width = tile_width // slabs
    bf16 = jnp.bfloat16
    weighted = (weights[:, None] * panel_jac).astype(bf16)
    code, places = slot_codes(tile_lists, tile_masks, tile_order, jnp.arange(owners))
    columns = jac.reshape(block_count, block_rows, slot_count, slabs, slab_width)
    chosen = code.astype(bf16).reshape(owners, CAP, block_count, slot_count)
    pieces = jnp.einsum("cjbk,bmkrt->rcjmt", chosen, columns, preferred_element_type=jnp.float32).astype(bf16)
    pieces = pieces.reshape(devices, -1)
    note = jnp.broadcast_to(places.astype(bf16)[None], (slabs, owners, CAP)).reshape(devices, CAP)
    note = jnp.pad(note, ((0, 0), (0, 128 - CAP)))
    sent = jnp.concatenate([pieces, note], axis=1)
    got = lax.all_to_all(sent, ("rows", "cols"), split_axis=0, concat_axis=0, tiled=True)
    size = pieces.shape[1]
    data = got[:, :size].reshape(devices, CAP, block_rows, slab_width)
    where = got[:, size : size + CAP].astype(jnp.int32)
    hot = (where[:, :, None] == jnp.arange(block_count * per_owner)).astype(bf16)
    hot = hot.reshape(devices, CAP, block_count, per_owner)
    mixed = jnp.einsum("djbn,djmt->dbmnt", hot, data, preferred_element_type=jnp.float32).astype(bf16)
    strips = max(1, devices * weighted.size * 2 // GATHERED)

    def strip_gram(strip):
        panels = lax.all_gather(strip, ("rows", "cols"), axis=0, tiled=True)
        panels = panels.reshape(devices, block_count, block_rows, -1)
        return jnp.einsum("dbmnt,dbmp->ntp", mixed, panels, preferred_element_type=jnp.float32)

    if strips == 1:
        gram = strip_gram(weighted)
    else:
        narrow = weighted.reshape(weighted.shape[0], strips, -1).swapaxes(0, 1)
        gram = jnp.moveaxis(lax.map(strip_gram, narrow), 0, 2)
        gram = gram.reshape(per_owner, slab_width, -1)
    return apply_inverse(gram, factor_inverse)


NEAR_FLIPS = (0, 0), (1, 2), (2, 1), (3, 3)


def shift(value, steps_z, e, flip_core=0):
    slabs, owners = lax.axis_size("rows"), lax.axis_size("cols")
    pairs = []
    for r in range(slabs):
        to_r = ((r // 2 + steps_z) % (slabs // 2)) * 2 + ((r % 2) ^ flip_core)
        for c in range(owners):
            pairs.append((r * owners + c, to_r * owners + (c ^ NEAR_FLIPS[e][r % 2])))
    return lax.ppermute(value, ("rows", "cols"), pairs)


def pack_kernel(sizes, lists_hbm, masks_hbm, order_hbm, weights_hbm, panel_hbm, jac_hbm, *refs):
    layers, owners, per_owner, block_count, slot_count, block_rows, tile_width = sizes
    weighted_ref, parcels = refs[0], refs[1 : 1 + layers]
    lists_ref, masks_ref, order_ref, weights_ref, panel_ref, jac_ref, places_ref, turned_ref, sems = refs[1 + layers :]
    copies = [
        pltpu.make_async_copy(order_hbm, order_ref, sems.at[0]),
        pltpu.make_async_copy(lists_hbm, lists_ref, sems.at[1]),
        pltpu.make_async_copy(masks_hbm, masks_ref, sems.at[2]),
        pltpu.make_async_copy(weights_hbm, weights_ref, sems.at[3]),
        pltpu.make_async_copy(panel_hbm, panel_ref, sems.at[4]),
        pltpu.make_async_copy(jac_hbm, jac_ref, sems.at[5]),
    ]
    for copy in copies:
        copy.start()
    f32, bf16 = jnp.float32, jnp.bfloat16
    rows, width = panel_ref.shape
    lane_group = CAP * block_rows
    slab = tile_width // layers
    part = slab // 2
    me_r, me_c = lax.axis_index("rows"), lax.axis_index("cols")
    me_z, me_core = me_r // 2, lax.rem(me_r, 2)
    for copy in copies:
        copy.wait()

    row_ids = lax.broadcasted_iota(jnp.int32, (rows, rows), 0)
    lane_ids = lax.broadcasted_iota(jnp.int32, (rows, rows), 1)
    column = jnp.sum(jnp.where(row_ids == lane_ids, weights_ref[...], 0.0), axis=1, keepdims=True)
    weighted = (column * panel_ref[...].astype(f32)).astype(bf16)
    weighted_ref[...] = weighted
    for parcel in parcels[1:]:
        for i in range(width // 128):
            parcel[i * rows : (i + 1) * rows, :] = weighted[:, i * 128 : (i + 1) * 128]

    for b in range(block_count):
        block = jac_ref[b * block_rows : (b + 1) * block_rows, :].astype(f32)
        start = b * slot_count * tile_width
        turned_ref[start : start + slot_count * tile_width, :] = block.T

    for i in range(order_ref.shape[0]):
        places_ref[order_ref[i]] = i
    slots = []
    for s in range(block_count * slot_count):
        b, k = divmod(s, slot_count)
        place = places_ref[lists_ref[b, k]]
        owner = jnp.int32(0)
        for c in range(1, owners):
            owner += (place >= c * per_owner).astype(jnp.int32)
        slots.append((place - owner * per_owner, jnp.where(masks_ref[b, k] == 1, owner, -1)))

    shape = (16, CAP * block_count * block_rows)
    lane = lax.broadcasted_iota(jnp.int32, shape, 1)
    notes = []
    for e in range(owners):
        wanted = me_c ^ jnp.where(me_core == 0, NEAR_FLIPS[e][0], NEAR_FLIPS[e][1])
        found = jnp.int32(0)
        chosen = [jnp.int32(0)] * CAP
        codes = [jnp.int32(-1)] * CAP
        for s, (place, owner) in enumerate(slots):
            hit = owner == wanted
            for j in range(CAP):
                take = hit & (found == j)
                chosen[j] = jnp.where(take, s, chosen[j])
                codes[j] = jnp.where(take, place, codes[j])
            found += hit.astype(jnp.int32)
        note = jnp.full(shape, -1, jnp.int32)
        for j in range(CAP):
            for b in range(block_count):
                at = (j * block_count + b) * block_rows
                here = (lane >= at) & (lane < at + block_rows)
                code = jnp.where(chosen[j] // slot_count == b, codes[j], -1)
                note = jnp.where(here, code, note)
        notes.append(note.astype(f32)[:1])
        for k, parcel in enumerate(parcels):
            z = lax.rem(me_z + k, layers)
            top = parcel.shape[0] - 16 - rows * (owners * lane_group // 128)
            for u in range(2):
                core = me_core ^ u
                for j in range(CAP):
                    first = pl.multiple_of(chosen[j] * tile_width + z * slab + core * part, part)
                    piece = turned_ref[pl.ds(first, part), :].astype(bf16)
                    below, to = divmod(e * lane_group + j * block_rows, 128)
                    start = top + below * rows + u * part
                    parcel[start : start + part, to : to + block_rows] = piece
    block = rows_from(notes)
    for parcel in parcels:
        parcel[parcel.shape[0] - 16 :, :] = block


def row_of(block, i):
    ids = lax.broadcasted_iota(jnp.int32, block.shape, 0)
    return jnp.sum(jnp.where(ids == i, block.astype(jnp.float32), 0.0), axis=0, keepdims=True)


def rows_from(notes):
    ids = lax.broadcasted_iota(jnp.int32, (16, notes[0].shape[1]), 0)
    block = jnp.full(ids.shape, -1.0, jnp.float32)
    for i, note in enumerate(notes):
        block = jnp.where(ids == i, note, block)
    return block.astype(jnp.bfloat16)


def sort_kernel(sizes, *refs):
    layers, owners, rows, width, lane_group = sizes
    parcels, (to_1_ref, to_2_ref, kept_ref) = refs[:layers], refs[-3:]
    part = rows // 2
    for k, parcel in enumerate(parcels[1:]):
        for i in range(width // 128):
            piece = parcel[i * rows : (i + 1) * rows, :]
            to_1_ref[k * rows : (k + 1) * rows, i * 128 : (i + 1) * 128] = piece
            to_2_ref[k * rows : (k + 1) * rows, i * 128 : (i + 1) * 128] = piece
    many = (layers - 1) * rows
    for e, (ref, start) in enumerate(((kept_ref, 0), (to_1_ref, many), (to_2_ref, many), (to_1_ref, many + part))):
        for k, parcel in enumerate(parcels):
            top = parcel.shape[0] - 16 - rows * (owners * lane_group // 128)
            below, lane = divmod(e * lane_group, 128)
            for u in range(2):
                at = top + below * rows + u * part
                to = (u * layers + k) * lane_group
                ref[start : start + part, to : to + lane_group] = parcel[at : at + part, lane : lane + lane_group]
    notes = [[row_of(parcel[parcel.shape[0] - 16 :, :], e) for parcel in parcels] for e in range(owners)]
    for ref, rows_of_codes in ((kept_ref, notes[0]), (to_1_ref, notes[1] + notes[3]), (to_2_ref, notes[2])):
        ref[ref.shape[0] - 16 :, :128] = rows_from(rows_of_codes)


def forward_1_kernel(many, by_1_ref, out_ref):
    first = out_ref.shape[0] - (by_1_ref.shape[0] - many - 16) // 2 - 16
    out_ref[:first, :] = by_1_ref[:first, :]
    out_ref[first:, :] = by_1_ref[by_1_ref.shape[0] - out_ref.shape[0] + first :, :]


def forward_2_kernel(many, first_2_ref, by_2_ref, out_ref):
    rows = first_2_ref.shape[0]
    out_ref[:rows, :] = first_2_ref[...]
    out_ref[rows:, :] = by_2_ref[many - out_ref.shape[0] + rows : many, :]


def place(out_ref, lanes, per_owner, pieces, notes, sizes):
    block_count, block_rows = sizes
    f32, bf16 = jnp.float32, jnp.bfloat16
    part, rows = pieces[0].shape[0], block_count * block_rows
    columns, codes = [], []
    for j in range(CAP):
        parts = []
        for piece in pieces:
            parts += [piece[:, j * block_rows : (j + 1) * block_rows].astype(f32)] * block_count
        columns.append(jnp.concatenate(parts, axis=1).astype(bf16))
        note = jnp.concatenate([note[:, j * rows : (j + 1) * rows] for note in notes], axis=1)
        codes.append(jnp.broadcast_to(note, columns[j].shape).astype(bf16))
    for n in range(per_owner):
        placed = jnp.zeros(columns[0].shape, bf16)
        for j in range(CAP):
            placed = jnp.where(codes[j] == jnp.asarray(n, bf16), columns[j], placed)
        out_ref[n * part : (n + 1) * part, lanes] = placed


def place_all(out_ref, start, sizes, u, columns, codes, row):
    layers, owners, per_owner, block_count, block_rows = sizes
    group, depth = CAP * block_rows, 2 * block_count * block_rows
    for h in range(layers // 2):
        pair = (2 * h, 2 * h + 1)
        pieces = [columns[:, (u * layers + k) * group : (u * layers + k + 1) * group] for k in pair]
        notes = [row_of(codes, row + k) for k in pair]
        lanes = slice(start + h * depth, start + (h + 1) * depth)
        place(out_ref, lanes, per_owner, pieces, notes, (block_count, block_rows))


def near_kernel(sizes, own_0_ref, own_ref, kept_ref, first_1_ref, by_1_ref, first_2_ref, by_2_ref, factor_ref, *refs):
    layers, owners, per_owner, block_count, block_rows = sizes
    sum_ref, other_sum_ref, high_ref, low_ref, placed_ref, rows_ref = refs
    f32, bf16 = jnp.float32, jnp.bfloat16
    turned = factor_ref[...].T
    high = turned.astype(bf16)
    high_ref[...] = high
    low_ref[...] = (turned - high.astype(f32)).astype(bf16)
    rows = block_count * block_rows
    part, many, depth = rows // 2, (layers - 1) * rows, layers * rows
    for e, (first_ref, ref) in enumerate(((own_0_ref, own_ref), (first_1_ref, by_1_ref), (first_2_ref, by_2_ref))):
        rows_ref[e * depth : e * depth + rows, :] = first_ref[...]
        rows_ref[e * depth + rows : (e + 1) * depth, :] = ref[:many, :]
    for u, out_ref in ((1, other_sum_ref), (0, sum_ref)):
        for e, (ref, start) in enumerate(((kept_ref, 0), (by_1_ref, many), (by_2_ref, many))):
            columns, codes = ref[start : start + part, :], ref[ref.shape[0] - 16 :, :128]
            place_all(placed_ref, e * depth, sizes, u, columns, codes, 0)
        out_ref[...] = jnp.dot(placed_ref[...], rows_ref[...], preferred_element_type=f32)


def far_kernel(sizes, u, near_ref, by_2_ref, by_1_ref, out_ref, placed_ref, rows_ref):
    layers, owners, per_owner, block_count, block_rows = sizes
    f32 = jnp.float32
    rows = block_count * block_rows
    part = rows // 2
    first = by_2_ref.shape[0] - part - 16
    rows_ref[:rows, :] = by_1_ref[:rows, :]
    rows_ref[rows : rows + first, :] = by_2_ref[:first, :]
    rows_ref[rows + first :, :] = by_1_ref[rows:, :]
    columns, codes = by_2_ref[first : first + part, :], by_2_ref[first + part :, :128]
    place_all(placed_ref, 0, sizes, u, columns, codes, layers)
    gram = near_ref[...] + jnp.dot(placed_ref[...], rows_ref[...], preferred_element_type=f32)
    out_ref[...] = gram.astype(out_ref.dtype)


def inverse_kernel(own_ref, other_ref, high_ref, low_ref, out_hbm, out_ref, sems):
    f32, bf16 = jnp.float32, jnp.bfloat16
    width = own_ref.shape[1]
    strips = sems.shape[0]
    height = own_ref.shape[0] // strips
    copies = []

    def times(a, b):
        return jnp.dot(a, b, preferred_element_type=f32)

    for i in range(strips):
        here = pl.ds(i * height, height)
        gram = own_ref[here, :] + other_ref[here, :].astype(f32)
        gram_high = gram.astype(bf16)
        gram_low = (gram - gram_high.astype(f32)).astype(bf16)
        for start, stop in ((0, width // 2), (width // 2, width)):
            high, low = high_ref[:stop, start:stop], low_ref[:stop, start:stop]
            a, b = gram_high[:, :stop], gram_low[:, :stop]
            out_ref[here, start:stop] = times(a, high) + (times(a, low) + times(b, high))
        copies.append(pltpu.make_async_copy(out_ref.at[here, :], out_hbm.at[here, :], sems.at[i]))
        copies[-1].start()
    for copy in copies:
        copy.wait()


def local(jac, panel_jac, weights, tile_lists, tile_masks, tile_order, factor_inverse):
    block_count, slot_count = tile_lists.shape
    rows, panel_width = panel_jac.shape
    block_rows = rows // block_count
    tile_width = jac.shape[1] // slot_count
    slabs, owners = lax.axis_size("rows"), lax.axis_size("cols")
    layers = slabs // 2
    per_owner = tile_order.shape[0] // owners
    slab_width = tile_width // slabs
    f32, bf16 = jnp.float32, jnp.bfloat16
    vmem, anywhere = pl.BlockSpec(memory_space=pltpu.VMEM), pl.BlockSpec(memory_space=pl.ANY)
    params = pltpu.CompilerParams(vmem_limit_bytes=24 << 20)
    shaped = jax.ShapeDtypeStruct

    def in_hbm(value):
        return pltpu.with_memory_space_constraint(value, pltpu.HBM)

    lane_group = CAP * block_rows
    sizes = (layers, owners, per_owner, block_count, slot_count, block_rows, tile_width)
    kept_height = rows * (owners * lane_group // 128) + 16
    height = rows * (panel_width // 128) + kept_height
    weighted, *parcels = pl.pallas_call(
        functools.partial(pack_kernel, sizes),
        out_shape=[shaped((rows, panel_width), bf16), shaped((kept_height, 128), bf16)]
        + [shaped((height, 128), bf16)] * (layers - 1),
        in_specs=[anywhere] * 6,
        out_specs=[vmem] * (layers + 1),
        scratch_shapes=[
            pltpu.SMEM(tile_lists.shape, jnp.int32),
            pltpu.SMEM(tile_masks.shape, jnp.int32),
            pltpu.SMEM(tile_order.shape, jnp.int32),
            pltpu.VMEM((1, rows), f32),
            pltpu.VMEM(panel_jac.shape, bf16),
            pltpu.VMEM(jac.shape, bf16),
            pltpu.SMEM(tile_order.shape, jnp.int32),
            pltpu.VMEM((block_count * slot_count * tile_width, block_rows), f32),
            pltpu.SemaphoreType.DMA((6,)),
        ],
        compiler_params=params,
        name="pack",
    )(*map(in_hbm, (tile_lists, tile_masks, tile_order, weights.reshape(1, rows), panel_jac, jac)))
    parcels = [parcels[0]] + [shift(parcels[k], k, 0) for k in range(1, layers)]
    first_1, first_2 = shift(weighted, 0, 1), shift(weighted, 0, 2)

    many, part = (layers - 1) * rows, rows // 2
    to_1, to_2, kept = pl.pallas_call(
        functools.partial(sort_kernel, (layers, owners, rows, panel_width, lane_group)),
        out_shape=[shaped((more + 16, panel_width), bf16) for more in (many + 2 * part, many + part, part)],
        in_specs=[vmem] * layers + [anywhere] * 2,
        out_specs=[vmem] * 3,
        compiler_params=params,
        name="sort",
    )(*parcels, first_1, first_2)
    by_1, by_2 = shift(to_1, 0, 1), shift(to_2, 0, 2)

    last = 16
    forward_1 = pl.pallas_call(
        functools.partial(forward_1_kernel, many),
        out_shape=shaped((many - last + part + 16, panel_width), bf16),
        in_specs=[vmem],
        out_specs=vmem,
        compiler_params=params,
        name="forward_1",
    )(by_1)
    across_2 = shift(forward_1, 0, 2)
    forward_2 = pl.pallas_call(
        functools.partial(forward_2_kernel, many),
        out_shape=shaped((rows + last, panel_width), bf16),
        in_specs=[vmem] * 2,
        out_specs=vmem,
        compiler_params=params,
        name="forward_2",
    )(first_2, by_2)
    across_1 = shift(forward_2, 0, 1)

    count = per_owner * slab_width
    depth = layers * rows
    sizes = (layers, owners, per_owner, block_count, block_rows)
    gram = shaped((count, panel_width), f32)
    own, other, high, low = pl.pallas_call(
        functools.partial(near_kernel, sizes),
        out_shape=[gram] * 2 + [shaped(factor_inverse.shape, bf16)] * 2,
        in_specs=[vmem] * 8,
        out_specs=[vmem] * 4,
        scratch_shapes=[
            pltpu.VMEM((count, (owners - 1) * depth), bf16),
            pltpu.VMEM(((owners - 1) * depth, panel_width), bf16),
        ],
        compiler_params=params,
        name="near",
    )(weighted, to_1, kept, first_1, by_1, first_2, by_2, factor_inverse)

    def far(u, near, kind):
        return pl.pallas_call(
            functools.partial(far_kernel, sizes, u),
            out_shape=shaped((count, panel_width), kind),
            in_specs=[vmem] * 3,
            out_specs=vmem,
            scratch_shapes=[pltpu.VMEM((count, depth), bf16), pltpu.VMEM((depth, panel_width), bf16)],
            compiler_params=params,
            name="far",
        )(near, across_2, across_1)

    other = shift(far(1, other, bf16), 0, 0, 1)
    out = pl.pallas_call(
        inverse_kernel,
        out_shape=shaped((count, panel_width), f32),
        in_specs=[vmem] * 4,
        out_specs=anywhere,
        scratch_shapes=[pltpu.VMEM((count, panel_width), f32), pltpu.SemaphoreType.DMA((3,))],
        compiler_params=params,
        name="inverse",
    )(far(0, own, f32), other, high, low)
    return out.reshape(per_owner, slab_width, panel_width)


def solution(mesh):
    in_specs = (
        P(("rows", "cols"), None),
        P(("rows", "cols"), None),
        P(("rows", "cols")),
        P(("rows", "cols"), None),
        P(("rows", "cols"), None),
        P(),
        P(),
    )
    out_specs = P("cols", "rows", None)
    body = local if (mesh.shape["rows"], mesh.shape["cols"]) == (8, 4) else local_general
    return jax.shard_map(body, mesh=mesh, in_specs=in_specs, out_specs=out_specs, check_vma=False)
```

```python
import functools

import jax
import jax.numpy as jnp
from jax import lax
from jax.experimental import pallas as pl
from jax.experimental.pallas import tpu as pltpu
from jax.sharding import PartitionSpec as P

CAP = 2
GATHERED = 1 << 22


def tile_positions(tile_lists, tile_order):
    tile_count = tile_order.shape[0]
    matches = tile_lists[:, :, None] == tile_order[None, None, :]
    return jnp.sum(jnp.where(matches, jnp.arange(tile_count, dtype=jnp.int32), 0), axis=2)


def apply_inverse(tiles, factor_inverse):
    return jnp.einsum("ntp,qp->ntq", tiles, factor_inverse, precision=lax.Precision.HIGHEST)


def slot_codes(tile_lists, tile_masks, tile_order, owner_ids):
    block_count, slot_count = tile_lists.shape
    per_owner = tile_order.shape[0] // lax.axis_size("cols")
    positions = tile_positions(tile_lists, tile_order).reshape(-1)
    active = tile_masks.reshape(-1) == 1
    owner = positions // per_owner
    same = (owner[:, None] == owner[None, :]) & active[None, :]
    earlier = jnp.tril(jnp.ones(same.shape, bool), -1)
    rank = jnp.sum(same & earlier, axis=1)
    code = (
        (owner[None, None, :] == owner_ids[:, None, None])
        & (rank[None, None, :] == jnp.arange(CAP)[None, :, None])
        & active[None, None, :]
    )
    block = jnp.arange(block_count * slot_count) // slot_count
    place = positions % per_owner + per_owner * block
    return code, jnp.sum(jnp.where(code, place + 1, 0), axis=2) - 1


def local_general(jac, panel_jac, weights, tile_lists, tile_masks, tile_order, factor_inverse):
    block_count, slot_count = tile_lists.shape
    block_rows = jac.shape[0] // block_count
    tile_width = jac.shape[1] // slot_count
    slabs, owners = lax.axis_size("rows"), lax.axis_size("cols")
    devices = slabs * owners
    per_owner = tile_order.shape[0] // owners
    slab_width = tile_width // slabs
    bf16 = jnp.bfloat16
    weighted = (weights[:, None] * panel_jac).astype(bf16)
    code, places = slot_codes(tile_lists, tile_masks, tile_order, jnp.arange(owners))
    columns = jac.reshape(block_count, block_rows, slot_count, slabs, slab_width)
    chosen = code.astype(bf16).reshape(owners, CAP, block_count, slot_count)
    pieces = jnp.einsum("cjbk,bmkrt->rcjmt", chosen, columns, preferred_element_type=jnp.float32).astype(bf16)
    pieces = pieces.reshape(devices, -1)
    note = jnp.broadcast_to(places.astype(bf16)[None], (slabs, owners, CAP)).reshape(devices, CAP)
    note = jnp.pad(note, ((0, 0), (0, 128 - CAP)))
    sent = jnp.concatenate([pieces, note], axis=1)
    got = lax.all_to_all(sent, ("rows", "cols"), split_axis=0, concat_axis=0, tiled=True)
    size = pieces.shape[1]
    data = got[:, :size].reshape(devices, CAP, block_rows, slab_width)
    where = got[:, size : size + CAP].astype(jnp.int32)
    hot = (where[:, :, None] == jnp.arange(block_count * per_owner)).astype(bf16)
    hot = hot.reshape(devices, CAP, block_count, per_owner)
    mixed = jnp.einsum("djbn,djmt->dbmnt", hot, data, preferred_element_type=jnp.float32).astype(bf16)
    strips = max(1, devices * weighted.size * 2 // GATHERED)

    def strip_gram(strip):
        panels = lax.all_gather(strip, ("rows", "cols"), axis=0, tiled=True)
        panels = panels.reshape(devices, block_count, block_rows, -1)
        return jnp.einsum("dbmnt,dbmp->ntp", mixed, panels, preferred_element_type=jnp.float32)

    if strips == 1:
        gram = strip_gram(weighted)
    else:
        narrow = weighted.reshape(weighted.shape[0], strips, -1).swapaxes(0, 1)
        gram = jnp.moveaxis(lax.map(strip_gram, narrow), 0, 2)
        gram = gram.reshape(per_owner, slab_width, -1)
    return apply_inverse(gram, factor_inverse)


def swap(value, flip_z, flip_cols, flip_core=0):
    slabs, owners = lax.axis_size("rows"), lax.axis_size("cols")
    pairs = []
    for r in range(slabs):
        to_r = r ^ (2 * flip_z + flip_core)
        for c in range(owners):
            pairs.append((r * owners + c, to_r * owners + (c ^ flip_cols)))
    return lax.ppermute(value, ("rows", "cols"), pairs)


def pack_kernel(sizes, lists_hbm, masks_hbm, order_hbm, weights_hbm, panel_hbm, jac_hbm, *refs):
    layers, owners, per_owner, block_count, slot_count, block_rows, tile_width = sizes
    weighted_ref, kept_ref, to_x_ref, to_y_ref = refs[:4]
    lists_ref, masks_ref, order_ref, weights_ref, panel_ref, jac_ref, places_ref, turned_ref, sems = refs[4:]
    copies = [
        pltpu.make_async_copy(order_hbm, order_ref, sems.at[0]),
        pltpu.make_async_copy(lists_hbm, lists_ref, sems.at[1]),
        pltpu.make_async_copy(masks_hbm, masks_ref, sems.at[2]),
        pltpu.make_async_copy(weights_hbm, weights_ref, sems.at[3]),
        pltpu.make_async_copy(panel_hbm, panel_ref, sems.at[4]),
        pltpu.make_async_copy(jac_hbm, jac_ref, sems.at[5]),
    ]
    for copy in copies:
        copy.start()
    f32, bf16 = jnp.float32, jnp.bfloat16
    rows, width = panel_ref.shape
    lane_group = CAP * block_rows
    post = layers * lane_group
    slab = tile_width // layers
    part = slab // 2
    me_r, me_c = lax.axis_index("rows"), lax.axis_index("cols")
    me_z, me_core = me_r // 2, lax.rem(me_r, 2)
    for copy in copies:
        copy.wait()

    row_ids = lax.broadcasted_iota(jnp.int32, (rows, rows), 0)
    lane_ids = lax.broadcasted_iota(jnp.int32, (rows, rows), 1)
    column = jnp.sum(jnp.where(row_ids == lane_ids, weights_ref[...], 0.0), axis=1, keepdims=True)
    weighted = (column * panel_ref[...].astype(f32)).astype(bf16)
    weighted_ref[...] = weighted
    to_x_ref[:, :width] = weighted
    to_y_ref[:, :width] = weighted

    for b in range(block_count):
        block = jac_ref[b * block_rows : (b + 1) * block_rows, :].astype(f32)
        start = b * slot_count * tile_width
        turned_ref[start : start + slot_count * tile_width, :] = block.T

    for i in range(order_ref.shape[0]):
        places_ref[order_ref[i]] = i
    slots = []
    for s in range(block_count * slot_count):
        b, k = divmod(s, slot_count)
        place = places_ref[lists_ref[b, k]]
        owner = jnp.int32(0)
        for c in range(1, owners):
            owner += (place >= c * per_owner).astype(jnp.int32)
        slots.append((place - owner * per_owner, jnp.where(masks_ref[b, k] == 1, owner, -1)))

    shape = (16, CAP * block_count * block_rows)
    lane, row = lax.broadcasted_iota(jnp.int32, shape, 1), lax.broadcasted_iota(jnp.int32, shape, 0)
    notes = []
    spots = [(kept_ref, 0), (to_x_ref, width), (to_y_ref, width), (to_y_ref, width + post)]
    for e, (parcel, start) in enumerate(spots):
        wanted = me_c ^ e
        found = jnp.int32(0)
        chosen = [jnp.int32(0)] * CAP
        codes = [jnp.int32(-1)] * CAP
        for s, (place, owner) in enumerate(slots):
            hit = owner == wanted
            for j in range(CAP):
                take = hit & (found == j)
                chosen[j] = jnp.where(take, s, chosen[j])
                codes[j] = jnp.where(take, place, codes[j])
            found += hit.astype(jnp.int32)
        note = jnp.full(shape, -1, jnp.int32)
        for j in range(CAP):
            for b in range(block_count):
                at = (j * block_count + b) * block_rows
                here = (lane >= at) & (lane < at + block_rows)
                code = jnp.where(chosen[j] // slot_count == b, codes[j], -1)
                note = jnp.where(here, code, note)
        notes.append(note)
        for k in range(layers):
            z = me_z ^ k
            for u in range(2):
                core = me_core ^ u
                for j in range(CAP):
                    first = pl.multiple_of(chosen[j] * tile_width + z * slab + core * part, part)
                    piece = turned_ref[pl.ds(first, part), :].astype(bf16)
                    to = start + k * lane_group + j * block_rows
                    parcel[u * part : (u + 1) * part, to : to + block_rows] = piece
    kept_ref[:16, post:] = notes[0].astype(f32).astype(bf16)
    to_x_ref[:16, width + post :] = notes[1].astype(f32).astype(bf16)
    to_y_ref[:16, width + 2 * post :] = jnp.where(row == 0, notes[2], notes[3]).astype(f32).astype(bf16)


def row_of(block, i):
    ids = lax.broadcasted_iota(jnp.int32, block.shape, 0)
    return jnp.sum(jnp.where(ids == i, block.astype(jnp.float32), 0.0), axis=0, keepdims=True)


def rows_from(notes):
    ids = lax.broadcasted_iota(jnp.int32, (16, notes[0].shape[1]), 0)
    block = jnp.full(ids.shape, -1.0, jnp.float32)
    for i, note in enumerate(notes):
        block = jnp.where(ids == i, note, block)
    return block.astype(jnp.bfloat16)


def sort_kernel(sizes, kept_ref, from_x_ref, from_y_ref, *refs):
    layers, width, lane_group, wide = sizes
    line, (stacked, *posts) = refs[: layers - 1], refs[layers - 1 :]
    post = layers * lane_group
    rows = kept_ref.shape[0]
    for k, ref in enumerate(line):
        stacked[k * rows : (k + 1) * rows, :] = ref[...]
    spots = [(kept_ref, 0), (from_x_ref, width), (from_y_ref, width), (from_y_ref, width + post)]
    notes = [row_of(ref[:16, ref.shape[1] - wide :], int(e == 3)) for e, (ref, start) in enumerate(spots)]
    block = rows_from(notes)
    for k, out in enumerate(posts):
        for e, (ref, start) in enumerate(spots):
            piece = ref[:, start + k * lane_group : start + (k + 1) * lane_group]
            out[:rows, e * lane_group : (e + 1) * lane_group] = piece
        out[rows:, :wide] = block


def rows_to_y_kernel(from_x_ref, by_x_ref, *refs):
    out_ref = refs[-1]
    rows = from_x_ref.shape[0]
    out_ref[:rows, :] = from_x_ref[:, : out_ref.shape[1]]
    out_ref[rows:, :] = by_x_ref[: out_ref.shape[0] - rows, :]


def rest_to_x_kernel(sizes, by_y_ref, *refs):
    layers, lane_group, wide = sizes
    posts, out_ref = refs[:layers], refs[layers]
    rows = posts[0].shape[0] - 16
    part = rows // 2
    last = out_ref.shape[0] - part - 16
    out_ref[:last, :] = by_y_ref[by_y_ref.shape[0] - last :, :]
    for k, ref in enumerate(posts):
        for u in range(2):
            piece = ref[u * part : (u + 1) * part, 3 * lane_group : 4 * lane_group]
            at = (u * layers + k) * lane_group
            out_ref[last : last + part, at : at + lane_group] = piece
    out_ref[last + part :, :wide] = rows_from([row_of(ref[rows:, :wide], 3) for ref in posts])


def place(out_ref, lanes, per_owner, pieces, notes, sizes):
    block_count, block_rows = sizes
    f32, bf16 = jnp.float32, jnp.bfloat16
    part, rows = pieces[0].shape[0], block_count * block_rows
    columns, codes = [], []
    for j in range(CAP):
        parts = []
        for piece in pieces:
            parts += [piece[:, j * block_rows : (j + 1) * block_rows].astype(f32)] * block_count
        columns.append(jnp.concatenate(parts, axis=1).astype(bf16))
        note = jnp.concatenate([note[:, j * rows : (j + 1) * rows] for note in notes], axis=1)
        codes.append(jnp.broadcast_to(note, columns[j].shape).astype(bf16))
    for n in range(per_owner):
        placed = jnp.zeros(columns[0].shape, bf16)
        for j in range(CAP):
            placed = jnp.where(codes[j] == jnp.asarray(n, bf16), columns[j], placed)
        out_ref[n * part : (n + 1) * part, lanes] = placed


def near_kernel(sizes, *refs):
    layers, owners, per_owner, block_count, block_rows = sizes
    panels, posts, factor_ref = refs[: 2 * (owners - 1)], refs[2 * (owners - 1) :][:layers], refs[2 * owners - 2 + layers]
    own_ref, other_ref, high_ref, low_ref, placed_ref, rows_ref = refs[2 * owners - 1 + layers :]
    f32, bf16 = jnp.float32, jnp.bfloat16
    turned = factor_ref[...].T
    high = turned.astype(bf16)
    high_ref[...] = high
    low_ref[...] = (turned - high.astype(f32)).astype(bf16)
    rows = block_count * block_rows
    group, wide = CAP * block_rows, CAP * rows
    part = rows // 2
    width = rows_ref.shape[1]
    at = 0
    for panel in panels:
        rows_ref[at : at + panel.shape[0], :] = panel[:, :width]
        at += panel.shape[0]
    for u, out_ref in ((1, other_ref), (0, own_ref)):
        for e in range(owners - 1):
            for h in range(layers // 2):
                pair = posts[2 * h : 2 * h + 2]
                pieces = [post[u * part : (u + 1) * part, e * group : (e + 1) * group] for post in pair]
                notes = [row_of(post[rows:, :wide], e) for post in pair]
                start = (e * layers + 2 * h) * rows
                place(placed_ref, slice(start, start + 2 * rows), per_owner, pieces, notes, (block_count, block_rows))
        out_ref[...] = jnp.dot(placed_ref[...], rows_ref[...], preferred_element_type=f32)


def far_kernel(sizes, u, near_ref, by_y_ref, by_x_ref, out_ref, placed_ref, rows_ref):
    layers, owners, per_owner, block_count, block_rows = sizes
    f32, bf16 = jnp.float32, jnp.bfloat16
    rows = block_count * block_rows
    group, wide = CAP * block_rows, CAP * rows
    part = rows // 2
    first = by_y_ref.shape[0]
    last = rows_ref.shape[0] - first
    rows_ref[:first, :] = by_y_ref[...]
    rows_ref[first:, :] = by_x_ref[:last, :]
    for h in range(layers // 2):
        pieces, notes = [], []
        for k in (2 * h, 2 * h + 1):
            at = (u * layers + k) * group
            pieces.append(by_x_ref[last : last + part, at : at + group])
            notes.append(row_of(by_x_ref[last + part :, :wide], k))
        start = 2 * h * rows
        place(placed_ref, slice(start, start + 2 * rows), per_owner, pieces, notes, (block_count, block_rows))
    gram = near_ref[...] + jnp.dot(placed_ref[...], rows_ref[...], preferred_element_type=f32)
    out_ref[...] = gram.astype(out_ref.dtype)


def times_inverse(gram, high, low):
    f32, bf16 = jnp.float32, jnp.bfloat16
    width = gram.shape[1]
    first = gram.astype(bf16)
    parts = []
    for start, stop in ((0, width // 2), (width // 2, width)):
        a, b = high[:stop, start:stop], low[:stop, start:stop]
        total = jnp.dot(first[:, :stop], a, preferred_element_type=f32)
        total += jnp.dot(first[:, :stop], b, preferred_element_type=f32)
        if gram.dtype == f32:
            second = (gram - first.astype(f32)).astype(bf16)
            total += jnp.dot(second[:, :stop], a, preferred_element_type=f32)
        parts.append(total)
    return parts


def own_inverse_kernel(gram_ref, high_ref, low_ref, out_ref):
    half = out_ref.shape[1] // 2
    left, right = times_inverse(gram_ref[...], high_ref[...], low_ref[...])
    out_ref[:, :half] = left
    out_ref[:, half:] = right


def sum_kernel(own_ref, other_ref, high_ref, low_ref, out_hbm, out_ref, sems):
    strips = sems.shape[0]
    height, half = own_ref.shape[0] // strips, own_ref.shape[1] // 2
    copies = []
    for i in range(strips):
        here = pl.ds(i * height, height)
        left, right = times_inverse(other_ref[here, :], high_ref[...], low_ref[...])
        out_ref[here, :half] = own_ref[here, :half] + left
        out_ref[here, half:] = own_ref[here, half:] + right
        copies.append(pltpu.make_async_copy(out_ref.at[here, :], out_hbm.at[here, :], sems.at[i]))
        copies[-1].start()
    for copy in copies:
        copy.wait()


def local(jac, panel_jac, weights, tile_lists, tile_masks, tile_order, factor_inverse):
    block_count, slot_count = tile_lists.shape
    rows, panel_width = panel_jac.shape
    block_rows = rows // block_count
    tile_width = jac.shape[1] // slot_count
    slabs, owners = lax.axis_size("rows"), lax.axis_size("cols")
    layers = slabs // 2
    per_owner = tile_order.shape[0] // owners
    slab_width = tile_width // slabs
    f32, bf16 = jnp.float32, jnp.bfloat16
    vmem, anywhere = pl.BlockSpec(memory_space=pltpu.VMEM), pl.BlockSpec(memory_space=pl.ANY)
    params = pltpu.CompilerParams(vmem_limit_bytes=24 << 20)
    shaped = jax.ShapeDtypeStruct

    def in_hbm(value):
        return pltpu.with_memory_space_constraint(value, pltpu.HBM)

    lane_group = CAP * block_rows
    post = layers * lane_group
    wide = CAP * rows
    sizes = (layers, owners, per_owner, block_count, slot_count, block_rows, tile_width)
    weighted, kept, to_x, to_y = pl.pallas_call(
        functools.partial(pack_kernel, sizes),
        out_shape=[
            shaped((rows, width), bf16)
            for width in (panel_width, post + wide, panel_width + post + wide, panel_width + 2 * post + wide)
        ],
        in_specs=[anywhere] * 6,
        out_specs=[vmem] * 4,
        scratch_shapes=[
            pltpu.SMEM(tile_lists.shape, jnp.int32),
            pltpu.SMEM(tile_masks.shape, jnp.int32),
            pltpu.SMEM(tile_order.shape, jnp.int32),
            pltpu.VMEM((1, rows), f32),
            pltpu.VMEM(panel_jac.shape, bf16),
            pltpu.VMEM(jac.shape, bf16),
            pltpu.SMEM(tile_order.shape, jnp.int32),
            pltpu.VMEM((block_count * slot_count * tile_width, block_rows), f32),
            pltpu.SemaphoreType.DMA((6,)),
        ],
        compiler_params=params,
        name="pack",
    )(*map(in_hbm, (tile_lists, tile_masks, tile_order, weights.reshape(1, rows), panel_jac, jac)))
    line = [swap(weighted, k, 0) for k in range(1, layers)]
    from_x, from_y = swap(to_x, 0, 1), swap(to_y, 0, 2)

    sizes = (layers, panel_width, lane_group, wide)
    others, *posts = pl.pallas_call(
        functools.partial(sort_kernel, sizes),
        out_shape=[shaped(((layers - 1) * rows, panel_width), bf16)]
        + [shaped((rows + 16, owners * lane_group), bf16)] * layers,
        in_specs=[vmem] * (layers + 2),
        out_specs=[vmem] * (layers + 1),
        compiler_params=params,
        name="sort",
    )(kept, from_x, from_y, *line)
    posts = [posts[0]] + [swap(posts[k], k, 0) for k in range(1, layers)]
    by_x, by_y = swap(others, 0, 1), swap(others, 0, 2)

    last = rows // 2
    rows_to_y = pl.pallas_call(
        rows_to_y_kernel,
        out_shape=shaped((rows + others.shape[0] - last, panel_width), bf16),
        in_specs=[vmem] * 2 + [anywhere] * (layers - 1),
        out_specs=vmem,
        compiler_params=params,
        name="rows_to_y",
    )(from_x, by_x, *posts[1:])
    across_y = swap(rows_to_y, 0, 2)
    rest_to_x = pl.pallas_call(
        functools.partial(rest_to_x_kernel, (layers, lane_group, wide)),
        out_shape=shaped((last + rows // 2 + 16, panel_width), bf16),
        in_specs=[vmem] * (layers + 1),
        out_specs=vmem,
        compiler_params=params,
        name="rest_to_x",
    )(by_y, *posts)
    across_x = swap(rest_to_x, 0, 1)

    count = per_owner * slab_width
    depth = layers * rows
    sizes = (layers, owners, per_owner, block_count, block_rows)
    gram = shaped((count, panel_width), f32)
    panels = [weighted, others, from_x, by_x, from_y, by_y]
    own, other, high, low = pl.pallas_call(
        functools.partial(near_kernel, sizes),
        out_shape=[gram] * 2 + [shaped(factor_inverse.shape, bf16)] * 2,
        in_specs=[vmem] * (len(panels) + layers + 1),
        out_specs=[vmem] * 4,
        scratch_shapes=[
            pltpu.VMEM((count, (owners - 1) * depth), bf16),
            pltpu.VMEM(((owners - 1) * depth, panel_width), bf16),
        ],
        compiler_params=params,
        name="near",
    )(*panels, *posts, factor_inverse)

    def far(u, near, kind):
        return pl.pallas_call(
            functools.partial(far_kernel, sizes, u),
            out_shape=shaped((count, panel_width), kind),
            in_specs=[vmem] * 3,
            out_specs=vmem,
            scratch_shapes=[pltpu.VMEM((count, depth), bf16), pltpu.VMEM((depth, panel_width), bf16)],
            compiler_params=params,
            name="far",
        )(near, across_y, across_x)

    other = swap(far(1, other, bf16), 0, 0, 1)
    own = pl.pallas_call(
        own_inverse_kernel,
        out_shape=gram,
        in_specs=[vmem] * 3,
        out_specs=vmem,
        compiler_params=params,
        name="own_inverse",
    )(far(0, own, f32), high, low)
    out = pl.pallas_call(
        sum_kernel,
        out_shape=gram,
        in_specs=[vmem] * 4,
        out_specs=anywhere,
        scratch_shapes=[pltpu.VMEM((count, panel_width), f32), pltpu.SemaphoreType.DMA((3,))],
        compiler_params=params,
        name="sum",
    )(own, other, high, low)
    return out.reshape(per_owner, slab_width, panel_width)


def solution(mesh):
    in_specs = (
        P(("rows", "cols"), None),
        P(("rows", "cols"), None),
        P(("rows", "cols")),
        P(("rows", "cols"), None),
        P(("rows", "cols"), None),
        P(),
        P(),
    )
    out_specs = P("cols", "rows", None)
    body = local if (mesh.shape["rows"], mesh.shape["cols"]) == (8, 4) else local_general
    return jax.shard_map(body, mesh=mesh, in_specs=in_specs, out_specs=out_specs, check_vma=False)
```

```python
import functools

import jax
import jax.numpy as jnp
from jax import lax
from jax.experimental import pallas as pl
from jax.experimental.pallas import tpu as pltpu
from jax.sharding import PartitionSpec as P

CAP = 2
GATHERED = 1 << 22


def tile_positions(tile_lists, tile_order):
    tile_count = tile_order.shape[0]
    matches = tile_lists[:, :, None] == tile_order[None, None, :]
    return jnp.sum(jnp.where(matches, jnp.arange(tile_count, dtype=jnp.int32), 0), axis=2)


def apply_inverse(tiles, factor_inverse):
    return jnp.einsum("ntp,qp->ntq", tiles, factor_inverse, precision=lax.Precision.HIGHEST)


def slot_codes(tile_lists, tile_masks, tile_order, owner_ids):
    block_count, slot_count = tile_lists.shape
    per_owner = tile_order.shape[0] // lax.axis_size("cols")
    positions = tile_positions(tile_lists, tile_order).reshape(-1)
    active = tile_masks.reshape(-1) == 1
    owner = positions // per_owner
    same = (owner[:, None] == owner[None, :]) & active[None, :]
    earlier = jnp.tril(jnp.ones(same.shape, bool), -1)
    rank = jnp.sum(same & earlier, axis=1)
    code = (
        (owner[None, None, :] == owner_ids[:, None, None])
        & (rank[None, None, :] == jnp.arange(CAP)[None, :, None])
        & active[None, None, :]
    )
    block = jnp.arange(block_count * slot_count) // slot_count
    place = positions % per_owner + per_owner * block
    return code, jnp.sum(jnp.where(code, place + 1, 0), axis=2) - 1


def local_general(jac, panel_jac, weights, tile_lists, tile_masks, tile_order, factor_inverse):
    block_count, slot_count = tile_lists.shape
    block_rows = jac.shape[0] // block_count
    tile_width = jac.shape[1] // slot_count
    slabs, owners = lax.axis_size("rows"), lax.axis_size("cols")
    devices = slabs * owners
    per_owner = tile_order.shape[0] // owners
    slab_width = tile_width // slabs
    bf16 = jnp.bfloat16
    weighted = (weights[:, None] * panel_jac).astype(bf16)
    code, places = slot_codes(tile_lists, tile_masks, tile_order, jnp.arange(owners))
    columns = jac.reshape(block_count, block_rows, slot_count, slabs, slab_width)
    chosen = code.astype(bf16).reshape(owners, CAP, block_count, slot_count)
    pieces = jnp.einsum("cjbk,bmkrt->rcjmt", chosen, columns, preferred_element_type=jnp.float32).astype(bf16)
    pieces = pieces.reshape(devices, -1)
    note = jnp.broadcast_to(places.astype(bf16)[None], (slabs, owners, CAP)).reshape(devices, CAP)
    note = jnp.pad(note, ((0, 0), (0, 128 - CAP)))
    sent = jnp.concatenate([pieces, note], axis=1)
    got = lax.all_to_all(sent, ("rows", "cols"), split_axis=0, concat_axis=0, tiled=True)
    size = pieces.shape[1]
    data = got[:, :size].reshape(devices, CAP, block_rows, slab_width)
    where = got[:, size : size + CAP].astype(jnp.int32)
    hot = (where[:, :, None] == jnp.arange(block_count * per_owner)).astype(bf16)
    hot = hot.reshape(devices, CAP, block_count, per_owner)
    mixed = jnp.einsum("djbn,djmt->dbmnt", hot, data, preferred_element_type=jnp.float32).astype(bf16)
    strips = max(1, devices * weighted.size * 2 // GATHERED)

    def strip_gram(strip):
        panels = lax.all_gather(strip, ("rows", "cols"), axis=0, tiled=True)
        panels = panels.reshape(devices, block_count, block_rows, -1)
        return jnp.einsum("dbmnt,dbmp->ntp", mixed, panels, preferred_element_type=jnp.float32)

    if strips == 1:
        gram = strip_gram(weighted)
    else:
        narrow = weighted.reshape(weighted.shape[0], strips, -1).swapaxes(0, 1)
        gram = jnp.moveaxis(lax.map(strip_gram, narrow), 0, 2)
        gram = gram.reshape(per_owner, slab_width, -1)
    return apply_inverse(gram, factor_inverse)


def shift(value, steps_z, flip_cols, flip_core=0):
    slabs, owners = lax.axis_size("rows"), lax.axis_size("cols")
    pairs = []
    for r in range(slabs):
        to_r = ((r // 2 + steps_z) % (slabs // 2)) * 2 + ((r % 2) ^ flip_core)
        for c in range(owners):
            pairs.append((r * owners + c, to_r * owners + (c ^ flip_cols)))
    return lax.ppermute(value, ("rows", "cols"), pairs)


def pack_kernel(sizes, lists_hbm, masks_hbm, order_hbm, weights_hbm, panel_hbm, jac_hbm, *refs):
    layers, owners, per_owner, block_count, slot_count, block_rows, tile_width = sizes
    weighted_ref, kept_ref, to_x_ref, to_y_ref = refs[:4]
    lists_ref, masks_ref, order_ref, weights_ref, panel_ref, jac_ref, places_ref, turned_ref, sems = refs[4:]
    copies = [
        pltpu.make_async_copy(order_hbm, order_ref, sems.at[0]),
        pltpu.make_async_copy(lists_hbm, lists_ref, sems.at[1]),
        pltpu.make_async_copy(masks_hbm, masks_ref, sems.at[2]),
        pltpu.make_async_copy(weights_hbm, weights_ref, sems.at[3]),
        pltpu.make_async_copy(panel_hbm, panel_ref, sems.at[4]),
        pltpu.make_async_copy(jac_hbm, jac_ref, sems.at[5]),
    ]
    for copy in copies:
        copy.start()
    f32, bf16 = jnp.float32, jnp.bfloat16
    rows, width = panel_ref.shape
    lane_group = CAP * block_rows
    post = layers * lane_group
    slab = tile_width // layers
    part = slab // 2
    me_r, me_c = lax.axis_index("rows"), lax.axis_index("cols")
    me_z, me_core = me_r // 2, lax.rem(me_r, 2)
    for copy in copies:
        copy.wait()

    row_ids = lax.broadcasted_iota(jnp.int32, (rows, rows), 0)
    lane_ids = lax.broadcasted_iota(jnp.int32, (rows, rows), 1)
    column = jnp.sum(jnp.where(row_ids == lane_ids, weights_ref[...], 0.0), axis=1, keepdims=True)
    weighted = (column * panel_ref[...].astype(f32)).astype(bf16)
    weighted_ref[...] = weighted
    to_x_ref[:, :width] = weighted
    to_y_ref[:, :width] = weighted

    for b in range(block_count):
        block = jac_ref[b * block_rows : (b + 1) * block_rows, :].astype(f32)
        start = b * slot_count * tile_width
        turned_ref[start : start + slot_count * tile_width, :] = block.T

    for i in range(order_ref.shape[0]):
        places_ref[order_ref[i]] = i
    slots = []
    for s in range(block_count * slot_count):
        b, k = divmod(s, slot_count)
        place = places_ref[lists_ref[b, k]]
        owner = jnp.int32(0)
        for c in range(1, owners):
            owner += (place >= c * per_owner).astype(jnp.int32)
        slots.append((place - owner * per_owner, jnp.where(masks_ref[b, k] == 1, owner, -1)))

    shape = (16, CAP * block_count * block_rows)
    lane, row = lax.broadcasted_iota(jnp.int32, shape, 1), lax.broadcasted_iota(jnp.int32, shape, 0)
    notes = []
    spots = [(kept_ref, 0), (to_x_ref, width), (to_y_ref, width), (to_y_ref, width + post)]
    for e, (parcel, start) in enumerate(spots):
        wanted = me_c ^ e
        found = jnp.int32(0)
        chosen = [jnp.int32(0)] * CAP
        codes = [jnp.int32(-1)] * CAP
        for s, (place, owner) in enumerate(slots):
            hit = owner == wanted
            for j in range(CAP):
                take = hit & (found == j)
                chosen[j] = jnp.where(take, s, chosen[j])
                codes[j] = jnp.where(take, place, codes[j])
            found += hit.astype(jnp.int32)
        note = jnp.full(shape, -1, jnp.int32)
        for j in range(CAP):
            for b in range(block_count):
                at = (j * block_count + b) * block_rows
                here = (lane >= at) & (lane < at + block_rows)
                code = jnp.where(chosen[j] // slot_count == b, codes[j], -1)
                note = jnp.where(here, code, note)
        notes.append(note)
        for k in range(layers):
            z = lax.rem(me_z + k, layers)
            for u in range(2):
                core = me_core ^ u
                for j in range(CAP):
                    first = pl.multiple_of(chosen[j] * tile_width + z * slab + core * part, part)
                    piece = turned_ref[pl.ds(first, part), :].astype(bf16)
                    to = start + k * lane_group + j * block_rows
                    parcel[u * part : (u + 1) * part, to : to + block_rows] = piece
    kept_ref[:16, post:] = notes[0].astype(f32).astype(bf16)
    to_x_ref[:16, width + post :] = notes[1].astype(f32).astype(bf16)
    to_y_ref[:16, width + 2 * post :] = jnp.where(row == 0, notes[2], notes[3]).astype(f32).astype(bf16)


def row_of(block, i):
    ids = lax.broadcasted_iota(jnp.int32, block.shape, 0)
    return jnp.sum(jnp.where(ids == i, block.astype(jnp.float32), 0.0), axis=0, keepdims=True)


def rows_from(notes):
    ids = lax.broadcasted_iota(jnp.int32, (16, notes[0].shape[1]), 0)
    block = jnp.full(ids.shape, -1.0, jnp.float32)
    for i, note in enumerate(notes):
        block = jnp.where(ids == i, note, block)
    return block.astype(jnp.bfloat16)


def sort_kernel(sizes, kept_ref, from_x_ref, from_y_ref, *refs):
    layers, width, lane_group, wide = sizes
    line, (stacked, *posts) = refs[: layers - 1], refs[layers - 1 :]
    post = layers * lane_group
    rows = kept_ref.shape[0]
    for k, ref in enumerate(line):
        stacked[k * rows : (k + 1) * rows, :] = ref[...]
    spots = [(kept_ref, 0), (from_x_ref, width), (from_y_ref, width), (from_y_ref, width + post)]
    notes = [row_of(ref[:16, ref.shape[1] - wide :], int(e == 3)) for e, (ref, start) in enumerate(spots)]
    block = rows_from(notes)
    for k, out in enumerate(posts):
        for e, (ref, start) in enumerate(spots):
            piece = ref[:, start + k * lane_group : start + (k + 1) * lane_group]
            out[:rows, e * lane_group : (e + 1) * lane_group] = piece
        out[rows:, :wide] = block


def rows_to_y_kernel(from_x_ref, by_x_ref, *refs):
    out_ref = refs[-1]
    rows = from_x_ref.shape[0]
    out_ref[:rows, :] = from_x_ref[:, : out_ref.shape[1]]
    out_ref[rows:, :] = by_x_ref[: out_ref.shape[0] - rows, :]


def rest_to_x_kernel(sizes, by_y_ref, *refs):
    layers, lane_group, wide = sizes
    posts, out_ref = refs[:layers], refs[layers]
    rows = posts[0].shape[0] - 16
    part = rows // 2
    last = out_ref.shape[0] - part - 16
    out_ref[:last, :] = by_y_ref[by_y_ref.shape[0] - last :, :]
    for k, ref in enumerate(posts):
        for u in range(2):
            piece = ref[u * part : (u + 1) * part, 3 * lane_group : 4 * lane_group]
            at = (u * layers + k) * lane_group
            out_ref[last : last + part, at : at + lane_group] = piece
    out_ref[last + part :, :wide] = rows_from([row_of(ref[rows:, :wide], 3) for ref in posts])


def place(out_ref, lanes, per_owner, pieces, notes, sizes):
    block_count, block_rows = sizes
    f32, bf16 = jnp.float32, jnp.bfloat16
    part, rows = pieces[0].shape[0], block_count * block_rows
    columns, codes = [], []
    for j in range(CAP):
        parts = []
        for piece in pieces:
            parts += [piece[:, j * block_rows : (j + 1) * block_rows].astype(f32)] * block_count
        columns.append(jnp.concatenate(parts, axis=1).astype(bf16))
        note = jnp.concatenate([note[:, j * rows : (j + 1) * rows] for note in notes], axis=1)
        codes.append(jnp.broadcast_to(note, columns[j].shape).astype(bf16))
    for n in range(per_owner):
        placed = jnp.zeros(columns[0].shape, bf16)
        for j in range(CAP):
            placed = jnp.where(codes[j] == jnp.asarray(n, bf16), columns[j], placed)
        out_ref[n * part : (n + 1) * part, lanes] = placed


def near_kernel(sizes, *refs):
    layers, owners, per_owner, block_count, block_rows = sizes
    panels, posts, factor_ref = refs[: 2 * (owners - 1)], refs[2 * (owners - 1) :][:layers], refs[2 * owners - 2 + layers]
    own_ref, other_ref, high_ref, low_ref, placed_ref, rows_ref = refs[2 * owners - 1 + layers :]
    f32, bf16 = jnp.float32, jnp.bfloat16
    turned = factor_ref[...].T
    high = turned.astype(bf16)
    high_ref[...] = high
    low_ref[...] = (turned - high.astype(f32)).astype(bf16)
    rows = block_count * block_rows
    group, wide = CAP * block_rows, CAP * rows
    part = rows // 2
    width = rows_ref.shape[1]
    at = 0
    for panel in panels:
        rows_ref[at : at + panel.shape[0], :] = panel[:, :width]
        at += panel.shape[0]
    for u, out_ref in ((1, other_ref), (0, own_ref)):
        for e in range(owners - 1):
            for h in range(layers // 2):
                pair = posts[2 * h : 2 * h + 2]
                pieces = [post[u * part : (u + 1) * part, e * group : (e + 1) * group] for post in pair]
                notes = [row_of(post[rows:, :wide], e) for post in pair]
                start = (e * layers + 2 * h) * rows
                place(placed_ref, slice(start, start + 2 * rows), per_owner, pieces, notes, (block_count, block_rows))
        out_ref[...] = jnp.dot(placed_ref[...], rows_ref[...], preferred_element_type=f32)


def far_kernel(sizes, u, near_ref, by_y_ref, by_x_ref, *refs):
    out_refs, (placed_ref, rows_ref) = refs[:-2], refs[-2:]
    layers, owners, per_owner, block_count, block_rows = sizes
    f32, bf16 = jnp.float32, jnp.bfloat16
    rows = block_count * block_rows
    group, wide = CAP * block_rows, CAP * rows
    part = rows // 2
    first = by_y_ref.shape[0]
    last = rows_ref.shape[0] - first
    rows_ref[:first, :] = by_y_ref[...]
    rows_ref[first:, :] = by_x_ref[:last, :]
    for h in range(layers // 2):
        pieces, notes = [], []
        for k in (2 * h, 2 * h + 1):
            at = (u * layers + k) * group
            pieces.append(by_x_ref[last : last + part, at : at + group])
            notes.append(row_of(by_x_ref[last + part :, :wide], k))
        start = 2 * h * rows
        place(placed_ref, slice(start, start + 2 * rows), per_owner, pieces, notes, (block_count, block_rows))
    for i, out_ref in enumerate(out_refs):
        here = pl.ds(i * out_ref.shape[0], out_ref.shape[0])
        gram = near_ref[here, :] + jnp.dot(placed_ref[here, :], rows_ref[...], preferred_element_type=f32)
        out_ref[...] = gram.astype(out_ref.dtype)


def times_inverse(gram, high, low):
    f32, bf16 = jnp.float32, jnp.bfloat16
    width = gram.shape[1]
    first = gram.astype(bf16)
    parts = []
    for start, stop in ((0, width // 2), (width // 2, width)):
        a, b = high[:stop, start:stop], low[:stop, start:stop]
        total = jnp.dot(first[:, :stop], a, preferred_element_type=f32)
        total += jnp.dot(first[:, :stop], b, preferred_element_type=f32)
        if gram.dtype == f32:
            second = (gram - first.astype(f32)).astype(bf16)
            total += jnp.dot(second[:, :stop], a, preferred_element_type=f32)
        parts.append(total)
    return parts


def own_inverse_kernel(gram_ref, high_ref, low_ref, out_ref):
    half = out_ref.shape[1] // 2
    left, right = times_inverse(gram_ref[...], high_ref[...], low_ref[...])
    out_ref[:, :half] = left
    out_ref[:, half:] = right


def sum_kernel(top, own_ref, other_ref, high_ref, low_ref, *refs):
    out_hbm, out_ref, sems = refs[-3:]
    strips = sems.shape[0]
    height, half = other_ref.shape[0] // strips, own_ref.shape[1] // 2
    copies = []
    for i in range(strips):
        here, there = pl.ds(i * height, height), pl.ds(top + i * height, height)
        left, right = times_inverse(other_ref[here, :], high_ref[...], low_ref[...])
        out_ref[here, :half] = own_ref[there, :half] + left
        out_ref[here, half:] = own_ref[there, half:] + right
        copies.append(pltpu.make_async_copy(out_ref.at[here, :], out_hbm.at[there, :], sems.at[i]))
        copies[-1].start()
    for copy in copies:
        copy.wait()


def local(jac, panel_jac, weights, tile_lists, tile_masks, tile_order, factor_inverse):
    block_count, slot_count = tile_lists.shape
    rows, panel_width = panel_jac.shape
    block_rows = rows // block_count
    tile_width = jac.shape[1] // slot_count
    slabs, owners = lax.axis_size("rows"), lax.axis_size("cols")
    layers = slabs // 2
    per_owner = tile_order.shape[0] // owners
    slab_width = tile_width // slabs
    f32, bf16 = jnp.float32, jnp.bfloat16
    vmem, anywhere = pl.BlockSpec(memory_space=pltpu.VMEM), pl.BlockSpec(memory_space=pl.ANY)
    params = pltpu.CompilerParams(vmem_limit_bytes=24 << 20)
    shaped = jax.ShapeDtypeStruct

    def in_hbm(value):
        return pltpu.with_memory_space_constraint(value, pltpu.HBM)

    lane_group = CAP * block_rows
    post = layers * lane_group
    wide = CAP * rows
    sizes = (layers, owners, per_owner, block_count, slot_count, block_rows, tile_width)
    weighted, kept, to_x, to_y = pl.pallas_call(
        functools.partial(pack_kernel, sizes),
        out_shape=[
            shaped((rows, width), bf16)
            for width in (panel_width, post + wide, panel_width + post + wide, panel_width + 2 * post + wide)
        ],
        in_specs=[anywhere] * 6,
        out_specs=[vmem] * 4,
        scratch_shapes=[
            pltpu.SMEM(tile_lists.shape, jnp.int32),
            pltpu.SMEM(tile_masks.shape, jnp.int32),
            pltpu.SMEM(tile_order.shape, jnp.int32),
            pltpu.VMEM((1, rows), f32),
            pltpu.VMEM(panel_jac.shape, bf16),
            pltpu.VMEM(jac.shape, bf16),
            pltpu.SMEM(tile_order.shape, jnp.int32),
            pltpu.VMEM((block_count * slot_count * tile_width, block_rows), f32),
            pltpu.SemaphoreType.DMA((6,)),
        ],
        compiler_params=params,
        name="pack",
    )(*map(in_hbm, (tile_lists, tile_masks, tile_order, weights.reshape(1, rows), panel_jac, jac)))
    line = [shift(weighted, k, 0) for k in range(1, layers)]
    from_x, from_y = shift(to_x, 0, 1), shift(to_y, 0, 2)

    sizes = (layers, panel_width, lane_group, wide)
    others, *posts = pl.pallas_call(
        functools.partial(sort_kernel, sizes),
        out_shape=[shaped(((layers - 1) * rows, panel_width), bf16)]
        + [shaped((rows + 16, owners * lane_group), bf16)] * layers,
        in_specs=[vmem] * (layers + 2),
        out_specs=[vmem] * (layers + 1),
        compiler_params=params,
        name="sort",
    )(kept, from_x, from_y, *line)
    posts = [posts[0]] + [shift(posts[k], k, 0) for k in range(1, layers)]
    by_x, by_y = shift(others, 0, 1), shift(others, 0, 2)

    last = rows // 2
    rows_to_y = pl.pallas_call(
        rows_to_y_kernel,
        out_shape=shaped((rows + others.shape[0] - last, panel_width), bf16),
        in_specs=[vmem] * 2 + [anywhere] * (layers - 1),
        out_specs=vmem,
        compiler_params=params,
        name="rows_to_y",
    )(from_x, by_x, *posts[1:])
    across_y = shift(rows_to_y, 0, 2)
    rest_to_x = pl.pallas_call(
        functools.partial(rest_to_x_kernel, (layers, lane_group, wide)),
        out_shape=shaped((last + rows // 2 + 16, panel_width), bf16),
        in_specs=[vmem] * (layers + 1),
        out_specs=vmem,
        compiler_params=params,
        name="rest_to_x",
    )(by_y, *posts)
    across_x = shift(rest_to_x, 0, 1)

    count = per_owner * slab_width
    depth = layers * rows
    sizes = (layers, owners, per_owner, block_count, block_rows)
    gram = shaped((count, panel_width), f32)
    panels = [weighted, others, from_x, by_x, from_y, by_y]
    own, other, high, low = pl.pallas_call(
        functools.partial(near_kernel, sizes),
        out_shape=[gram] * 2 + [shaped(factor_inverse.shape, bf16)] * 2,
        in_specs=[vmem] * (len(panels) + layers + 1),
        out_specs=[vmem] * 4,
        scratch_shapes=[
            pltpu.VMEM((count, (owners - 1) * depth), bf16),
            pltpu.VMEM(((owners - 1) * depth, panel_width), bf16),
        ],
        compiler_params=params,
        name="near",
    )(*panels, *posts, factor_inverse)

    def far(u, near, kind, pieces):
        return pl.pallas_call(
            functools.partial(far_kernel, sizes, u),
            out_shape=[shaped((count // pieces, panel_width), kind)] * pieces,
            in_specs=[vmem] * 3,
            out_specs=[vmem] * pieces,
            scratch_shapes=[pltpu.VMEM((count, depth), bf16), pltpu.VMEM((depth, panel_width), bf16)],
            compiler_params=params,
            name="far",
        )(near, across_y, across_x)

    others = [shift(piece, 0, 0, 1) for piece in far(1, other, bf16, 2)]
    own = pl.pallas_call(
        own_inverse_kernel,
        out_shape=gram,
        in_specs=[vmem] * 3,
        out_specs=vmem,
        compiler_params=params,
        name="own_inverse",
    )(*far(0, own, f32, 1), high, low)
    out = []
    for i, other in enumerate(others):
        height = other.shape[0]
        out = [
            pl.pallas_call(
                functools.partial(sum_kernel, i * height),
                out_shape=gram,
                in_specs=[vmem] * 4 + [anywhere] * len(out),
                out_specs=anywhere,
                input_output_aliases={4: 0} if out else {},
                scratch_shapes=[pltpu.VMEM((height, panel_width), f32), pltpu.SemaphoreType.DMA((2,))],
                compiler_params=params,
                name="sum",
            )(own, other, high, low, *out)
        ]
    (out,) = out
    return out.reshape(per_owner, slab_width, panel_width)


def solution(mesh):
    in_specs = (
        P(("rows", "cols"), None),
        P(("rows", "cols"), None),
        P(("rows", "cols")),
        P(("rows", "cols"), None),
        P(("rows", "cols"), None),
        P(),
        P(),
    )
    out_specs = P("cols", "rows", None)
    body = local if (mesh.shape["rows"], mesh.shape["cols"]) == (8, 4) else local_general
    return jax.shard_map(body, mesh=mesh, in_specs=in_specs, out_specs=out_specs, check_vma=False)
```

```python
import functools

import jax
import jax.numpy as jnp
from jax import lax
from jax.experimental import pallas as pl
from jax.experimental.pallas import tpu as pltpu
from jax.sharding import PartitionSpec as P

CAP = 2
GATHERED = 1 << 22


def tile_positions(tile_lists, tile_order):
    tile_count = tile_order.shape[0]
    matches = tile_lists[:, :, None] == tile_order[None, None, :]
    return jnp.sum(jnp.where(matches, jnp.arange(tile_count, dtype=jnp.int32), 0), axis=2)


def apply_inverse(tiles, factor_inverse):
    return jnp.einsum("ntp,qp->ntq", tiles, factor_inverse, precision=lax.Precision.HIGHEST)


def slot_codes(tile_lists, tile_masks, tile_order, owner_ids):
    block_count, slot_count = tile_lists.shape
    per_owner = tile_order.shape[0] // lax.axis_size("cols")
    positions = tile_positions(tile_lists, tile_order).reshape(-1)
    active = tile_masks.reshape(-1) == 1
    owner = positions // per_owner
    same = (owner[:, None] == owner[None, :]) & active[None, :]
    earlier = jnp.tril(jnp.ones(same.shape, bool), -1)
    rank = jnp.sum(same & earlier, axis=1)
    code = (
        (owner[None, None, :] == owner_ids[:, None, None])
        & (rank[None, None, :] == jnp.arange(CAP)[None, :, None])
        & active[None, None, :]
    )
    block = jnp.arange(block_count * slot_count) // slot_count
    place = positions % per_owner + per_owner * block
    return code, jnp.sum(jnp.where(code, place + 1, 0), axis=2) - 1


def local_general(jac, panel_jac, weights, tile_lists, tile_masks, tile_order, factor_inverse):
    block_count, slot_count = tile_lists.shape
    block_rows = jac.shape[0] // block_count
    tile_width = jac.shape[1] // slot_count
    slabs, owners = lax.axis_size("rows"), lax.axis_size("cols")
    devices = slabs * owners
    per_owner = tile_order.shape[0] // owners
    slab_width = tile_width // slabs
    bf16 = jnp.bfloat16
    weighted = (weights[:, None] * panel_jac).astype(bf16)
    code, places = slot_codes(tile_lists, tile_masks, tile_order, jnp.arange(owners))
    columns = jac.reshape(block_count, block_rows, slot_count, slabs, slab_width)
    chosen = code.astype(bf16).reshape(owners, CAP, block_count, slot_count)
    pieces = jnp.einsum("cjbk,bmkrt->rcjmt", chosen, columns, preferred_element_type=jnp.float32).astype(bf16)
    pieces = pieces.reshape(devices, -1)
    note = jnp.broadcast_to(places.astype(bf16)[None], (slabs, owners, CAP)).reshape(devices, CAP)
    note = jnp.pad(note, ((0, 0), (0, 128 - CAP)))
    sent = jnp.concatenate([pieces, note], axis=1)
    got = lax.all_to_all(sent, ("rows", "cols"), split_axis=0, concat_axis=0, tiled=True)
    size = pieces.shape[1]
    data = got[:, :size].reshape(devices, CAP, block_rows, slab_width)
    where = got[:, size : size + CAP].astype(jnp.int32)
    hot = (where[:, :, None] == jnp.arange(block_count * per_owner)).astype(bf16)
    hot = hot.reshape(devices, CAP, block_count, per_owner)
    mixed = jnp.einsum("djbn,djmt->dbmnt", hot, data, preferred_element_type=jnp.float32).astype(bf16)
    strips = max(1, devices * weighted.size * 2 // GATHERED)

    def strip_gram(strip):
        panels = lax.all_gather(strip, ("rows", "cols"), axis=0, tiled=True)
        panels = panels.reshape(devices, block_count, block_rows, -1)
        return jnp.einsum("dbmnt,dbmp->ntp", mixed, panels, preferred_element_type=jnp.float32)

    if strips == 1:
        gram = strip_gram(weighted)
    else:
        narrow = weighted.reshape(weighted.shape[0], strips, -1).swapaxes(0, 1)
        gram = jnp.moveaxis(lax.map(strip_gram, narrow), 0, 2)
        gram = gram.reshape(per_owner, slab_width, -1)
    return apply_inverse(gram, factor_inverse)


def shift(value, steps_z, flip_cols, flip_core=0):
    slabs, owners = lax.axis_size("rows"), lax.axis_size("cols")
    pairs = []
    for r in range(slabs):
        to_r = ((r // 2 + steps_z) % (slabs // 2)) * 2 + ((r % 2) ^ flip_core)
        for c in range(owners):
            pairs.append((r * owners + c, to_r * owners + (c ^ flip_cols)))
    return lax.ppermute(value, ("rows", "cols"), pairs)


def pack_kernel(sizes, lists_hbm, masks_hbm, order_hbm, weights_hbm, panel_hbm, jac_hbm, *refs):
    layers, owners, per_owner, block_count, slot_count, block_rows, tile_width = sizes
    weighted_ref, kept_ref, to_x_ref, to_y_ref = refs[:4]
    lists_ref, masks_ref, order_ref, weights_ref, panel_ref, jac_ref, places_ref, turned_ref, sems = refs[4:]
    copies = [
        pltpu.make_async_copy(order_hbm, order_ref, sems.at[0]),
        pltpu.make_async_copy(lists_hbm, lists_ref, sems.at[1]),
        pltpu.make_async_copy(masks_hbm, masks_ref, sems.at[2]),
        pltpu.make_async_copy(weights_hbm, weights_ref, sems.at[3]),
        pltpu.make_async_copy(panel_hbm, panel_ref, sems.at[4]),
        pltpu.make_async_copy(jac_hbm, jac_ref, sems.at[5]),
    ]
    for copy in copies:
        copy.start()
    f32, bf16 = jnp.float32, jnp.bfloat16
    rows, width = panel_ref.shape
    lane_group = CAP * block_rows
    post = layers * lane_group
    slab = tile_width // layers
    part = slab // 2
    me_r, me_c = lax.axis_index("rows"), lax.axis_index("cols")
    me_z, me_core = me_r // 2, lax.rem(me_r, 2)
    for copy in copies:
        copy.wait()

    row_ids = lax.broadcasted_iota(jnp.int32, (rows, rows), 0)
    lane_ids = lax.broadcasted_iota(jnp.int32, (rows, rows), 1)
    column = jnp.sum(jnp.where(row_ids == lane_ids, weights_ref[...], 0.0), axis=1, keepdims=True)
    weighted = (column * panel_ref[...].astype(f32)).astype(bf16)
    weighted_ref[...] = weighted
    to_x_ref[:, :width] = weighted
    to_y_ref[:, :width] = weighted

    for b in range(block_count):
        block = jac_ref[b * block_rows : (b + 1) * block_rows, :].astype(f32)
        start = b * slot_count * tile_width
        turned_ref[start : start + slot_count * tile_width, :] = block.T

    for i in range(order_ref.shape[0]):
        places_ref[order_ref[i]] = i
    slots = []
    for s in range(block_count * slot_count):
        b, k = divmod(s, slot_count)
        place = places_ref[lists_ref[b, k]]
        owner = jnp.int32(0)
        for c in range(1, owners):
            owner += (place >= c * per_owner).astype(jnp.int32)
        slots.append((place - owner * per_owner, jnp.where(masks_ref[b, k] == 1, owner, -1)))

    shape = (16, CAP * block_count * block_rows)
    lane, row = lax.broadcasted_iota(jnp.int32, shape, 1), lax.broadcasted_iota(jnp.int32, shape, 0)
    notes = []
    spots = [(kept_ref, 0), (to_x_ref, width), (to_y_ref, width), (to_y_ref, width + post)]
    for e, (parcel, start) in enumerate(spots):
        wanted = me_c ^ e
        found = jnp.int32(0)
        chosen = [jnp.int32(0)] * CAP
        codes = [jnp.int32(-1)] * CAP
        for s, (place, owner) in enumerate(slots):
            hit = owner == wanted
            for j in range(CAP):
                take = hit & (found == j)
                chosen[j] = jnp.where(take, s, chosen[j])
                codes[j] = jnp.where(take, place, codes[j])
            found += hit.astype(jnp.int32)
        note = jnp.full(shape, -1, jnp.int32)
        for j in range(CAP):
            for b in range(block_count):
                at = (j * block_count + b) * block_rows
                here = (lane >= at) & (lane < at + block_rows)
                code = jnp.where(chosen[j] // slot_count == b, codes[j], -1)
                note = jnp.where(here, code, note)
        notes.append(note)
        for k in range(layers):
            z = lax.rem(me_z + k, layers)
            for u in range(2):
                core = me_core ^ u
                for j in range(CAP):
                    first = pl.multiple_of(chosen[j] * tile_width + z * slab + core * part, part)
                    piece = turned_ref[pl.ds(first, part), :].astype(bf16)
                    to = start + k * lane_group + j * block_rows
                    parcel[u * part : (u + 1) * part, to : to + block_rows] = piece
    kept_ref[:16, post:] = notes[0].astype(f32).astype(bf16)
    to_x_ref[:16, width + post :] = notes[1].astype(f32).astype(bf16)
    to_y_ref[:16, width + 2 * post :] = jnp.where(row == 0, notes[2], notes[3]).astype(f32).astype(bf16)


def row_of(block, i):
    ids = lax.broadcasted_iota(jnp.int32, block.shape, 0)
    return jnp.sum(jnp.where(ids == i, block.astype(jnp.float32), 0.0), axis=0, keepdims=True)


def rows_from(notes):
    ids = lax.broadcasted_iota(jnp.int32, (16, notes[0].shape[1]), 0)
    block = jnp.full(ids.shape, -1.0, jnp.float32)
    for i, note in enumerate(notes):
        block = jnp.where(ids == i, note, block)
    return block.astype(jnp.bfloat16)


def sort_kernel(sizes, kept_ref, from_x_ref, from_y_ref, *refs):
    layers, width, lane_group, wide = sizes
    line, (stacked, *posts) = refs[: layers - 1], refs[layers - 1 :]
    post = layers * lane_group
    rows = kept_ref.shape[0]
    for k, ref in enumerate(line):
        stacked[k * rows : (k + 1) * rows, :] = ref[...]
    spots = [(kept_ref, 0), (from_x_ref, width), (from_y_ref, width), (from_y_ref, width + post)]
    notes = [row_of(ref[:16, ref.shape[1] - wide :], int(e == 3)) for e, (ref, start) in enumerate(spots)]
    block = rows_from(notes)
    for k, out in enumerate(posts):
        for e, (ref, start) in enumerate(spots):
            piece = ref[:, start + k * lane_group : start + (k + 1) * lane_group]
            out[:rows, e * lane_group : (e + 1) * lane_group] = piece
        out[rows:, :wide] = block


def rows_to_y_kernel(from_x_ref, by_x_ref, *refs):
    out_ref = refs[-1]
    rows = from_x_ref.shape[0]
    out_ref[:rows, :] = from_x_ref[:, : out_ref.shape[1]]
    out_ref[rows:, :] = by_x_ref[: out_ref.shape[0] - rows, :]


def rest_to_x_kernel(sizes, by_y_ref, *refs):
    layers, lane_group, wide = sizes
    posts, out_ref = refs[:layers], refs[layers]
    rows = posts[0].shape[0] - 16
    part = rows // 2
    last = out_ref.shape[0] - part - 16
    out_ref[:last, :] = by_y_ref[by_y_ref.shape[0] - last :, :]
    for k, ref in enumerate(posts):
        for u in range(2):
            piece = ref[u * part : (u + 1) * part, 3 * lane_group : 4 * lane_group]
            at = (u * layers + k) * lane_group
            out_ref[last : last + part, at : at + lane_group] = piece
    out_ref[last + part :, :wide] = rows_from([row_of(ref[rows:, :wide], 3) for ref in posts])


def place(out_ref, lanes, per_owner, pieces, notes, sizes):
    block_count, block_rows = sizes
    f32, bf16 = jnp.float32, jnp.bfloat16
    part, rows = pieces[0].shape[0], block_count * block_rows
    columns, codes = [], []
    for j in range(CAP):
        parts = []
        for piece in pieces:
            parts += [piece[:, j * block_rows : (j + 1) * block_rows].astype(f32)] * block_count
        columns.append(jnp.concatenate(parts, axis=1).astype(bf16))
        note = jnp.concatenate([note[:, j * rows : (j + 1) * rows] for note in notes], axis=1)
        codes.append(jnp.broadcast_to(note, columns[j].shape).astype(bf16))
    for n in range(per_owner):
        placed = jnp.zeros(columns[0].shape, bf16)
        for j in range(CAP):
            placed = jnp.where(codes[j] == jnp.asarray(n, bf16), columns[j], placed)
        out_ref[n * part : (n + 1) * part, lanes] = placed


def inverse_rows(rows_ref, factor_ref, high_ref, low_ref):
    f32, bf16 = jnp.float32, jnp.bfloat16
    width = rows_ref.shape[1]
    for start, stop in ((0, width // 2), (width // 2, width)):
        rows = rows_ref[:, :stop]
        total = jnp.dot(rows, factor_ref[0, :stop, start:stop], preferred_element_type=f32)
        total += jnp.dot(rows, factor_ref[1, :stop, start:stop], preferred_element_type=f32)
        high = total.astype(bf16)
        high_ref[:, start:stop] = high
        low_ref[:, start:stop] = (total - high.astype(f32)).astype(bf16)


def near_kernel(sizes, *refs):
    layers, owners, per_owner, block_count, block_rows = sizes
    panels, posts, factor_ref = refs[: 2 * (owners - 1)], refs[2 * (owners - 1) :][:layers], refs[2 * owners - 2 + layers]
    own_ref, other_ref, turned_ref, placed_ref, rows_ref, high_ref, low_ref = refs[2 * owners - 1 + layers :]
    f32, bf16 = jnp.float32, jnp.bfloat16
    turned = factor_ref[...].T
    high = turned.astype(bf16)
    turned_ref[0, :, :] = high
    turned_ref[1, :, :] = (turned - high.astype(f32)).astype(bf16)
    rows = block_count * block_rows
    group, wide = CAP * block_rows, CAP * rows
    part = rows // 2
    width = rows_ref.shape[1]
    at = 0
    for panel in panels:
        rows_ref[at : at + panel.shape[0], :] = panel[:, :width]
        at += panel.shape[0]
    inverse_rows(rows_ref, turned_ref, high_ref, low_ref)
    for u, out_ref in ((1, other_ref), (0, own_ref)):
        for e in range(owners - 1):
            for h in range(layers // 2):
                pair = posts[2 * h : 2 * h + 2]
                pieces = [post[u * part : (u + 1) * part, e * group : (e + 1) * group] for post in pair]
                notes = [row_of(post[rows:, :wide], e) for post in pair]
                start = (e * layers + 2 * h) * rows
                place(placed_ref, slice(start, start + 2 * rows), per_owner, pieces, notes, (block_count, block_rows))
        placed = placed_ref[...]
        total = jnp.dot(placed, high_ref[...], preferred_element_type=f32)
        out_ref[...] = total + jnp.dot(placed, low_ref[...], preferred_element_type=f32)


def far_kernel(sizes, u, near_ref, by_y_ref, by_x_ref, turned_ref, out_ref, placed_ref, rows_ref, high_ref, low_ref):
    layers, owners, per_owner, block_count, block_rows = sizes
    f32 = jnp.float32
    rows = block_count * block_rows
    group, wide = CAP * block_rows, CAP * rows
    part = rows // 2
    first = by_y_ref.shape[0]
    last = rows_ref.shape[0] - first
    rows_ref[:first, :] = by_y_ref[...]
    rows_ref[first:, :] = by_x_ref[:last, :]
    inverse_rows(rows_ref, turned_ref, high_ref, low_ref)
    for h in range(layers // 2):
        pieces, notes = [], []
        for k in (2 * h, 2 * h + 1):
            at = (u * layers + k) * group
            pieces.append(by_x_ref[last : last + part, at : at + group])
            notes.append(row_of(by_x_ref[last + part :, :wide], k))
        start = 2 * h * rows
        place(placed_ref, slice(start, start + 2 * rows), per_owner, pieces, notes, (block_count, block_rows))
    placed = placed_ref[...]
    total = near_ref[...] + jnp.dot(placed, high_ref[...], preferred_element_type=f32)
    total += jnp.dot(placed, low_ref[...], preferred_element_type=f32)
    out_ref[...] = total.astype(out_ref.dtype)


def add_kernel(own_ref, other_ref, out_hbm, sum_ref, sems):
    strips = sems.shape[0]
    height = sum_ref.shape[0] // strips
    copies = []
    for i in range(strips):
        here = pl.ds(i * height, height)
        sum_ref[here, :] = own_ref[here, :] + other_ref[here, :].astype(jnp.float32)
        copies.append(pltpu.make_async_copy(sum_ref.at[here, :], out_hbm.at[here, :], sems.at[i]))
        copies[-1].start()
    for copy in copies:
        copy.wait()


def local(jac, panel_jac, weights, tile_lists, tile_masks, tile_order, factor_inverse):
    block_count, slot_count = tile_lists.shape
    rows, panel_width = panel_jac.shape
    block_rows = rows // block_count
    tile_width = jac.shape[1] // slot_count
    slabs, owners = lax.axis_size("rows"), lax.axis_size("cols")
    layers = slabs // 2
    per_owner = tile_order.shape[0] // owners
    slab_width = tile_width // slabs
    f32, bf16 = jnp.float32, jnp.bfloat16
    vmem, anywhere = pl.BlockSpec(memory_space=pltpu.VMEM), pl.BlockSpec(memory_space=pl.ANY)
    params = pltpu.CompilerParams(vmem_limit_bytes=24 << 20)
    shaped = jax.ShapeDtypeStruct

    def in_hbm(value):
        return pltpu.with_memory_space_constraint(value, pltpu.HBM)

    lane_group = CAP * block_rows
    post = layers * lane_group
    wide = CAP * rows
    sizes = (layers, owners, per_owner, block_count, slot_count, block_rows, tile_width)
    weighted, kept, to_x, to_y = pl.pallas_call(
        functools.partial(pack_kernel, sizes),
        out_shape=[
            shaped((rows, width), bf16)
            for width in (panel_width, post + wide, panel_width + post + wide, panel_width + 2 * post + wide)
        ],
        in_specs=[anywhere] * 6,
        out_specs=[vmem] * 4,
        scratch_shapes=[
            pltpu.SMEM(tile_lists.shape, jnp.int32),
            pltpu.SMEM(tile_masks.shape, jnp.int32),
            pltpu.SMEM(tile_order.shape, jnp.int32),
            pltpu.VMEM((1, rows), f32),
            pltpu.VMEM(panel_jac.shape, bf16),
            pltpu.VMEM(jac.shape, bf16),
            pltpu.SMEM(tile_order.shape, jnp.int32),
            pltpu.VMEM((block_count * slot_count * tile_width, block_rows), f32),
            pltpu.SemaphoreType.DMA((6,)),
        ],
        compiler_params=params,
        name="pack",
    )(*map(in_hbm, (tile_lists, tile_masks, tile_order, weights.reshape(1, rows), panel_jac, jac)))
    line = [shift(weighted, k, 0) for k in range(1, layers)]
    from_x, from_y = shift(to_x, 0, 1), shift(to_y, 0, 2)

    sizes = (layers, panel_width, lane_group, wide)
    others, *posts = pl.pallas_call(
        functools.partial(sort_kernel, sizes),
        out_shape=[shaped(((layers - 1) * rows, panel_width), bf16)]
        + [shaped((rows + 16, owners * lane_group), bf16)] * layers,
        in_specs=[vmem] * (layers + 2),
        out_specs=[vmem] * (layers + 1),
        compiler_params=params,
        name="sort",
    )(kept, from_x, from_y, *line)
    posts = [posts[0]] + [shift(posts[k], k, 0) for k in range(1, layers)]
    by_x, by_y = shift(others, 0, 1), shift(others, 0, 2)

    last = rows // 2
    rows_to_y = pl.pallas_call(
        rows_to_y_kernel,
        out_shape=shaped((rows + others.shape[0] - last, panel_width), bf16),
        in_specs=[vmem] * 2 + [anywhere] * (layers - 1),
        out_specs=vmem,
        compiler_params=params,
        name="rows_to_y",
    )(from_x, by_x, *posts[1:])
    across_y = shift(rows_to_y, 0, 2)
    rest_to_x = pl.pallas_call(
        functools.partial(rest_to_x_kernel, (layers, lane_group, wide)),
        out_shape=shaped((last + rows // 2 + 16, panel_width), bf16),
        in_specs=[vmem] * (layers + 1),
        out_specs=vmem,
        compiler_params=params,
        name="rest_to_x",
    )(by_y, *posts)
    across_x = shift(rest_to_x, 0, 1)

    count = per_owner * slab_width
    depth = layers * rows
    sizes = (layers, owners, per_owner, block_count, block_rows)
    result = shaped((count, panel_width), f32)
    panels = [weighted, others, from_x, by_x, from_y, by_y]
    own, other, turned = pl.pallas_call(
        functools.partial(near_kernel, sizes),
        out_shape=[result] * 2 + [shaped((2, *factor_inverse.shape), bf16)],
        in_specs=[vmem] * (len(panels) + layers + 1),
        out_specs=[vmem] * 3,
        scratch_shapes=[pltpu.VMEM((count, (owners - 1) * depth), bf16)]
        + [pltpu.VMEM(((owners - 1) * depth, panel_width), bf16)] * 3,
        compiler_params=params,
        name="near",
    )(*panels, *posts, factor_inverse)

    def far(u, near, kind):
        return pl.pallas_call(
            functools.partial(far_kernel, sizes, u),
            out_shape=shaped((count, panel_width), kind),
            in_specs=[vmem] * 4,
            out_specs=vmem,
            scratch_shapes=[pltpu.VMEM((count, depth), bf16)] + [pltpu.VMEM((depth, panel_width), bf16)] * 3,
            compiler_params=params,
            name="far",
        )(near, across_y, across_x, turned)

    other = shift(far(1, other, bf16), 0, 0, 1)
    out = pl.pallas_call(
        add_kernel,
        out_shape=result,
        in_specs=[vmem] * 2,
        out_specs=anywhere,
        scratch_shapes=[pltpu.VMEM((count, panel_width), f32), pltpu.SemaphoreType.DMA((6,))],
        compiler_params=params,
        name="add",
    )(far(0, own, f32), other)
    return out.reshape(per_owner, slab_width, panel_width)


def solution(mesh):
    in_specs = (
        P(("rows", "cols"), None),
        P(("rows", "cols"), None),
        P(("rows", "cols")),
        P(("rows", "cols"), None),
        P(("rows", "cols"), None),
        P(),
        P(),
    )
    out_specs = P("cols", "rows", None)
    body = local if (mesh.shape["rows"], mesh.shape["cols"]) == (8, 4) else local_general
    return jax.shard_map(body, mesh=mesh, in_specs=in_specs, out_specs=out_specs, check_vma=False)
```

```python
import functools

import jax
import jax.numpy as jnp
from jax import lax
from jax.experimental import pallas as pl
from jax.experimental.pallas import tpu as pltpu
from jax.sharding import PartitionSpec as P

CAP = 2
GATHERED = 1 << 22


def tile_positions(tile_lists, tile_order):
    tile_count = tile_order.shape[0]
    matches = tile_lists[:, :, None] == tile_order[None, None, :]
    return jnp.sum(jnp.where(matches, jnp.arange(tile_count, dtype=jnp.int32), 0), axis=2)


def apply_inverse(tiles, factor_inverse):
    return jnp.einsum("ntp,qp->ntq", tiles, factor_inverse, precision=lax.Precision.HIGHEST)


def slot_codes(tile_lists, tile_masks, tile_order, owner_ids):
    block_count, slot_count = tile_lists.shape
    per_owner = tile_order.shape[0] // lax.axis_size("cols")
    positions = tile_positions(tile_lists, tile_order).reshape(-1)
    active = tile_masks.reshape(-1) == 1
    owner = positions // per_owner
    same = (owner[:, None] == owner[None, :]) & active[None, :]
    earlier = jnp.tril(jnp.ones(same.shape, bool), -1)
    rank = jnp.sum(same & earlier, axis=1)
    code = (
        (owner[None, None, :] == owner_ids[:, None, None])
        & (rank[None, None, :] == jnp.arange(CAP)[None, :, None])
        & active[None, None, :]
    )
    block = jnp.arange(block_count * slot_count) // slot_count
    place = positions % per_owner + per_owner * block
    return code, jnp.sum(jnp.where(code, place + 1, 0), axis=2) - 1


def local_general(jac, panel_jac, weights, tile_lists, tile_masks, tile_order, factor_inverse):
    block_count, slot_count = tile_lists.shape
    block_rows = jac.shape[0] // block_count
    tile_width = jac.shape[1] // slot_count
    slabs, owners = lax.axis_size("rows"), lax.axis_size("cols")
    devices = slabs * owners
    per_owner = tile_order.shape[0] // owners
    slab_width = tile_width // slabs
    bf16 = jnp.bfloat16
    weighted = (weights[:, None] * panel_jac).astype(bf16)
    code, places = slot_codes(tile_lists, tile_masks, tile_order, jnp.arange(owners))
    columns = jac.reshape(block_count, block_rows, slot_count, slabs, slab_width)
    chosen = code.astype(bf16).reshape(owners, CAP, block_count, slot_count)
    pieces = jnp.einsum("cjbk,bmkrt->rcjmt", chosen, columns, preferred_element_type=jnp.float32).astype(bf16)
    pieces = pieces.reshape(devices, -1)
    note = jnp.broadcast_to(places.astype(bf16)[None], (slabs, owners, CAP)).reshape(devices, CAP)
    note = jnp.pad(note, ((0, 0), (0, 128 - CAP)))
    sent = jnp.concatenate([pieces, note], axis=1)
    got = lax.all_to_all(sent, ("rows", "cols"), split_axis=0, concat_axis=0, tiled=True)
    size = pieces.shape[1]
    data = got[:, :size].reshape(devices, CAP, block_rows, slab_width)
    where = got[:, size : size + CAP].astype(jnp.int32)
    hot = (where[:, :, None] == jnp.arange(block_count * per_owner)).astype(bf16)
    hot = hot.reshape(devices, CAP, block_count, per_owner)
    mixed = jnp.einsum("djbn,djmt->dbmnt", hot, data, preferred_element_type=jnp.float32).astype(bf16)
    strips = max(1, devices * weighted.size * 2 // GATHERED)

    def strip_gram(strip):
        panels = lax.all_gather(strip, ("rows", "cols"), axis=0, tiled=True)
        panels = panels.reshape(devices, block_count, block_rows, -1)
        return jnp.einsum("dbmnt,dbmp->ntp", mixed, panels, preferred_element_type=jnp.float32)

    if strips == 1:
        gram = strip_gram(weighted)
    else:
        narrow = weighted.reshape(weighted.shape[0], strips, -1).swapaxes(0, 1)
        gram = jnp.moveaxis(lax.map(strip_gram, narrow), 0, 2)
        gram = gram.reshape(per_owner, slab_width, -1)
    return apply_inverse(gram, factor_inverse)


def shift(value, steps_z, flip_cols, flip_core=0):
    slabs, owners = lax.axis_size("rows"), lax.axis_size("cols")
    pairs = []
    for r in range(slabs):
        to_r = ((r // 2 + steps_z) % (slabs // 2)) * 2 + ((r % 2) ^ flip_core)
        for c in range(owners):
            pairs.append((r * owners + c, to_r * owners + (c ^ flip_cols)))
    return lax.ppermute(value, ("rows", "cols"), pairs)


def pack_kernel(sizes, lists_hbm, masks_hbm, order_hbm, weights_hbm, panel_hbm, jac_hbm, *refs):
    layers, owners, per_owner, block_count, slot_count, block_rows, tile_width = sizes
    weighted_ref, kept_ref, to_x_ref, to_y_ref = refs[:4]
    lists_ref, masks_ref, order_ref, weights_ref, panel_ref, jac_ref, places_ref, turned_ref, sems = refs[4:]
    copies = [
        pltpu.make_async_copy(order_hbm, order_ref, sems.at[0]),
        pltpu.make_async_copy(lists_hbm, lists_ref, sems.at[1]),
        pltpu.make_async_copy(masks_hbm, masks_ref, sems.at[2]),
        pltpu.make_async_copy(weights_hbm, weights_ref, sems.at[3]),
        pltpu.make_async_copy(panel_hbm, panel_ref, sems.at[4]),
        pltpu.make_async_copy(jac_hbm, jac_ref, sems.at[5]),
    ]
    for copy in copies:
        copy.start()
    f32, bf16 = jnp.float32, jnp.bfloat16
    rows, width = panel_ref.shape
    lane_group = CAP * block_rows
    post = layers * lane_group
    slab = tile_width // layers
    part = slab // 2
    me_r, me_c = lax.axis_index("rows"), lax.axis_index("cols")
    me_z, me_core = me_r // 2, lax.rem(me_r, 2)
    for copy in copies:
        copy.wait()

    row_ids = lax.broadcasted_iota(jnp.int32, (rows, rows), 0)
    lane_ids = lax.broadcasted_iota(jnp.int32, (rows, rows), 1)
    column = jnp.sum(jnp.where(row_ids == lane_ids, weights_ref[...], 0.0), axis=1, keepdims=True)
    weighted = (column * panel_ref[...].astype(f32)).astype(bf16)
    weighted_ref[...] = weighted
    to_x_ref[:, :width] = weighted
    to_y_ref[:, :width] = weighted

    for b in range(block_count):
        block = jac_ref[b * block_rows : (b + 1) * block_rows, :].astype(f32)
        start = b * slot_count * tile_width
        turned_ref[start : start + slot_count * tile_width, :] = block.T

    for i in range(order_ref.shape[0]):
        places_ref[order_ref[i]] = i
    slots = []
    for s in range(block_count * slot_count):
        b, k = divmod(s, slot_count)
        place = places_ref[lists_ref[b, k]]
        owner = jnp.int32(0)
        for c in range(1, owners):
            owner += (place >= c * per_owner).astype(jnp.int32)
        slots.append((place - owner * per_owner, jnp.where(masks_ref[b, k] == 1, owner, -1)))

    shape = (16, CAP * block_count * block_rows)
    lane, row = lax.broadcasted_iota(jnp.int32, shape, 1), lax.broadcasted_iota(jnp.int32, shape, 0)
    notes = []
    spots = [(kept_ref, 0), (to_x_ref, width), (to_y_ref, width), (to_y_ref, width + post)]
    for e, (parcel, start) in enumerate(spots):
        wanted = me_c ^ e
        found = jnp.int32(0)
        chosen = [jnp.int32(0)] * CAP
        codes = [jnp.int32(-1)] * CAP
        for s, (place, owner) in enumerate(slots):
            hit = owner == wanted
            for j in range(CAP):
                take = hit & (found == j)
                chosen[j] = jnp.where(take, s, chosen[j])
                codes[j] = jnp.where(take, place, codes[j])
            found += hit.astype(jnp.int32)
        note = jnp.full(shape, -1, jnp.int32)
        for j in range(CAP):
            for b in range(block_count):
                at = (j * block_count + b) * block_rows
                here = (lane >= at) & (lane < at + block_rows)
                code = jnp.where(chosen[j] // slot_count == b, codes[j], -1)
                note = jnp.where(here, code, note)
        notes.append(note)
        for k in range(layers):
            z = lax.rem(me_z + k, layers)
            for u in range(2):
                core = me_core ^ u
                for j in range(CAP):
                    first = pl.multiple_of(chosen[j] * tile_width + z * slab + core * part, part)
                    piece = turned_ref[pl.ds(first, part), :].astype(bf16)
                    to = start + k * lane_group + j * block_rows
                    parcel[u * part : (u + 1) * part, to : to + block_rows] = piece
    kept_ref[:16, post:] = notes[0].astype(f32).astype(bf16)
    to_x_ref[:16, width + post :] = notes[1].astype(f32).astype(bf16)
    to_y_ref[:16, width + 2 * post :] = jnp.where(row == 0, notes[2], notes[3]).astype(f32).astype(bf16)


def row_of(block, i):
    ids = lax.broadcasted_iota(jnp.int32, block.shape, 0)
    return jnp.sum(jnp.where(ids == i, block.astype(jnp.float32), 0.0), axis=0, keepdims=True)


def rows_from(notes):
    ids = lax.broadcasted_iota(jnp.int32, (16, notes[0].shape[1]), 0)
    block = jnp.full(ids.shape, -1.0, jnp.float32)
    for i, note in enumerate(notes):
        block = jnp.where(ids == i, note, block)
    return block.astype(jnp.bfloat16)


def sort_kernel(sizes, kept_ref, from_x_ref, from_y_ref, *refs):
    layers, width, lane_group, wide = sizes
    line, (stacked, *posts) = refs[: layers - 1], refs[layers - 1 :]
    post = layers * lane_group
    rows = kept_ref.shape[0]
    for k, ref in enumerate(line):
        stacked[k * rows : (k + 1) * rows, :] = ref[...]
    spots = [(kept_ref, 0), (from_x_ref, width), (from_y_ref, width), (from_y_ref, width + post)]
    notes = [row_of(ref[:16, ref.shape[1] - wide :], int(e == 3)) for e, (ref, start) in enumerate(spots)]
    block = rows_from(notes)
    for k, out in enumerate(posts):
        for e, (ref, start) in enumerate(spots):
            piece = ref[:, start + k * lane_group : start + (k + 1) * lane_group]
            out[:rows, e * lane_group : (e + 1) * lane_group] = piece
        out[rows:, :wide] = block


def rows_to_y_kernel(from_x_ref, by_x_ref, *refs):
    out_ref = refs[-1]
    rows = from_x_ref.shape[0]
    out_ref[:rows, :] = from_x_ref[:, : out_ref.shape[1]]
    out_ref[rows:, :] = by_x_ref[: out_ref.shape[0] - rows, :]


def rest_to_x_kernel(sizes, by_y_ref, *refs):
    layers, lane_group, wide = sizes
    posts, out_ref = refs[:layers], refs[layers]
    rows = posts[0].shape[0] - 16
    part = rows // 2
    last = out_ref.shape[0] - part - 16
    out_ref[:last, :] = by_y_ref[by_y_ref.shape[0] - last :, :]
    for k, ref in enumerate(posts):
        for u in range(2):
            piece = ref[u * part : (u + 1) * part, 3 * lane_group : 4 * lane_group]
            at = (u * layers + k) * lane_group
            out_ref[last : last + part, at : at + lane_group] = piece
    out_ref[last + part :, :wide] = rows_from([row_of(ref[rows:, :wide], 3) for ref in posts])


def place(out_ref, lanes, per_owner, pieces, notes, sizes):
    block_count, block_rows = sizes
    f32, bf16 = jnp.float32, jnp.bfloat16
    part, rows = pieces[0].shape[0], block_count * block_rows
    columns, codes = [], []
    for j in range(CAP):
        parts = []
        for piece in pieces:
            parts += [piece[:, j * block_rows : (j + 1) * block_rows].astype(f32)] * block_count
        columns.append(jnp.concatenate(parts, axis=1).astype(bf16))
        note = jnp.concatenate([note[:, j * rows : (j + 1) * rows] for note in notes], axis=1)
        codes.append(jnp.broadcast_to(note, columns[j].shape).astype(bf16))
    for n in range(per_owner):
        placed = jnp.zeros(columns[0].shape, bf16)
        for j in range(CAP):
            placed = jnp.where(codes[j] == jnp.asarray(n, bf16), columns[j], placed)
        out_ref[n * part : (n + 1) * part, lanes] = placed


def inverse_rows(rows_ref, factor_ref, high_ref, low_ref):
    f32, bf16 = jnp.float32, jnp.bfloat16
    width = rows_ref.shape[1]
    for start, stop in ((0, width // 2), (width // 2, width)):
        rows = rows_ref[:, :stop]
        total = jnp.dot(rows, factor_ref[0, :stop, start:stop], preferred_element_type=f32)
        total += jnp.dot(rows, factor_ref[1, :stop, start:stop], preferred_element_type=f32)
        high = total.astype(bf16)
        high_ref[:, start:stop] = high
        low_ref[:, start:stop] = (total - high.astype(f32)).astype(bf16)


def near_kernel(sizes, u, earlier, *refs):
    layers, owners, per_owner, block_count, block_rows = sizes
    refs = refs[earlier:]
    inputs = 2 * (owners - 1) + layers
    panels, posts = refs[: 2 * (owners - 1)], refs[2 * (owners - 1) : inputs]
    factors, (placed_ref, rows_ref) = refs[inputs:-2], refs[-2:]
    f32, bf16 = jnp.float32, jnp.bfloat16
    if u == 0:
        factor_ref, out_ref, turned_ref = factors
        turned = factor_ref[...].T
        high = turned.astype(bf16)
        turned_ref[0, :, :] = high
        turned_ref[1, :, :] = (turned - high.astype(f32)).astype(bf16)
    else:
        (out_ref,) = factors
    rows = block_count * block_rows
    group, wide = CAP * block_rows, CAP * rows
    part = rows // 2
    width = rows_ref.shape[1]
    at = 0
    for panel in panels:
        rows_ref[at : at + panel.shape[0], :] = panel[:, :width]
        at += panel.shape[0]
    for e in range(owners - 1):
        for h in range(layers // 2):
            pair = posts[2 * h : 2 * h + 2]
            pieces = [post[u * part : (u + 1) * part, e * group : (e + 1) * group] for post in pair]
            notes = [row_of(post[rows:, :wide], e) for post in pair]
            start = (e * layers + 2 * h) * rows
            place(placed_ref, slice(start, start + 2 * rows), per_owner, pieces, notes, (block_count, block_rows))
    gram = jnp.dot(placed_ref[...], rows_ref[...], preferred_element_type=f32)
    out_ref[...] = gram.astype(out_ref.dtype)


def join_kernel(above_ref, below_ref, earlier_ref, out_ref):
    rows = above_ref.shape[0]
    out_ref[:rows, :] = above_ref[...]
    out_ref[rows:, :] = below_ref[...]


def middle_kernel(own_ref, other_ref, turned_ref, out_ref):
    f32, bf16 = jnp.float32, jnp.bfloat16
    width = own_ref.shape[1]
    gram = own_ref[...] + other_ref[...].astype(f32)
    high = gram.astype(bf16)
    low = (gram - high.astype(f32)).astype(bf16)
    for start, stop in ((0, width // 2), (width // 2, width)):
        a, b = turned_ref[0, :stop, start:stop], turned_ref[1, :stop, start:stop]
        total = jnp.dot(high[:, :stop], a, preferred_element_type=f32)
        total += jnp.dot(high[:, :stop], b, preferred_element_type=f32)
        out_ref[:, start:stop] = total + jnp.dot(low[:, :stop], a, preferred_element_type=f32)


def final_kernel(sizes, near_ref, own_ref, other_ref, turned_ref, out_hbm, *refs):
    layers, owners, per_owner, block_count, block_rows = sizes
    sum_ref, placed_ref, rows_ref, high_ref, low_ref, sems = refs
    f32 = jnp.float32
    rows = block_count * block_rows
    group, wide = CAP * block_rows, CAP * rows
    part, depth = rows // 2, layers * rows
    for u, ref in enumerate((own_ref, other_ref)):
        rows_ref[u * depth : (u + 1) * depth, :] = ref[:depth, :]
        for h in range(layers // 2):
            pieces, notes = [], []
            for k in (2 * h, 2 * h + 1):
                at = (u * layers + k) * group
                pieces.append(ref[depth : depth + part, at : at + group])
                notes.append(row_of(ref[depth + part :, :wide], k))
            start = u * depth + 2 * h * rows
            place(placed_ref, slice(start, start + 2 * rows), per_owner, pieces, notes, (block_count, block_rows))
    inverse_rows(rows_ref, turned_ref, high_ref, low_ref)
    strips = sems.shape[0]
    height = sum_ref.shape[0] // strips
    copies = []
    for i in range(strips):
        here = pl.ds(i * height, height)
        placed = placed_ref[here, :]
        total = near_ref[here, :] + jnp.dot(placed, high_ref[...], preferred_element_type=f32)
        sum_ref[here, :] = total + jnp.dot(placed, low_ref[...], preferred_element_type=f32)
        copies.append(pltpu.make_async_copy(sum_ref.at[here, :], out_hbm.at[here, :], sems.at[i]))
        copies[-1].start()
    for copy in copies:
        copy.wait()


def local(jac, panel_jac, weights, tile_lists, tile_masks, tile_order, factor_inverse):
    block_count, slot_count = tile_lists.shape
    rows, panel_width = panel_jac.shape
    block_rows = rows // block_count
    tile_width = jac.shape[1] // slot_count
    slabs, owners = lax.axis_size("rows"), lax.axis_size("cols")
    layers = slabs // 2
    per_owner = tile_order.shape[0] // owners
    slab_width = tile_width // slabs
    f32, bf16 = jnp.float32, jnp.bfloat16
    vmem, anywhere = pl.BlockSpec(memory_space=pltpu.VMEM), pl.BlockSpec(memory_space=pl.ANY)
    params = pltpu.CompilerParams(vmem_limit_bytes=24 << 20)
    shaped = jax.ShapeDtypeStruct

    def in_hbm(value):
        return pltpu.with_memory_space_constraint(value, pltpu.HBM)

    lane_group = CAP * block_rows
    post = layers * lane_group
    wide = CAP * rows
    sizes = (layers, owners, per_owner, block_count, slot_count, block_rows, tile_width)
    weighted, kept, to_x, to_y = pl.pallas_call(
        functools.partial(pack_kernel, sizes),
        out_shape=[
            shaped((rows, width), bf16)
            for width in (panel_width, post + wide, panel_width + post + wide, panel_width + 2 * post + wide)
        ],
        in_specs=[anywhere] * 6,
        out_specs=[vmem] * 4,
        scratch_shapes=[
            pltpu.SMEM(tile_lists.shape, jnp.int32),
            pltpu.SMEM(tile_masks.shape, jnp.int32),
            pltpu.SMEM(tile_order.shape, jnp.int32),
            pltpu.VMEM((1, rows), f32),
            pltpu.VMEM(panel_jac.shape, bf16),
            pltpu.VMEM(jac.shape, bf16),
            pltpu.SMEM(tile_order.shape, jnp.int32),
            pltpu.VMEM((block_count * slot_count * tile_width, block_rows), f32),
            pltpu.SemaphoreType.DMA((6,)),
        ],
        compiler_params=params,
        name="pack",
    )(*map(in_hbm, (tile_lists, tile_masks, tile_order, weights.reshape(1, rows), panel_jac, jac)))
    line = [shift(weighted, k, 0) for k in range(1, layers)]
    from_x, from_y = shift(to_x, 0, 1), shift(to_y, 0, 2)

    sizes = (layers, panel_width, lane_group, wide)
    others, *posts = pl.pallas_call(
        functools.partial(sort_kernel, sizes),
        out_shape=[shaped(((layers - 1) * rows, panel_width), bf16)]
        + [shaped((rows + 16, owners * lane_group), bf16)] * layers,
        in_specs=[vmem] * (layers + 2),
        out_specs=[vmem] * (layers + 1),
        compiler_params=params,
        name="sort",
    )(kept, from_x, from_y, *line)
    posts = [posts[0]] + [shift(posts[k], k, 0) for k in range(1, layers)]
    by_x, by_y = shift(others, 0, 1), shift(others, 0, 2)

    last = rows // 2
    rows_to_y = pl.pallas_call(
        rows_to_y_kernel,
        out_shape=shaped((rows + others.shape[0] - last, panel_width), bf16),
        in_specs=[vmem] * 2 + [anywhere] * (layers - 1),
        out_specs=vmem,
        compiler_params=params,
        name="rows_to_y",
    )(from_x, by_x, *posts[1:])
    across_y = shift(rows_to_y, 0, 2)
    rest_to_x = pl.pallas_call(
        functools.partial(rest_to_x_kernel, (layers, lane_group, wide)),
        out_shape=shaped((last + rows // 2 + 16, panel_width), bf16),
        in_specs=[vmem] * (layers + 1),
        out_specs=vmem,
        compiler_params=params,
        name="rest_to_x",
    )(by_y, *posts)
    across_x = shift(rest_to_x, 0, 1)

    count = per_owner * slab_width
    depth = layers * rows
    sizes = (layers, owners, per_owner, block_count, block_rows)
    result = shaped((count, panel_width), f32)
    panels = [weighted, others, from_x, by_x, from_y, by_y]
    def near(u, out_shape, earlier, *factors):
        return pl.pallas_call(
            functools.partial(near_kernel, sizes, u, len(earlier)),
            out_shape=out_shape,
            in_specs=[anywhere] * len(earlier) + [vmem] * (len(panels) + layers + len(factors)),
            out_specs=[vmem] * len(out_shape),
            scratch_shapes=[
                pltpu.VMEM((count, (owners - 1) * depth), bf16),
                pltpu.VMEM(((owners - 1) * depth, panel_width), bf16),
            ],
            compiler_params=params,
            name="near",
        )(*earlier, *panels, *posts, *factors)

    other = shift(*near(1, [shaped((count, panel_width), bf16)], [rows_to_y, rest_to_x]), 0, 0, 1)
    own, turned = near(0, [result, shaped((2, *factor_inverse.shape), bf16)], [], factor_inverse)
    joined = pl.pallas_call(
        join_kernel,
        out_shape=shaped((across_y.shape[0] + across_x.shape[0], panel_width), bf16),
        in_specs=[vmem] * 2 + [anywhere],
        out_specs=vmem,
        compiler_params=params,
        name="join",
    )(across_y, across_x, own)
    other_joined = shift(joined, 0, 0, 1)
    middle = pl.pallas_call(
        middle_kernel,
        out_shape=result,
        in_specs=[vmem] * 3,
        out_specs=vmem,
        compiler_params=params,
        name="middle",
    )(own, other, turned)
    out = pl.pallas_call(
        functools.partial(final_kernel, sizes),
        out_shape=result,
        in_specs=[vmem] * 4,
        out_specs=anywhere,
        scratch_shapes=[pltpu.VMEM((count, panel_width), f32), pltpu.VMEM((count, 2 * depth), bf16)]
        + [pltpu.VMEM((2 * depth, panel_width), bf16)] * 3
        + [pltpu.SemaphoreType.DMA((4,))],
        compiler_params=params,
        name="final",
    )(middle, joined, other_joined, turned)
    return out.reshape(per_owner, slab_width, panel_width)


def solution(mesh):
    in_specs = (
        P(("rows", "cols"), None),
        P(("rows", "cols"), None),
        P(("rows", "cols")),
        P(("rows", "cols"), None),
        P(("rows", "cols"), None),
        P(),
        P(),
    )
    out_specs = P("cols", "rows", None)
    body = local if (mesh.shape["rows"], mesh.shape["cols"]) == (8, 4) else local_general
    return jax.shard_map(body, mesh=mesh, in_specs=in_specs, out_specs=out_specs, check_vma=False)
```

```python
import functools

import jax
import jax.numpy as jnp
from jax import lax
from jax.experimental import pallas as pl
from jax.experimental.pallas import tpu as pltpu
from jax.sharding import PartitionSpec as P

CAP = 2
GATHERED = 1 << 22


def tile_positions(tile_lists, tile_order):
    tile_count = tile_order.shape[0]
    matches = tile_lists[:, :, None] == tile_order[None, None, :]
    return jnp.sum(jnp.where(matches, jnp.arange(tile_count, dtype=jnp.int32), 0), axis=2)


def apply_inverse(tiles, factor_inverse):
    return jnp.einsum("ntp,qp->ntq", tiles, factor_inverse, precision=lax.Precision.HIGHEST)


def slot_codes(tile_lists, tile_masks, tile_order, owner_ids):
    block_count, slot_count = tile_lists.shape
    per_owner = tile_order.shape[0] // lax.axis_size("cols")
    positions = tile_positions(tile_lists, tile_order).reshape(-1)
    active = tile_masks.reshape(-1) == 1
    owner = positions // per_owner
    same = (owner[:, None] == owner[None, :]) & active[None, :]
    earlier = jnp.tril(jnp.ones(same.shape, bool), -1)
    rank = jnp.sum(same & earlier, axis=1)
    code = (
        (owner[None, None, :] == owner_ids[:, None, None])
        & (rank[None, None, :] == jnp.arange(CAP)[None, :, None])
        & active[None, None, :]
    )
    block = jnp.arange(block_count * slot_count) // slot_count
    place = positions % per_owner + per_owner * block
    return code, jnp.sum(jnp.where(code, place + 1, 0), axis=2) - 1


def local_general(jac, panel_jac, weights, tile_lists, tile_masks, tile_order, factor_inverse):
    block_count, slot_count = tile_lists.shape
    block_rows = jac.shape[0] // block_count
    tile_width = jac.shape[1] // slot_count
    slabs, owners = lax.axis_size("rows"), lax.axis_size("cols")
    devices = slabs * owners
    per_owner = tile_order.shape[0] // owners
    slab_width = tile_width // slabs
    bf16 = jnp.bfloat16
    weighted = (weights[:, None] * panel_jac).astype(bf16)
    code, places = slot_codes(tile_lists, tile_masks, tile_order, jnp.arange(owners))
    columns = jac.reshape(block_count, block_rows, slot_count, slabs, slab_width)
    chosen = code.astype(bf16).reshape(owners, CAP, block_count, slot_count)
    pieces = jnp.einsum("cjbk,bmkrt->rcjmt", chosen, columns, preferred_element_type=jnp.float32).astype(bf16)
    pieces = pieces.reshape(devices, -1)
    note = jnp.broadcast_to(places.astype(bf16)[None], (slabs, owners, CAP)).reshape(devices, CAP)
    note = jnp.pad(note, ((0, 0), (0, 128 - CAP)))
    sent = jnp.concatenate([pieces, note], axis=1)
    got = lax.all_to_all(sent, ("rows", "cols"), split_axis=0, concat_axis=0, tiled=True)
    size = pieces.shape[1]
    data = got[:, :size].reshape(devices, CAP, block_rows, slab_width)
    where = got[:, size : size + CAP].astype(jnp.int32)
    hot = (where[:, :, None] == jnp.arange(block_count * per_owner)).astype(bf16)
    hot = hot.reshape(devices, CAP, block_count, per_owner)
    mixed = jnp.einsum("djbn,djmt->dbmnt", hot, data, preferred_element_type=jnp.float32).astype(bf16)
    strips = max(1, devices * weighted.size * 2 // GATHERED)

    def strip_gram(strip):
        panels = lax.all_gather(strip, ("rows", "cols"), axis=0, tiled=True)
        panels = panels.reshape(devices, block_count, block_rows, -1)
        return jnp.einsum("dbmnt,dbmp->ntp", mixed, panels, preferred_element_type=jnp.float32)

    if strips == 1:
        gram = strip_gram(weighted)
    else:
        narrow = weighted.reshape(weighted.shape[0], strips, -1).swapaxes(0, 1)
        gram = jnp.moveaxis(lax.map(strip_gram, narrow), 0, 2)
        gram = gram.reshape(per_owner, slab_width, -1)
    return apply_inverse(gram, factor_inverse)


def shift(value, steps_z, flip_cols, flip_core=0):
    slabs, owners = lax.axis_size("rows"), lax.axis_size("cols")
    pairs = []
    for r in range(slabs):
        to_r = ((r // 2 + steps_z) % (slabs // 2)) * 2 + ((r % 2) ^ flip_core)
        for c in range(owners):
            pairs.append((r * owners + c, to_r * owners + (c ^ flip_cols)))
    return lax.ppermute(value, ("rows", "cols"), pairs)


def lasting(flops):
    return pl.CostEstimate(flops=flops, bytes_accessed=0, transcendentals=0)


def pack_kernel(sizes, lists_hbm, masks_hbm, order_hbm, weights_hbm, panel_hbm, jac_hbm, *refs):
    layers, owners, per_owner, block_count, slot_count, block_rows, tile_width = sizes
    weighted_ref, kept_ref, to_x_ref, to_y_ref = refs[:4]
    lists_ref, masks_ref, order_ref, weights_ref, panel_ref, jac_ref, places_ref, turned_ref, sems = refs[4:]
    copies = [
        pltpu.make_async_copy(order_hbm, order_ref, sems.at[0]),
        pltpu.make_async_copy(lists_hbm, lists_ref, sems.at[1]),
        pltpu.make_async_copy(masks_hbm, masks_ref, sems.at[2]),
        pltpu.make_async_copy(weights_hbm, weights_ref, sems.at[3]),
        pltpu.make_async_copy(panel_hbm, panel_ref, sems.at[4]),
        pltpu.make_async_copy(jac_hbm, jac_ref, sems.at[5]),
    ]
    for copy in copies:
        copy.start()
    f32, bf16 = jnp.float32, jnp.bfloat16
    rows, width = panel_ref.shape
    lane_group = CAP * block_rows
    post = layers * lane_group
    slab = tile_width // layers
    part = slab // 2
    me_r, me_c = lax.axis_index("rows"), lax.axis_index("cols")
    me_z, me_core = me_r // 2, lax.rem(me_r, 2)
    for copy in copies:
        copy.wait()

    row_ids = lax.broadcasted_iota(jnp.int32, (rows, rows), 0)
    lane_ids = lax.broadcasted_iota(jnp.int32, (rows, rows), 1)
    column = jnp.sum(jnp.where(row_ids == lane_ids, weights_ref[...], 0.0), axis=1, keepdims=True)
    weighted = (column * panel_ref[...].astype(f32)).astype(bf16)
    weighted_ref[...] = weighted
    to_x_ref[:, :width] = weighted
    to_y_ref[:, :width] = weighted

    for b in range(block_count):
        block = jac_ref[b * block_rows : (b + 1) * block_rows, :].astype(f32)
        start = b * slot_count * tile_width
        turned_ref[start : start + slot_count * tile_width, :] = block.T

    for i in range(order_ref.shape[0]):
        places_ref[order_ref[i]] = i
    slots = []
    for s in range(block_count * slot_count):
        b, k = divmod(s, slot_count)
        place = places_ref[lists_ref[b, k]]
        owner = jnp.int32(0)
        for c in range(1, owners):
            owner += (place >= c * per_owner).astype(jnp.int32)
        slots.append((place - owner * per_owner, jnp.where(masks_ref[b, k] == 1, owner, -1)))

    shape = (16, CAP * block_count * block_rows)
    lane, row = lax.broadcasted_iota(jnp.int32, shape, 1), lax.broadcasted_iota(jnp.int32, shape, 0)
    notes = []
    spots = [(kept_ref, 0), (to_x_ref, width), (to_y_ref, width), (to_y_ref, width + post)]
    for e, (parcel, start) in enumerate(spots):
        wanted = me_c ^ e
        found = jnp.int32(0)
        chosen = [jnp.int32(0)] * CAP
        codes = [jnp.int32(-1)] * CAP
        for s, (place, owner) in enumerate(slots):
            hit = owner == wanted
            for j in range(CAP):
                take = hit & (found == j)
                chosen[j] = jnp.where(take, s, chosen[j])
                codes[j] = jnp.where(take, place, codes[j])
            found += hit.astype(jnp.int32)
        note = jnp.full(shape, -1, jnp.int32)
        for j in range(CAP):
            for b in range(block_count):
                at = (j * block_count + b) * block_rows
                here = (lane >= at) & (lane < at + block_rows)
                code = jnp.where(chosen[j] // slot_count == b, codes[j], -1)
                note = jnp.where(here, code, note)
        notes.append(note)
        for k in range(layers):
            z = lax.rem(me_z + k, layers)
            for u in range(2):
                core = me_core ^ u
                for j in range(CAP):
                    first = pl.multiple_of(chosen[j] * tile_width + z * slab + core * part, part)
                    piece = turned_ref[pl.ds(first, part), :].astype(bf16)
                    to = start + k * lane_group + j * block_rows
                    parcel[u * part : (u + 1) * part, to : to + block_rows] = piece
    kept_ref[:16, post:] = notes[0].astype(f32).astype(bf16)
    to_x_ref[:16, width + post :] = notes[1].astype(f32).astype(bf16)
    to_y_ref[:16, width + 2 * post :] = jnp.where(row == 0, notes[2], notes[3]).astype(f32).astype(bf16)


def row_of(block, i):
    ids = lax.broadcasted_iota(jnp.int32, block.shape, 0)
    return jnp.sum(jnp.where(ids == i, block.astype(jnp.float32), 0.0), axis=0, keepdims=True)


def rows_from(notes):
    ids = lax.broadcasted_iota(jnp.int32, (16, notes[0].shape[1]), 0)
    block = jnp.full(ids.shape, -1.0, jnp.float32)
    for i, note in enumerate(notes):
        block = jnp.where(ids == i, note, block)
    return block.astype(jnp.bfloat16)


def stack_kernel(*refs):
    at = 0
    for ref in refs[:-1]:
        refs[-1][at : at + ref.shape[0], :] = ref[...]
        at += ref.shape[0]


def sort_kernel(sizes, kept_ref, from_x_ref, from_y_ref, *posts):
    layers, width, lane_group, wide = sizes
    post = layers * lane_group
    rows = kept_ref.shape[0]
    spots = [(kept_ref, 0), (from_x_ref, width), (from_y_ref, width), (from_y_ref, width + post)]
    notes = [row_of(ref[:16, ref.shape[1] - wide :], int(e == 3)) for e, (ref, start) in enumerate(spots)]
    block = rows_from(notes)
    for k, out in enumerate(posts):
        for e, (ref, start) in enumerate(spots):
            piece = ref[:, start + k * lane_group : start + (k + 1) * lane_group]
            out[:rows, e * lane_group : (e + 1) * lane_group] = piece
        out[rows:, :wide] = block


def rows_to_y_kernel(from_x_ref, by_x_ref, *refs):
    out_ref = refs[-1]
    rows = from_x_ref.shape[0]
    out_ref[:rows, :] = from_x_ref[:, : out_ref.shape[1]]
    out_ref[rows:, :] = by_x_ref[: out_ref.shape[0] - rows, :]


def rest_to_x_kernel(sizes, by_y_ref, *refs):
    layers, lane_group, wide = sizes
    posts, out_ref = refs[:layers], refs[layers]
    rows = posts[0].shape[0] - 16
    part = rows // 2
    last = out_ref.shape[0] - part - 16
    out_ref[:last, :] = by_y_ref[by_y_ref.shape[0] - last :, :]
    for k, ref in enumerate(posts):
        for u in range(2):
            piece = ref[u * part : (u + 1) * part, 3 * lane_group : 4 * lane_group]
            at = (u * layers + k) * lane_group
            out_ref[last : last + part, at : at + lane_group] = piece
    out_ref[last + part :, :wide] = rows_from([row_of(ref[rows:, :wide], 3) for ref in posts])


def place(out_ref, lanes, per_owner, pieces, notes, sizes):
    block_count, block_rows = sizes
    f32, bf16 = jnp.float32, jnp.bfloat16
    part, rows = pieces[0].shape[0], block_count * block_rows
    columns, codes = [], []
    for j in range(CAP):
        parts = []
        for piece in pieces:
            parts += [piece[:, j * block_rows : (j + 1) * block_rows].astype(f32)] * block_count
        columns.append(jnp.concatenate(parts, axis=1).astype(bf16))
        note = jnp.concatenate([note[:, j * rows : (j + 1) * rows] for note in notes], axis=1)
        codes.append(jnp.broadcast_to(note, columns[j].shape).astype(bf16))
    for n in range(per_owner):
        placed = jnp.zeros(columns[0].shape, bf16)
        for j in range(CAP):
            placed = jnp.where(codes[j] == jnp.asarray(n, bf16), columns[j], placed)
        out_ref[n * part : (n + 1) * part, lanes] = placed


def inverse_rows(rows_ref, factor_ref, high_ref, low_ref):
    f32, bf16 = jnp.float32, jnp.bfloat16
    width = rows_ref.shape[1]
    for start, stop in ((0, width // 2), (width // 2, width)):
        rows = rows_ref[:, :stop]
        total = jnp.dot(rows, factor_ref[0, :stop, start:stop], preferred_element_type=f32)
        total += jnp.dot(rows, factor_ref[1, :stop, start:stop], preferred_element_type=f32)
        high = total.astype(bf16)
        high_ref[:, start:stop] = high
        low_ref[:, start:stop] = (total - high.astype(f32)).astype(bf16)


def near_kernel(sizes, u, earlier, *refs):
    layers, owners, per_owner, block_count, block_rows = sizes
    refs = refs[earlier:]
    inputs = 2 * (owners - 1) + layers
    panels, posts = refs[: 2 * (owners - 1)], refs[2 * (owners - 1) : inputs]
    factors, (placed_ref, rows_ref) = refs[inputs:-2], refs[-2:]
    f32, bf16 = jnp.float32, jnp.bfloat16
    if u == 0:
        factor_ref, out_ref, turned_ref = factors
        turned = factor_ref[...].T
        high = turned.astype(bf16)
        turned_ref[0, :, :] = high
        turned_ref[1, :, :] = (turned - high.astype(f32)).astype(bf16)
    else:
        (out_ref,) = factors
    rows = block_count * block_rows
    group, wide = CAP * block_rows, CAP * rows
    part = rows // 2
    width = rows_ref.shape[1]
    at = 0
    for panel in panels:
        rows_ref[at : at + panel.shape[0], :] = panel[:, :width]
        at += panel.shape[0]
    for e in range(owners - 1):
        for h in range(layers // 2):
            pair = posts[2 * h : 2 * h + 2]
            pieces = [post[u * part : (u + 1) * part, e * group : (e + 1) * group] for post in pair]
            notes = [row_of(post[rows:, :wide], e) for post in pair]
            start = (e * layers + 2 * h) * rows
            place(placed_ref, slice(start, start + 2 * rows), per_owner, pieces, notes, (block_count, block_rows))
    gram = jnp.dot(placed_ref[...], rows_ref[...], preferred_element_type=f32)
    out_ref[...] = gram.astype(out_ref.dtype)


def join_kernel(above_ref, below_ref, out_ref):
    rows = above_ref.shape[0]
    out_ref[:rows, :] = above_ref[...]
    out_ref[rows:, :] = below_ref[...]


def middle_kernel(own_ref, other_ref, turned_ref, out_ref):
    f32, bf16 = jnp.float32, jnp.bfloat16
    width = own_ref.shape[1]
    gram = own_ref[...] + other_ref[...].astype(f32)
    high = gram.astype(bf16)
    low = (gram - high.astype(f32)).astype(bf16)
    for start, stop in ((0, width // 2), (width // 2, width)):
        a, b = turned_ref[0, :stop, start:stop], turned_ref[1, :stop, start:stop]
        total = jnp.dot(high[:, :stop], a, preferred_element_type=f32)
        total += jnp.dot(high[:, :stop], b, preferred_element_type=f32)
        out_ref[:, start:stop] = total + jnp.dot(low[:, :stop], a, preferred_element_type=f32)


def final_kernel(sizes, near_ref, own_ref, other_ref, turned_ref, out_hbm, *refs):
    layers, owners, per_owner, block_count, block_rows = sizes
    sum_ref, placed_ref, rows_ref, high_ref, low_ref, sems = refs
    f32 = jnp.float32
    rows = block_count * block_rows
    group, wide = CAP * block_rows, CAP * rows
    part, depth = rows // 2, layers * rows
    for u, ref in enumerate((own_ref, other_ref)):
        rows_ref[u * depth : (u + 1) * depth, :] = ref[:depth, :]
        for h in range(layers // 2):
            pieces, notes = [], []
            for k in (2 * h, 2 * h + 1):
                at = (u * layers + k) * group
                pieces.append(ref[depth : depth + part, at : at + group])
                notes.append(row_of(ref[depth + part :, :wide], k))
            start = u * depth + 2 * h * rows
            place(placed_ref, slice(start, start + 2 * rows), per_owner, pieces, notes, (block_count, block_rows))
    inverse_rows(rows_ref, turned_ref, high_ref, low_ref)
    strips = sems.shape[0]
    height = sum_ref.shape[0] // strips
    copies = []
    for i in range(strips):
        here = pl.ds(i * height, height)
        placed = placed_ref[here, :]
        total = near_ref[here, :] + jnp.dot(placed, high_ref[...], preferred_element_type=f32)
        sum_ref[here, :] = total + jnp.dot(placed, low_ref[...], preferred_element_type=f32)
        copies.append(pltpu.make_async_copy(sum_ref.at[here, :], out_hbm.at[here, :], sems.at[i]))
        copies[-1].start()
    for copy in copies:
        copy.wait()


def local(jac, panel_jac, weights, tile_lists, tile_masks, tile_order, factor_inverse):
    block_count, slot_count = tile_lists.shape
    rows, panel_width = panel_jac.shape
    block_rows = rows // block_count
    tile_width = jac.shape[1] // slot_count
    slabs, owners = lax.axis_size("rows"), lax.axis_size("cols")
    layers = slabs // 2
    per_owner = tile_order.shape[0] // owners
    slab_width = tile_width // slabs
    f32, bf16 = jnp.float32, jnp.bfloat16
    vmem, anywhere = pl.BlockSpec(memory_space=pltpu.VMEM), pl.BlockSpec(memory_space=pl.ANY)
    params = pltpu.CompilerParams(vmem_limit_bytes=24 << 20)
    shaped = jax.ShapeDtypeStruct

    def in_hbm(value):
        return pltpu.with_memory_space_constraint(value, pltpu.HBM)

    lane_group = CAP * block_rows
    post = layers * lane_group
    wide = CAP * rows
    sizes = (layers, owners, per_owner, block_count, slot_count, block_rows, tile_width)
    weighted, kept, to_x, to_y = pl.pallas_call(
        functools.partial(pack_kernel, sizes),
        out_shape=[
            shaped((rows, width), bf16)
            for width in (panel_width, post + wide, panel_width + post + wide, panel_width + 2 * post + wide)
        ],
        in_specs=[anywhere] * 6,
        out_specs=[vmem] * 4,
        scratch_shapes=[
            pltpu.SMEM(tile_lists.shape, jnp.int32),
            pltpu.SMEM(tile_masks.shape, jnp.int32),
            pltpu.SMEM(tile_order.shape, jnp.int32),
            pltpu.VMEM((1, rows), f32),
            pltpu.VMEM(panel_jac.shape, bf16),
            pltpu.VMEM(jac.shape, bf16),
            pltpu.SMEM(tile_order.shape, jnp.int32),
            pltpu.VMEM((block_count * slot_count * tile_width, block_rows), f32),
            pltpu.SemaphoreType.DMA((6,)),
        ],
        compiler_params=params,
        name="pack",
    )(*map(in_hbm, (tile_lists, tile_masks, tile_order, weights.reshape(1, rows), panel_jac, jac)))
    line = [shift(weighted, k, 0) for k in range(1, layers)]
    from_x, from_y = shift(to_x, 0, 1), shift(to_y, 0, 2)

    sizes = (layers, panel_width, lane_group, wide)
    others = pl.pallas_call(
        stack_kernel,
        out_shape=shaped(((layers - 1) * rows, panel_width), bf16),
        in_specs=[vmem] * (layers - 1),
        out_specs=vmem,
        compiler_params=params,
        cost_estimate=lasting(10**10),
        name="stack",
    )(*line)
    posts = pl.pallas_call(
        functools.partial(sort_kernel, sizes),
        out_shape=[shaped((rows + 16, owners * lane_group), bf16)] * layers,
        in_specs=[vmem] * 3,
        out_specs=[vmem] * layers,
        compiler_params=params,
        cost_estimate=lasting(10**10),
        name="sort",
    )(kept, from_x, from_y)
    posts = [posts[0]] + [shift(posts[k], k, 0) for k in range(1, layers)]
    by_x, by_y = shift(others, 0, 1), shift(others, 0, 2)

    last = rows // 2
    rows_to_y = pl.pallas_call(
        rows_to_y_kernel,
        out_shape=shaped((rows + others.shape[0] - last, panel_width), bf16),
        in_specs=[vmem] * 2 + [anywhere] * (layers - 1),
        out_specs=vmem,
        compiler_params=params,
        name="rows_to_y",
    )(from_x, by_x, *posts[1:])
    across_y = shift(rows_to_y, 0, 2)
    rest_to_x = pl.pallas_call(
        functools.partial(rest_to_x_kernel, (layers, lane_group, wide)),
        out_shape=shaped((last + rows // 2 + 16, panel_width), bf16),
        in_specs=[vmem] * (layers + 1),
        out_specs=vmem,
        compiler_params=params,
        name="rest_to_x",
    )(by_y, *posts)
    across_x = shift(rest_to_x, 0, 1)

    count = per_owner * slab_width
    depth = layers * rows
    sizes = (layers, owners, per_owner, block_count, block_rows)
    result = shaped((count, panel_width), f32)
    panels = [weighted, others, from_x, by_x, from_y, by_y]
    def near(u, out_shape, earlier, *factors):
        return pl.pallas_call(
            functools.partial(near_kernel, sizes, u, len(earlier)),
            out_shape=out_shape,
            in_specs=[anywhere] * len(earlier) + [vmem] * (len(panels) + layers + len(factors)),
            out_specs=[vmem] * len(out_shape),
            scratch_shapes=[
                pltpu.VMEM((count, (owners - 1) * depth), bf16),
                pltpu.VMEM(((owners - 1) * depth, panel_width), bf16),
            ],
            compiler_params=params,
            cost_estimate=lasting(0 if u else 10**10),
            name="near",
        )(*earlier, *panels, *posts, *factors)

    other = shift(*near(1, [shaped((count, panel_width), bf16)], [rows_to_y, rest_to_x]), 0, 0, 1)
    own, turned = near(0, [result, shaped((2, *factor_inverse.shape), bf16)], [], factor_inverse)
    joined = pl.pallas_call(
        join_kernel,
        out_shape=shaped((across_y.shape[0] + across_x.shape[0], panel_width), bf16),
        in_specs=[vmem] * 2,
        out_specs=vmem,
        compiler_params=params,
        name="join",
    )(across_y, across_x)
    other_joined = shift(joined, 0, 0, 1)
    middle = pl.pallas_call(
        middle_kernel,
        out_shape=result,
        in_specs=[vmem] * 3,
        out_specs=vmem,
        compiler_params=params,
        name="middle",
    )(own, other, turned)
    out = pl.pallas_call(
        functools.partial(final_kernel, sizes),
        out_shape=result,
        in_specs=[vmem] * 4,
        out_specs=anywhere,
        scratch_shapes=[pltpu.VMEM((count, panel_width), f32), pltpu.VMEM((count, 2 * depth), bf16)]
        + [pltpu.VMEM((2 * depth, panel_width), bf16)] * 3
        + [pltpu.SemaphoreType.DMA((4,))],
        compiler_params=params,
        name="final",
    )(middle, joined, other_joined, turned)
    return out.reshape(per_owner, slab_width, panel_width)


def solution(mesh):
    in_specs = (
        P(("rows", "cols"), None),
        P(("rows", "cols"), None),
        P(("rows", "cols")),
        P(("rows", "cols"), None),
        P(("rows", "cols"), None),
        P(),
        P(),
    )
    out_specs = P("cols", "rows", None)
    body = local if (mesh.shape["rows"], mesh.shape["cols"]) == (8, 4) else local_general
    return jax.shard_map(body, mesh=mesh, in_specs=in_specs, out_specs=out_specs, check_vma=False)
```

```python
import functools

import jax
import jax.numpy as jnp
from jax import lax
from jax.experimental import pallas as pl
from jax.experimental.pallas import tpu as pltpu
from jax.sharding import PartitionSpec as P

CAP = 2
GATHERED = 1 << 22


def tile_positions(tile_lists, tile_order):
    tile_count = tile_order.shape[0]
    matches = tile_lists[:, :, None] == tile_order[None, None, :]
    return jnp.sum(jnp.where(matches, jnp.arange(tile_count, dtype=jnp.int32), 0), axis=2)


def apply_inverse(tiles, factor_inverse):
    return jnp.einsum("ntp,qp->ntq", tiles, factor_inverse, precision=lax.Precision.HIGHEST)


def slot_codes(tile_lists, tile_masks, tile_order, owner_ids):
    block_count, slot_count = tile_lists.shape
    per_owner = tile_order.shape[0] // lax.axis_size("cols")
    positions = tile_positions(tile_lists, tile_order).reshape(-1)
    active = tile_masks.reshape(-1) == 1
    owner = positions // per_owner
    same = (owner[:, None] == owner[None, :]) & active[None, :]
    earlier = jnp.tril(jnp.ones(same.shape, bool), -1)
    rank = jnp.sum(same & earlier, axis=1)
    code = (
        (owner[None, None, :] == owner_ids[:, None, None])
        & (rank[None, None, :] == jnp.arange(CAP)[None, :, None])
        & active[None, None, :]
    )
    block = jnp.arange(block_count * slot_count) // slot_count
    place = positions % per_owner + per_owner * block
    return code, jnp.sum(jnp.where(code, place + 1, 0), axis=2) - 1


def local_general(jac, panel_jac, weights, tile_lists, tile_masks, tile_order, factor_inverse):
    block_count, slot_count = tile_lists.shape
    block_rows = jac.shape[0] // block_count
    tile_width = jac.shape[1] // slot_count
    slabs, owners = lax.axis_size("rows"), lax.axis_size("cols")
    devices = slabs * owners
    per_owner = tile_order.shape[0] // owners
    slab_width = tile_width // slabs
    bf16 = jnp.bfloat16
    weighted = (weights[:, None] * panel_jac).astype(bf16)
    code, places = slot_codes(tile_lists, tile_masks, tile_order, jnp.arange(owners))
    columns = jac.reshape(block_count, block_rows, slot_count, slabs, slab_width)
    chosen = code.astype(bf16).reshape(owners, CAP, block_count, slot_count)
    pieces = jnp.einsum("cjbk,bmkrt->rcjmt", chosen, columns, preferred_element_type=jnp.float32).astype(bf16)
    pieces = pieces.reshape(devices, -1)
    note = jnp.broadcast_to(places.astype(bf16)[None], (slabs, owners, CAP)).reshape(devices, CAP)
    note = jnp.pad(note, ((0, 0), (0, 128 - CAP)))
    sent = jnp.concatenate([pieces, note], axis=1)
    got = lax.all_to_all(sent, ("rows", "cols"), split_axis=0, concat_axis=0, tiled=True)
    size = pieces.shape[1]
    data = got[:, :size].reshape(devices, CAP, block_rows, slab_width)
    where = got[:, size : size + CAP].astype(jnp.int32)
    hot = (where[:, :, None] == jnp.arange(block_count * per_owner)).astype(bf16)
    hot = hot.reshape(devices, CAP, block_count, per_owner)
    mixed = jnp.einsum("djbn,djmt->dbmnt", hot, data, preferred_element_type=jnp.float32).astype(bf16)
    strips = max(1, devices * weighted.size * 2 // GATHERED)

    def strip_gram(strip):
        panels = lax.all_gather(strip, ("rows", "cols"), axis=0, tiled=True)
        panels = panels.reshape(devices, block_count, block_rows, -1)
        return jnp.einsum("dbmnt,dbmp->ntp", mixed, panels, preferred_element_type=jnp.float32)

    if strips == 1:
        gram = strip_gram(weighted)
    else:
        narrow = weighted.reshape(weighted.shape[0], strips, -1).swapaxes(0, 1)
        gram = jnp.moveaxis(lax.map(strip_gram, narrow), 0, 2)
        gram = gram.reshape(per_owner, slab_width, -1)
    return apply_inverse(gram, factor_inverse)


def shift(value, steps_z, flip_cols, flip_core=0):
    slabs, owners = lax.axis_size("rows"), lax.axis_size("cols")
    pairs = []
    for r in range(slabs):
        to_r = ((r // 2 + steps_z) % (slabs // 2)) * 2 + ((r % 2) ^ flip_core)
        for c in range(owners):
            pairs.append((r * owners + c, to_r * owners + (c ^ flip_cols)))
    return lax.ppermute(value, ("rows", "cols"), pairs)


def lasting(flops):
    return pl.CostEstimate(flops=flops, bytes_accessed=0, transcendentals=0)


def pack_kernel(sizes, lists_hbm, masks_hbm, order_hbm, weights_hbm, panel_hbm, jac_hbm, *refs):
    layers, owners, per_owner, block_count, slot_count, block_rows, tile_width = sizes
    weighted_ref, kept_ref, to_x_ref, to_y_ref = refs[:4]
    lists_ref, masks_ref, order_ref, weights_ref, panel_ref, jac_ref, places_ref, turned_ref, sems = refs[4:]
    copies = [
        pltpu.make_async_copy(order_hbm, order_ref, sems.at[0]),
        pltpu.make_async_copy(lists_hbm, lists_ref, sems.at[1]),
        pltpu.make_async_copy(masks_hbm, masks_ref, sems.at[2]),
        pltpu.make_async_copy(weights_hbm, weights_ref, sems.at[3]),
        pltpu.make_async_copy(panel_hbm, panel_ref, sems.at[4]),
        pltpu.make_async_copy(jac_hbm, jac_ref, sems.at[5]),
    ]
    for copy in copies:
        copy.start()
    f32, bf16 = jnp.float32, jnp.bfloat16
    rows, width = panel_ref.shape
    lane_group = CAP * block_rows
    post = layers * lane_group
    slab = tile_width // layers
    part = slab // 2
    me_r, me_c = lax.axis_index("rows"), lax.axis_index("cols")
    me_z, me_core = me_r // 2, lax.rem(me_r, 2)
    for copy in copies:
        copy.wait()

    row_ids = lax.broadcasted_iota(jnp.int32, (rows, rows), 0)
    lane_ids = lax.broadcasted_iota(jnp.int32, (rows, rows), 1)
    column = jnp.sum(jnp.where(row_ids == lane_ids, weights_ref[...], 0.0), axis=1, keepdims=True)
    weighted = (column * panel_ref[...].astype(f32)).astype(bf16)
    weighted_ref[...] = weighted
    to_x_ref[:, :width] = weighted
    to_y_ref[:, :width] = weighted

    for b in range(block_count):
        block = jac_ref[b * block_rows : (b + 1) * block_rows, :].astype(f32)
        start = b * slot_count * tile_width
        turned_ref[start : start + slot_count * tile_width, :] = block.T

    for i in range(order_ref.shape[0]):
        places_ref[order_ref[i]] = i
    slots = []
    for s in range(block_count * slot_count):
        b, k = divmod(s, slot_count)
        place = places_ref[lists_ref[b, k]]
        owner = jnp.int32(0)
        for c in range(1, owners):
            owner += (place >= c * per_owner).astype(jnp.int32)
        slots.append((place - owner * per_owner, jnp.where(masks_ref[b, k] == 1, owner, -1)))

    shape = (16, CAP * block_count * block_rows)
    lane, row = lax.broadcasted_iota(jnp.int32, shape, 1), lax.broadcasted_iota(jnp.int32, shape, 0)
    notes = []
    spots = [(kept_ref, 0), (to_x_ref, width), (to_y_ref, width), (to_y_ref, width + post)]
    for e, (parcel, start) in enumerate(spots):
        wanted = me_c ^ e
        found = jnp.int32(0)
        chosen = [jnp.int32(0)] * CAP
        codes = [jnp.int32(-1)] * CAP
        for s, (place, owner) in enumerate(slots):
            hit = owner == wanted
            for j in range(CAP):
                take = hit & (found == j)
                chosen[j] = jnp.where(take, s, chosen[j])
                codes[j] = jnp.where(take, place, codes[j])
            found += hit.astype(jnp.int32)
        note = jnp.full(shape, -1, jnp.int32)
        for j in range(CAP):
            for b in range(block_count):
                at = (j * block_count + b) * block_rows
                here = (lane >= at) & (lane < at + block_rows)
                code = jnp.where(chosen[j] // slot_count == b, codes[j], -1)
                note = jnp.where(here, code, note)
        notes.append(note)
        for k in range(layers):
            z = lax.rem(me_z + k, layers)
            for u in range(2):
                core = me_core ^ u
                for j in range(CAP):
                    first = pl.multiple_of(chosen[j] * tile_width + z * slab + core * part, part)
                    piece = turned_ref[pl.ds(first, part), :].astype(bf16)
                    to = start + k * lane_group + j * block_rows
                    parcel[u * part : (u + 1) * part, to : to + block_rows] = piece
    kept_ref[:16, post:] = notes[0].astype(f32).astype(bf16)
    to_x_ref[:16, width + post :] = notes[1].astype(f32).astype(bf16)
    to_y_ref[:16, width + 2 * post :] = jnp.where(row == 0, notes[2], notes[3]).astype(f32).astype(bf16)


def row_of(block, i):
    ids = lax.broadcasted_iota(jnp.int32, block.shape, 0)
    return jnp.sum(jnp.where(ids == i, block.astype(jnp.float32), 0.0), axis=0, keepdims=True)


def rows_from(notes):
    ids = lax.broadcasted_iota(jnp.int32, (16, notes[0].shape[1]), 0)
    block = jnp.full(ids.shape, -1.0, jnp.float32)
    for i, note in enumerate(notes):
        block = jnp.where(ids == i, note, block)
    return block.astype(jnp.bfloat16)


def stack_kernel(*refs):
    at = 0
    for ref in refs[:-1]:
        refs[-1][at : at + ref.shape[0], :] = ref[...]
        at += ref.shape[0]


def sort_kernel(sizes, kept_ref, from_x_ref, from_y_ref, *posts):
    layers, width, lane_group, wide = sizes
    post = layers * lane_group
    rows = kept_ref.shape[0]
    spots = [(kept_ref, 0), (from_x_ref, width), (from_y_ref, width), (from_y_ref, width + post)]
    notes = [row_of(ref[:16, ref.shape[1] - wide :], int(e == 3)) for e, (ref, start) in enumerate(spots)]
    block = rows_from(notes)
    for k, out in enumerate(posts):
        for e, (ref, start) in enumerate(spots):
            piece = ref[:, start + k * lane_group : start + (k + 1) * lane_group]
            out[:rows, e * lane_group : (e + 1) * lane_group] = piece
        out[rows:, :wide] = block


def rows_to_y_kernel(from_x_ref, by_x_ref, out_ref):
    rows = from_x_ref.shape[0]
    out_ref[:rows, :] = from_x_ref[:, : out_ref.shape[1]]
    out_ref[rows:, :] = by_x_ref[: out_ref.shape[0] - rows, :]


def rest_to_x_kernel(sizes, by_y_ref, *refs):
    layers, lane_group, wide = sizes
    posts, out_ref = refs[:layers], refs[layers]
    rows = posts[0].shape[0] - 16
    part = rows // 2
    last = out_ref.shape[0] - part - 16
    out_ref[:last, :] = by_y_ref[by_y_ref.shape[0] - last :, :]
    for k, ref in enumerate(posts):
        for u in range(2):
            piece = ref[u * part : (u + 1) * part, 3 * lane_group : 4 * lane_group]
            at = (u * layers + k) * lane_group
            out_ref[last : last + part, at : at + lane_group] = piece
    out_ref[last + part :, :wide] = rows_from([row_of(ref[rows:, :wide], 3) for ref in posts])


def place(out_ref, lanes, per_owner, pieces, notes, sizes):
    block_count, block_rows = sizes
    f32, bf16 = jnp.float32, jnp.bfloat16
    part, rows = pieces[0].shape[0], block_count * block_rows
    columns, codes = [], []
    for j in range(CAP):
        parts = []
        for piece in pieces:
            parts += [piece[:, j * block_rows : (j + 1) * block_rows].astype(f32)] * block_count
        columns.append(jnp.concatenate(parts, axis=1).astype(bf16))
        note = jnp.concatenate([note[:, j * rows : (j + 1) * rows] for note in notes], axis=1)
        codes.append(jnp.broadcast_to(note, columns[j].shape).astype(bf16))
    for n in range(per_owner):
        placed = jnp.zeros(columns[0].shape, bf16)
        for j in range(CAP):
            placed = jnp.where(codes[j] == jnp.asarray(n, bf16), columns[j], placed)
        out_ref[n * part : (n + 1) * part, lanes] = placed


def inverse_rows(rows_ref, factor_ref, high_ref, low_ref):
    f32, bf16 = jnp.float32, jnp.bfloat16
    height, width = high_ref.shape
    for start, stop in ((0, width // 2), (width // 2, width)):
        rows = rows_ref[:height, :stop]
        total = jnp.dot(rows, factor_ref[0, :stop, start:stop], preferred_element_type=f32)
        total += jnp.dot(rows, factor_ref[1, :stop, start:stop], preferred_element_type=f32)
        high = total.astype(bf16)
        high_ref[:, start:stop] = high
        low_ref[:, start:stop] = (total - high.astype(f32)).astype(bf16)


def near_kernel(sizes, earlier, *refs):
    layers, owners, per_owner, block_count, block_rows = sizes
    refs = refs[earlier:]
    inputs = 2 * (owners - 1) + layers
    panels, posts = refs[: 2 * (owners - 1)], refs[2 * (owners - 1) : inputs]
    factor_ref, own_ref, other_ref, turned_ref, placed_ref, rows_ref = refs[inputs:]
    f32, bf16 = jnp.float32, jnp.bfloat16
    rows = block_count * block_rows
    group, wide = CAP * block_rows, CAP * rows
    part = rows // 2
    width = rows_ref.shape[1]
    at = 0
    for panel in panels:
        rows_ref[at : at + panel.shape[0], :] = panel[:, :width]
        at += panel.shape[0]
    for u, out_ref in ((1, other_ref), (0, own_ref)):
        for e in range(owners - 1):
            for h in range(layers // 2):
                pair = posts[2 * h : 2 * h + 2]
                pieces = [post[u * part : (u + 1) * part, e * group : (e + 1) * group] for post in pair]
                notes = [row_of(post[rows:, :wide], e) for post in pair]
                start = (e * layers + 2 * h) * rows
                place(placed_ref, slice(start, start + 2 * rows), per_owner, pieces, notes, (block_count, block_rows))
        gram = jnp.dot(placed_ref[...], rows_ref[...], preferred_element_type=f32)
        out_ref[...] = gram.astype(out_ref.dtype)
    turned = factor_ref[...].T
    high = turned.astype(bf16)
    turned_ref[0, :, :] = high
    turned_ref[1, :, :] = (turned - high.astype(f32)).astype(bf16)


def join_kernel(above_ref, below_ref, out_ref):
    rows = above_ref.shape[0]
    out_ref[:rows, :] = above_ref[...]
    out_ref[rows:, :] = below_ref[...]


def place_far(sizes, u, ref, placed_ref):
    layers, owners, per_owner, block_count, block_rows = sizes
    rows = block_count * block_rows
    group, wide = CAP * block_rows, CAP * rows
    part, depth = rows // 2, layers * rows
    for h in range(layers // 2):
        pieces, notes = [], []
        for k in (2 * h, 2 * h + 1):
            at = (u * layers + k) * group
            pieces.append(ref[depth : depth + part, at : at + group])
            notes.append(row_of(ref[depth + part :, :wide], k))
        lanes = slice(2 * h * rows, 2 * (h + 1) * rows)
        place(placed_ref, lanes, per_owner, pieces, notes, (block_count, block_rows))


def middle_kernel(sizes, own_ref, other_ref, joined_ref, turned_ref, out_ref, placed_ref, high_ref, low_ref):
    f32, bf16 = jnp.float32, jnp.bfloat16
    width = own_ref.shape[1]
    place_far(sizes, 0, joined_ref, placed_ref)
    inverse_rows(joined_ref, turned_ref, high_ref, low_ref)
    placed = placed_ref[...]
    gram = own_ref[...] + other_ref[...].astype(f32)
    high = gram.astype(bf16)
    low = (gram - high.astype(f32)).astype(bf16)
    for start, stop in ((0, width // 2), (width // 2, width)):
        a, b = turned_ref[0, :stop, start:stop], turned_ref[1, :stop, start:stop]
        total = jnp.dot(high[:, :stop], a, preferred_element_type=f32)
        total += jnp.dot(high[:, :stop], b, preferred_element_type=f32)
        total += jnp.dot(low[:, :stop], a, preferred_element_type=f32)
        total += jnp.dot(placed, high_ref[:, start:stop], preferred_element_type=f32)
        out_ref[:, start:stop] = total + jnp.dot(placed, low_ref[:, start:stop], preferred_element_type=f32)


def final_kernel(sizes, middle_ref, joined_ref, turned_ref, out_hbm, sum_ref, placed_ref, high_ref, low_ref, sems):
    f32 = jnp.float32
    place_far(sizes, 1, joined_ref, placed_ref)
    inverse_rows(joined_ref, turned_ref, high_ref, low_ref)
    strips = sems.shape[0]
    height = sum_ref.shape[0] // strips
    copies = []
    for i in range(strips):
        here = pl.ds(i * height, height)
        placed = placed_ref[here, :]
        total = middle_ref[here, :] + jnp.dot(placed, high_ref[...], preferred_element_type=f32)
        sum_ref[here, :] = total + jnp.dot(placed, low_ref[...], preferred_element_type=f32)
        copies.append(pltpu.make_async_copy(sum_ref.at[here, :], out_hbm.at[here, :], sems.at[i]))
        copies[-1].start()
    for copy in copies:
        copy.wait()


def local(jac, panel_jac, weights, tile_lists, tile_masks, tile_order, factor_inverse):
    block_count, slot_count = tile_lists.shape
    rows, panel_width = panel_jac.shape
    block_rows = rows // block_count
    tile_width = jac.shape[1] // slot_count
    slabs, owners = lax.axis_size("rows"), lax.axis_size("cols")
    layers = slabs // 2
    per_owner = tile_order.shape[0] // owners
    slab_width = tile_width // slabs
    f32, bf16 = jnp.float32, jnp.bfloat16
    vmem, anywhere = pl.BlockSpec(memory_space=pltpu.VMEM), pl.BlockSpec(memory_space=pl.ANY)
    params = pltpu.CompilerParams(vmem_limit_bytes=24 << 20)
    shaped = jax.ShapeDtypeStruct

    def in_hbm(value):
        return pltpu.with_memory_space_constraint(value, pltpu.HBM)

    lane_group = CAP * block_rows
    post = layers * lane_group
    wide = CAP * rows
    sizes = (layers, owners, per_owner, block_count, slot_count, block_rows, tile_width)
    weighted, kept, to_x, to_y = pl.pallas_call(
        functools.partial(pack_kernel, sizes),
        out_shape=[
            shaped((rows, width), bf16)
            for width in (panel_width, post + wide, panel_width + post + wide, panel_width + 2 * post + wide)
        ],
        in_specs=[anywhere] * 6,
        out_specs=[vmem] * 4,
        scratch_shapes=[
            pltpu.SMEM(tile_lists.shape, jnp.int32),
            pltpu.SMEM(tile_masks.shape, jnp.int32),
            pltpu.SMEM(tile_order.shape, jnp.int32),
            pltpu.VMEM((1, rows), f32),
            pltpu.VMEM(panel_jac.shape, bf16),
            pltpu.VMEM(jac.shape, bf16),
            pltpu.SMEM(tile_order.shape, jnp.int32),
            pltpu.VMEM((block_count * slot_count * tile_width, block_rows), f32),
            pltpu.SemaphoreType.DMA((6,)),
        ],
        compiler_params=params,
        name="pack",
    )(*map(in_hbm, (tile_lists, tile_masks, tile_order, weights.reshape(1, rows), panel_jac, jac)))
    line = [shift(weighted, k, 0) for k in range(1, layers)]
    from_x, from_y = shift(to_x, 0, 1), shift(to_y, 0, 2)

    sizes = (layers, panel_width, lane_group, wide)
    others = pl.pallas_call(
        stack_kernel,
        out_shape=shaped(((layers - 1) * rows, panel_width), bf16),
        in_specs=[vmem] * (layers - 1),
        out_specs=vmem,
        compiler_params=params,
        cost_estimate=lasting(10**10),
        name="stack",
    )(*line)
    posts = pl.pallas_call(
        functools.partial(sort_kernel, sizes),
        out_shape=[shaped((rows + 16, owners * lane_group), bf16)] * layers,
        in_specs=[vmem] * 3,
        out_specs=[vmem] * layers,
        compiler_params=params,
        cost_estimate=lasting(10**10),
        name="sort",
    )(kept, from_x, from_y)
    posts = [posts[0]] + [shift(posts[k], k, 0) for k in range(1, layers)]
    by_x, by_y = shift(others, 0, 1), shift(others, 0, 2)

    last = rows // 2
    rows_to_y = pl.pallas_call(
        rows_to_y_kernel,
        out_shape=shaped((rows + others.shape[0] - last, panel_width), bf16),
        in_specs=[vmem] * 2,
        out_specs=vmem,
        compiler_params=params,
        name="rows_to_y",
    )(from_x, by_x)
    across_y = shift(rows_to_y, 0, 2)
    rest_to_x = pl.pallas_call(
        functools.partial(rest_to_x_kernel, (layers, lane_group, wide)),
        out_shape=shaped((last + rows // 2 + 16, panel_width), bf16),
        in_specs=[vmem] * (layers + 1),
        out_specs=vmem,
        compiler_params=params,
        cost_estimate=lasting(3 * 10**9),
        name="rest_to_x",
    )(by_y, *posts)
    across_x = shift(rest_to_x, 0, 1)

    count = per_owner * slab_width
    depth = layers * rows
    sizes = (layers, owners, per_owner, block_count, block_rows)
    result = shaped((count, panel_width), f32)
    panels = [weighted, others, from_x, by_x, from_y, by_y]
    own, other, turned = pl.pallas_call(
        functools.partial(near_kernel, sizes, 2),
        out_shape=[result, shaped((count, panel_width), bf16), shaped((2, *factor_inverse.shape), bf16)],
        in_specs=[anywhere] * 2 + [vmem] * (len(panels) + layers + 1),
        out_specs=[vmem] * 3,
        scratch_shapes=[
            pltpu.VMEM((count, (owners - 1) * depth), bf16),
            pltpu.VMEM(((owners - 1) * depth, panel_width), bf16),
        ],
        compiler_params=params,
        cost_estimate=lasting(10**9),
        name="near",
    )(rows_to_y, rest_to_x, *panels, *posts, factor_inverse)
    other = shift(other, 0, 0, 1)
    joined = pl.pallas_call(
        join_kernel,
        out_shape=shaped((across_y.shape[0] + across_x.shape[0], panel_width), bf16),
        in_specs=[vmem] * 2,
        out_specs=vmem,
        compiler_params=params,
        cost_estimate=lasting(10**10),
        name="join",
    )(across_y, across_x)
    other_joined = shift(joined, 0, 0, 1)
    far_scratch = [pltpu.VMEM((count, depth), bf16)] + [pltpu.VMEM((depth, panel_width), bf16)] * 2
    middle = pl.pallas_call(
        functools.partial(middle_kernel, sizes),
        out_shape=result,
        in_specs=[vmem] * 4,
        out_specs=vmem,
        scratch_shapes=far_scratch,
        compiler_params=params,
        name="middle",
    )(own, other, joined, turned)
    out = pl.pallas_call(
        functools.partial(final_kernel, sizes),
        out_shape=result,
        in_specs=[vmem] * 3,
        out_specs=anywhere,
        scratch_shapes=[pltpu.VMEM((count, panel_width), f32)] + far_scratch + [pltpu.SemaphoreType.DMA((4,))],
        compiler_params=params,
        name="final",
    )(middle, other_joined, turned)
    return out.reshape(per_owner, slab_width, panel_width)


def solution(mesh):
    in_specs = (
        P(("rows", "cols"), None),
        P(("rows", "cols"), None),
        P(("rows", "cols")),
        P(("rows", "cols"), None),
        P(("rows", "cols"), None),
        P(),
        P(),
    )
    out_specs = P("cols", "rows", None)
    body = local if (mesh.shape["rows"], mesh.shape["cols"]) == (8, 4) else local_general
    return jax.shard_map(body, mesh=mesh, in_specs=in_specs, out_specs=out_specs, check_vma=False)
```

```python
import functools

import jax
import jax.numpy as jnp
from jax import lax
from jax.experimental import pallas as pl
from jax.experimental.pallas import tpu as pltpu
from jax.sharding import PartitionSpec as P

CAP = 2
GATHERED = 1 << 22


def tile_positions(tile_lists, tile_order):
    tile_count = tile_order.shape[0]
    matches = tile_lists[:, :, None] == tile_order[None, None, :]
    return jnp.sum(jnp.where(matches, jnp.arange(tile_count, dtype=jnp.int32), 0), axis=2)


def apply_inverse(tiles, factor_inverse):
    return jnp.einsum("ntp,qp->ntq", tiles, factor_inverse, precision=lax.Precision.HIGHEST)


def slot_codes(tile_lists, tile_masks, tile_order, owner_ids):
    block_count, slot_count = tile_lists.shape
    per_owner = tile_order.shape[0] // lax.axis_size("cols")
    positions = tile_positions(tile_lists, tile_order).reshape(-1)
    active = tile_masks.reshape(-1) == 1
    owner = positions // per_owner
    same = (owner[:, None] == owner[None, :]) & active[None, :]
    earlier = jnp.tril(jnp.ones(same.shape, bool), -1)
    rank = jnp.sum(same & earlier, axis=1)
    code = (
        (owner[None, None, :] == owner_ids[:, None, None])
        & (rank[None, None, :] == jnp.arange(CAP)[None, :, None])
        & active[None, None, :]
    )
    block = jnp.arange(block_count * slot_count) // slot_count
    place = positions % per_owner + per_owner * block
    return code, jnp.sum(jnp.where(code, place + 1, 0), axis=2) - 1


def local_general(jac, panel_jac, weights, tile_lists, tile_masks, tile_order, factor_inverse):
    block_count, slot_count = tile_lists.shape
    block_rows = jac.shape[0] // block_count
    tile_width = jac.shape[1] // slot_count
    slabs, owners = lax.axis_size("rows"), lax.axis_size("cols")
    devices = slabs * owners
    per_owner = tile_order.shape[0] // owners
    slab_width = tile_width // slabs
    bf16 = jnp.bfloat16
    weighted = (weights[:, None] * panel_jac).astype(bf16)
    code, places = slot_codes(tile_lists, tile_masks, tile_order, jnp.arange(owners))
    columns = jac.reshape(block_count, block_rows, slot_count, slabs, slab_width)
    chosen = code.astype(bf16).reshape(owners, CAP, block_count, slot_count)
    pieces = jnp.einsum("cjbk,bmkrt->rcjmt", chosen, columns, preferred_element_type=jnp.float32).astype(bf16)
    pieces = pieces.reshape(devices, -1)
    note = jnp.broadcast_to(places.astype(bf16)[None], (slabs, owners, CAP)).reshape(devices, CAP)
    note = jnp.pad(note, ((0, 0), (0, 128 - CAP)))
    sent = jnp.concatenate([pieces, note], axis=1)
    got = lax.all_to_all(sent, ("rows", "cols"), split_axis=0, concat_axis=0, tiled=True)
    size = pieces.shape[1]
    data = got[:, :size].reshape(devices, CAP, block_rows, slab_width)
    where = got[:, size : size + CAP].astype(jnp.int32)
    hot = (where[:, :, None] == jnp.arange(block_count * per_owner)).astype(bf16)
    hot = hot.reshape(devices, CAP, block_count, per_owner)
    mixed = jnp.einsum("djbn,djmt->dbmnt", hot, data, preferred_element_type=jnp.float32).astype(bf16)
    strips = max(1, devices * weighted.size * 2 // GATHERED)

    def strip_gram(strip):
        panels = lax.all_gather(strip, ("rows", "cols"), axis=0, tiled=True)
        panels = panels.reshape(devices, block_count, block_rows, -1)
        return jnp.einsum("dbmnt,dbmp->ntp", mixed, panels, preferred_element_type=jnp.float32)

    if strips == 1:
        gram = strip_gram(weighted)
    else:
        narrow = weighted.reshape(weighted.shape[0], strips, -1).swapaxes(0, 1)
        gram = jnp.moveaxis(lax.map(strip_gram, narrow), 0, 2)
        gram = gram.reshape(per_owner, slab_width, -1)
    return apply_inverse(gram, factor_inverse)


def shift(value, steps_z, flip_cols, flip_core=0):
    slabs, owners = lax.axis_size("rows"), lax.axis_size("cols")
    pairs = []
    for r in range(slabs):
        to_r = ((r // 2 + steps_z) % (slabs // 2)) * 2 + ((r % 2) ^ flip_core)
        for c in range(owners):
            pairs.append((r * owners + c, to_r * owners + (c ^ flip_cols)))
    return lax.ppermute(value, ("rows", "cols"), pairs)


def lasting(flops):
    return pl.CostEstimate(flops=flops, bytes_accessed=0, transcendentals=0)


def pack_kernel(sizes, lists_hbm, masks_hbm, order_hbm, weights_hbm, panel_hbm, jac_hbm, *refs):
    layers, owners, per_owner, block_count, slot_count, block_rows, tile_width = sizes
    weighted_ref, kept_ref, to_x_ref, to_y_ref = refs[:4]
    lists_ref, masks_ref, order_ref, weights_ref, panel_ref, jac_ref, places_ref, turned_ref, sems = refs[4:]
    copies = [
        pltpu.make_async_copy(order_hbm, order_ref, sems.at[0]),
        pltpu.make_async_copy(lists_hbm, lists_ref, sems.at[1]),
        pltpu.make_async_copy(masks_hbm, masks_ref, sems.at[2]),
        pltpu.make_async_copy(weights_hbm, weights_ref, sems.at[3]),
        pltpu.make_async_copy(panel_hbm, panel_ref, sems.at[4]),
        pltpu.make_async_copy(jac_hbm, jac_ref, sems.at[5]),
    ]
    for copy in copies:
        copy.start()
    f32, bf16 = jnp.float32, jnp.bfloat16
    rows, width = panel_ref.shape
    lane_group = CAP * block_rows
    post = layers * lane_group
    slab = tile_width // layers
    part = slab // 2
    me_r, me_c = lax.axis_index("rows"), lax.axis_index("cols")
    me_z, me_core = me_r // 2, lax.rem(me_r, 2)
    for copy in copies:
        copy.wait()

    row_ids = lax.broadcasted_iota(jnp.int32, (rows, rows), 0)
    lane_ids = lax.broadcasted_iota(jnp.int32, (rows, rows), 1)
    column = jnp.sum(jnp.where(row_ids == lane_ids, weights_ref[...], 0.0), axis=1, keepdims=True)
    weighted = (column * panel_ref[...].astype(f32)).astype(bf16)
    weighted_ref[...] = weighted
    to_x_ref[:, :width] = weighted

    for b in range(block_count):
        block = jac_ref[b * block_rows : (b + 1) * block_rows, :].astype(f32)
        start = b * slot_count * tile_width
        turned_ref[start : start + slot_count * tile_width, :] = block.T

    for i in range(order_ref.shape[0]):
        places_ref[order_ref[i]] = i
    slots = []
    for s in range(block_count * slot_count):
        b, k = divmod(s, slot_count)
        place = places_ref[lists_ref[b, k]]
        owner = jnp.int32(0)
        for c in range(1, owners):
            owner += (place >= c * per_owner).astype(jnp.int32)
        slots.append((place - owner * per_owner, jnp.where(masks_ref[b, k] == 1, owner, -1)))

    shape = (16, CAP * block_count * block_rows)
    lane, row = lax.broadcasted_iota(jnp.int32, shape, 1), lax.broadcasted_iota(jnp.int32, shape, 0)
    notes = []
    spots = [(kept_ref, 0), (to_x_ref, width), (to_y_ref, 0), (to_y_ref, post)]
    for e, (parcel, start) in enumerate(spots):
        wanted = me_c ^ e
        found = jnp.int32(0)
        chosen = [jnp.int32(0)] * CAP
        codes = [jnp.int32(-1)] * CAP
        for s, (place, owner) in enumerate(slots):
            hit = owner == wanted
            for j in range(CAP):
                take = hit & (found == j)
                chosen[j] = jnp.where(take, s, chosen[j])
                codes[j] = jnp.where(take, place, codes[j])
            found += hit.astype(jnp.int32)
        note = jnp.full(shape, -1, jnp.int32)
        for j in range(CAP):
            for b in range(block_count):
                at = (j * block_count + b) * block_rows
                here = (lane >= at) & (lane < at + block_rows)
                code = jnp.where(chosen[j] // slot_count == b, codes[j], -1)
                note = jnp.where(here, code, note)
        notes.append(note)
        for k in range(layers):
            z = lax.rem(me_z + k, layers)
            for u in range(2):
                core = me_core ^ u
                for j in range(CAP):
                    first = pl.multiple_of(chosen[j] * tile_width + z * slab + core * part, part)
                    piece = turned_ref[pl.ds(first, part), :].astype(bf16)
                    to = start + k * lane_group + j * block_rows
                    parcel[u * part : (u + 1) * part, to : to + block_rows] = piece
    kept_ref[:16, post:] = notes[0].astype(f32).astype(bf16)
    to_x_ref[:16, width + post :] = notes[1].astype(f32).astype(bf16)
    to_y_ref[:16, 2 * post :] = jnp.where(row == 0, notes[2], notes[3]).astype(f32).astype(bf16)


def row_of(block, i):
    ids = lax.broadcasted_iota(jnp.int32, block.shape, 0)
    return jnp.sum(jnp.where(ids == i, block.astype(jnp.float32), 0.0), axis=0, keepdims=True)


def rows_from(notes):
    ids = lax.broadcasted_iota(jnp.int32, (16, notes[0].shape[1]), 0)
    block = jnp.full(ids.shape, -1.0, jnp.float32)
    for i, note in enumerate(notes):
        block = jnp.where(ids == i, note, block)
    return block.astype(jnp.bfloat16)


def stack_kernel(*refs):
    inputs, (rest_ref, all_ref) = refs[:-2], refs[-2:]
    rows = inputs[0].shape[0]
    for i, ref in enumerate(inputs):
        all_ref[i * rows : (i + 1) * rows, :] = ref[...]
        if i:
            rest_ref[(i - 1) * rows : i * rows, :] = ref[...]


def sort_kernel(sizes, kept_ref, from_x_ref, from_y_ref, *posts):
    layers, width, lane_group, wide = sizes
    post = layers * lane_group
    rows = kept_ref.shape[0]
    spots = [(kept_ref, 0), (from_x_ref, width), (from_y_ref, 0), (from_y_ref, post)]
    notes = [row_of(ref[:16, ref.shape[1] - wide :], int(e == 3)) for e, (ref, start) in enumerate(spots)]
    block = rows_from(notes)
    for k, out in enumerate(posts):
        for e, (ref, start) in enumerate(spots):
            piece = ref[:, start + k * lane_group : start + (k + 1) * lane_group]
            out[:rows, e * lane_group : (e + 1) * lane_group] = piece
        out[rows:, :wide] = block


def rows_to_y_kernel(from_x_ref, by_x_ref, out_ref):
    rows = from_x_ref.shape[0]
    out_ref[:rows, :] = from_x_ref[:, : out_ref.shape[1]]
    out_ref[rows:, :] = by_x_ref[...]


def columns_to_x_kernel(sizes, *refs):
    layers, lane_group, wide = sizes
    posts, out_ref = refs[:layers], refs[-1]
    rows = posts[0].shape[0] - 16
    part = rows // 2
    for k, ref in enumerate(posts):
        for u in range(2):
            piece = ref[u * part : (u + 1) * part, 3 * lane_group : 4 * lane_group]
            at = (u * layers + k) * lane_group
            out_ref[:part, at : at + lane_group] = piece
    out_ref[part:, :wide] = rows_from([row_of(ref[rows:, :wide], 3) for ref in posts])


def place(out_ref, lanes, per_owner, pieces, notes, sizes):
    block_count, block_rows = sizes
    f32, bf16 = jnp.float32, jnp.bfloat16
    part, rows = pieces[0].shape[0], block_count * block_rows
    columns, codes = [], []
    for j in range(CAP):
        parts = []
        for piece in pieces:
            parts += [piece[:, j * block_rows : (j + 1) * block_rows].astype(f32)] * block_count
        columns.append(jnp.concatenate(parts, axis=1).astype(bf16))
        note = jnp.concatenate([note[:, j * rows : (j + 1) * rows] for note in notes], axis=1)
        codes.append(jnp.broadcast_to(note, columns[j].shape).astype(bf16))
    for n in range(per_owner):
        placed = jnp.zeros(columns[0].shape, bf16)
        for j in range(CAP):
            placed = jnp.where(codes[j] == jnp.asarray(n, bf16), columns[j], placed)
        out_ref[n * part : (n + 1) * part, lanes] = placed


def inverse_rows(rows_ref, factor_ref, high_ref, low_ref):
    f32, bf16 = jnp.float32, jnp.bfloat16
    height, width = high_ref.shape
    for start, stop in ((0, width // 2), (width // 2, width)):
        rows = rows_ref[:height, :stop]
        total = jnp.dot(rows, factor_ref[0, :stop, start:stop], preferred_element_type=f32)
        total += jnp.dot(rows, factor_ref[1, :stop, start:stop], preferred_element_type=f32)
        high = total.astype(bf16)
        high_ref[:, start:stop] = high
        low_ref[:, start:stop] = (total - high.astype(f32)).astype(bf16)


def near_kernel(sizes, earlier, *refs):
    layers, owners, per_owner, block_count, block_rows = sizes
    panels, posts, refs = refs[earlier : earlier + 4], refs[earlier + 4 : earlier + 4 + layers], refs[earlier + 4 + layers :]
    factor_hbm, own_ref, other_ref, turned_ref, placed_ref, rows_ref, factor_ref, sem = refs
    copy = pltpu.make_async_copy(factor_hbm, factor_ref, sem)
    copy.start()
    f32, bf16 = jnp.float32, jnp.bfloat16
    rows = block_count * block_rows
    group, wide = CAP * block_rows, CAP * rows
    part = rows // 2
    width = rows_ref.shape[1]
    at = 0
    for panel in panels:
        rows_ref[at : at + panel.shape[0], :] = panel[:, :width]
        at += panel.shape[0]
    for u, out_ref in ((1, other_ref), (0, own_ref)):
        for e in range(owners - 1):
            for h in range(layers // 2):
                pair = posts[2 * h : 2 * h + 2]
                pieces = [post[u * part : (u + 1) * part, e * group : (e + 1) * group] for post in pair]
                notes = [row_of(post[rows:, :wide], e) for post in pair]
                start = (e * layers + 2 * h) * rows
                place(placed_ref, slice(start, start + 2 * rows), per_owner, pieces, notes, (block_count, block_rows))
        gram = jnp.dot(placed_ref[...], rows_ref[...], preferred_element_type=f32)
        out_ref[...] = gram.astype(out_ref.dtype)
    copy.wait()
    turned = factor_ref[...].T
    high = turned.astype(bf16)
    turned_ref[0, :, :] = high
    turned_ref[1, :, :] = (turned - high.astype(f32)).astype(bf16)


def join_kernel(above_ref, below_ref, out_ref):
    rows = above_ref.shape[0]
    out_ref[:rows, :] = above_ref[...]
    out_ref[rows:, :] = below_ref[...]


def place_far(sizes, u, ref, placed_ref):
    layers, owners, per_owner, block_count, block_rows = sizes
    rows = block_count * block_rows
    group, wide = CAP * block_rows, CAP * rows
    part, depth = rows // 2, layers * rows
    for h in range(layers // 2):
        pieces, notes = [], []
        for k in (2 * h, 2 * h + 1):
            at = (u * layers + k) * group
            pieces.append(ref[depth : depth + part, at : at + group])
            notes.append(row_of(ref[depth + part :, :wide], k))
        lanes = slice(2 * h * rows, 2 * (h + 1) * rows)
        place(placed_ref, lanes, per_owner, pieces, notes, (block_count, block_rows))


def middle_kernel(sizes, own_ref, other_ref, joined_ref, turned_ref, out_ref, placed_ref, high_ref, low_ref):
    f32, bf16 = jnp.float32, jnp.bfloat16
    width = own_ref.shape[1]
    place_far(sizes, 0, joined_ref, placed_ref)
    inverse_rows(joined_ref, turned_ref, high_ref, low_ref)
    placed = placed_ref[...]
    gram = own_ref[...] + other_ref[...].astype(f32)
    high = gram.astype(bf16)
    low = (gram - high.astype(f32)).astype(bf16)
    for start, stop in ((0, width // 2), (width // 2, width)):
        a, b = turned_ref[0, :stop, start:stop], turned_ref[1, :stop, start:stop]
        total = jnp.dot(high[:, :stop], a, preferred_element_type=f32)
        total += jnp.dot(high[:, :stop], b, preferred_element_type=f32)
        total += jnp.dot(low[:, :stop], a, preferred_element_type=f32)
        total += jnp.dot(placed, high_ref[:, start:stop], preferred_element_type=f32)
        out_ref[:, start:stop] = total + jnp.dot(placed, low_ref[:, start:stop], preferred_element_type=f32)


def final_kernel(sizes, middle_ref, joined_ref, turned_ref, out_hbm, sum_ref, placed_ref, high_ref, low_ref, sems):
    f32 = jnp.float32
    place_far(sizes, 1, joined_ref, placed_ref)
    inverse_rows(joined_ref, turned_ref, high_ref, low_ref)
    strips = sems.shape[0]
    height = sum_ref.shape[0] // strips
    copies = []
    for i in range(strips):
        here = pl.ds(i * height, height)
        placed = placed_ref[here, :]
        total = middle_ref[here, :] + jnp.dot(placed, high_ref[...], preferred_element_type=f32)
        sum_ref[here, :] = total + jnp.dot(placed, low_ref[...], preferred_element_type=f32)
        copies.append(pltpu.make_async_copy(sum_ref.at[here, :], out_hbm.at[here, :], sems.at[i]))
        copies[-1].start()
    for copy in copies:
        copy.wait()


def local(jac, panel_jac, weights, tile_lists, tile_masks, tile_order, factor_inverse):
    block_count, slot_count = tile_lists.shape
    rows, panel_width = panel_jac.shape
    block_rows = rows // block_count
    tile_width = jac.shape[1] // slot_count
    slabs, owners = lax.axis_size("rows"), lax.axis_size("cols")
    layers = slabs // 2
    per_owner = tile_order.shape[0] // owners
    slab_width = tile_width // slabs
    f32, bf16 = jnp.float32, jnp.bfloat16
    vmem, anywhere = pl.BlockSpec(memory_space=pltpu.VMEM), pl.BlockSpec(memory_space=pl.ANY)
    params = pltpu.CompilerParams(vmem_limit_bytes=24 << 20)
    shaped = jax.ShapeDtypeStruct

    def in_hbm(value):
        return pltpu.with_memory_space_constraint(value, pltpu.HBM)

    lane_group = CAP * block_rows
    post = layers * lane_group
    wide = CAP * rows
    sizes = (layers, owners, per_owner, block_count, slot_count, block_rows, tile_width)
    weighted, kept, to_x, to_y = pl.pallas_call(
        functools.partial(pack_kernel, sizes),
        out_shape=[
            shaped((rows, width), bf16)
            for width in (panel_width, post + wide, panel_width + post + wide, 2 * post + wide)
        ],
        in_specs=[anywhere] * 6,
        out_specs=[vmem] * 4,
        scratch_shapes=[
            pltpu.SMEM(tile_lists.shape, jnp.int32),
            pltpu.SMEM(tile_masks.shape, jnp.int32),
            pltpu.SMEM(tile_order.shape, jnp.int32),
            pltpu.VMEM((1, rows), f32),
            pltpu.VMEM(panel_jac.shape, bf16),
            pltpu.VMEM(jac.shape, bf16),
            pltpu.SMEM(tile_order.shape, jnp.int32),
            pltpu.VMEM((block_count * slot_count * tile_width, block_rows), f32),
            pltpu.SemaphoreType.DMA((6,)),
        ],
        compiler_params=params,
        name="pack",
    )(*map(in_hbm, (tile_lists, tile_masks, tile_order, weights.reshape(1, rows), panel_jac, jac)))
    line = [shift(weighted, k, 0) for k in range(1, layers)]
    from_x, from_y = shift(to_x, 0, 1), shift(to_y, 0, 2)

    sizes = (layers, panel_width, lane_group, wide)
    others, column = pl.pallas_call(
        stack_kernel,
        out_shape=[shaped((height * rows, panel_width), bf16) for height in (layers - 1, layers)],
        in_specs=[vmem] * layers,
        out_specs=[vmem] * 2,
        compiler_params=params,
        cost_estimate=lasting(10**10),
        name="stack",
    )(weighted, *line)
    posts = pl.pallas_call(
        functools.partial(sort_kernel, sizes),
        out_shape=[shaped((rows + 16, owners * lane_group), bf16)] * layers,
        in_specs=[vmem] * 3,
        out_specs=[vmem] * layers,
        compiler_params=params,
        cost_estimate=lasting(10**10),
        name="sort",
    )(kept, from_x, from_y)
    posts = [posts[0]] + [shift(posts[k], k, 0) for k in range(1, layers)]
    by_x, by_y = shift(others, 0, 1), shift(column, 0, 2)

    rows_to_y = pl.pallas_call(
        rows_to_y_kernel,
        out_shape=shaped(column.shape, bf16),
        in_specs=[vmem] * 2,
        out_specs=vmem,
        compiler_params=params,
        name="rows_to_y",
    )(from_x, by_x)
    across_y = shift(rows_to_y, 0, 2)
    columns_to_x = pl.pallas_call(
        functools.partial(columns_to_x_kernel, (layers, lane_group, wide)),
        out_shape=shaped((rows // 2 + 16, panel_width), bf16),
        in_specs=[vmem] * layers + [anywhere],
        out_specs=vmem,
        compiler_params=params,
        cost_estimate=lasting(3 * 10**9),
        name="columns_to_x",
    )(*posts, by_y)
    across_x = shift(columns_to_x, 0, 1)

    count = per_owner * slab_width
    depth = layers * rows
    sizes = (layers, owners, per_owner, block_count, block_rows)
    result = shaped((count, panel_width), f32)
    panels = [column, from_x, by_x, by_y]
    own, other, turned = pl.pallas_call(
        functools.partial(near_kernel, sizes, 2),
        out_shape=[result, shaped((count, panel_width), bf16), shaped((2, *factor_inverse.shape), bf16)],
        in_specs=[anywhere] * 2 + [vmem] * (len(panels) + layers) + [anywhere],
        out_specs=[vmem] * 3,
        scratch_shapes=[
            pltpu.VMEM((count, (owners - 1) * depth), bf16),
            pltpu.VMEM(((owners - 1) * depth, panel_width), bf16),
            pltpu.VMEM(factor_inverse.shape, f32),
            pltpu.SemaphoreType.DMA,
        ],
        compiler_params=params,
        cost_estimate=lasting(10**9),
        name="near",
    )(rows_to_y, columns_to_x, *panels, *posts, in_hbm(factor_inverse))
    other = shift(other, 0, 0, 1)
    joined = pl.pallas_call(
        join_kernel,
        out_shape=shaped((across_y.shape[0] + across_x.shape[0], panel_width), bf16),
        in_specs=[vmem] * 2,
        out_specs=vmem,
        compiler_params=params,
        cost_estimate=lasting(10**10),
        name="join",
    )(across_y, across_x)
    other_joined = shift(joined, 0, 0, 1)
    far_scratch = [pltpu.VMEM((count, depth), bf16)] + [pltpu.VMEM((depth, panel_width), bf16)] * 2
    middle = pl.pallas_call(
        functools.partial(middle_kernel, sizes),
        out_shape=result,
        in_specs=[vmem] * 4,
        out_specs=vmem,
        scratch_shapes=far_scratch,
        compiler_params=params,
        name="middle",
    )(own, other, joined, turned)
    out = pl.pallas_call(
        functools.partial(final_kernel, sizes),
        out_shape=result,
        in_specs=[vmem] * 3,
        out_specs=anywhere,
        scratch_shapes=[pltpu.VMEM((count, panel_width), f32)] + far_scratch + [pltpu.SemaphoreType.DMA((4,))],
        compiler_params=params,
        name="final",
    )(middle, other_joined, turned)
    return out.reshape(per_owner, slab_width, panel_width)


def solution(mesh):
    in_specs = (
        P(("rows", "cols"), None),
        P(("rows", "cols"), None),
        P(("rows", "cols")),
        P(("rows", "cols"), None),
        P(("rows", "cols"), None),
        P(),
        P(),
    )
    out_specs = P("cols", "rows", None)
    body = local if (mesh.shape["rows"], mesh.shape["cols"]) == (8, 4) else local_general
    return jax.shard_map(body, mesh=mesh, in_specs=in_specs, out_specs=out_specs, check_vma=False)
```

```python
import functools

import jax
import jax.numpy as jnp
from jax import lax
from jax.experimental import pallas as pl
from jax.experimental.pallas import tpu as pltpu
from jax.sharding import PartitionSpec as P

CAP = 2
GATHERED = 1 << 22


def tile_positions(tile_lists, tile_order):
    tile_count = tile_order.shape[0]
    matches = tile_lists[:, :, None] == tile_order[None, None, :]
    return jnp.sum(jnp.where(matches, jnp.arange(tile_count, dtype=jnp.int32), 0), axis=2)


def apply_inverse(tiles, factor_inverse):
    return jnp.einsum("ntp,qp->ntq", tiles, factor_inverse, precision=lax.Precision.HIGHEST)


def slot_codes(tile_lists, tile_masks, tile_order, owner_ids):
    block_count, slot_count = tile_lists.shape
    per_owner = tile_order.shape[0] // lax.axis_size("cols")
    positions = tile_positions(tile_lists, tile_order).reshape(-1)
    active = tile_masks.reshape(-1) == 1
    owner = positions // per_owner
    same = (owner[:, None] == owner[None, :]) & active[None, :]
    earlier = jnp.tril(jnp.ones(same.shape, bool), -1)
    rank = jnp.sum(same & earlier, axis=1)
    code = (
        (owner[None, None, :] == owner_ids[:, None, None])
        & (rank[None, None, :] == jnp.arange(CAP)[None, :, None])
        & active[None, None, :]
    )
    block = jnp.arange(block_count * slot_count) // slot_count
    place = positions % per_owner + per_owner * block
    return code, jnp.sum(jnp.where(code, place + 1, 0), axis=2) - 1


def local_general(jac, panel_jac, weights, tile_lists, tile_masks, tile_order, factor_inverse):
    block_count, slot_count = tile_lists.shape
    block_rows = jac.shape[0] // block_count
    tile_width = jac.shape[1] // slot_count
    slabs, owners = lax.axis_size("rows"), lax.axis_size("cols")
    devices = slabs * owners
    per_owner = tile_order.shape[0] // owners
    slab_width = tile_width // slabs
    bf16 = jnp.bfloat16
    weighted = (weights[:, None] * panel_jac).astype(bf16)
    code, places = slot_codes(tile_lists, tile_masks, tile_order, jnp.arange(owners))
    columns = jac.reshape(block_count, block_rows, slot_count, slabs, slab_width)
    chosen = code.astype(bf16).reshape(owners, CAP, block_count, slot_count)
    pieces = jnp.einsum("cjbk,bmkrt->rcjmt", chosen, columns, preferred_element_type=jnp.float32).astype(bf16)
    pieces = pieces.reshape(devices, -1)
    note = jnp.broadcast_to(places.astype(bf16)[None], (slabs, owners, CAP)).reshape(devices, CAP)
    note = jnp.pad(note, ((0, 0), (0, 128 - CAP)))
    sent = jnp.concatenate([pieces, note], axis=1)
    got = lax.all_to_all(sent, ("rows", "cols"), split_axis=0, concat_axis=0, tiled=True)
    size = pieces.shape[1]
    data = got[:, :size].reshape(devices, CAP, block_rows, slab_width)
    where = got[:, size : size + CAP].astype(jnp.int32)
    hot = (where[:, :, None] == jnp.arange(block_count * per_owner)).astype(bf16)
    hot = hot.reshape(devices, CAP, block_count, per_owner)
    mixed = jnp.einsum("djbn,djmt->dbmnt", hot, data, preferred_element_type=jnp.float32).astype(bf16)
    strips = max(1, devices * weighted.size * 2 // GATHERED)

    def strip_gram(strip):
        panels = lax.all_gather(strip, ("rows", "cols"), axis=0, tiled=True)
        panels = panels.reshape(devices, block_count, block_rows, -1)
        return jnp.einsum("dbmnt,dbmp->ntp", mixed, panels, preferred_element_type=jnp.float32)

    if strips == 1:
        gram = strip_gram(weighted)
    else:
        narrow = weighted.reshape(weighted.shape[0], strips, -1).swapaxes(0, 1)
        gram = jnp.moveaxis(lax.map(strip_gram, narrow), 0, 2)
        gram = gram.reshape(per_owner, slab_width, -1)
    return apply_inverse(gram, factor_inverse)


def shift(value, steps_z, flip_cols, flip_core=0):
    slabs, owners = lax.axis_size("rows"), lax.axis_size("cols")
    pairs = []
    for r in range(slabs):
        to_r = ((r // 2 + steps_z) % (slabs // 2)) * 2 + ((r % 2) ^ flip_core)
        for c in range(owners):
            pairs.append((r * owners + c, to_r * owners + (c ^ flip_cols)))
    return lax.ppermute(value, ("rows", "cols"), pairs)


def lasting(flops):
    return pl.CostEstimate(flops=flops, bytes_accessed=0, transcendentals=0)


def pack_kernel(sizes, lists_hbm, masks_hbm, order_hbm, weights_hbm, panel_hbm, jac_hbm, *refs):
    layers, owners, per_owner, block_count, slot_count, block_rows, tile_width = sizes
    weighted_ref, kept_ref, to_x_ref, to_y_ref = refs[:4]
    lists_ref, masks_ref, order_ref, weights_ref, panel_ref, jac_ref, places_ref, turned_ref, sems = refs[4:]
    copies = [
        pltpu.make_async_copy(order_hbm, order_ref, sems.at[0]),
        pltpu.make_async_copy(lists_hbm, lists_ref, sems.at[1]),
        pltpu.make_async_copy(masks_hbm, masks_ref, sems.at[2]),
        pltpu.make_async_copy(weights_hbm, weights_ref, sems.at[3]),
        pltpu.make_async_copy(panel_hbm, panel_ref, sems.at[4]),
        pltpu.make_async_copy(jac_hbm, jac_ref, sems.at[5]),
    ]
    for copy in copies:
        copy.start()
    f32, bf16 = jnp.float32, jnp.bfloat16
    rows, width = panel_ref.shape
    lane_group = CAP * block_rows
    post = layers * lane_group
    slab = tile_width // layers
    part = slab // 2
    me_r, me_c = lax.axis_index("rows"), lax.axis_index("cols")
    me_z, me_core = me_r // 2, lax.rem(me_r, 2)
    for copy in copies:
        copy.wait()

    row_ids = lax.broadcasted_iota(jnp.int32, (rows, rows), 0)
    lane_ids = lax.broadcasted_iota(jnp.int32, (rows, rows), 1)
    column = jnp.sum(jnp.where(row_ids == lane_ids, weights_ref[...], 0.0), axis=1, keepdims=True)
    weighted = (column * panel_ref[...].astype(f32)).astype(bf16)
    weighted_ref[...] = weighted
    to_x_ref[:, :width] = weighted

    for b in range(block_count):
        block = jac_ref[b * block_rows : (b + 1) * block_rows, :].astype(f32)
        start = b * slot_count * tile_width
        turned_ref[start : start + slot_count * tile_width, :] = block.T

    for i in range(order_ref.shape[0]):
        places_ref[order_ref[i]] = i
    slots = []
    for s in range(block_count * slot_count):
        b, k = divmod(s, slot_count)
        place = places_ref[lists_ref[b, k]]
        owner = jnp.int32(0)
        for c in range(1, owners):
            owner += (place >= c * per_owner).astype(jnp.int32)
        slots.append((place - owner * per_owner, jnp.where(masks_ref[b, k] == 1, owner, -1)))

    shape = (16, CAP * block_count * block_rows)
    lane, row = lax.broadcasted_iota(jnp.int32, shape, 1), lax.broadcasted_iota(jnp.int32, shape, 0)
    notes = []
    spots = [(kept_ref, 0), (to_x_ref, width), (to_y_ref, 0), (to_y_ref, post)]
    for e, (parcel, start) in enumerate(spots):
        wanted = me_c ^ e
        found = jnp.int32(0)
        chosen = [jnp.int32(0)] * CAP
        codes = [jnp.int32(-1)] * CAP
        for s, (place, owner) in enumerate(slots):
            hit = owner == wanted
            for j in range(CAP):
                take = hit & (found == j)
                chosen[j] = jnp.where(take, s, chosen[j])
                codes[j] = jnp.where(take, place, codes[j])
            found += hit.astype(jnp.int32)
        note = jnp.full(shape, -1, jnp.int32)
        for j in range(CAP):
            for b in range(block_count):
                at = (j * block_count + b) * block_rows
                here = (lane >= at) & (lane < at + block_rows)
                code = jnp.where(chosen[j] // slot_count == b, codes[j], -1)
                note = jnp.where(here, code, note)
        notes.append(note)
        for k in range(layers):
            z = lax.rem(me_z + k, layers)
            for u in range(2):
                core = me_core ^ u
                for j in range(CAP):
                    first = pl.multiple_of(chosen[j] * tile_width + z * slab + core * part, part)
                    piece = turned_ref[pl.ds(first, part), :].astype(bf16)
                    to = start + k * lane_group + j * block_rows
                    parcel[u * part : (u + 1) * part, to : to + block_rows] = piece
    kept_ref[:16, post:] = notes[0].astype(f32).astype(bf16)
    to_x_ref[:16, width + post :] = notes[1].astype(f32).astype(bf16)
    to_y_ref[:16, 2 * post :] = jnp.where(row == 0, notes[2], notes[3]).astype(f32).astype(bf16)


def row_of(block, i):
    ids = lax.broadcasted_iota(jnp.int32, block.shape, 0)
    return jnp.sum(jnp.where(ids == i, block.astype(jnp.float32), 0.0), axis=0, keepdims=True)


def rows_from(notes):
    ids = lax.broadcasted_iota(jnp.int32, (16, notes[0].shape[1]), 0)
    block = jnp.full(ids.shape, -1.0, jnp.float32)
    for i, note in enumerate(notes):
        block = jnp.where(ids == i, note, block)
    return block.astype(jnp.bfloat16)


def stack_kernel(*refs):
    inputs, (rest_ref, all_ref) = refs[:-2], refs[-2:]
    rows = inputs[0].shape[0]
    for i, ref in enumerate(reversed(inputs)):
        all_ref[i * rows : (i + 1) * rows, :] = ref[...]
        if i:
            rest_ref[(i - 1) * rows : i * rows, :] = ref[...]


def sort_kernel(sizes, kept_ref, from_x_ref, from_y_ref, *posts):
    layers, width, lane_group, wide = sizes
    post = layers * lane_group
    rows = kept_ref.shape[0]
    spots = [(kept_ref, 0), (from_x_ref, width), (from_y_ref, 0), (from_y_ref, post)]
    notes = [row_of(ref[:16, ref.shape[1] - wide :], int(e == 3)) for e, (ref, start) in enumerate(spots)]
    block = rows_from(notes)
    for k, out in enumerate(posts):
        for e, (ref, start) in enumerate(spots):
            piece = ref[:, start + k * lane_group : start + (k + 1) * lane_group]
            out[:rows, e * lane_group : (e + 1) * lane_group] = piece
        out[rows:, :wide] = block


def rows_to_y_kernel(from_x_ref, by_x_ref, out_ref):
    rows = from_x_ref.shape[0]
    out_ref[:rows, :] = from_x_ref[:, : out_ref.shape[1]]
    out_ref[rows:, :] = by_x_ref[...]


def columns_to_x_kernel(sizes, *refs):
    layers, lane_group, wide = sizes
    posts, out_ref = refs[:layers], refs[-1]
    rows = posts[0].shape[0] - 16
    part = rows // 2
    for k, ref in enumerate(posts):
        for u in range(2):
            piece = ref[u * part : (u + 1) * part, 3 * lane_group : 4 * lane_group]
            at = (u * layers + k) * lane_group
            out_ref[:part, at : at + lane_group] = piece
    out_ref[part:, :wide] = rows_from([row_of(ref[rows:, :wide], 3) for ref in posts])


def place(out_ref, lanes, per_owner, pieces, notes, sizes):
    block_count, block_rows = sizes
    f32, bf16 = jnp.float32, jnp.bfloat16
    part, rows = pieces[0].shape[0], block_count * block_rows
    columns, codes = [], []
    for j in range(CAP):
        parts = []
        for piece in pieces:
            parts += [piece[:, j * block_rows : (j + 1) * block_rows].astype(f32)] * block_count
        columns.append(jnp.concatenate(parts, axis=1).astype(bf16))
        note = jnp.concatenate([note[:, j * rows : (j + 1) * rows] for note in notes], axis=1)
        codes.append(jnp.broadcast_to(note, columns[j].shape).astype(bf16))
    for n in range(per_owner):
        placed = jnp.zeros(columns[0].shape, bf16)
        for j in range(CAP):
            placed = jnp.where(codes[j] == jnp.asarray(n, bf16), columns[j], placed)
        out_ref[n * part : (n + 1) * part, lanes] = placed


def inverse_rows(rows_ref, factor_ref, high_ref, low_ref):
    f32, bf16 = jnp.float32, jnp.bfloat16
    height, width = high_ref.shape
    for start, stop in ((0, width // 2), (width // 2, width)):
        rows = rows_ref[:height, :stop]
        total = jnp.dot(rows, factor_ref[0, :stop, start:stop], preferred_element_type=f32)
        total += jnp.dot(rows, factor_ref[1, :stop, start:stop], preferred_element_type=f32)
        high = total.astype(bf16)
        high_ref[:, start:stop] = high
        low_ref[:, start:stop] = (total - high.astype(f32)).astype(bf16)


def turn_kernel(factor_hbm, out_ref, factor_ref, sem):
    copy = pltpu.make_async_copy(factor_hbm, factor_ref, sem)
    copy.start()
    copy.wait()
    turned = factor_ref[...].T
    high = turned.astype(jnp.bfloat16)
    out_ref[0, :, :] = high
    out_ref[1, :, :] = (turned - high.astype(jnp.float32)).astype(jnp.bfloat16)


def near_kernel(sizes, earlier, *refs):
    layers, owners, per_owner, block_count, block_rows = sizes
    panels, posts, refs = refs[earlier : earlier + 4], refs[earlier + 4 : earlier + 4 + layers], refs[earlier + 4 + layers :]
    own_ref, other_ref, placed_ref, rows_ref = refs
    f32, bf16 = jnp.float32, jnp.bfloat16
    rows = block_count * block_rows
    group, wide = CAP * block_rows, CAP * rows
    part = rows // 2
    width = rows_ref.shape[1]
    at = 0
    for panel in panels:
        rows_ref[at : at + panel.shape[0], :] = panel[:, :width]
        at += panel.shape[0]
    for u, out_ref in ((1, other_ref), (0, own_ref)):
        for e in range(owners - 1):
            for h in range(layers // 2):
                pair = posts[2 * h : 2 * h + 2]
                pieces = [post[u * part : (u + 1) * part, e * group : (e + 1) * group] for post in pair]
                notes = [row_of(post[rows:, :wide], e) for post in pair]
                start = (e * layers + 2 * h) * rows
                place(placed_ref, slice(start, start + 2 * rows), per_owner, pieces, notes, (block_count, block_rows))
        gram = jnp.dot(placed_ref[...], rows_ref[...], preferred_element_type=f32)
        out_ref[...] = gram.astype(out_ref.dtype)


def join_kernel(above_ref, below_ref, out_ref):
    rows = above_ref.shape[0]
    out_ref[:rows, :] = above_ref[...]
    out_ref[rows:, :] = below_ref[...]


def place_far(sizes, u, ref, placed_ref):
    layers, owners, per_owner, block_count, block_rows = sizes
    rows = block_count * block_rows
    group, wide = CAP * block_rows, CAP * rows
    part, depth = rows // 2, layers * rows
    for h in range(layers // 2):
        pieces, notes = [], []
        for k in (2 * h, 2 * h + 1):
            at = (u * layers + k) * group
            pieces.append(ref[depth : depth + part, at : at + group])
            notes.append(row_of(ref[depth + part :, :wide], k))
        lanes = slice(2 * h * rows, 2 * (h + 1) * rows)
        place(placed_ref, lanes, per_owner, pieces, notes, (block_count, block_rows))


def far_kernel(sizes, joined_ref, turned_ref, out_ref, placed_ref, high_ref, low_ref):
    place_far(sizes, 0, joined_ref, placed_ref)
    inverse_rows(joined_ref, turned_ref, high_ref, low_ref)
    placed = placed_ref[...]
    total = jnp.dot(placed, high_ref[...], preferred_element_type=jnp.float32)
    out_ref[...] = total + jnp.dot(placed, low_ref[...], preferred_element_type=jnp.float32)


def middle_kernel(far_ref, own_ref, other_ref, turned_ref, out_ref):
    f32, bf16 = jnp.float32, jnp.bfloat16
    width = own_ref.shape[1]
    gram = own_ref[...] + other_ref[...].astype(f32)
    high = gram.astype(bf16)
    low = (gram - high.astype(f32)).astype(bf16)
    for start, stop in ((0, width // 2), (width // 2, width)):
        a, b = turned_ref[0, :stop, start:stop], turned_ref[1, :stop, start:stop]
        total = far_ref[:, start:stop] + jnp.dot(high[:, :stop], a, preferred_element_type=f32)
        total += jnp.dot(high[:, :stop], b, preferred_element_type=f32)
        out_ref[:, start:stop] = total + jnp.dot(low[:, :stop], a, preferred_element_type=f32)


def final_kernel(sizes, middle_ref, joined_ref, turned_ref, out_hbm, sum_ref, placed_ref, high_ref, low_ref, sems):
    f32 = jnp.float32
    place_far(sizes, 1, joined_ref, placed_ref)
    inverse_rows(joined_ref, turned_ref, high_ref, low_ref)
    strips = sems.shape[0]
    height = sum_ref.shape[0] // strips
    copies = []
    for i in range(strips):
        here = pl.ds(i * height, height)
        placed = placed_ref[here, :]
        total = middle_ref[here, :] + jnp.dot(placed, high_ref[...], preferred_element_type=f32)
        sum_ref[here, :] = total + jnp.dot(placed, low_ref[...], preferred_element_type=f32)
        copies.append(pltpu.make_async_copy(sum_ref.at[here, :], out_hbm.at[here, :], sems.at[i]))
        copies[-1].start()
    for copy in copies:
        copy.wait()


def local(jac, panel_jac, weights, tile_lists, tile_masks, tile_order, factor_inverse):
    block_count, slot_count = tile_lists.shape
    rows, panel_width = panel_jac.shape
    block_rows = rows // block_count
    tile_width = jac.shape[1] // slot_count
    slabs, owners = lax.axis_size("rows"), lax.axis_size("cols")
    layers = slabs // 2
    per_owner = tile_order.shape[0] // owners
    slab_width = tile_width // slabs
    f32, bf16 = jnp.float32, jnp.bfloat16
    vmem, anywhere = pl.BlockSpec(memory_space=pltpu.VMEM), pl.BlockSpec(memory_space=pl.ANY)
    params = pltpu.CompilerParams(vmem_limit_bytes=24 << 20)
    shaped = jax.ShapeDtypeStruct

    def in_hbm(value):
        return pltpu.with_memory_space_constraint(value, pltpu.HBM)

    lane_group = CAP * block_rows
    post = layers * lane_group
    wide = CAP * rows
    sizes = (layers, owners, per_owner, block_count, slot_count, block_rows, tile_width)
    weighted, kept, to_x, to_y = pl.pallas_call(
        functools.partial(pack_kernel, sizes),
        out_shape=[
            shaped((rows, width), bf16)
            for width in (panel_width, post + wide, panel_width + post + wide, 2 * post + wide)
        ],
        in_specs=[anywhere] * 6,
        out_specs=[vmem] * 4,
        scratch_shapes=[
            pltpu.SMEM(tile_lists.shape, jnp.int32),
            pltpu.SMEM(tile_masks.shape, jnp.int32),
            pltpu.SMEM(tile_order.shape, jnp.int32),
            pltpu.VMEM((1, rows), f32),
            pltpu.VMEM(panel_jac.shape, bf16),
            pltpu.VMEM(jac.shape, bf16),
            pltpu.SMEM(tile_order.shape, jnp.int32),
            pltpu.VMEM((block_count * slot_count * tile_width, block_rows), f32),
            pltpu.SemaphoreType.DMA((6,)),
        ],
        compiler_params=params,
        name="pack",
    )(*map(in_hbm, (tile_lists, tile_masks, tile_order, weights.reshape(1, rows), panel_jac, jac)))
    line = [shift(weighted, k, 0) for k in range(1, layers)]
    from_x, from_y = shift(to_x, 0, 1), shift(to_y, 0, 2)

    sizes = (layers, panel_width, lane_group, wide)
    others, column = pl.pallas_call(
        stack_kernel,
        out_shape=[shaped((height * rows, panel_width), bf16) for height in (layers - 1, layers)],
        in_specs=[vmem] * layers,
        out_specs=[vmem] * 2,
        compiler_params=params,
        cost_estimate=lasting(10**10),
        name="stack",
    )(*reversed(line), weighted)
    posts = pl.pallas_call(
        functools.partial(sort_kernel, sizes),
        out_shape=[shaped((rows + 16, owners * lane_group), bf16)] * layers,
        in_specs=[vmem] * 3,
        out_specs=[vmem] * layers,
        compiler_params=params,
        cost_estimate=lasting(10**10),
        name="sort",
    )(kept, from_x, from_y)
    posts = [posts[0]] + [shift(posts[k], k, 0) for k in range(1, layers)]
    by_x, by_y = shift(others, 0, 1), shift(column, 0, 2)

    rows_to_y = pl.pallas_call(
        rows_to_y_kernel,
        out_shape=shaped(column.shape, bf16),
        in_specs=[vmem] * 2,
        out_specs=vmem,
        compiler_params=params,
        name="rows_to_y",
    )(from_x, by_x)
    across_y = shift(rows_to_y, 0, 2)
    turned = pl.pallas_call(
        turn_kernel,
        out_shape=shaped((2, *factor_inverse.shape), bf16),
        in_specs=[anywhere],
        out_specs=vmem,
        scratch_shapes=[pltpu.VMEM(factor_inverse.shape, f32), pltpu.SemaphoreType.DMA],
        compiler_params=params,
        name="turn",
    )(in_hbm(factor_inverse))
    columns_to_x = pl.pallas_call(
        functools.partial(columns_to_x_kernel, (layers, lane_group, wide)),
        out_shape=shaped((rows // 2 + 16, panel_width), bf16),
        in_specs=[vmem] * layers + [anywhere] * 2,
        out_specs=vmem,
        compiler_params=params,
        cost_estimate=lasting(3 * 10**9),
        name="columns_to_x",
    )(*posts, by_y, turned)
    across_x = shift(columns_to_x, 0, 1)

    count = per_owner * slab_width
    depth = layers * rows
    sizes = (layers, owners, per_owner, block_count, block_rows)
    result = shaped((count, panel_width), f32)
    panels = [column, from_x, by_x, by_y]
    own, other = pl.pallas_call(
        functools.partial(near_kernel, sizes, 2),
        out_shape=[result, shaped((count, panel_width), bf16)],
        in_specs=[anywhere] * 2 + [vmem] * (len(panels) + layers),
        out_specs=[vmem] * 2,
        scratch_shapes=[
            pltpu.VMEM((count, (owners - 1) * depth), bf16),
            pltpu.VMEM(((owners - 1) * depth, panel_width), bf16),
        ],
        compiler_params=params,
        cost_estimate=lasting(10**9),
        name="near",
    )(rows_to_y, columns_to_x, *panels, *posts)
    other = shift(other, 0, 0, 1)
    joined = pl.pallas_call(
        join_kernel,
        out_shape=shaped((across_y.shape[0] + across_x.shape[0], panel_width), bf16),
        in_specs=[vmem] * 2,
        out_specs=vmem,
        compiler_params=params,
        cost_estimate=lasting(10**10),
        name="join",
    )(across_y, across_x)
    other_joined = shift(joined, 0, 0, 1)
    far_scratch = [pltpu.VMEM((count, depth), bf16)] + [pltpu.VMEM((depth, panel_width), bf16)] * 2
    far = pl.pallas_call(
        functools.partial(far_kernel, sizes),
        out_shape=result,
        in_specs=[vmem] * 2,
        out_specs=vmem,
        scratch_shapes=far_scratch,
        compiler_params=params,
        name="far",
    )(joined, turned)
    middle = pl.pallas_call(
        middle_kernel,
        out_shape=result,
        in_specs=[vmem] * 4,
        out_specs=vmem,
        compiler_params=params,
        name="middle",
    )(far, own, other, turned)
    out = pl.pallas_call(
        functools.partial(final_kernel, sizes),
        out_shape=result,
        in_specs=[vmem] * 3,
        out_specs=anywhere,
        scratch_shapes=[pltpu.VMEM((count, panel_width), f32)] + far_scratch + [pltpu.SemaphoreType.DMA((4,))],
        compiler_params=params,
        name="final",
    )(middle, other_joined, turned)
    return out.reshape(per_owner, slab_width, panel_width)


def solution(mesh):
    in_specs = (
        P(("rows", "cols"), None),
        P(("rows", "cols"), None),
        P(("rows", "cols")),
        P(("rows", "cols"), None),
        P(("rows", "cols"), None),
        P(),
        P(),
    )
    out_specs = P("cols", "rows", None)
    body = local if (mesh.shape["rows"], mesh.shape["cols"]) == (8, 4) else local_general
    return jax.shard_map(body, mesh=mesh, in_specs=in_specs, out_specs=out_specs, check_vma=False)
```

```python
import functools

import jax
import jax.numpy as jnp
from jax import lax
from jax.experimental import pallas as pl
from jax.experimental.pallas import tpu as pltpu
from jax.sharding import PartitionSpec as P

CAP = 2
GATHERED = 1 << 22


def tile_positions(tile_lists, tile_order):
    tile_count = tile_order.shape[0]
    matches = tile_lists[:, :, None] == tile_order[None, None, :]
    return jnp.sum(jnp.where(matches, jnp.arange(tile_count, dtype=jnp.int32), 0), axis=2)


def apply_inverse(tiles, factor_inverse):
    return jnp.einsum("ntp,qp->ntq", tiles, factor_inverse, precision=lax.Precision.HIGHEST)


def slot_codes(tile_lists, tile_masks, tile_order, owner_ids):
    block_count, slot_count = tile_lists.shape
    per_owner = tile_order.shape[0] // lax.axis_size("cols")
    positions = tile_positions(tile_lists, tile_order).reshape(-1)
    active = tile_masks.reshape(-1) == 1
    owner = positions // per_owner
    same = (owner[:, None] == owner[None, :]) & active[None, :]
    earlier = jnp.tril(jnp.ones(same.shape, bool), -1)
    rank = jnp.sum(same & earlier, axis=1)
    code = (
        (owner[None, None, :] == owner_ids[:, None, None])
        & (rank[None, None, :] == jnp.arange(CAP)[None, :, None])
        & active[None, None, :]
    )
    block = jnp.arange(block_count * slot_count) // slot_count
    place = positions % per_owner + per_owner * block
    return code, jnp.sum(jnp.where(code, place + 1, 0), axis=2) - 1


def local_general(jac, panel_jac, weights, tile_lists, tile_masks, tile_order, factor_inverse):
    block_count, slot_count = tile_lists.shape
    block_rows = jac.shape[0] // block_count
    tile_width = jac.shape[1] // slot_count
    slabs, owners = lax.axis_size("rows"), lax.axis_size("cols")
    devices = slabs * owners
    per_owner = tile_order.shape[0] // owners
    slab_width = tile_width // slabs
    bf16 = jnp.bfloat16
    weighted = (weights[:, None] * panel_jac).astype(bf16)
    code, places = slot_codes(tile_lists, tile_masks, tile_order, jnp.arange(owners))
    columns = jac.reshape(block_count, block_rows, slot_count, slabs, slab_width)
    chosen = code.astype(bf16).reshape(owners, CAP, block_count, slot_count)
    pieces = jnp.einsum("cjbk,bmkrt->rcjmt", chosen, columns, preferred_element_type=jnp.float32).astype(bf16)
    pieces = pieces.reshape(devices, -1)
    note = jnp.broadcast_to(places.astype(bf16)[None], (slabs, owners, CAP)).reshape(devices, CAP)
    note = jnp.pad(note, ((0, 0), (0, 128 - CAP)))
    sent = jnp.concatenate([pieces, note], axis=1)
    got = lax.all_to_all(sent, ("rows", "cols"), split_axis=0, concat_axis=0, tiled=True)
    size = pieces.shape[1]
    data = got[:, :size].reshape(devices, CAP, block_rows, slab_width)
    where = got[:, size : size + CAP].astype(jnp.int32)
    hot = (where[:, :, None] == jnp.arange(block_count * per_owner)).astype(bf16)
    hot = hot.reshape(devices, CAP, block_count, per_owner)
    mixed = jnp.einsum("djbn,djmt->dbmnt", hot, data, preferred_element_type=jnp.float32).astype(bf16)
    strips = max(1, devices * weighted.size * 2 // GATHERED)

    def strip_gram(strip):
        panels = lax.all_gather(strip, ("rows", "cols"), axis=0, tiled=True)
        panels = panels.reshape(devices, block_count, block_rows, -1)
        return jnp.einsum("dbmnt,dbmp->ntp", mixed, panels, preferred_element_type=jnp.float32)

    if strips == 1:
        gram = strip_gram(weighted)
    else:
        narrow = weighted.reshape(weighted.shape[0], strips, -1).swapaxes(0, 1)
        gram = jnp.moveaxis(lax.map(strip_gram, narrow), 0, 2)
        gram = gram.reshape(per_owner, slab_width, -1)
    return apply_inverse(gram, factor_inverse)


def shift(value, steps_z, flip_cols, flip_core=0):
    slabs, owners = lax.axis_size("rows"), lax.axis_size("cols")
    pairs = []
    for r in range(slabs):
        to_r = ((r // 2 + steps_z) % (slabs // 2)) * 2 + ((r % 2) ^ flip_core)
        for c in range(owners):
            pairs.append((r * owners + c, to_r * owners + (c ^ flip_cols)))
    return lax.ppermute(value, ("rows", "cols"), pairs)


def lasting(flops):
    return pl.CostEstimate(flops=flops, bytes_accessed=0, transcendentals=0)


def pack_kernel(sizes, lists_hbm, masks_hbm, order_hbm, weights_hbm, panel_hbm, jac_hbm, factor_hbm, *refs):
    layers, owners, per_owner, block_count, slot_count, block_rows, tile_width = sizes
    weighted_ref, kept_ref, to_x_ref, to_y_ref, factor_ref = refs[:5]
    lists_ref, masks_ref, order_ref, weights_ref, panel_ref, jac_ref, places_ref, turned_ref, sems = refs[5:]
    copies = [
        pltpu.make_async_copy(order_hbm, order_ref, sems.at[0]),
        pltpu.make_async_copy(lists_hbm, lists_ref, sems.at[1]),
        pltpu.make_async_copy(masks_hbm, masks_ref, sems.at[2]),
        pltpu.make_async_copy(weights_hbm, weights_ref, sems.at[3]),
        pltpu.make_async_copy(panel_hbm, panel_ref, sems.at[4]),
        pltpu.make_async_copy(jac_hbm, jac_ref, sems.at[5]),
    ]
    for copy in copies:
        copy.start()
    factor_copy = pltpu.make_async_copy(factor_hbm, factor_ref, sems.at[6])
    factor_copy.start()
    f32, bf16 = jnp.float32, jnp.bfloat16
    rows, width = panel_ref.shape
    lane_group = CAP * block_rows
    post = layers * lane_group
    slab = tile_width // layers
    part = slab // 2
    me_r, me_c = lax.axis_index("rows"), lax.axis_index("cols")
    me_z, me_core = me_r // 2, lax.rem(me_r, 2)
    for copy in copies:
        copy.wait()

    row_ids = lax.broadcasted_iota(jnp.int32, (rows, rows), 0)
    lane_ids = lax.broadcasted_iota(jnp.int32, (rows, rows), 1)
    column = jnp.sum(jnp.where(row_ids == lane_ids, weights_ref[...], 0.0), axis=1, keepdims=True)
    weighted = (column * panel_ref[...].astype(f32)).astype(bf16)
    weighted_ref[...] = weighted

    for b in range(block_count):
        block = jac_ref[b * block_rows : (b + 1) * block_rows, :].astype(f32)
        start = b * slot_count * tile_width
        turned_ref[start : start + slot_count * tile_width, :] = block.T

    for i in range(order_ref.shape[0]):
        places_ref[order_ref[i]] = i
    slots = []
    for s in range(block_count * slot_count):
        b, k = divmod(s, slot_count)
        place = places_ref[lists_ref[b, k]]
        owner = jnp.int32(0)
        for c in range(1, owners):
            owner += (place >= c * per_owner).astype(jnp.int32)
        slots.append((place - owner * per_owner, jnp.where(masks_ref[b, k] == 1, owner, -1)))

    shape = (16, CAP * block_count * block_rows)
    lane, row = lax.broadcasted_iota(jnp.int32, shape, 1), lax.broadcasted_iota(jnp.int32, shape, 0)
    notes = []
    spots = [(kept_ref, 0), (to_x_ref, 0), (to_y_ref, 0), (to_y_ref, post)]
    for e, (parcel, start) in enumerate(spots):
        wanted = me_c ^ e
        found = jnp.int32(0)
        chosen = [jnp.int32(0)] * CAP
        codes = [jnp.int32(-1)] * CAP
        for s, (place, owner) in enumerate(slots):
            hit = owner == wanted
            for j in range(CAP):
                take = hit & (found == j)
                chosen[j] = jnp.where(take, s, chosen[j])
                codes[j] = jnp.where(take, place, codes[j])
            found += hit.astype(jnp.int32)
        note = jnp.full(shape, -1, jnp.int32)
        for j in range(CAP):
            for b in range(block_count):
                at = (j * block_count + b) * block_rows
                here = (lane >= at) & (lane < at + block_rows)
                code = jnp.where(chosen[j] // slot_count == b, codes[j], -1)
                note = jnp.where(here, code, note)
        notes.append(note)
        for k in range(layers):
            z = lax.rem(me_z + k, layers)
            for u in range(2):
                core = me_core ^ u
                for j in range(CAP):
                    first = pl.multiple_of(chosen[j] * tile_width + z * slab + core * part, part)
                    piece = turned_ref[pl.ds(first, part), :].astype(bf16)
                    to = start + k * lane_group + j * block_rows
                    parcel[u * part : (u + 1) * part, to : to + block_rows] = piece
    kept_ref[:16, post:] = notes[0].astype(f32).astype(bf16)
    to_x_ref[:16, post:] = notes[1].astype(f32).astype(bf16)
    to_y_ref[:16, 2 * post :] = jnp.where(row == 0, notes[2], notes[3]).astype(f32).astype(bf16)
    factor_copy.wait()


def row_of(block, i):
    ids = lax.broadcasted_iota(jnp.int32, block.shape, 0)
    return jnp.sum(jnp.where(ids == i, block.astype(jnp.float32), 0.0), axis=0, keepdims=True)


def rows_from(notes):
    ids = lax.broadcasted_iota(jnp.int32, (16, notes[0].shape[1]), 0)
    block = jnp.full(ids.shape, -1.0, jnp.float32)
    for i, note in enumerate(notes):
        block = jnp.where(ids == i, note, block)
    return block.astype(jnp.bfloat16)


def stack_kernel(*refs):
    inputs, out_ref = refs[:-1], refs[-1]
    rows = inputs[0].shape[0]
    for i, ref in enumerate(reversed(inputs)):
        out_ref[i * rows : (i + 1) * rows, :] = ref[...]


def sort_kernel(sizes, kept_ref, from_x_ref, from_y_ref, *posts):
    layers, width, lane_group, wide = sizes
    post = layers * lane_group
    rows = kept_ref.shape[0]
    spots = [(kept_ref, 0), (from_x_ref, 0), (from_y_ref, 0), (from_y_ref, post)]
    notes = [row_of(ref[:16, ref.shape[1] - wide :], int(e == 3)) for e, (ref, start) in enumerate(spots)]
    block = rows_from(notes)
    for k, out in enumerate(posts):
        for e, (ref, start) in enumerate(spots):
            piece = ref[:, start + k * lane_group : start + (k + 1) * lane_group]
            out[:rows, e * lane_group : (e + 1) * lane_group] = piece
        out[rows:, :wide] = block


def columns_to_x_kernel(sizes, *refs):
    layers, lane_group, wide = sizes
    posts, out_ref = refs[:layers], refs[-1]
    rows = posts[0].shape[0] - 16
    part = rows // 2
    for k, ref in enumerate(posts):
        for u in range(2):
            piece = ref[u * part : (u + 1) * part, 3 * lane_group : 4 * lane_group]
            at = (u * layers + k) * lane_group
            out_ref[:part, at : at + lane_group] = piece
    out_ref[part:, :wide] = rows_from([row_of(ref[rows:, :wide], 3) for ref in posts])


def place(out_ref, lanes, per_owner, pieces, notes, sizes):
    block_count, block_rows = sizes
    f32, bf16 = jnp.float32, jnp.bfloat16
    part, rows = pieces[0].shape[0], block_count * block_rows
    columns, codes = [], []
    for j in range(CAP):
        parts = []
        for piece in pieces:
            parts += [piece[:, j * block_rows : (j + 1) * block_rows].astype(f32)] * block_count
        columns.append(jnp.concatenate(parts, axis=1).astype(bf16))
        note = jnp.concatenate([note[:, j * rows : (j + 1) * rows] for note in notes], axis=1)
        codes.append(jnp.broadcast_to(note, columns[j].shape).astype(bf16))
    for n in range(per_owner):
        placed = jnp.zeros(columns[0].shape, bf16)
        for j in range(CAP):
            placed = jnp.where(codes[j] == jnp.asarray(n, bf16), columns[j], placed)
        out_ref[n * part : (n + 1) * part, lanes] = placed


def inverse_rows(rows_ref, factor_ref, high_ref, low_ref):
    f32, bf16 = jnp.float32, jnp.bfloat16
    height, width = high_ref.shape
    for start, stop in ((0, width // 2), (width // 2, width)):
        rows = rows_ref[:height, :stop]
        total = jnp.dot(rows, factor_ref[0, :stop, start:stop], preferred_element_type=f32)
        total += jnp.dot(rows, factor_ref[1, :stop, start:stop], preferred_element_type=f32)
        high = total.astype(bf16)
        high_ref[:, start:stop] = high
        low_ref[:, start:stop] = (total - high.astype(f32)).astype(bf16)


def turn_kernel(factor_ref, out_ref):
    turned = factor_ref[...].T
    high = turned.astype(jnp.bfloat16)
    out_ref[0, :, :] = high
    out_ref[1, :, :] = (turned - high.astype(jnp.float32)).astype(jnp.bfloat16)


def near_kernel(sizes, earlier, *refs):
    layers, owners, per_owner, block_count, block_rows = sizes
    panels, posts, refs = refs[earlier : earlier + 3], refs[earlier + 3 : earlier + 3 + layers], refs[earlier + 3 + layers :]
    own_ref, other_ref, placed_ref, rows_ref = refs
    f32, bf16 = jnp.float32, jnp.bfloat16
    rows = block_count * block_rows
    group, wide = CAP * block_rows, CAP * rows
    part = rows // 2
    width = rows_ref.shape[1]
    at = 0
    for panel in panels:
        rows_ref[at : at + panel.shape[0], :] = panel[:, :width]
        at += panel.shape[0]
    for u, out_ref in ((1, other_ref), (0, own_ref)):
        for e in range(owners - 1):
            for h in range(layers // 2):
                pair = posts[2 * h : 2 * h + 2]
                pieces = [post[u * part : (u + 1) * part, e * group : (e + 1) * group] for post in pair]
                notes = [row_of(post[rows:, :wide], e) for post in pair]
                start = (e * layers + 2 * h) * rows
                place(placed_ref, slice(start, start + 2 * rows), per_owner, pieces, notes, (block_count, block_rows))
        gram = jnp.dot(placed_ref[...], rows_ref[...], preferred_element_type=f32)
        out_ref[...] = gram.astype(out_ref.dtype)


def join_kernel(above_ref, below_ref, out_ref):
    rows = above_ref.shape[0]
    out_ref[:rows, :] = above_ref[...]
    out_ref[rows:, :] = below_ref[...]


def place_far(sizes, u, ref, placed_ref):
    layers, owners, per_owner, block_count, block_rows = sizes
    rows = block_count * block_rows
    group, wide = CAP * block_rows, CAP * rows
    part, depth = rows // 2, layers * rows
    for h in range(layers // 2):
        pieces, notes = [], []
        for k in (2 * h, 2 * h + 1):
            at = (u * layers + k) * group
            pieces.append(ref[depth : depth + part, at : at + group])
            notes.append(row_of(ref[depth + part :, :wide], k))
        lanes = slice(2 * h * rows, 2 * (h + 1) * rows)
        place(placed_ref, lanes, per_owner, pieces, notes, (block_count, block_rows))


def far_kernel(sizes, joined_ref, turned_ref, out_ref, placed_ref, high_ref, low_ref):
    place_far(sizes, 0, joined_ref, placed_ref)
    inverse_rows(joined_ref, turned_ref, high_ref, low_ref)
    placed = placed_ref[...]
    total = jnp.dot(placed, high_ref[...], preferred_element_type=jnp.float32)
    out_ref[...] = total + jnp.dot(placed, low_ref[...], preferred_element_type=jnp.float32)


def middle_kernel(far_ref, own_ref, other_ref, turned_ref, out_ref):
    f32, bf16 = jnp.float32, jnp.bfloat16
    width = own_ref.shape[1]
    gram = own_ref[...] + other_ref[...].astype(f32)
    high = gram.astype(bf16)
    low = (gram - high.astype(f32)).astype(bf16)
    for start, stop in ((0, width // 2), (width // 2, width)):
        a, b = turned_ref[0, :stop, start:stop], turned_ref[1, :stop, start:stop]
        total = far_ref[:, start:stop] + jnp.dot(high[:, :stop], a, preferred_element_type=f32)
        total += jnp.dot(high[:, :stop], b, preferred_element_type=f32)
        out_ref[:, start:stop] = total + jnp.dot(low[:, :stop], a, preferred_element_type=f32)


def final_kernel(sizes, middle_ref, joined_ref, turned_ref, out_hbm, sum_ref, placed_ref, high_ref, low_ref, sems):
    f32 = jnp.float32
    place_far(sizes, 1, joined_ref, placed_ref)
    inverse_rows(joined_ref, turned_ref, high_ref, low_ref)
    strips = sems.shape[0]
    height = sum_ref.shape[0] // strips
    copies = []
    for i in range(strips):
        here = pl.ds(i * height, height)
        placed = placed_ref[here, :]
        total = middle_ref[here, :] + jnp.dot(placed, high_ref[...], preferred_element_type=f32)
        sum_ref[here, :] = total + jnp.dot(placed, low_ref[...], preferred_element_type=f32)
        copies.append(pltpu.make_async_copy(sum_ref.at[here, :], out_hbm.at[here, :], sems.at[i]))
        copies[-1].start()
    for copy in copies:
        copy.wait()


def local(jac, panel_jac, weights, tile_lists, tile_masks, tile_order, factor_inverse):
    block_count, slot_count = tile_lists.shape
    rows, panel_width = panel_jac.shape
    block_rows = rows // block_count
    tile_width = jac.shape[1] // slot_count
    slabs, owners = lax.axis_size("rows"), lax.axis_size("cols")
    layers = slabs // 2
    per_owner = tile_order.shape[0] // owners
    slab_width = tile_width // slabs
    f32, bf16 = jnp.float32, jnp.bfloat16
    vmem, anywhere = pl.BlockSpec(memory_space=pltpu.VMEM), pl.BlockSpec(memory_space=pl.ANY)
    params = pltpu.CompilerParams(vmem_limit_bytes=24 << 20)
    shaped = jax.ShapeDtypeStruct

    def in_hbm(value):
        return pltpu.with_memory_space_constraint(value, pltpu.HBM)

    lane_group = CAP * block_rows
    post = layers * lane_group
    wide = CAP * rows
    sizes = (layers, owners, per_owner, block_count, slot_count, block_rows, tile_width)
    weighted, kept, to_x, to_y, factor = pl.pallas_call(
        functools.partial(pack_kernel, sizes),
        out_shape=[
            shaped((rows, width), bf16)
            for width in (panel_width, post + wide, post + wide, 2 * post + wide)
        ]
        + [shaped(factor_inverse.shape, f32)],
        in_specs=[anywhere] * 7,
        out_specs=[vmem] * 5,
        scratch_shapes=[
            pltpu.SMEM(tile_lists.shape, jnp.int32),
            pltpu.SMEM(tile_masks.shape, jnp.int32),
            pltpu.SMEM(tile_order.shape, jnp.int32),
            pltpu.VMEM((1, rows), f32),
            pltpu.VMEM(panel_jac.shape, bf16),
            pltpu.VMEM(jac.shape, bf16),
            pltpu.SMEM(tile_order.shape, jnp.int32),
            pltpu.VMEM((block_count * slot_count * tile_width, block_rows), f32),
            pltpu.SemaphoreType.DMA((7,)),
        ],
        compiler_params=params,
        name="pack",
    )(*map(in_hbm, (tile_lists, tile_masks, tile_order, weights.reshape(1, rows), panel_jac, jac, factor_inverse)))
    line = [shift(weighted, k, 0) for k in range(1, layers)]
    from_x, from_y = shift(to_x, 0, 1), shift(to_y, 0, 2)

    sizes = (layers, panel_width, lane_group, wide)
    column = pl.pallas_call(
        stack_kernel,
        out_shape=shaped((layers * rows, panel_width), bf16),
        in_specs=[vmem] * layers,
        out_specs=vmem,
        compiler_params=params,
        cost_estimate=lasting(10**10),
        name="stack",
    )(*reversed(line), weighted)
    posts = pl.pallas_call(
        functools.partial(sort_kernel, sizes),
        out_shape=[shaped((rows + 16, owners * lane_group), bf16)] * layers,
        in_specs=[vmem] * 3,
        out_specs=[vmem] * layers,
        compiler_params=params,
        cost_estimate=lasting(10**10),
        name="sort",
    )(kept, from_x, from_y)
    posts = [posts[0]] + [shift(posts[k], k, 0) for k in range(1, layers)]
    by_x, by_y = shift(column, 0, 1), shift(column, 0, 2)

    across_y = shift(by_x, 0, 2)
    turned = pl.pallas_call(
        turn_kernel,
        out_shape=shaped((2, *factor_inverse.shape), bf16),
        in_specs=[vmem],
        out_specs=vmem,
        compiler_params=params,
        name="turn",
    )(factor)
    columns_to_x = pl.pallas_call(
        functools.partial(columns_to_x_kernel, (layers, lane_group, wide)),
        out_shape=shaped((rows // 2 + 16, panel_width), bf16),
        in_specs=[vmem] * layers + [anywhere] * 2,
        out_specs=vmem,
        compiler_params=params,
        cost_estimate=lasting(3 * 10**9),
        name="columns_to_x",
    )(*posts, by_y, turned)
    across_x = shift(columns_to_x, 0, 1)

    count = per_owner * slab_width
    depth = layers * rows
    sizes = (layers, owners, per_owner, block_count, block_rows)
    result = shaped((count, panel_width), f32)
    panels = [column, by_x, by_y]
    own, other = pl.pallas_call(
        functools.partial(near_kernel, sizes, 1),
        out_shape=[result, shaped((count, panel_width), bf16)],
        in_specs=[anywhere] + [vmem] * (len(panels) + layers),
        out_specs=[vmem] * 2,
        scratch_shapes=[
            pltpu.VMEM((count, (owners - 1) * depth), bf16),
            pltpu.VMEM(((owners - 1) * depth, panel_width), bf16),
        ],
        compiler_params=params,
        cost_estimate=lasting(10**9),
        name="near",
    )(columns_to_x, *panels, *posts)
    other = shift(other, 0, 0, 1)
    joined = pl.pallas_call(
        join_kernel,
        out_shape=shaped((across_y.shape[0] + across_x.shape[0], panel_width), bf16),
        in_specs=[vmem] * 2,
        out_specs=vmem,
        compiler_params=params,
        cost_estimate=lasting(10**10),
        name="join",
    )(across_y, across_x)
    other_joined = shift(joined, 0, 0, 1)
    far_scratch = [pltpu.VMEM((count, depth), bf16)] + [pltpu.VMEM((depth, panel_width), bf16)] * 2
    far = pl.pallas_call(
        functools.partial(far_kernel, sizes),
        out_shape=result,
        in_specs=[vmem] * 2,
        out_specs=vmem,
        scratch_shapes=far_scratch,
        compiler_params=params,
        name="far",
    )(joined, turned)
    middle = pl.pallas_call(
        middle_kernel,
        out_shape=result,
        in_specs=[vmem] * 4,
        out_specs=vmem,
        compiler_params=params,
        name="middle",
    )(far, own, other, turned)
    out = pl.pallas_call(
        functools.partial(final_kernel, sizes),
        out_shape=result,
        in_specs=[vmem] * 3,
        out_specs=anywhere,
        scratch_shapes=[pltpu.VMEM((count, panel_width), f32)] + far_scratch + [pltpu.SemaphoreType.DMA((4,))],
        compiler_params=params,
        name="final",
    )(middle, other_joined, turned)
    return out.reshape(per_owner, slab_width, panel_width)


def solution(mesh):
    in_specs = (
        P(("rows", "cols"), None),
        P(("rows", "cols"), None),
        P(("rows", "cols")),
        P(("rows", "cols"), None),
        P(("rows", "cols"), None),
        P(),
        P(),
    )
    out_specs = P("cols", "rows", None)
    body = local if (mesh.shape["rows"], mesh.shape["cols"]) == (8, 4) else local_general
    return jax.shard_map(body, mesh=mesh, in_specs=in_specs, out_specs=out_specs, check_vma=False)
```

```python
import functools

import jax
import jax.numpy as jnp
from jax import lax
from jax.experimental import pallas as pl
from jax.experimental.pallas import tpu as pltpu
from jax.sharding import PartitionSpec as P

CAP = 2
GATHERED = 1 << 22


def tile_positions(tile_lists, tile_order):
    tile_count = tile_order.shape[0]
    matches = tile_lists[:, :, None] == tile_order[None, None, :]
    return jnp.sum(jnp.where(matches, jnp.arange(tile_count, dtype=jnp.int32), 0), axis=2)


def apply_inverse(tiles, factor_inverse):
    return jnp.einsum("ntp,qp->ntq", tiles, factor_inverse, precision=lax.Precision.HIGHEST)


def slot_codes(tile_lists, tile_masks, tile_order, owner_ids):
    block_count, slot_count = tile_lists.shape
    per_owner = tile_order.shape[0] // lax.axis_size("cols")
    positions = tile_positions(tile_lists, tile_order).reshape(-1)
    active = tile_masks.reshape(-1) == 1
    owner = positions // per_owner
    same = (owner[:, None] == owner[None, :]) & active[None, :]
    earlier = jnp.tril(jnp.ones(same.shape, bool), -1)
    rank = jnp.sum(same & earlier, axis=1)
    code = (
        (owner[None, None, :] == owner_ids[:, None, None])
        & (rank[None, None, :] == jnp.arange(CAP)[None, :, None])
        & active[None, None, :]
    )
    block = jnp.arange(block_count * slot_count) // slot_count
    place = positions % per_owner + per_owner * block
    return code, jnp.sum(jnp.where(code, place + 1, 0), axis=2) - 1


def local_general(jac, panel_jac, weights, tile_lists, tile_masks, tile_order, factor_inverse):
    block_count, slot_count = tile_lists.shape
    block_rows = jac.shape[0] // block_count
    tile_width = jac.shape[1] // slot_count
    slabs, owners = lax.axis_size("rows"), lax.axis_size("cols")
    devices = slabs * owners
    per_owner = tile_order.shape[0] // owners
    slab_width = tile_width // slabs
    bf16 = jnp.bfloat16
    weighted = (weights[:, None] * panel_jac).astype(bf16)
    code, places = slot_codes(tile_lists, tile_masks, tile_order, jnp.arange(owners))
    columns = jac.reshape(block_count, block_rows, slot_count, slabs, slab_width)
    chosen = code.astype(bf16).reshape(owners, CAP, block_count, slot_count)
    pieces = jnp.einsum("cjbk,bmkrt->rcjmt", chosen, columns, preferred_element_type=jnp.float32).astype(bf16)
    pieces = pieces.reshape(devices, -1)
    note = jnp.broadcast_to(places.astype(bf16)[None], (slabs, owners, CAP)).reshape(devices, CAP)
    note = jnp.pad(note, ((0, 0), (0, 128 - CAP)))
    sent = jnp.concatenate([pieces, note], axis=1)
    got = lax.all_to_all(sent, ("rows", "cols"), split_axis=0, concat_axis=0, tiled=True)
    size = pieces.shape[1]
    data = got[:, :size].reshape(devices, CAP, block_rows, slab_width)
    where = got[:, size : size + CAP].astype(jnp.int32)
    hot = (where[:, :, None] == jnp.arange(block_count * per_owner)).astype(bf16)
    hot = hot.reshape(devices, CAP, block_count, per_owner)
    mixed = jnp.einsum("djbn,djmt->dbmnt", hot, data, preferred_element_type=jnp.float32).astype(bf16)
    strips = max(1, devices * weighted.size * 2 // GATHERED)

    def strip_gram(strip):
        panels = lax.all_gather(strip, ("rows", "cols"), axis=0, tiled=True)
        panels = panels.reshape(devices, block_count, block_rows, -1)
        return jnp.einsum("dbmnt,dbmp->ntp", mixed, panels, preferred_element_type=jnp.float32)

    if strips == 1:
        gram = strip_gram(weighted)
    else:
        narrow = weighted.reshape(weighted.shape[0], strips, -1).swapaxes(0, 1)
        gram = jnp.moveaxis(lax.map(strip_gram, narrow), 0, 2)
        gram = gram.reshape(per_owner, slab_width, -1)
    return apply_inverse(gram, factor_inverse)


def shift(value, steps_z, flip_cols, flip_core=0):
    slabs, owners = lax.axis_size("rows"), lax.axis_size("cols")
    pairs = []
    for r in range(slabs):
        to_r = ((r // 2 + steps_z) % (slabs // 2)) * 2 + ((r % 2) ^ flip_core)
        for c in range(owners):
            pairs.append((r * owners + c, to_r * owners + (c ^ flip_cols)))
    return lax.ppermute(value, ("rows", "cols"), pairs)


def lasting(flops):
    return pl.CostEstimate(flops=flops, bytes_accessed=0, transcendentals=0)


def pack_kernel(sizes, lists_hbm, masks_hbm, order_hbm, weights_hbm, panel_hbm, jac_hbm, factor_hbm, *refs):
    layers, owners, per_owner, block_count, slot_count, block_rows, tile_width = sizes
    weighted_ref, kept_ref, to_x_ref, to_y_ref, factor_ref = refs[:5]
    lists_ref, masks_ref, order_ref, weights_ref, panel_ref, jac_ref, places_ref, turned_ref, sems = refs[5:]
    copies = [
        pltpu.make_async_copy(order_hbm, order_ref, sems.at[0]),
        pltpu.make_async_copy(lists_hbm, lists_ref, sems.at[1]),
        pltpu.make_async_copy(masks_hbm, masks_ref, sems.at[2]),
        pltpu.make_async_copy(weights_hbm, weights_ref, sems.at[3]),
        pltpu.make_async_copy(panel_hbm, panel_ref, sems.at[4]),
        pltpu.make_async_copy(jac_hbm, jac_ref, sems.at[5]),
    ]
    for copy in copies:
        copy.start()
    factor_copy = pltpu.make_async_copy(factor_hbm, factor_ref, sems.at[6])
    factor_copy.start()
    f32, bf16 = jnp.float32, jnp.bfloat16
    rows, width = panel_ref.shape
    lane_group = CAP * block_rows
    post = layers * lane_group
    slab = tile_width // layers
    part = slab // 2
    me_r, me_c = lax.axis_index("rows"), lax.axis_index("cols")
    me_z, me_core = me_r // 2, lax.rem(me_r, 2)
    for copy in copies:
        copy.wait()

    row_ids = lax.broadcasted_iota(jnp.int32, (rows, rows), 0)
    lane_ids = lax.broadcasted_iota(jnp.int32, (rows, rows), 1)
    column = jnp.sum(jnp.where(row_ids == lane_ids, weights_ref[...], 0.0), axis=1, keepdims=True)
    weighted = (column * panel_ref[...].astype(f32)).astype(bf16)
    weighted_ref[...] = weighted

    for b in range(block_count):
        block = jac_ref[b * block_rows : (b + 1) * block_rows, :].astype(f32)
        start = b * slot_count * tile_width
        turned_ref[start : start + slot_count * tile_width, :] = block.T.astype(bf16)

    for i in range(order_ref.shape[0]):
        places_ref[order_ref[i]] = i
    slots = []
    for s in range(block_count * slot_count):
        b, k = divmod(s, slot_count)
        place = places_ref[lists_ref[b, k]]
        owner = jnp.int32(0)
        for c in range(1, owners):
            owner += (place >= c * per_owner).astype(jnp.int32)
        slots.append((place - owner * per_owner, jnp.where(masks_ref[b, k] == 1, owner, -1)))

    shape = (16, CAP * block_count * block_rows)
    lane, row = lax.broadcasted_iota(jnp.int32, shape, 1), lax.broadcasted_iota(jnp.int32, shape, 0)
    notes = []
    spots = [(kept_ref, 0), (to_x_ref, 0), (to_y_ref, 0), (to_y_ref, post)]
    for e, (parcel, start) in enumerate(spots):
        wanted = me_c ^ e
        found = jnp.int32(0)
        chosen = [jnp.int32(0)] * CAP
        codes = [jnp.int32(-1)] * CAP
        for s, (place, owner) in enumerate(slots):
            hit = owner == wanted
            for j in range(CAP):
                take = hit & (found == j)
                chosen[j] = jnp.where(take, s, chosen[j])
                codes[j] = jnp.where(take, place, codes[j])
            found += hit.astype(jnp.int32)
        note = jnp.full(shape, -1, jnp.int32)
        for j in range(CAP):
            for b in range(block_count):
                at = (j * block_count + b) * block_rows
                here = (lane >= at) & (lane < at + block_rows)
                code = jnp.where(chosen[j] // slot_count == b, codes[j], -1)
                note = jnp.where(here, code, note)
        notes.append(note)
        for u in range(2):
            core = me_core ^ u
            for k in range(0, layers, 2):
                pieces = []
                for z in (lax.rem(me_z + k, layers), lax.rem(me_z + k + 1, layers)):
                    for j in range(CAP):
                        first = pl.multiple_of(chosen[j] * tile_width + z * slab + core * part, part)
                        pieces.append(turned_ref[pl.ds(first, part), :])
                lanes = slice(start + k * lane_group, start + (k + 2) * lane_group)
                parcel[u * part : (u + 1) * part, lanes] = jnp.concatenate(pieces, axis=1)
    kept_ref[:16, post:] = notes[0].astype(f32).astype(bf16)
    to_x_ref[:16, post:] = notes[1].astype(f32).astype(bf16)
    to_y_ref[:16, 2 * post :] = jnp.where(row == 0, notes[2], notes[3]).astype(f32).astype(bf16)
    factor_copy.wait()


def row_of(block, i):
    ids = lax.broadcasted_iota(jnp.int32, block.shape, 0)
    return jnp.sum(jnp.where(ids == i, block.astype(jnp.float32), 0.0), axis=0, keepdims=True)


def rows_from(notes):
    ids = lax.broadcasted_iota(jnp.int32, (16, notes[0].shape[1]), 0)
    block = jnp.full(ids.shape, -1.0, jnp.float32)
    for i, note in enumerate(notes):
        block = jnp.where(ids == i, note, block)
    return block.astype(jnp.bfloat16)


def stack_kernel(*refs):
    inputs, out_ref = refs[:-1], refs[-1]
    rows = inputs[0].shape[0]
    for i, ref in enumerate(reversed(inputs)):
        out_ref[i * rows : (i + 1) * rows, :] = ref[...]


def sort_kernel(sizes, kept_ref, from_x_ref, from_y_ref, *posts):
    layers, width, lane_group, wide = sizes
    post = layers * lane_group
    rows = kept_ref.shape[0]
    spots = [(kept_ref, 0), (from_x_ref, 0), (from_y_ref, 0), (from_y_ref, post)]
    notes = [row_of(ref[:16, ref.shape[1] - wide :], int(e == 3)) for e, (ref, start) in enumerate(spots)]
    block = rows_from(notes)
    for k, out in enumerate(posts):
        for e, (ref, start) in enumerate(spots):
            piece = ref[:, start + k * lane_group : start + (k + 1) * lane_group]
            out[:rows, e * lane_group : (e + 1) * lane_group] = piece
        out[rows:, :wide] = block


def columns_to_x_kernel(sizes, *refs):
    layers, lane_group, wide = sizes
    posts, out_ref = refs[:layers], refs[-1]
    rows = posts[0].shape[0] - 16
    part = rows // 2
    for k, ref in enumerate(posts):
        for u in range(2):
            piece = ref[u * part : (u + 1) * part, 3 * lane_group : 4 * lane_group]
            at = (u * layers + k) * lane_group
            out_ref[:part, at : at + lane_group] = piece
    out_ref[part:, :wide] = rows_from([row_of(ref[rows:, :wide], 3) for ref in posts])


def place(out_ref, lanes, per_owner, pieces, notes, sizes):
    block_count, block_rows = sizes
    f32, bf16 = jnp.float32, jnp.bfloat16
    part, rows = pieces[0].shape[0], block_count * block_rows
    columns, codes = [], []
    for j in range(CAP):
        parts = []
        for piece in pieces:
            parts += [piece[:, j * block_rows : (j + 1) * block_rows].astype(f32)] * block_count
        columns.append(jnp.concatenate(parts, axis=1).astype(bf16))
        note = jnp.concatenate([note[:, j * rows : (j + 1) * rows] for note in notes], axis=1)
        codes.append(jnp.broadcast_to(note, columns[j].shape).astype(bf16))
    for n in range(per_owner):
        placed = jnp.zeros(columns[0].shape, bf16)
        for j in range(CAP):
            placed = jnp.where(codes[j] == jnp.asarray(n, bf16), columns[j], placed)
        out_ref[n * part : (n + 1) * part, lanes] = placed


def inverse_rows(rows_ref, factor_ref, high_ref, low_ref):
    f32, bf16 = jnp.float32, jnp.bfloat16
    height, width = high_ref.shape
    for start, stop in ((0, width // 2), (width // 2, width)):
        rows = rows_ref[:height, :stop]
        total = jnp.dot(rows, factor_ref[0, :stop, start:stop], preferred_element_type=f32)
        total += jnp.dot(rows, factor_ref[1, :stop, start:stop], preferred_element_type=f32)
        high = total.astype(bf16)
        high_ref[:, start:stop] = high
        low_ref[:, start:stop] = (total - high.astype(f32)).astype(bf16)


def turn_kernel(factor_ref, out_ref):
    turned = factor_ref[...].T
    high = turned.astype(jnp.bfloat16)
    out_ref[0, :, :] = high
    out_ref[1, :, :] = (turned - high.astype(jnp.float32)).astype(jnp.bfloat16)


def near_kernel(sizes, earlier, *refs):
    layers, owners, per_owner, block_count, block_rows = sizes
    panels, posts, refs = refs[earlier : earlier + 3], refs[earlier + 3 : earlier + 3 + layers], refs[earlier + 3 + layers :]
    own_ref, other_ref, placed_ref, rows_ref = refs
    f32, bf16 = jnp.float32, jnp.bfloat16
    rows = block_count * block_rows
    group, wide = CAP * block_rows, CAP * rows
    part = rows // 2
    width = rows_ref.shape[1]
    at = 0
    for panel in panels:
        rows_ref[at : at + panel.shape[0], :] = panel[:, :width]
        at += panel.shape[0]
    for u, out_ref in ((1, other_ref), (0, own_ref)):
        for e in range(owners - 1):
            for h in range(layers // 2):
                pair = posts[2 * h : 2 * h + 2]
                pieces = [post[u * part : (u + 1) * part, e * group : (e + 1) * group] for post in pair]
                notes = [row_of(post[rows:, :wide], e) for post in pair]
                start = (e * layers + 2 * h) * rows
                place(placed_ref, slice(start, start + 2 * rows), per_owner, pieces, notes, (block_count, block_rows))
        gram = jnp.dot(placed_ref[...], rows_ref[...], preferred_element_type=f32)
        out_ref[...] = gram.astype(out_ref.dtype)


def join_kernel(above_ref, below_ref, earlier_ref, out_ref):
    rows = above_ref.shape[0]
    out_ref[:rows, :] = above_ref[...]
    out_ref[rows:, :] = below_ref[...]


def place_far(sizes, u, ref, placed_ref):
    layers, owners, per_owner, block_count, block_rows = sizes
    rows = block_count * block_rows
    group, wide = CAP * block_rows, CAP * rows
    part, depth = rows // 2, layers * rows
    for h in range(layers // 2):
        pieces, notes = [], []
        for k in (2 * h, 2 * h + 1):
            at = (u * layers + k) * group
            pieces.append(ref[depth : depth + part, at : at + group])
            notes.append(row_of(ref[depth + part :, :wide], k))
        lanes = slice(2 * h * rows, 2 * (h + 1) * rows)
        place(placed_ref, lanes, per_owner, pieces, notes, (block_count, block_rows))


def far_kernel(sizes, joined_ref, turned_ref, out_ref, placed_ref, high_ref, low_ref):
    place_far(sizes, 0, joined_ref, placed_ref)
    inverse_rows(joined_ref, turned_ref, high_ref, low_ref)
    placed = placed_ref[...]
    total = jnp.dot(placed, high_ref[...], preferred_element_type=jnp.float32)
    out_ref[...] = total + jnp.dot(placed, low_ref[...], preferred_element_type=jnp.float32)


def times_inverse(out_ref, terms, turned_ref, added):
    width = out_ref.shape[1]
    for start, stop in ((0, width // 2), (width // 2, width)):
        total = sum(ref[:, start:stop] for ref in added)
        for i, j in ((0, 0), (0, 1), (1, 0))[: len(terms) + 1]:
            total += jnp.dot(terms[i][:, :stop], turned_ref[j, :stop, start:stop], preferred_element_type=jnp.float32)
        out_ref[:, start:stop] = total


def own_kernel(own_ref, turned_ref, out_ref):
    high = own_ref[...].astype(jnp.bfloat16)
    low = (own_ref[...] - high.astype(jnp.float32)).astype(jnp.bfloat16)
    times_inverse(out_ref, (high, low), turned_ref, ())


def middle_kernel(own_ref, other_ref, far_ref, turned_ref, out_ref):
    times_inverse(out_ref, (other_ref[...],), turned_ref, (own_ref, far_ref))


def final_kernel(sizes, middle_ref, joined_ref, turned_ref, out_hbm, sum_ref, placed_ref, high_ref, low_ref, sems):
    f32 = jnp.float32
    place_far(sizes, 1, joined_ref, placed_ref)
    inverse_rows(joined_ref, turned_ref, high_ref, low_ref)
    strips = sems.shape[0]
    height = sum_ref.shape[0] // strips
    copies = []
    for i in range(strips):
        here = pl.ds(i * height, height)
        placed = placed_ref[here, :]
        total = middle_ref[here, :] + jnp.dot(placed, high_ref[...], preferred_element_type=f32)
        sum_ref[here, :] = total + jnp.dot(placed, low_ref[...], preferred_element_type=f32)
        copies.append(pltpu.make_async_copy(sum_ref.at[here, :], out_hbm.at[here, :], sems.at[i]))
        copies[-1].start()
    for copy in copies:
        copy.wait()


def local(jac, panel_jac, weights, tile_lists, tile_masks, tile_order, factor_inverse):
    block_count, slot_count = tile_lists.shape
    rows, panel_width = panel_jac.shape
    block_rows = rows // block_count
    tile_width = jac.shape[1] // slot_count
    slabs, owners = lax.axis_size("rows"), lax.axis_size("cols")
    layers = slabs // 2
    per_owner = tile_order.shape[0] // owners
    slab_width = tile_width // slabs
    f32, bf16 = jnp.float32, jnp.bfloat16
    vmem, anywhere = pl.BlockSpec(memory_space=pltpu.VMEM), pl.BlockSpec(memory_space=pl.ANY)
    params = pltpu.CompilerParams(vmem_limit_bytes=24 << 20)
    shaped = jax.ShapeDtypeStruct

    def in_hbm(value):
        return pltpu.with_memory_space_constraint(value, pltpu.HBM)

    lane_group = CAP * block_rows
    post = layers * lane_group
    wide = CAP * rows
    sizes = (layers, owners, per_owner, block_count, slot_count, block_rows, tile_width)
    weighted, kept, to_x, to_y, factor = pl.pallas_call(
        functools.partial(pack_kernel, sizes),
        out_shape=[
            shaped((rows, width), bf16)
            for width in (panel_width, post + wide, post + wide, 2 * post + wide)
        ]
        + [shaped(factor_inverse.shape, f32)],
        in_specs=[anywhere] * 7,
        out_specs=[vmem] * 5,
        scratch_shapes=[
            pltpu.SMEM(tile_lists.shape, jnp.int32),
            pltpu.SMEM(tile_masks.shape, jnp.int32),
            pltpu.SMEM(tile_order.shape, jnp.int32),
            pltpu.VMEM((1, rows), f32),
            pltpu.VMEM(panel_jac.shape, bf16),
            pltpu.VMEM(jac.shape, bf16),
            pltpu.SMEM(tile_order.shape, jnp.int32),
            pltpu.VMEM((block_count * slot_count * tile_width, block_rows), bf16),
            pltpu.SemaphoreType.DMA((7,)),
        ],
        compiler_params=params,
        name="pack",
    )(*map(in_hbm, (tile_lists, tile_masks, tile_order, weights.reshape(1, rows), panel_jac, jac, factor_inverse)))
    line = [shift(weighted, k, 0) for k in range(1, layers)]
    from_x, from_y = shift(to_x, 0, 1), shift(to_y, 0, 2)

    sizes = (layers, panel_width, lane_group, wide)
    column = pl.pallas_call(
        stack_kernel,
        out_shape=shaped((layers * rows, panel_width), bf16),
        in_specs=[vmem] * layers,
        out_specs=vmem,
        compiler_params=params,
        cost_estimate=lasting(10**10),
        name="stack",
    )(*reversed(line), weighted)
    posts = pl.pallas_call(
        functools.partial(sort_kernel, sizes),
        out_shape=[shaped((rows + 16, owners * lane_group), bf16)] * layers,
        in_specs=[vmem] * 3,
        out_specs=[vmem] * layers,
        compiler_params=params,
        cost_estimate=lasting(10**10),
        name="sort",
    )(kept, from_x, from_y)
    posts = [posts[0]] + [shift(posts[k], k, 0) for k in range(1, layers)]
    by_x, by_y = shift(column, 0, 1), shift(column, 0, 2)

    across_y = shift(by_x, 0, 2)
    turned = pl.pallas_call(
        turn_kernel,
        out_shape=shaped((2, *factor_inverse.shape), bf16),
        in_specs=[vmem],
        out_specs=vmem,
        compiler_params=params,
        name="turn",
    )(factor)
    columns_to_x = pl.pallas_call(
        functools.partial(columns_to_x_kernel, (layers, lane_group, wide)),
        out_shape=shaped((rows // 2 + 16, panel_width), bf16),
        in_specs=[vmem] * layers + [anywhere] * 2,
        out_specs=vmem,
        compiler_params=params,
        cost_estimate=lasting(3 * 10**9),
        name="columns_to_x",
    )(*posts, by_y, turned)
    across_x = shift(columns_to_x, 0, 1)

    count = per_owner * slab_width
    depth = layers * rows
    sizes = (layers, owners, per_owner, block_count, block_rows)
    result = shaped((count, panel_width), f32)
    panels = [column, by_x, by_y]
    own, other = pl.pallas_call(
        functools.partial(near_kernel, sizes, 1),
        out_shape=[result, shaped((count, panel_width), bf16)],
        in_specs=[anywhere] + [vmem] * (len(panels) + layers),
        out_specs=[vmem] * 2,
        scratch_shapes=[
            pltpu.VMEM((count, (owners - 1) * depth), bf16),
            pltpu.VMEM(((owners - 1) * depth, panel_width), bf16),
        ],
        compiler_params=params,
        cost_estimate=lasting(10**9),
        name="near",
    )(columns_to_x, *panels, *posts)
    other = shift(other, 0, 0, 1)
    own = pl.pallas_call(
        own_kernel,
        out_shape=result,
        in_specs=[vmem] * 2,
        out_specs=vmem,
        compiler_params=params,
        cost_estimate=lasting(10**9),
        name="own",
    )(own, turned)
    joined = pl.pallas_call(
        join_kernel,
        out_shape=shaped((across_y.shape[0] + across_x.shape[0], panel_width), bf16),
        in_specs=[vmem] * 2 + [anywhere],
        out_specs=vmem,
        compiler_params=params,
        cost_estimate=lasting(10**10),
        name="join",
    )(across_y, across_x, own)
    other_joined = shift(joined, 0, 0, 1)
    far_scratch = [pltpu.VMEM((count, depth), bf16)] + [pltpu.VMEM((depth, panel_width), bf16)] * 2
    far = pl.pallas_call(
        functools.partial(far_kernel, sizes),
        out_shape=result,
        in_specs=[vmem] * 2,
        out_specs=vmem,
        scratch_shapes=far_scratch,
        compiler_params=params,
        name="far",
    )(joined, turned)
    middle = pl.pallas_call(
        middle_kernel,
        out_shape=result,
        in_specs=[vmem] * 4,
        out_specs=vmem,
        compiler_params=params,
        name="middle",
    )(own, other, far, turned)
    out = pl.pallas_call(
        functools.partial(final_kernel, sizes),
        out_shape=result,
        in_specs=[vmem] * 3,
        out_specs=anywhere,
        scratch_shapes=[pltpu.VMEM((count, panel_width), f32)] + far_scratch + [pltpu.SemaphoreType.DMA((4,))],
        compiler_params=params,
        name="final",
    )(middle, other_joined, turned)
    return out.reshape(per_owner, slab_width, panel_width)


def solution(mesh):
    in_specs = (
        P(("rows", "cols"), None),
        P(("rows", "cols"), None),
        P(("rows", "cols")),
        P(("rows", "cols"), None),
        P(("rows", "cols"), None),
        P(),
        P(),
    )
    out_specs = P("cols", "rows", None)
    body = local if (mesh.shape["rows"], mesh.shape["cols"]) == (8, 4) else local_general
    return jax.shard_map(body, mesh=mesh, in_specs=in_specs, out_specs=out_specs, check_vma=False)
```

```python
import functools

import jax
import jax.numpy as jnp
from jax import lax
from jax.experimental import pallas as pl
from jax.experimental.pallas import tpu as pltpu
from jax.sharding import PartitionSpec as P

CAP = 2
GATHERED = 1 << 22


def tile_positions(tile_lists, tile_order):
    tile_count = tile_order.shape[0]
    matches = tile_lists[:, :, None] == tile_order[None, None, :]
    return jnp.sum(jnp.where(matches, jnp.arange(tile_count, dtype=jnp.int32), 0), axis=2)


def apply_inverse(tiles, factor_inverse):
    return jnp.einsum("ntp,qp->ntq", tiles, factor_inverse, precision=lax.Precision.HIGHEST)


def slot_codes(tile_lists, tile_masks, tile_order, owner_ids):
    block_count, slot_count = tile_lists.shape
    per_owner = tile_order.shape[0] // lax.axis_size("cols")
    positions = tile_positions(tile_lists, tile_order).reshape(-1)
    active = tile_masks.reshape(-1) == 1
    owner = positions // per_owner
    same = (owner[:, None] == owner[None, :]) & active[None, :]
    earlier = jnp.tril(jnp.ones(same.shape, bool), -1)
    rank = jnp.sum(same & earlier, axis=1)
    code = (
        (owner[None, None, :] == owner_ids[:, None, None])
        & (rank[None, None, :] == jnp.arange(CAP)[None, :, None])
        & active[None, None, :]
    )
    block = jnp.arange(block_count * slot_count) // slot_count
    place = positions % per_owner + per_owner * block
    return code, jnp.sum(jnp.where(code, place + 1, 0), axis=2) - 1


def local_general(jac, panel_jac, weights, tile_lists, tile_masks, tile_order, factor_inverse):
    block_count, slot_count = tile_lists.shape
    block_rows = jac.shape[0] // block_count
    tile_width = jac.shape[1] // slot_count
    slabs, owners = lax.axis_size("rows"), lax.axis_size("cols")
    devices = slabs * owners
    per_owner = tile_order.shape[0] // owners
    slab_width = tile_width // slabs
    bf16 = jnp.bfloat16
    weighted = (weights[:, None] * panel_jac).astype(bf16)
    code, places = slot_codes(tile_lists, tile_masks, tile_order, jnp.arange(owners))
    columns = jac.reshape(block_count, block_rows, slot_count, slabs, slab_width)
    chosen = code.astype(bf16).reshape(owners, CAP, block_count, slot_count)
    pieces = jnp.einsum("cjbk,bmkrt->rcjmt", chosen, columns, preferred_element_type=jnp.float32).astype(bf16)
    pieces = pieces.reshape(devices, -1)
    note = jnp.broadcast_to(places.astype(bf16)[None], (slabs, owners, CAP)).reshape(devices, CAP)
    note = jnp.pad(note, ((0, 0), (0, 128 - CAP)))
    sent = jnp.concatenate([pieces, note], axis=1)
    got = lax.all_to_all(sent, ("rows", "cols"), split_axis=0, concat_axis=0, tiled=True)
    size = pieces.shape[1]
    data = got[:, :size].reshape(devices, CAP, block_rows, slab_width)
    where = got[:, size : size + CAP].astype(jnp.int32)
    hot = (where[:, :, None] == jnp.arange(block_count * per_owner)).astype(bf16)
    hot = hot.reshape(devices, CAP, block_count, per_owner)
    mixed = jnp.einsum("djbn,djmt->dbmnt", hot, data, preferred_element_type=jnp.float32).astype(bf16)
    strips = max(1, devices * weighted.size * 2 // GATHERED)

    def strip_gram(strip):
        panels = lax.all_gather(strip, ("rows", "cols"), axis=0, tiled=True)
        panels = panels.reshape(devices, block_count, block_rows, -1)
        return jnp.einsum("dbmnt,dbmp->ntp", mixed, panels, preferred_element_type=jnp.float32)

    if strips == 1:
        gram = strip_gram(weighted)
    else:
        narrow = weighted.reshape(weighted.shape[0], strips, -1).swapaxes(0, 1)
        gram = jnp.moveaxis(lax.map(strip_gram, narrow), 0, 2)
        gram = gram.reshape(per_owner, slab_width, -1)
    return apply_inverse(gram, factor_inverse)


def shift(value, steps_z, flip_cols, flip_core=0):
    slabs, owners = lax.axis_size("rows"), lax.axis_size("cols")
    pairs = []
    for r in range(slabs):
        to_r = ((r // 2 + steps_z) % (slabs // 2)) * 2 + ((r % 2) ^ flip_core)
        for c in range(owners):
            pairs.append((r * owners + c, to_r * owners + (c ^ flip_cols)))
    return lax.ppermute(value, ("rows", "cols"), pairs)


def lasting(flops):
    return pl.CostEstimate(flops=flops, bytes_accessed=0, transcendentals=0)


def pack_kernel(sizes, lists_hbm, masks_hbm, order_hbm, weights_hbm, panel_hbm, jac_hbm, factor_hbm, *refs):
    layers, owners, per_owner, block_count, slot_count, block_rows, tile_width = sizes
    weighted_ref, parcels, factor_ref = refs[0], refs[1 : 1 + owners], refs[1 + owners]
    lists_ref, masks_ref, order_ref, weights_ref, panel_ref, jac_ref, places_ref, turned_ref, sems = refs[2 + owners :]
    copies = [
        pltpu.make_async_copy(order_hbm, order_ref, sems.at[0]),
        pltpu.make_async_copy(lists_hbm, lists_ref, sems.at[1]),
        pltpu.make_async_copy(masks_hbm, masks_ref, sems.at[2]),
        pltpu.make_async_copy(weights_hbm, weights_ref, sems.at[3]),
        pltpu.make_async_copy(panel_hbm, panel_ref, sems.at[4]),
        pltpu.make_async_copy(jac_hbm, jac_ref, sems.at[5]),
    ]
    for copy in copies:
        copy.start()
    factor_copy = pltpu.make_async_copy(factor_hbm, factor_ref, sems.at[6])
    factor_copy.start()
    f32, bf16 = jnp.float32, jnp.bfloat16
    rows, width = panel_ref.shape
    lane_group = CAP * block_rows
    post = layers * lane_group
    slab = tile_width // layers
    part = slab // 2
    me_r, me_c = lax.axis_index("rows"), lax.axis_index("cols")
    me_z, me_core = me_r // 2, lax.rem(me_r, 2)
    for copy in copies:
        copy.wait()

    row_ids = lax.broadcasted_iota(jnp.int32, (rows, rows), 0)
    lane_ids = lax.broadcasted_iota(jnp.int32, (rows, rows), 1)
    column = jnp.sum(jnp.where(row_ids == lane_ids, weights_ref[...], 0.0), axis=1, keepdims=True)
    weighted = (column * panel_ref[...].astype(f32)).astype(bf16)
    weighted_ref[...] = weighted

    for b in range(block_count):
        block = jac_ref[b * block_rows : (b + 1) * block_rows, :].astype(f32)
        start = b * slot_count * tile_width
        turned_ref[start : start + slot_count * tile_width, :] = block.T.astype(bf16)

    for i in range(order_ref.shape[0]):
        places_ref[order_ref[i]] = i
    slots = []
    for s in range(block_count * slot_count):
        b, k = divmod(s, slot_count)
        place = places_ref[lists_ref[b, k]]
        owner = jnp.int32(0)
        for c in range(1, owners):
            owner += (place >= c * per_owner).astype(jnp.int32)
        slots.append((place - owner * per_owner, jnp.where(masks_ref[b, k] == 1, owner, -1)))

    shape = (16, CAP * block_count * block_rows)
    lane = lax.broadcasted_iota(jnp.int32, shape, 1)
    for e, parcel in enumerate(parcels):
        wanted = me_c ^ e
        found = jnp.int32(0)
        chosen = [jnp.int32(0)] * CAP
        codes = [jnp.int32(-1)] * CAP
        for s, (place, owner) in enumerate(slots):
            hit = owner == wanted
            for j in range(CAP):
                take = hit & (found == j)
                chosen[j] = jnp.where(take, s, chosen[j])
                codes[j] = jnp.where(take, place, codes[j])
            found += hit.astype(jnp.int32)
        note = jnp.full(shape, -1, jnp.int32)
        for j in range(CAP):
            for b in range(block_count):
                at = (j * block_count + b) * block_rows
                here = (lane >= at) & (lane < at + block_rows)
                code = jnp.where(chosen[j] // slot_count == b, codes[j], -1)
                note = jnp.where(here, code, note)
        parcel[:16, post:] = note.astype(f32).astype(bf16)
        for u in range(2):
            core = me_core ^ u
            for k in range(0, layers, 2):
                pieces = []
                for z in (lax.rem(me_z + k, layers), lax.rem(me_z + k + 1, layers)):
                    for j in range(CAP):
                        first = pl.multiple_of(chosen[j] * tile_width + z * slab + core * part, part)
                        pieces.append(turned_ref[pl.ds(first, part), :])
                lanes = slice(k * lane_group, (k + 2) * lane_group)
                parcel[u * part : (u + 1) * part, lanes] = jnp.concatenate(pieces, axis=1)
    factor_copy.wait()


def row_of(block, i):
    ids = lax.broadcasted_iota(jnp.int32, block.shape, 0)
    return jnp.sum(jnp.where(ids == i, block.astype(jnp.float32), 0.0), axis=0, keepdims=True)


def rows_from(notes):
    ids = lax.broadcasted_iota(jnp.int32, (16, notes[0].shape[1]), 0)
    block = jnp.full(ids.shape, -1.0, jnp.float32)
    for i, note in enumerate(notes):
        block = jnp.where(ids == i, note, block)
    return block.astype(jnp.bfloat16)


def stack_kernel(*refs):
    inputs, out_ref = refs[:-1], refs[-1]
    rows = inputs[0].shape[0]
    for i, ref in enumerate(reversed(inputs)):
        out_ref[i * rows : (i + 1) * rows, :] = ref[...]


def sort_kernel(sizes, *refs):
    layers, owners, lane_group = sizes
    parcels, posts = refs[:owners], refs[owners:]
    rows, codes_at = parcels[0].shape[0], layers * lane_group
    block = rows_from([row_of(parcel[:16, codes_at:], 0) for parcel in parcels])
    for k, out in enumerate(posts):
        for e, parcel in enumerate(parcels):
            piece = parcel[:, k * lane_group : (k + 1) * lane_group]
            out[:rows, e * lane_group : (e + 1) * lane_group] = piece
        out[rows:, : block.shape[1]] = block


def first_kernel(in_ref, out_ref):
    out_ref[...] = in_ref[: out_ref.shape[0], :]


def last_kernel(in_ref, out_ref):
    out_ref[...] = in_ref[in_ref.shape[0] - out_ref.shape[0] :, :]


def place(out_ref, lanes, per_owner, pieces, notes, sizes):
    block_count, block_rows = sizes
    f32, bf16 = jnp.float32, jnp.bfloat16
    part, rows = pieces[0].shape[0], block_count * block_rows
    columns, codes = [], []
    for j in range(CAP):
        parts = []
        for piece in pieces:
            parts += [piece[:, j * block_rows : (j + 1) * block_rows].astype(f32)] * block_count
        columns.append(jnp.concatenate(parts, axis=1).astype(bf16))
        note = jnp.concatenate([note[:, j * rows : (j + 1) * rows] for note in notes], axis=1)
        codes.append(jnp.broadcast_to(note, columns[j].shape).astype(bf16))
    for n in range(per_owner):
        placed = jnp.zeros(columns[0].shape, bf16)
        for j in range(CAP):
            placed = jnp.where(codes[j] == jnp.asarray(n, bf16), columns[j], placed)
        out_ref[n * part : (n + 1) * part, lanes] = placed


def inverse_rows(rows_ref, factor_ref, high_ref, low_ref):
    f32, bf16 = jnp.float32, jnp.bfloat16
    height, width = high_ref.shape
    for start, stop in ((0, width // 2), (width // 2, width)):
        rows = rows_ref[:height, :stop]
        total = jnp.dot(rows, factor_ref[0, :stop, start:stop], preferred_element_type=f32)
        total += jnp.dot(rows, factor_ref[1, :stop, start:stop], preferred_element_type=f32)
        high = total.astype(bf16)
        high_ref[:, start:stop] = high
        low_ref[:, start:stop] = (total - high.astype(f32)).astype(bf16)


def turn_kernel(factor_ref, out_ref):
    turned = factor_ref[...].T
    high = turned.astype(jnp.bfloat16)
    out_ref[0, :, :] = high
    out_ref[1, :, :] = (turned - high.astype(jnp.float32)).astype(jnp.bfloat16)


def near_kernel(sizes, earlier, *refs):
    layers, owners, per_owner, block_count, block_rows = sizes
    panels, posts, refs = refs[earlier : earlier + 3], refs[earlier + 3 : earlier + 3 + layers], refs[earlier + 3 + layers :]
    own_ref, other_ref, placed_ref, rows_ref = refs
    f32, bf16 = jnp.float32, jnp.bfloat16
    rows = block_count * block_rows
    group, wide = CAP * block_rows, CAP * rows
    part = rows // 2
    width = rows_ref.shape[1]
    at = 0
    for panel in panels:
        rows_ref[at : at + panel.shape[0], :] = panel[:, :width]
        at += panel.shape[0]
    for u, out_ref in ((1, other_ref), (0, own_ref)):
        for e in range(owners - 1):
            for h in range(layers // 2):
                pair = posts[2 * h : 2 * h + 2]
                pieces = [post[u * part : (u + 1) * part, e * group : (e + 1) * group] for post in pair]
                notes = [row_of(post[rows:, :wide], e) for post in pair]
                start = (e * layers + 2 * h) * rows
                place(placed_ref, slice(start, start + 2 * rows), per_owner, pieces, notes, (block_count, block_rows))
        gram = jnp.dot(placed_ref[...], rows_ref[...], preferred_element_type=f32)
        out_ref[...] = gram.astype(out_ref.dtype)


def join_kernel(sizes, above_ref, below_ref, *refs):
    layers, lane_group, wide = sizes
    posts, out_ref = refs[:layers], refs[-1]
    half, rows = above_ref.shape[0], posts[0].shape[0] - 16
    part, depth = rows // 2, 2 * half
    out_ref[:half, :] = above_ref[...]
    out_ref[half:depth, :] = below_ref[...]
    for k, ref in enumerate(posts):
        for u in range(2):
            piece = ref[u * part : (u + 1) * part, 3 * lane_group : 4 * lane_group]
            at = (u * layers + k) * lane_group
            out_ref[depth : depth + part, at : at + lane_group] = piece
    out_ref[depth + part :, :wide] = rows_from([row_of(ref[rows:, :wide], 3) for ref in posts])


def place_far(sizes, u, ref, placed_ref):
    layers, owners, per_owner, block_count, block_rows = sizes
    rows = block_count * block_rows
    group, wide = CAP * block_rows, CAP * rows
    part, depth = rows // 2, layers * rows
    for h in range(layers // 2):
        pieces, notes = [], []
        for k in (2 * h, 2 * h + 1):
            at = (u * layers + k) * group
            pieces.append(ref[depth : depth + part, at : at + group])
            notes.append(row_of(ref[depth + part :, :wide], k))
        lanes = slice(2 * h * rows, 2 * (h + 1) * rows)
        place(placed_ref, lanes, per_owner, pieces, notes, (block_count, block_rows))


def far_kernel(sizes, joined_ref, turned_ref, out_ref, placed_ref, high_ref, low_ref):
    place_far(sizes, 0, joined_ref, placed_ref)
    inverse_rows(joined_ref, turned_ref, high_ref, low_ref)
    placed = placed_ref[...]
    total = jnp.dot(placed, high_ref[...], preferred_element_type=jnp.float32)
    out_ref[...] = total + jnp.dot(placed, low_ref[...], preferred_element_type=jnp.float32)


def times_inverse(out_ref, terms, turned_ref, added):
    width = out_ref.shape[1]
    for start, stop in ((0, width // 2), (width // 2, width)):
        total = sum(ref[:, start:stop] for ref in added)
        for i, j in ((0, 0), (0, 1), (1, 0))[: len(terms) + 1]:
            total += jnp.dot(terms[i][:, :stop], turned_ref[j, :stop, start:stop], preferred_element_type=jnp.float32)
        out_ref[:, start:stop] = total


def own_kernel(own_ref, turned_ref, out_ref):
    high = own_ref[...].astype(jnp.bfloat16)
    low = (own_ref[...] - high.astype(jnp.float32)).astype(jnp.bfloat16)
    times_inverse(out_ref, (high, low), turned_ref, ())


def middle_kernel(own_ref, other_ref, far_ref, turned_ref, out_ref):
    times_inverse(out_ref, (other_ref[...],), turned_ref, (own_ref, far_ref))


def final_kernel(sizes, middle_ref, joined_ref, turned_ref, out_hbm, sum_ref, placed_ref, high_ref, low_ref, sems):
    f32 = jnp.float32
    place_far(sizes, 1, joined_ref, placed_ref)
    inverse_rows(joined_ref, turned_ref, high_ref, low_ref)
    strips = sems.shape[0]
    height = sum_ref.shape[0] // strips
    copies = []
    for i in range(strips):
        here = pl.ds(i * height, height)
        placed = placed_ref[here, :]
        total = middle_ref[here, :] + jnp.dot(placed, high_ref[...], preferred_element_type=f32)
        sum_ref[here, :] = total + jnp.dot(placed, low_ref[...], preferred_element_type=f32)
        copies.append(pltpu.make_async_copy(sum_ref.at[here, :], out_hbm.at[here, :], sems.at[i]))
        copies[-1].start()
    for copy in copies:
        copy.wait()


def local(jac, panel_jac, weights, tile_lists, tile_masks, tile_order, factor_inverse):
    block_count, slot_count = tile_lists.shape
    rows, panel_width = panel_jac.shape
    block_rows = rows // block_count
    tile_width = jac.shape[1] // slot_count
    slabs, owners = lax.axis_size("rows"), lax.axis_size("cols")
    layers = slabs // 2
    per_owner = tile_order.shape[0] // owners
    slab_width = tile_width // slabs
    f32, bf16 = jnp.float32, jnp.bfloat16
    vmem, anywhere = pl.BlockSpec(memory_space=pltpu.VMEM), pl.BlockSpec(memory_space=pl.ANY)
    params = pltpu.CompilerParams(vmem_limit_bytes=24 << 20)
    shaped = jax.ShapeDtypeStruct

    def in_hbm(value):
        return pltpu.with_memory_space_constraint(value, pltpu.HBM)

    lane_group = CAP * block_rows
    post = layers * lane_group
    wide = CAP * rows
    sizes = (layers, owners, per_owner, block_count, slot_count, block_rows, tile_width)
    weighted, *parcels, factor = pl.pallas_call(
        functools.partial(pack_kernel, sizes),
        out_shape=[shaped((rows, panel_width), bf16)]
        + [shaped((rows, post + wide), bf16)] * owners
        + [shaped(factor_inverse.shape, f32)],
        in_specs=[anywhere] * 7,
        out_specs=[vmem] * (owners + 2),
        scratch_shapes=[
            pltpu.SMEM(tile_lists.shape, jnp.int32),
            pltpu.SMEM(tile_masks.shape, jnp.int32),
            pltpu.SMEM(tile_order.shape, jnp.int32),
            pltpu.VMEM((1, rows), f32),
            pltpu.VMEM(panel_jac.shape, bf16),
            pltpu.VMEM(jac.shape, bf16),
            pltpu.SMEM(tile_order.shape, jnp.int32),
            pltpu.VMEM((block_count * slot_count * tile_width, block_rows), bf16),
            pltpu.SemaphoreType.DMA((7,)),
        ],
        compiler_params=params,
        name="pack",
    )(*map(in_hbm, (tile_lists, tile_masks, tile_order, weights.reshape(1, rows), panel_jac, jac, factor_inverse)))
    line = [shift(weighted, k, 0) for k in range(1, layers)]
    parcels = [parcels[0]] + [shift(parcels[e], 0, e) for e in range(1, owners)]

    column = pl.pallas_call(
        stack_kernel,
        out_shape=shaped((layers * rows, panel_width), bf16),
        in_specs=[vmem] * layers,
        out_specs=vmem,
        compiler_params=params,
        cost_estimate=lasting(10**10),
        name="stack",
    )(*reversed(line), weighted)
    posts = pl.pallas_call(
        functools.partial(sort_kernel, (layers, owners, lane_group)),
        out_shape=[shaped((rows + 16, owners * lane_group), bf16)] * layers,
        in_specs=[vmem] * owners,
        out_specs=[vmem] * layers,
        compiler_params=params,
        cost_estimate=lasting(10**10),
        name="sort",
    )(*parcels)
    posts = [posts[0]] + [shift(posts[k], k, 0) for k in range(1, layers)]
    by_x, by_y = shift(column, 0, 1), shift(column, 0, 2)


    def cut(kernel, value, name):
        return pl.pallas_call(
            kernel,
            out_shape=shaped((value.shape[0] // 2, panel_width), bf16),
            in_specs=[vmem],
            out_specs=vmem,
            compiler_params=params,
            name=name,
        )(value)

    rows_to_y, rows_to_x = cut(first_kernel, by_x, "first"), cut(last_kernel, by_y, "last")
    across_y, across_x = shift(rows_to_y, 0, 2), shift(rows_to_x, 0, 1)
    turned = pl.pallas_call(
        turn_kernel,
        out_shape=shaped((2, *factor_inverse.shape), bf16),
        in_specs=[vmem],
        out_specs=vmem,
        compiler_params=params,
        name="turn",
    )(factor)
    count = per_owner * slab_width
    depth = layers * rows
    sizes = (layers, owners, per_owner, block_count, block_rows)
    result = shaped((count, panel_width), f32)
    panels = [column, by_x, by_y]
    own, other = pl.pallas_call(
        functools.partial(near_kernel, sizes, 3),
        out_shape=[result, shaped((count, panel_width), bf16)],
        in_specs=[anywhere] * 3 + [vmem] * (len(panels) + layers),
        out_specs=[vmem] * 2,
        scratch_shapes=[
            pltpu.VMEM((count, (owners - 1) * depth), bf16),
            pltpu.VMEM(((owners - 1) * depth, panel_width), bf16),
        ],
        compiler_params=params,
        cost_estimate=lasting(10**9),
        name="near",
    )(rows_to_y, rows_to_x, turned, *panels, *posts)
    other = shift(other, 0, 0, 1)
    own = pl.pallas_call(
        own_kernel,
        out_shape=result,
        in_specs=[vmem] * 2,
        out_specs=vmem,
        compiler_params=params,
        cost_estimate=lasting(10**9),
        name="own",
    )(own, turned)
    joined = pl.pallas_call(
        functools.partial(join_kernel, (layers, lane_group, wide)),
        out_shape=shaped((depth + rows // 2 + 16, panel_width), bf16),
        in_specs=[vmem] * (2 + layers) + [anywhere],
        out_specs=vmem,
        compiler_params=params,
        cost_estimate=lasting(10**10),
        name="join",
    )(across_y, across_x, *posts, own)
    other_joined = shift(joined, 0, 0, 1)
    far_scratch = [pltpu.VMEM((count, depth), bf16)] + [pltpu.VMEM((depth, panel_width), bf16)] * 2
    far = pl.pallas_call(
        functools.partial(far_kernel, sizes),
        out_shape=result,
        in_specs=[vmem] * 2,
        out_specs=vmem,
        scratch_shapes=far_scratch,
        compiler_params=params,
        name="far",
    )(joined, turned)
    middle = pl.pallas_call(
        middle_kernel,
        out_shape=result,
        in_specs=[vmem] * 4,
        out_specs=vmem,
        compiler_params=params,
        name="middle",
    )(own, other, far, turned)
    out = pl.pallas_call(
        functools.partial(final_kernel, sizes),
        out_shape=result,
        in_specs=[vmem] * 3,
        out_specs=anywhere,
        scratch_shapes=[pltpu.VMEM((count, panel_width), f32)] + far_scratch + [pltpu.SemaphoreType.DMA((4,))],
        compiler_params=params,
        name="final",
    )(middle, other_joined, turned)
    return out.reshape(per_owner, slab_width, panel_width)


def solution(mesh):
    in_specs = (
        P(("rows", "cols"), None),
        P(("rows", "cols"), None),
        P(("rows", "cols")),
        P(("rows", "cols"), None),
        P(("rows", "cols"), None),
        P(),
        P(),
    )
    out_specs = P("cols", "rows", None)
    body = local if (mesh.shape["rows"], mesh.shape["cols"]) == (8, 4) else local_general
    return jax.shard_map(body, mesh=mesh, in_specs=in_specs, out_specs=out_specs, check_vma=False)
```

```python
import functools

import jax
import jax.numpy as jnp
from jax import lax
from jax.experimental import pallas as pl
from jax.experimental.pallas import tpu as pltpu
from jax.sharding import PartitionSpec as P

CAP = 2
GATHERED = 1 << 22


def tile_positions(tile_lists, tile_order):
    tile_count = tile_order.shape[0]
    matches = tile_lists[:, :, None] == tile_order[None, None, :]
    return jnp.sum(jnp.where(matches, jnp.arange(tile_count, dtype=jnp.int32), 0), axis=2)


def apply_inverse(tiles, factor_inverse):
    return jnp.einsum("ntp,qp->ntq", tiles, factor_inverse, precision=lax.Precision.HIGHEST)


def slot_codes(tile_lists, tile_masks, tile_order, owner_ids):
    block_count, slot_count = tile_lists.shape
    per_owner = tile_order.shape[0] // lax.axis_size("cols")
    positions = tile_positions(tile_lists, tile_order).reshape(-1)
    active = tile_masks.reshape(-1) == 1
    owner = positions // per_owner
    same = (owner[:, None] == owner[None, :]) & active[None, :]
    earlier = jnp.tril(jnp.ones(same.shape, bool), -1)
    rank = jnp.sum(same & earlier, axis=1)
    code = (
        (owner[None, None, :] == owner_ids[:, None, None])
        & (rank[None, None, :] == jnp.arange(CAP)[None, :, None])
        & active[None, None, :]
    )
    block = jnp.arange(block_count * slot_count) // slot_count
    place = positions % per_owner + per_owner * block
    return code, jnp.sum(jnp.where(code, place + 1, 0), axis=2) - 1


def local_general(jac, panel_jac, weights, tile_lists, tile_masks, tile_order, factor_inverse):
    block_count, slot_count = tile_lists.shape
    block_rows = jac.shape[0] // block_count
    tile_width = jac.shape[1] // slot_count
    slabs, owners = lax.axis_size("rows"), lax.axis_size("cols")
    devices = slabs * owners
    per_owner = tile_order.shape[0] // owners
    slab_width = tile_width // slabs
    bf16 = jnp.bfloat16
    weighted = (weights[:, None] * panel_jac).astype(bf16)
    code, places = slot_codes(tile_lists, tile_masks, tile_order, jnp.arange(owners))
    columns = jac.reshape(block_count, block_rows, slot_count, slabs, slab_width)
    chosen = code.astype(bf16).reshape(owners, CAP, block_count, slot_count)
    pieces = jnp.einsum("cjbk,bmkrt->rcjmt", chosen, columns, preferred_element_type=jnp.float32).astype(bf16)
    pieces = pieces.reshape(devices, -1)
    note = jnp.broadcast_to(places.astype(bf16)[None], (slabs, owners, CAP)).reshape(devices, CAP)
    note = jnp.pad(note, ((0, 0), (0, 128 - CAP)))
    sent = jnp.concatenate([pieces, note], axis=1)
    got = lax.all_to_all(sent, ("rows", "cols"), split_axis=0, concat_axis=0, tiled=True)
    size = pieces.shape[1]
    data = got[:, :size].reshape(devices, CAP, block_rows, slab_width)
    where = got[:, size : size + CAP].astype(jnp.int32)
    hot = (where[:, :, None] == jnp.arange(block_count * per_owner)).astype(bf16)
    hot = hot.reshape(devices, CAP, block_count, per_owner)
    mixed = jnp.einsum("djbn,djmt->dbmnt", hot, data, preferred_element_type=jnp.float32).astype(bf16)
    strips = max(1, devices * weighted.size * 2 // GATHERED)

    def strip_gram(strip):
        panels = lax.all_gather(strip, ("rows", "cols"), axis=0, tiled=True)
        panels = panels.reshape(devices, block_count, block_rows, -1)
        return jnp.einsum("dbmnt,dbmp->ntp", mixed, panels, preferred_element_type=jnp.float32)

    if strips == 1:
        gram = strip_gram(weighted)
    else:
        narrow = weighted.reshape(weighted.shape[0], strips, -1).swapaxes(0, 1)
        gram = jnp.moveaxis(lax.map(strip_gram, narrow), 0, 2)
        gram = gram.reshape(per_owner, slab_width, -1)
    return apply_inverse(gram, factor_inverse)


def shift(value, steps_z, flip_cols, flip_core=0):
    slabs, owners = lax.axis_size("rows"), lax.axis_size("cols")
    pairs = []
    for r in range(slabs):
        to_r = ((r // 2 + steps_z) % (slabs // 2)) * 2 + ((r % 2) ^ flip_core)
        for c in range(owners):
            pairs.append((r * owners + c, to_r * owners + (c ^ flip_cols)))
    return lax.ppermute(value, ("rows", "cols"), pairs)


def lasting(flops):
    return pl.CostEstimate(flops=flops, bytes_accessed=0, transcendentals=0)


def pack_kernel(sizes, lists_hbm, masks_hbm, order_hbm, weights_hbm, panel_hbm, jac_hbm, factor_hbm, *refs):
    layers, owners, per_owner, block_count, slot_count, block_rows, tile_width = sizes
    weighted_ref, parcels, factor_ref = refs[0], refs[1 : 1 + owners], refs[1 + owners]
    lists_ref, masks_ref, order_ref, weights_ref, panel_ref, jac_ref, places_ref, turned_ref, sems = refs[2 + owners :]
    copies = [
        pltpu.make_async_copy(order_hbm, order_ref, sems.at[0]),
        pltpu.make_async_copy(lists_hbm, lists_ref, sems.at[1]),
        pltpu.make_async_copy(masks_hbm, masks_ref, sems.at[2]),
        pltpu.make_async_copy(weights_hbm, weights_ref, sems.at[3]),
        pltpu.make_async_copy(panel_hbm, panel_ref, sems.at[4]),
        pltpu.make_async_copy(jac_hbm, jac_ref, sems.at[5]),
    ]
    for copy in copies:
        copy.start()
    factor_copy = pltpu.make_async_copy(factor_hbm, factor_ref, sems.at[6])
    factor_copy.start()
    f32, bf16 = jnp.float32, jnp.bfloat16
    rows, width = panel_ref.shape
    lane_group = CAP * block_rows
    post = layers * lane_group
    slab = tile_width // layers
    part = slab // 2
    me_r, me_c = lax.axis_index("rows"), lax.axis_index("cols")
    me_z, me_core = me_r // 2, lax.rem(me_r, 2)
    for copy in copies:
        copy.wait()

    row_ids = lax.broadcasted_iota(jnp.int32, (rows, rows), 0)
    lane_ids = lax.broadcasted_iota(jnp.int32, (rows, rows), 1)
    column = jnp.sum(jnp.where(row_ids == lane_ids, weights_ref[...], 0.0), axis=1, keepdims=True)
    weighted = (column * panel_ref[...].astype(f32)).astype(bf16)
    weighted_ref[...] = weighted

    for b in range(block_count):
        block = jac_ref[b * block_rows : (b + 1) * block_rows, :].astype(f32)
        start = b * slot_count * tile_width
        turned_ref[start : start + slot_count * tile_width, :] = block.T.astype(bf16)

    for i in range(order_ref.shape[0]):
        places_ref[order_ref[i]] = i
    slots = []
    for s in range(block_count * slot_count):
        b, k = divmod(s, slot_count)
        place = places_ref[lists_ref[b, k]]
        owner = jnp.int32(0)
        for c in range(1, owners):
            owner += (place >= c * per_owner).astype(jnp.int32)
        slots.append((place - owner * per_owner, jnp.where(masks_ref[b, k] == 1, owner, -1)))

    shape = (16, CAP * block_count * block_rows)
    lane = lax.broadcasted_iota(jnp.int32, shape, 1)
    for e, parcel in enumerate(parcels):
        wanted = me_c ^ e
        found = jnp.int32(0)
        chosen = [jnp.int32(0)] * CAP
        codes = [jnp.int32(-1)] * CAP
        for s, (place, owner) in enumerate(slots):
            hit = owner == wanted
            for j in range(CAP):
                take = hit & (found == j)
                chosen[j] = jnp.where(take, s, chosen[j])
                codes[j] = jnp.where(take, place, codes[j])
            found += hit.astype(jnp.int32)
        note = jnp.full(shape, -1, jnp.int32)
        for j in range(CAP):
            for b in range(block_count):
                at = (j * block_count + b) * block_rows
                here = (lane >= at) & (lane < at + block_rows)
                code = jnp.where(chosen[j] // slot_count == b, codes[j], -1)
                note = jnp.where(here, code, note)
        parcel[:16, post:] = note.astype(f32).astype(bf16)
        for u in range(2):
            core = me_core ^ u
            for k in range(0, layers, 2):
                pieces = []
                for z in (lax.rem(me_z + k, layers), lax.rem(me_z + k + 1, layers)):
                    for j in range(CAP):
                        first = pl.multiple_of(chosen[j] * tile_width + z * slab + core * part, part)
                        pieces.append(turned_ref[pl.ds(first, part), :])
                lanes = slice(k * lane_group, (k + 2) * lane_group)
                parcel[u * part : (u + 1) * part, lanes] = jnp.concatenate(pieces, axis=1)
    factor_copy.wait()


def row_of(block, i):
    ids = lax.broadcasted_iota(jnp.int32, block.shape, 0)
    return jnp.sum(jnp.where(ids == i, block.astype(jnp.float32), 0.0), axis=0, keepdims=True)


def rows_from(notes):
    ids = lax.broadcasted_iota(jnp.int32, (16, notes[0].shape[1]), 0)
    block = jnp.full(ids.shape, -1.0, jnp.float32)
    for i, note in enumerate(notes):
        block = jnp.where(ids == i, note, block)
    return block.astype(jnp.bfloat16)


def stack_kernel(*refs):
    inputs, out_ref = refs[:-1], refs[-1]
    rows = inputs[0].shape[0]
    for i, ref in enumerate(reversed(inputs)):
        out_ref[i * rows : (i + 1) * rows, :] = ref[...]


def sort_kernel(sizes, *refs):
    layers, owners, lane_group = sizes
    parcels, posts = (refs[0], refs[3], refs[2], refs[1]), refs[owners:]
    rows, codes_at = parcels[0].shape[0], layers * lane_group
    block = rows_from([row_of(parcel[:16, codes_at:], 0) for parcel in parcels])
    for k, out in enumerate(posts):
        for e, parcel in enumerate(parcels):
            piece = parcel[:, k * lane_group : (k + 1) * lane_group]
            out[:rows, e * lane_group : (e + 1) * lane_group] = piece
        out[rows:, : block.shape[1]] = block


def first_kernel(in_ref, out_ref):
    out_ref[...] = in_ref[: out_ref.shape[0], :]


def last_kernel(in_ref, out_ref):
    out_ref[...] = in_ref[in_ref.shape[0] - out_ref.shape[0] :, :]


def place(out_ref, lanes, per_owner, pieces, notes, sizes):
    block_count, block_rows = sizes
    f32, bf16 = jnp.float32, jnp.bfloat16
    part, rows = pieces[0].shape[0], block_count * block_rows
    columns, codes = [], []
    for j in range(CAP):
        parts = []
        for piece in pieces:
            parts += [piece[:, j * block_rows : (j + 1) * block_rows].astype(f32)] * block_count
        columns.append(jnp.concatenate(parts, axis=1).astype(bf16))
        note = jnp.concatenate([note[:, j * rows : (j + 1) * rows] for note in notes], axis=1)
        codes.append(jnp.broadcast_to(note, columns[j].shape).astype(bf16))
    for n in range(per_owner):
        placed = jnp.zeros(columns[0].shape, bf16)
        for j in range(CAP):
            placed = jnp.where(codes[j] == jnp.asarray(n, bf16), columns[j], placed)
        out_ref[n * part : (n + 1) * part, lanes] = placed


def inverse_rows(rows_ref, factor_ref, high_ref, low_ref):
    f32, bf16 = jnp.float32, jnp.bfloat16
    height, width = high_ref.shape
    for start, stop in ((0, width // 2), (width // 2, width)):
        rows = rows_ref[:height, :stop]
        total = jnp.dot(rows, factor_ref[0, :stop, start:stop], preferred_element_type=f32)
        total += jnp.dot(rows, factor_ref[1, :stop, start:stop], preferred_element_type=f32)
        high = total.astype(bf16)
        high_ref[:, start:stop] = high
        low_ref[:, start:stop] = (total - high.astype(f32)).astype(bf16)


def turn_kernel(factor_ref, out_ref):
    turned = factor_ref[...].T
    high = turned.astype(jnp.bfloat16)
    out_ref[0, :, :] = high
    out_ref[1, :, :] = (turned - high.astype(jnp.float32)).astype(jnp.bfloat16)


def near_kernel(sizes, earlier, *refs):
    layers, owners, per_owner, block_count, block_rows = sizes
    panels, posts, refs = refs[earlier : earlier + 3], refs[earlier + 3 : earlier + 3 + layers], refs[earlier + 3 + layers :]
    own_ref, other_ref, placed_ref, rows_ref = refs
    f32, bf16 = jnp.float32, jnp.bfloat16
    rows = block_count * block_rows
    group, wide = CAP * block_rows, CAP * rows
    part = rows // 2
    width = rows_ref.shape[1]
    at = 0
    for panel in panels:
        rows_ref[at : at + panel.shape[0], :] = panel[:, :width]
        at += panel.shape[0]
    for u, out_ref in ((1, other_ref), (0, own_ref)):
        for e in range(owners - 1):
            for h in range(layers // 2):
                pair = posts[2 * h : 2 * h + 2]
                pieces = [post[u * part : (u + 1) * part, e * group : (e + 1) * group] for post in pair]
                notes = [row_of(post[rows:, :wide], e) for post in pair]
                start = (e * layers + 2 * h) * rows
                place(placed_ref, slice(start, start + 2 * rows), per_owner, pieces, notes, (block_count, block_rows))
        gram = jnp.dot(placed_ref[...], rows_ref[...], preferred_element_type=f32)
        out_ref[...] = gram.astype(out_ref.dtype)


def join_kernel(sizes, above_ref, below_ref, *refs):
    layers, lane_group, wide = sizes
    posts, out_ref = refs[:layers], refs[-1]
    half, rows = above_ref.shape[0], posts[0].shape[0] - 16
    part, depth = rows // 2, 2 * half
    out_ref[:half, :] = above_ref[...]
    out_ref[half:depth, :] = below_ref[...]
    for k, ref in enumerate(posts):
        for u in range(2):
            piece = ref[u * part : (u + 1) * part, 3 * lane_group : 4 * lane_group]
            at = (u * layers + k) * lane_group
            out_ref[depth : depth + part, at : at + lane_group] = piece
    out_ref[depth + part :, :wide] = rows_from([row_of(ref[rows:, :wide], 3) for ref in posts])


def place_far(sizes, u, ref, placed_ref):
    layers, owners, per_owner, block_count, block_rows = sizes
    rows = block_count * block_rows
    group, wide = CAP * block_rows, CAP * rows
    part, depth = rows // 2, layers * rows
    for h in range(layers // 2):
        pieces, notes = [], []
        for k in (2 * h, 2 * h + 1):
            at = (u * layers + k) * group
            pieces.append(ref[depth : depth + part, at : at + group])
            notes.append(row_of(ref[depth + part :, :wide], k))
        lanes = slice(2 * h * rows, 2 * (h + 1) * rows)
        place(placed_ref, lanes, per_owner, pieces, notes, (block_count, block_rows))


def far_kernel(sizes, joined_ref, turned_ref, out_ref, placed_ref, high_ref, low_ref):
    place_far(sizes, 0, joined_ref, placed_ref)
    inverse_rows(joined_ref, turned_ref, high_ref, low_ref)
    placed = placed_ref[...]
    total = jnp.dot(placed, high_ref[...], preferred_element_type=jnp.float32)
    out_ref[...] = total + jnp.dot(placed, low_ref[...], preferred_element_type=jnp.float32)


def times_inverse(out_ref, terms, turned_ref, added):
    width = out_ref.shape[1]
    for start, stop in ((0, width // 2), (width // 2, width)):
        total = sum(ref[:, start:stop] for ref in added)
        for i, j in ((0, 0), (0, 1), (1, 0))[: len(terms) + 1]:
            total += jnp.dot(terms[i][:, :stop], turned_ref[j, :stop, start:stop], preferred_element_type=jnp.float32)
        out_ref[:, start:stop] = total


def own_kernel(own_ref, turned_ref, out_ref):
    high = own_ref[...].astype(jnp.bfloat16)
    low = (own_ref[...] - high.astype(jnp.float32)).astype(jnp.bfloat16)
    times_inverse(out_ref, (high, low), turned_ref, ())


def middle_kernel(own_ref, other_ref, far_ref, turned_ref, out_ref):
    times_inverse(out_ref, (other_ref[...],), turned_ref, (own_ref, far_ref))


def final_kernel(sizes, middle_ref, joined_ref, turned_ref, out_hbm, sum_ref, placed_ref, high_ref, low_ref, sems):
    f32 = jnp.float32
    place_far(sizes, 1, joined_ref, placed_ref)
    inverse_rows(joined_ref, turned_ref, high_ref, low_ref)
    strips = sems.shape[0]
    height = sum_ref.shape[0] // strips
    copies = []
    for i in range(strips):
        here = pl.ds(i * height, height)
        placed = placed_ref[here, :]
        total = middle_ref[here, :] + jnp.dot(placed, high_ref[...], preferred_element_type=f32)
        sum_ref[here, :] = total + jnp.dot(placed, low_ref[...], preferred_element_type=f32)
        copies.append(pltpu.make_async_copy(sum_ref.at[here, :], out_hbm.at[here, :], sems.at[i]))
        copies[-1].start()
    for copy in copies:
        copy.wait()


def local(jac, panel_jac, weights, tile_lists, tile_masks, tile_order, factor_inverse):
    block_count, slot_count = tile_lists.shape
    rows, panel_width = panel_jac.shape
    block_rows = rows // block_count
    tile_width = jac.shape[1] // slot_count
    slabs, owners = lax.axis_size("rows"), lax.axis_size("cols")
    layers = slabs // 2
    per_owner = tile_order.shape[0] // owners
    slab_width = tile_width // slabs
    f32, bf16 = jnp.float32, jnp.bfloat16
    vmem, anywhere = pl.BlockSpec(memory_space=pltpu.VMEM), pl.BlockSpec(memory_space=pl.ANY)
    params = pltpu.CompilerParams(vmem_limit_bytes=24 << 20)
    shaped = jax.ShapeDtypeStruct

    def in_hbm(value):
        return pltpu.with_memory_space_constraint(value, pltpu.HBM)

    lane_group = CAP * block_rows
    post = layers * lane_group
    wide = CAP * rows
    sizes = (layers, owners, per_owner, block_count, slot_count, block_rows, tile_width)
    weighted, *parcels, factor = pl.pallas_call(
        functools.partial(pack_kernel, sizes),
        out_shape=[shaped((rows, panel_width), bf16)]
        + [shaped((rows, post + wide), bf16)] * owners
        + [shaped(factor_inverse.shape, f32)],
        in_specs=[anywhere] * 7,
        out_specs=[vmem] * (owners + 2),
        scratch_shapes=[
            pltpu.SMEM(tile_lists.shape, jnp.int32),
            pltpu.SMEM(tile_masks.shape, jnp.int32),
            pltpu.SMEM(tile_order.shape, jnp.int32),
            pltpu.VMEM((1, rows), f32),
            pltpu.VMEM(panel_jac.shape, bf16),
            pltpu.VMEM(jac.shape, bf16),
            pltpu.SMEM(tile_order.shape, jnp.int32),
            pltpu.VMEM((block_count * slot_count * tile_width, block_rows), bf16),
            pltpu.SemaphoreType.DMA((7,)),
        ],
        compiler_params=params,
        name="pack",
    )(*map(in_hbm, (tile_lists, tile_masks, tile_order, weights.reshape(1, rows), panel_jac, jac, factor_inverse)))
    line = [shift(weighted, k, 0) for k in range(1, layers)]
    parcels = [parcels[0]] + [shift(parcels[e], 0, e) for e in range(1, owners)]

    column = pl.pallas_call(
        stack_kernel,
        out_shape=shaped((layers * rows, panel_width), bf16),
        in_specs=[vmem] * layers,
        out_specs=vmem,
        compiler_params=params,
        cost_estimate=lasting(10**10),
        name="stack",
    )(*reversed(line), weighted)
    posts = pl.pallas_call(
        functools.partial(sort_kernel, (layers, owners, lane_group)),
        out_shape=[shaped((rows + 16, owners * lane_group), bf16)] * layers,
        in_specs=[vmem] * owners,
        out_specs=[vmem] * layers,
        compiler_params=params,
        cost_estimate=lasting(10**10),
        name="sort",
    )(parcels[0], parcels[3], parcels[2], parcels[1])
    posts = [posts[0]] + [shift(posts[k], k, 0) for k in range(1, layers)]
    by_x, by_y = shift(column, 0, 1), shift(column, 0, 2)


    def cut(kernel, value, name):
        return pl.pallas_call(
            kernel,
            out_shape=shaped((value.shape[0] // 2, panel_width), bf16),
            in_specs=[vmem],
            out_specs=vmem,
            compiler_params=params,
            name=name,
        )(value)

    rows_to_y, rows_to_x = cut(first_kernel, by_x, "first"), cut(last_kernel, by_y, "last")
    across_y, across_x = shift(rows_to_y, 0, 2), shift(rows_to_x, 0, 1)
    turned = pl.pallas_call(
        turn_kernel,
        out_shape=shaped((2, *factor_inverse.shape), bf16),
        in_specs=[vmem],
        out_specs=vmem,
        compiler_params=params,
        name="turn",
    )(factor)
    count = per_owner * slab_width
    depth = layers * rows
    sizes = (layers, owners, per_owner, block_count, block_rows)
    result = shaped((count, panel_width), f32)
    panels = [column, by_x, by_y]
    own, other = pl.pallas_call(
        functools.partial(near_kernel, sizes, 3),
        out_shape=[result, shaped((count, panel_width), bf16)],
        in_specs=[anywhere] * 3 + [vmem] * (len(panels) + layers),
        out_specs=[vmem] * 2,
        scratch_shapes=[
            pltpu.VMEM((count, (owners - 1) * depth), bf16),
            pltpu.VMEM(((owners - 1) * depth, panel_width), bf16),
        ],
        compiler_params=params,
        cost_estimate=lasting(10**9),
        name="near",
    )(rows_to_y, rows_to_x, turned, *panels, *posts)
    other = shift(other, 0, 0, 1)
    own = pl.pallas_call(
        own_kernel,
        out_shape=result,
        in_specs=[vmem] * 2,
        out_specs=vmem,
        compiler_params=params,
        cost_estimate=lasting(10**9),
        name="own",
    )(own, turned)
    joined = pl.pallas_call(
        functools.partial(join_kernel, (layers, lane_group, wide)),
        out_shape=shaped((depth + rows // 2 + 16, panel_width), bf16),
        in_specs=[vmem] * (2 + layers) + [anywhere],
        out_specs=vmem,
        compiler_params=params,
        cost_estimate=lasting(10**10),
        name="join",
    )(across_y, across_x, *posts, own)
    other_joined = shift(joined, 0, 0, 1)
    far_scratch = [pltpu.VMEM((count, depth), bf16)] + [pltpu.VMEM((depth, panel_width), bf16)] * 2
    far = pl.pallas_call(
        functools.partial(far_kernel, sizes),
        out_shape=result,
        in_specs=[vmem] * 2,
        out_specs=vmem,
        scratch_shapes=far_scratch,
        compiler_params=params,
        name="far",
    )(joined, turned)
    middle = pl.pallas_call(
        middle_kernel,
        out_shape=result,
        in_specs=[vmem] * 4,
        out_specs=vmem,
        compiler_params=params,
        name="middle",
    )(own, other, far, turned)
    out = pl.pallas_call(
        functools.partial(final_kernel, sizes),
        out_shape=result,
        in_specs=[vmem] * 3,
        out_specs=anywhere,
        scratch_shapes=[pltpu.VMEM((count, panel_width), f32)] + far_scratch + [pltpu.SemaphoreType.DMA((4,))],
        compiler_params=params,
        name="final",
    )(middle, other_joined, turned)
    return out.reshape(per_owner, slab_width, panel_width)


def solution(mesh):
    in_specs = (
        P(("rows", "cols"), None),
        P(("rows", "cols"), None),
        P(("rows", "cols")),
        P(("rows", "cols"), None),
        P(("rows", "cols"), None),
        P(),
        P(),
    )
    out_specs = P("cols", "rows", None)
    body = local if (mesh.shape["rows"], mesh.shape["cols"]) == (8, 4) else local_general
    return jax.shard_map(body, mesh=mesh, in_specs=in_specs, out_specs=out_specs, check_vma=False)
```

```python
import functools

import jax
import jax.numpy as jnp
from jax import lax
from jax.experimental import pallas as pl
from jax.experimental.pallas import tpu as pltpu
from jax.sharding import PartitionSpec as P

CAP = 2
GATHERED = 1 << 22


def tile_positions(tile_lists, tile_order):
    tile_count = tile_order.shape[0]
    matches = tile_lists[:, :, None] == tile_order[None, None, :]
    return jnp.sum(jnp.where(matches, jnp.arange(tile_count, dtype=jnp.int32), 0), axis=2)


def apply_inverse(tiles, factor_inverse):
    return jnp.einsum("ntp,qp->ntq", tiles, factor_inverse, precision=lax.Precision.HIGHEST)


def slot_codes(tile_lists, tile_masks, tile_order, owner_ids):
    block_count, slot_count = tile_lists.shape
    per_owner = tile_order.shape[0] // lax.axis_size("cols")
    positions = tile_positions(tile_lists, tile_order).reshape(-1)
    active = tile_masks.reshape(-1) == 1
    owner = positions // per_owner
    same = (owner[:, None] == owner[None, :]) & active[None, :]
    earlier = jnp.tril(jnp.ones(same.shape, bool), -1)
    rank = jnp.sum(same & earlier, axis=1)
    code = (
        (owner[None, None, :] == owner_ids[:, None, None])
        & (rank[None, None, :] == jnp.arange(CAP)[None, :, None])
        & active[None, None, :]
    )
    block = jnp.arange(block_count * slot_count) // slot_count
    place = positions % per_owner + per_owner * block
    return code, jnp.sum(jnp.where(code, place + 1, 0), axis=2) - 1


def local_general(jac, panel_jac, weights, tile_lists, tile_masks, tile_order, factor_inverse):
    block_count, slot_count = tile_lists.shape
    block_rows = jac.shape[0] // block_count
    tile_width = jac.shape[1] // slot_count
    slabs, owners = lax.axis_size("rows"), lax.axis_size("cols")
    devices = slabs * owners
    per_owner = tile_order.shape[0] // owners
    slab_width = tile_width // slabs
    bf16 = jnp.bfloat16
    weighted = (weights[:, None] * panel_jac).astype(bf16)
    code, places = slot_codes(tile_lists, tile_masks, tile_order, jnp.arange(owners))
    columns = jac.reshape(block_count, block_rows, slot_count, slabs, slab_width)
    chosen = code.astype(bf16).reshape(owners, CAP, block_count, slot_count)
    pieces = jnp.einsum("cjbk,bmkrt->rcjmt", chosen, columns, preferred_element_type=jnp.float32).astype(bf16)
    pieces = pieces.reshape(devices, -1)
    note = jnp.broadcast_to(places.astype(bf16)[None], (slabs, owners, CAP)).reshape(devices, CAP)
    note = jnp.pad(note, ((0, 0), (0, 128 - CAP)))
    sent = jnp.concatenate([pieces, note], axis=1)
    got = lax.all_to_all(sent, ("rows", "cols"), split_axis=0, concat_axis=0, tiled=True)
    size = pieces.shape[1]
    data = got[:, :size].reshape(devices, CAP, block_rows, slab_width)
    where = got[:, size : size + CAP].astype(jnp.int32)
    hot = (where[:, :, None] == jnp.arange(block_count * per_owner)).astype(bf16)
    hot = hot.reshape(devices, CAP, block_count, per_owner)
    mixed = jnp.einsum("djbn,djmt->dbmnt", hot, data, preferred_element_type=jnp.float32).astype(bf16)
    strips = max(1, devices * weighted.size * 2 // GATHERED)

    def strip_gram(strip):
        panels = lax.all_gather(strip, ("rows", "cols"), axis=0, tiled=True)
        panels = panels.reshape(devices, block_count, block_rows, -1)
        return jnp.einsum("dbmnt,dbmp->ntp", mixed, panels, preferred_element_type=jnp.float32)

    if strips == 1:
        gram = strip_gram(weighted)
    else:
        narrow = weighted.reshape(weighted.shape[0], strips, -1).swapaxes(0, 1)
        gram = jnp.moveaxis(lax.map(strip_gram, narrow), 0, 2)
        gram = gram.reshape(per_owner, slab_width, -1)
    return apply_inverse(gram, factor_inverse)


def shift(value, steps_z, flip_cols, flip_core=0):
    slabs, owners = lax.axis_size("rows"), lax.axis_size("cols")
    pairs = []
    for r in range(slabs):
        to_r = ((r // 2 + steps_z) % (slabs // 2)) * 2 + ((r % 2) ^ flip_core)
        for c in range(owners):
            pairs.append((r * owners + c, to_r * owners + (c ^ flip_cols)))
    return lax.ppermute(value, ("rows", "cols"), pairs)


def lasting(flops):
    return pl.CostEstimate(flops=flops, bytes_accessed=0, transcendentals=0)


def pack_kernel(sizes, lists_hbm, masks_hbm, order_hbm, weights_hbm, panel_hbm, jac_hbm, factor_hbm, *refs):
    layers, owners, per_owner, block_count, slot_count, block_rows, tile_width = sizes
    weighted_ref, parcels, factor_ref = refs[0], refs[1 : 1 + owners], refs[1 + owners]
    lists_ref, masks_ref, order_ref, weights_ref, panel_ref, jac_ref, places_ref, turned_ref, sems = refs[2 + owners :]
    copies = [
        pltpu.make_async_copy(order_hbm, order_ref, sems.at[0]),
        pltpu.make_async_copy(lists_hbm, lists_ref, sems.at[1]),
        pltpu.make_async_copy(masks_hbm, masks_ref, sems.at[2]),
        pltpu.make_async_copy(weights_hbm, weights_ref, sems.at[3]),
        pltpu.make_async_copy(panel_hbm, panel_ref, sems.at[4]),
        pltpu.make_async_copy(jac_hbm, jac_ref, sems.at[5]),
    ]
    for copy in copies:
        copy.start()
    factor_copy = pltpu.make_async_copy(factor_hbm, factor_ref, sems.at[6])
    factor_copy.start()
    f32, bf16 = jnp.float32, jnp.bfloat16
    rows, width = panel_ref.shape
    lane_group = CAP * block_rows
    post = layers * lane_group
    slab = tile_width // layers
    part = slab // 2
    me_r, me_c = lax.axis_index("rows"), lax.axis_index("cols")
    me_z, me_core = me_r // 2, lax.rem(me_r, 2)
    for copy in copies[:3]:
        copy.wait()
    for i in range(order_ref.shape[0]):
        places_ref[order_ref[i]] = i
    slots = []
    for s in range(block_count * slot_count):
        b, k = divmod(s, slot_count)
        place = places_ref[lists_ref[b, k]]
        owner = jnp.int32(0)
        for c in range(1, owners):
            owner += (place >= c * per_owner).astype(jnp.int32)
        slots.append((place - owner * per_owner, jnp.where(masks_ref[b, k] == 1, owner, -1)))

    found_slots = []
    for e in range(owners):
        wanted = me_c ^ e
        found = jnp.int32(0)
        chosen = [jnp.int32(0)] * CAP
        codes = [jnp.int32(-1)] * CAP
        for s, (place, owner) in enumerate(slots):
            hit = owner == wanted
            for j in range(CAP):
                take = hit & (found == j)
                chosen[j] = jnp.where(take, s, chosen[j])
                codes[j] = jnp.where(take, place, codes[j])
            found += hit.astype(jnp.int32)
        found_slots.append((chosen, codes))

    for copy in copies[3:]:
        copy.wait()

    row_ids = lax.broadcasted_iota(jnp.int32, (rows, rows), 0)
    lane_ids = lax.broadcasted_iota(jnp.int32, (rows, rows), 1)
    column = jnp.sum(jnp.where(row_ids == lane_ids, weights_ref[...], 0.0), axis=1, keepdims=True)
    weighted = (column * panel_ref[...].astype(f32)).astype(bf16)
    weighted_ref[...] = weighted

    for b in range(block_count):
        block = jac_ref[b * block_rows : (b + 1) * block_rows, :].astype(f32)
        start = b * slot_count * tile_width
        turned_ref[start : start + slot_count * tile_width, :] = block.T.astype(bf16)

    shape = (16, CAP * block_count * block_rows)
    lane = lax.broadcasted_iota(jnp.int32, shape, 1)
    for parcel, (chosen, codes) in zip(parcels, found_slots):
        note = jnp.full(shape, -1, jnp.int32)
        for j in range(CAP):
            for b in range(block_count):
                at = (j * block_count + b) * block_rows
                here = (lane >= at) & (lane < at + block_rows)
                code = jnp.where(chosen[j] // slot_count == b, codes[j], -1)
                note = jnp.where(here, code, note)
        parcel[:16, post:] = note.astype(f32).astype(bf16)
        for u in range(2):
            core = me_core ^ u
            for k in range(0, layers, 2):
                pieces = []
                for z in (lax.rem(me_z + k, layers), lax.rem(me_z + k + 1, layers)):
                    for j in range(CAP):
                        first = pl.multiple_of(chosen[j] * tile_width + z * slab + core * part, part)
                        pieces.append(turned_ref[pl.ds(first, part), :])
                lanes = slice(k * lane_group, (k + 2) * lane_group)
                parcel[u * part : (u + 1) * part, lanes] = jnp.concatenate(pieces, axis=1)
    factor_copy.wait()


def row_of(block, i):
    ids = lax.broadcasted_iota(jnp.int32, block.shape, 0)
    return jnp.sum(jnp.where(ids == i, block.astype(jnp.float32), 0.0), axis=0, keepdims=True)


def rows_from(notes):
    ids = lax.broadcasted_iota(jnp.int32, (16, notes[0].shape[1]), 0)
    block = jnp.full(ids.shape, -1.0, jnp.float32)
    for i, note in enumerate(notes):
        block = jnp.where(ids == i, note, block)
    return block.astype(jnp.bfloat16)


def stack_kernel(*refs):
    inputs, out_ref = refs[:-1], refs[-1]
    rows = inputs[0].shape[0]
    for i, ref in enumerate(reversed(inputs)):
        out_ref[i * rows : (i + 1) * rows, :] = ref[...]


def sort_kernel(sizes, *refs):
    layers, owners, lane_group = sizes
    parcels, posts = (refs[0], refs[3], refs[2], refs[1]), refs[owners:]
    rows, codes_at = parcels[0].shape[0], layers * lane_group
    block = rows_from([row_of(parcel[:16, codes_at:], 0) for parcel in parcels])
    for k, out in enumerate(posts):
        for e, parcel in enumerate(parcels):
            piece = parcel[:, k * lane_group : (k + 1) * lane_group]
            out[:rows, e * lane_group : (e + 1) * lane_group] = piece
        out[rows:, : block.shape[1]] = block


def first_kernel(in_ref, out_ref):
    out_ref[...] = in_ref[: out_ref.shape[0], :]


def last_kernel(in_ref, out_ref):
    out_ref[...] = in_ref[in_ref.shape[0] - out_ref.shape[0] :, :]


def place(out_ref, lanes, per_owner, pieces, notes, sizes):
    block_count, block_rows = sizes
    f32, bf16 = jnp.float32, jnp.bfloat16
    part, rows = pieces[0].shape[0], block_count * block_rows
    columns, codes = [], []
    for j in range(CAP):
        parts = []
        for piece in pieces:
            parts += [piece[:, j * block_rows : (j + 1) * block_rows].astype(f32)] * block_count
        columns.append(jnp.concatenate(parts, axis=1).astype(bf16))
        note = jnp.concatenate([note[:, j * rows : (j + 1) * rows] for note in notes], axis=1)
        codes.append(jnp.broadcast_to(note, columns[j].shape).astype(bf16))
    for n in range(per_owner):
        placed = jnp.zeros(columns[0].shape, bf16)
        for j in range(CAP):
            placed = jnp.where(codes[j] == jnp.asarray(n, bf16), columns[j], placed)
        out_ref[n * part : (n + 1) * part, lanes] = placed


def inverse_rows(rows_ref, factor_ref, high_ref, low_ref):
    f32, bf16 = jnp.float32, jnp.bfloat16
    height, width = high_ref.shape
    for start, stop in ((0, width // 2), (width // 2, width)):
        rows = rows_ref[:height, :stop]
        total = jnp.dot(rows, factor_ref[0, :stop, start:stop], preferred_element_type=f32)
        total += jnp.dot(rows, factor_ref[1, :stop, start:stop], preferred_element_type=f32)
        high = total.astype(bf16)
        high_ref[:, start:stop] = high
        low_ref[:, start:stop] = (total - high.astype(f32)).astype(bf16)


def turn_kernel(factor_ref, out_ref):
    turned = factor_ref[...].T
    high = turned.astype(jnp.bfloat16)
    out_ref[0, :, :] = high
    out_ref[1, :, :] = (turned - high.astype(jnp.float32)).astype(jnp.bfloat16)


def near_kernel(sizes, earlier, *refs):
    layers, owners, per_owner, block_count, block_rows = sizes
    panels, posts, refs = refs[earlier : earlier + 3], refs[earlier + 3 : earlier + 3 + layers], refs[earlier + 3 + layers :]
    own_ref, other_ref, placed_ref, rows_ref = refs
    f32, bf16 = jnp.float32, jnp.bfloat16
    rows = block_count * block_rows
    group, wide = CAP * block_rows, CAP * rows
    part = rows // 2
    width = rows_ref.shape[1]
    at = 0
    for panel in panels:
        rows_ref[at : at + panel.shape[0], :] = panel[:, :width]
        at += panel.shape[0]
    for u, out_ref in ((1, other_ref), (0, own_ref)):
        for e in range(owners - 1):
            for h in range(layers // 2):
                pair = posts[2 * h : 2 * h + 2]
                pieces = [post[u * part : (u + 1) * part, e * group : (e + 1) * group] for post in pair]
                notes = [row_of(post[rows:, :wide], e) for post in pair]
                start = (e * layers + 2 * h) * rows
                place(placed_ref, slice(start, start + 2 * rows), per_owner, pieces, notes, (block_count, block_rows))
        gram = jnp.dot(placed_ref[...], rows_ref[...], preferred_element_type=f32)
        out_ref[...] = gram.astype(out_ref.dtype)


def join_kernel(sizes, above_ref, below_ref, *refs):
    layers, lane_group, wide = sizes
    posts, out_ref = refs[:layers], refs[-1]
    half, rows = above_ref.shape[0], posts[0].shape[0] - 16
    part, depth = rows // 2, 2 * half
    out_ref[:half, :] = above_ref[...]
    out_ref[half:depth, :] = below_ref[...]
    for k, ref in enumerate(posts):
        for u in range(2):
            piece = ref[u * part : (u + 1) * part, 3 * lane_group : 4 * lane_group]
            at = (u * layers + k) * lane_group
            out_ref[depth : depth + part, at : at + lane_group] = piece
    out_ref[depth + part :, :wide] = rows_from([row_of(ref[rows:, :wide], 3) for ref in posts])


def place_far(sizes, u, ref, placed_ref):
    layers, owners, per_owner, block_count, block_rows = sizes
    rows = block_count * block_rows
    group, wide = CAP * block_rows, CAP * rows
    part, depth = rows // 2, layers * rows
    for h in range(layers // 2):
        pieces, notes = [], []
        for k in (2 * h, 2 * h + 1):
            at = (u * layers + k) * group
            pieces.append(ref[depth : depth + part, at : at + group])
            notes.append(row_of(ref[depth + part :, :wide], k))
        lanes = slice(2 * h * rows, 2 * (h + 1) * rows)
        place(placed_ref, lanes, per_owner, pieces, notes, (block_count, block_rows))


def far_kernel(sizes, joined_ref, turned_ref, out_ref, placed_ref, high_ref, low_ref):
    place_far(sizes, 0, joined_ref, placed_ref)
    inverse_rows(joined_ref, turned_ref, high_ref, low_ref)
    placed = placed_ref[...]
    total = jnp.dot(placed, high_ref[...], preferred_element_type=jnp.float32)
    out_ref[...] = total + jnp.dot(placed, low_ref[...], preferred_element_type=jnp.float32)


def times_inverse(out_ref, terms, turned_ref, added):
    width = out_ref.shape[1]
    for start, stop in ((0, width // 2), (width // 2, width)):
        total = sum(ref[:, start:stop] for ref in added)
        for i, j in ((0, 0), (0, 1), (1, 0))[: len(terms) + 1]:
            total += jnp.dot(terms[i][:, :stop], turned_ref[j, :stop, start:stop], preferred_element_type=jnp.float32)
        out_ref[:, start:stop] = total


def own_kernel(own_ref, turned_ref, out_ref):
    high = own_ref[...].astype(jnp.bfloat16)
    low = (own_ref[...] - high.astype(jnp.float32)).astype(jnp.bfloat16)
    times_inverse(out_ref, (high, low), turned_ref, ())


def middle_kernel(own_ref, other_ref, far_ref, turned_ref, out_ref):
    times_inverse(out_ref, (other_ref[...],), turned_ref, (own_ref, far_ref))


def final_kernel(sizes, middle_ref, joined_ref, turned_ref, out_hbm, sum_ref, placed_ref, high_ref, low_ref, sems):
    f32 = jnp.float32
    place_far(sizes, 1, joined_ref, placed_ref)
    inverse_rows(joined_ref, turned_ref, high_ref, low_ref)
    strips = sems.shape[0]
    height = sum_ref.shape[0] // strips
    copies = []
    for i in range(strips):
        here = pl.ds(i * height, height)
        placed = placed_ref[here, :]
        total = middle_ref[here, :] + jnp.dot(placed, high_ref[...], preferred_element_type=f32)
        sum_ref[here, :] = total + jnp.dot(placed, low_ref[...], preferred_element_type=f32)
        copies.append(pltpu.make_async_copy(sum_ref.at[here, :], out_hbm.at[here, :], sems.at[i]))
        copies[-1].start()
    for copy in copies:
        copy.wait()


def local(jac, panel_jac, weights, tile_lists, tile_masks, tile_order, factor_inverse):
    block_count, slot_count = tile_lists.shape
    rows, panel_width = panel_jac.shape
    block_rows = rows // block_count
    tile_width = jac.shape[1] // slot_count
    slabs, owners = lax.axis_size("rows"), lax.axis_size("cols")
    layers = slabs // 2
    per_owner = tile_order.shape[0] // owners
    slab_width = tile_width // slabs
    f32, bf16 = jnp.float32, jnp.bfloat16
    vmem, anywhere = pl.BlockSpec(memory_space=pltpu.VMEM), pl.BlockSpec(memory_space=pl.ANY)
    params = pltpu.CompilerParams(vmem_limit_bytes=24 << 20)
    shaped = jax.ShapeDtypeStruct

    def in_hbm(value):
        return pltpu.with_memory_space_constraint(value, pltpu.HBM)

    lane_group = CAP * block_rows
    post = layers * lane_group
    wide = CAP * rows
    sizes = (layers, owners, per_owner, block_count, slot_count, block_rows, tile_width)
    weighted, *parcels, factor = pl.pallas_call(
        functools.partial(pack_kernel, sizes),
        out_shape=[shaped((rows, panel_width), bf16)]
        + [shaped((rows, post + wide), bf16)] * owners
        + [shaped(factor_inverse.shape, f32)],
        in_specs=[anywhere] * 7,
        out_specs=[vmem] * (owners + 2),
        scratch_shapes=[
            pltpu.SMEM(tile_lists.shape, jnp.int32),
            pltpu.SMEM(tile_masks.shape, jnp.int32),
            pltpu.SMEM(tile_order.shape, jnp.int32),
            pltpu.VMEM((1, rows), f32),
            pltpu.VMEM(panel_jac.shape, bf16),
            pltpu.VMEM(jac.shape, bf16),
            pltpu.SMEM(tile_order.shape, jnp.int32),
            pltpu.VMEM((block_count * slot_count * tile_width, block_rows), bf16),
            pltpu.SemaphoreType.DMA((7,)),
        ],
        compiler_params=params,
        name="pack",
    )(*map(in_hbm, (tile_lists, tile_masks, tile_order, weights.reshape(1, rows), panel_jac, jac, factor_inverse)))
    line = [shift(weighted, k, 0) for k in range(1, layers)]
    parcels = [parcels[0]] + [shift(parcels[e], 0, e) for e in range(1, owners)]

    column = pl.pallas_call(
        stack_kernel,
        out_shape=shaped((layers * rows, panel_width), bf16),
        in_specs=[vmem] * layers,
        out_specs=vmem,
        compiler_params=params,
        cost_estimate=lasting(10**10),
        name="stack",
    )(*reversed(line), weighted)
    posts = pl.pallas_call(
        functools.partial(sort_kernel, (layers, owners, lane_group)),
        out_shape=[shaped((rows + 16, owners * lane_group), bf16)] * layers,
        in_specs=[vmem] * owners,
        out_specs=[vmem] * layers,
        compiler_params=params,
        cost_estimate=lasting(10**10),
        name="sort",
    )(parcels[0], parcels[3], parcels[2], parcels[1])
    posts = [posts[0]] + [shift(posts[k], k, 0) for k in range(1, layers)]
    by_x, by_y = shift(column, 0, 1), shift(column, 0, 2)


    def cut(kernel, value, name):
        return pl.pallas_call(
            kernel,
            out_shape=shaped((value.shape[0] // 2, panel_width), bf16),
            in_specs=[vmem],
            out_specs=vmem,
            compiler_params=params,
            name=name,
        )(value)

    rows_to_y, rows_to_x = cut(first_kernel, by_x, "first"), cut(last_kernel, by_y, "last")
    across_y, across_x = shift(rows_to_y, 0, 2), shift(rows_to_x, 0, 1)
    turned = pl.pallas_call(
        turn_kernel,
        out_shape=shaped((2, *factor_inverse.shape), bf16),
        in_specs=[vmem],
        out_specs=vmem,
        compiler_params=params,
        name="turn",
    )(factor)
    count = per_owner * slab_width
    depth = layers * rows
    sizes = (layers, owners, per_owner, block_count, block_rows)
    result = shaped((count, panel_width), f32)
    panels = [column, by_x, by_y]
    own, other = pl.pallas_call(
        functools.partial(near_kernel, sizes, 3),
        out_shape=[result, shaped((count, panel_width), bf16)],
        in_specs=[anywhere] * 3 + [vmem] * (len(panels) + layers),
        out_specs=[vmem] * 2,
        scratch_shapes=[
            pltpu.VMEM((count, (owners - 1) * depth), bf16),
            pltpu.VMEM(((owners - 1) * depth, panel_width), bf16),
        ],
        compiler_params=params,
        cost_estimate=lasting(10**9),
        name="near",
    )(rows_to_y, rows_to_x, turned, *panels, *posts)
    other = shift(other, 0, 0, 1)
    own = pl.pallas_call(
        own_kernel,
        out_shape=result,
        in_specs=[vmem] * 2,
        out_specs=vmem,
        compiler_params=params,
        cost_estimate=lasting(10**9),
        name="own",
    )(own, turned)
    joined = pl.pallas_call(
        functools.partial(join_kernel, (layers, lane_group, wide)),
        out_shape=shaped((depth + rows // 2 + 16, panel_width), bf16),
        in_specs=[vmem] * (2 + layers) + [anywhere],
        out_specs=vmem,
        compiler_params=params,
        cost_estimate=lasting(10**10),
        name="join",
    )(across_y, across_x, *posts, own)
    other_joined = shift(joined, 0, 0, 1)
    far_scratch = [pltpu.VMEM((count, depth), bf16)] + [pltpu.VMEM((depth, panel_width), bf16)] * 2
    far = pl.pallas_call(
        functools.partial(far_kernel, sizes),
        out_shape=result,
        in_specs=[vmem] * 2,
        out_specs=vmem,
        scratch_shapes=far_scratch,
        compiler_params=params,
        name="far",
    )(joined, turned)
    middle = pl.pallas_call(
        middle_kernel,
        out_shape=result,
        in_specs=[vmem] * 4,
        out_specs=vmem,
        compiler_params=params,
        name="middle",
    )(own, other, far, turned)
    out = pl.pallas_call(
        functools.partial(final_kernel, sizes),
        out_shape=result,
        in_specs=[vmem] * 3,
        out_specs=anywhere,
        scratch_shapes=[pltpu.VMEM((count, panel_width), f32)] + far_scratch + [pltpu.SemaphoreType.DMA((4,))],
        compiler_params=params,
        name="final",
    )(middle, other_joined, turned)
    return out.reshape(per_owner, slab_width, panel_width)


def solution(mesh):
    in_specs = (
        P(("rows", "cols"), None),
        P(("rows", "cols"), None),
        P(("rows", "cols")),
        P(("rows", "cols"), None),
        P(("rows", "cols"), None),
        P(),
        P(),
    )
    out_specs = P("cols", "rows", None)
    body = local if (mesh.shape["rows"], mesh.shape["cols"]) == (8, 4) else local_general
    return jax.shard_map(body, mesh=mesh, in_specs=in_specs, out_specs=out_specs, check_vma=False)
```

```python
import functools

import jax
import jax.numpy as jnp
from jax import lax
from jax.experimental import pallas as pl
from jax.experimental.pallas import tpu as pltpu
from jax.sharding import PartitionSpec as P

CAP = 2
GATHERED = 1 << 22


def tile_positions(tile_lists, tile_order):
    tile_count = tile_order.shape[0]
    matches = tile_lists[:, :, None] == tile_order[None, None, :]
    return jnp.sum(jnp.where(matches, jnp.arange(tile_count, dtype=jnp.int32), 0), axis=2)


def apply_inverse(tiles, factor_inverse):
    return jnp.einsum("ntp,qp->ntq", tiles, factor_inverse, precision=lax.Precision.HIGHEST)


def slot_codes(tile_lists, tile_masks, tile_order, owner_ids):
    block_count, slot_count = tile_lists.shape
    per_owner = tile_order.shape[0] // lax.axis_size("cols")
    positions = tile_positions(tile_lists, tile_order).reshape(-1)
    active = tile_masks.reshape(-1) == 1
    owner = positions // per_owner
    same = (owner[:, None] == owner[None, :]) & active[None, :]
    earlier = jnp.tril(jnp.ones(same.shape, bool), -1)
    rank = jnp.sum(same & earlier, axis=1)
    code = (
        (owner[None, None, :] == owner_ids[:, None, None])
        & (rank[None, None, :] == jnp.arange(CAP)[None, :, None])
        & active[None, None, :]
    )
    block = jnp.arange(block_count * slot_count) // slot_count
    place = positions % per_owner + per_owner * block
    return code, jnp.sum(jnp.where(code, place + 1, 0), axis=2) - 1


def local_general(jac, panel_jac, weights, tile_lists, tile_masks, tile_order, factor_inverse):
    block_count, slot_count = tile_lists.shape
    block_rows = jac.shape[0] // block_count
    tile_width = jac.shape[1] // slot_count
    slabs, owners = lax.axis_size("rows"), lax.axis_size("cols")
    devices = slabs * owners
    per_owner = tile_order.shape[0] // owners
    slab_width = tile_width // slabs
    bf16 = jnp.bfloat16
    weighted = (weights[:, None] * panel_jac).astype(bf16)
    code, places = slot_codes(tile_lists, tile_masks, tile_order, jnp.arange(owners))
    columns = jac.reshape(block_count, block_rows, slot_count, slabs, slab_width)
    chosen = code.astype(bf16).reshape(owners, CAP, block_count, slot_count)
    pieces = jnp.einsum("cjbk,bmkrt->rcjmt", chosen, columns, preferred_element_type=jnp.float32).astype(bf16)
    pieces = pieces.reshape(devices, -1)
    note = jnp.broadcast_to(places.astype(bf16)[None], (slabs, owners, CAP)).reshape(devices, CAP)
    note = jnp.pad(note, ((0, 0), (0, 128 - CAP)))
    sent = jnp.concatenate([pieces, note], axis=1)
    got = lax.all_to_all(sent, ("rows", "cols"), split_axis=0, concat_axis=0, tiled=True)
    size = pieces.shape[1]
    data = got[:, :size].reshape(devices, CAP, block_rows, slab_width)
    where = got[:, size : size + CAP].astype(jnp.int32)
    hot = (where[:, :, None] == jnp.arange(block_count * per_owner)).astype(bf16)
    hot = hot.reshape(devices, CAP, block_count, per_owner)
    mixed = jnp.einsum("djbn,djmt->dbmnt", hot, data, preferred_element_type=jnp.float32).astype(bf16)
    strips = max(1, devices * weighted.size * 2 // GATHERED)

    def strip_gram(strip):
        panels = lax.all_gather(strip, ("rows", "cols"), axis=0, tiled=True)
        panels = panels.reshape(devices, block_count, block_rows, -1)
        return jnp.einsum("dbmnt,dbmp->ntp", mixed, panels, preferred_element_type=jnp.float32)

    if strips == 1:
        gram = strip_gram(weighted)
    else:
        narrow = weighted.reshape(weighted.shape[0], strips, -1).swapaxes(0, 1)
        gram = jnp.moveaxis(lax.map(strip_gram, narrow), 0, 2)
        gram = gram.reshape(per_owner, slab_width, -1)
    return apply_inverse(gram, factor_inverse)


def shift(value, steps_z, flip_cols, flip_core=0):
    slabs, owners = lax.axis_size("rows"), lax.axis_size("cols")
    pairs = []
    for r in range(slabs):
        to_r = ((r // 2 + steps_z) % (slabs // 2)) * 2 + ((r % 2) ^ flip_core)
        for c in range(owners):
            pairs.append((r * owners + c, to_r * owners + (c ^ flip_cols)))
    return lax.ppermute(value, ("rows", "cols"), pairs)


def lasting(flops):
    return pl.CostEstimate(flops=flops, bytes_accessed=0, transcendentals=0)


def pack_kernel(sizes, lists_hbm, masks_hbm, order_hbm, weights_hbm, panel_hbm, jac_hbm, factor_hbm, *refs):
    layers, owners, per_owner, block_count, slot_count, block_rows, tile_width = sizes
    weighted_ref, parcels, factor_ref = refs[0], refs[1 : 1 + owners], refs[1 + owners]
    lists_ref, masks_ref, order_ref, weights_ref, panel_ref, jac_ref, places_ref, turned_ref, sems = refs[2 + owners :]
    copies = [
        pltpu.make_async_copy(order_hbm, order_ref, sems.at[0]),
        pltpu.make_async_copy(lists_hbm, lists_ref, sems.at[1]),
        pltpu.make_async_copy(masks_hbm, masks_ref, sems.at[2]),
        pltpu.make_async_copy(weights_hbm, weights_ref, sems.at[3]),
        pltpu.make_async_copy(panel_hbm, panel_ref, sems.at[4]),
        pltpu.make_async_copy(jac_hbm, jac_ref, sems.at[5]),
    ]
    for copy in copies:
        copy.start()
    factor_copy = pltpu.make_async_copy(factor_hbm, factor_ref, sems.at[6])
    factor_copy.start()
    f32, bf16 = jnp.float32, jnp.bfloat16
    rows, width = panel_ref.shape
    lane_group = CAP * block_rows
    post = layers * lane_group
    slab = tile_width // layers
    part = slab // 2
    me_r, me_c = lax.axis_index("rows"), lax.axis_index("cols")
    me_z, me_core = me_r // 2, lax.rem(me_r, 2)
    for copy in copies[:3]:
        copy.wait()
    for i in range(order_ref.shape[0]):
        places_ref[order_ref[i]] = i
    slots = []
    for s in range(block_count * slot_count):
        b, k = divmod(s, slot_count)
        place = places_ref[lists_ref[b, k]]
        owner = jnp.int32(0)
        for c in range(1, owners):
            owner += (place >= c * per_owner).astype(jnp.int32)
        slots.append((place - owner * per_owner, jnp.where(masks_ref[b, k] == 1, owner, -1)))

    found_slots = []
    for e in range(owners):
        wanted = me_c ^ e
        found = jnp.int32(0)
        chosen = [jnp.int32(0)] * CAP
        codes = [jnp.int32(-1)] * CAP
        for s, (place, owner) in enumerate(slots):
            hit = owner == wanted
            for j in range(CAP):
                take = hit & (found == j)
                chosen[j] = jnp.where(take, s, chosen[j])
                codes[j] = jnp.where(take, place, codes[j])
            found += hit.astype(jnp.int32)
        found_slots.append((chosen, codes))

    for copy in copies[3:]:
        copy.wait()

    row_ids = lax.broadcasted_iota(jnp.int32, (rows, rows), 0)
    lane_ids = lax.broadcasted_iota(jnp.int32, (rows, rows), 1)
    column = jnp.sum(jnp.where(row_ids == lane_ids, weights_ref[...], 0.0), axis=1, keepdims=True)
    weighted = (column * panel_ref[...].astype(f32)).astype(bf16)
    weighted_ref[...] = weighted

    for b in range(block_count):
        block = jac_ref[b * block_rows : (b + 1) * block_rows, :].astype(f32)
        start = b * slot_count * tile_width
        turned_ref[start : start + slot_count * tile_width, :] = block.T.astype(bf16)

    shape = (16, CAP * block_count * block_rows)
    lane = lax.broadcasted_iota(jnp.int32, shape, 1)
    for parcel, (chosen, codes) in zip(parcels, found_slots):
        note = jnp.full(shape, -1, jnp.int32)
        for j in range(CAP):
            for b in range(block_count):
                at = (j * block_count + b) * block_rows
                here = (lane >= at) & (lane < at + block_rows)
                code = jnp.where(chosen[j] // slot_count == b, codes[j], -1)
                note = jnp.where(here, code, note)
        parcel[:16, post:] = note.astype(f32).astype(bf16)
        for u in range(2):
            core = me_core ^ u
            for k in range(0, layers, 2):
                pieces = []
                for z in (lax.rem(me_z + k, layers), lax.rem(me_z + k + 1, layers)):
                    for j in range(CAP):
                        first = pl.multiple_of(chosen[j] * tile_width + z * slab + core * part, part)
                        pieces.append(turned_ref[pl.ds(first, part), :])
                lanes = slice(k * lane_group, (k + 2) * lane_group)
                parcel[u * part : (u + 1) * part, lanes] = jnp.concatenate(pieces, axis=1)
    factor_copy.wait()


def row_of(block, i):
    ids = lax.broadcasted_iota(jnp.int32, block.shape, 0)
    return jnp.sum(jnp.where(ids == i, block.astype(jnp.float32), 0.0), axis=0, keepdims=True)


def rows_from(notes):
    ids = lax.broadcasted_iota(jnp.int32, (16, notes[0].shape[1]), 0)
    block = jnp.full(ids.shape, -1.0, jnp.float32)
    for i, note in enumerate(notes):
        block = jnp.where(ids == i, note, block)
    return block.astype(jnp.bfloat16)


def stack_kernel(*refs):
    inputs, out_ref = refs[:-1], refs[-1]
    rows = inputs[0].shape[0]
    for i, ref in enumerate(reversed(inputs)):
        out_ref[i * rows : (i + 1) * rows, :] = ref[...]


def sort_kernel(sizes, *refs):
    layers, owners, lane_group = sizes
    parcels, posts = (refs[0], refs[3], refs[2], refs[1]), refs[owners:]
    rows, codes_at = parcels[0].shape[0], layers * lane_group
    block = rows_from([row_of(parcel[:16, codes_at:], 0) for parcel in parcels])
    for k, out in enumerate(posts):
        for e, parcel in enumerate(parcels):
            piece = parcel[:, k * lane_group : (k + 1) * lane_group]
            out[:rows, e * lane_group : (e + 1) * lane_group] = piece
        out[rows:, : block.shape[1]] = block


def first_kernel(in_ref, out_ref):
    out_ref[...] = in_ref[: out_ref.shape[0], :]


def last_kernel(in_ref, out_ref):
    out_ref[...] = in_ref[in_ref.shape[0] - out_ref.shape[0] :, :]


def place(out_ref, lanes, per_owner, pieces, notes, sizes):
    block_count, block_rows = sizes
    f32, bf16 = jnp.float32, jnp.bfloat16
    part, rows = pieces[0].shape[0], block_count * block_rows
    columns, codes = [], []
    for j in range(CAP):
        parts = []
        for piece in pieces:
            parts += [piece[:, j * block_rows : (j + 1) * block_rows].astype(f32)] * block_count
        columns.append(jnp.concatenate(parts, axis=1).astype(bf16))
        note = jnp.concatenate([note[:, j * rows : (j + 1) * rows] for note in notes], axis=1)
        codes.append(jnp.broadcast_to(note, columns[j].shape).astype(bf16))
    for n in range(per_owner):
        placed = jnp.zeros(columns[0].shape, bf16)
        for j in range(CAP):
            placed = jnp.where(codes[j] == jnp.asarray(n, bf16), columns[j], placed)
        out_ref[n * part : (n + 1) * part, lanes] = placed


def inverse_rows(rows_ref, factor_ref, high_ref, low_ref):
    f32, bf16 = jnp.float32, jnp.bfloat16
    height, width = high_ref.shape
    for start, stop in ((0, width // 2), (width // 2, width)):
        rows = rows_ref[:height, :stop]
        total = jnp.dot(rows, factor_ref[0, :stop, start:stop], preferred_element_type=f32)
        total += jnp.dot(rows, factor_ref[1, :stop, start:stop], preferred_element_type=f32)
        high = total.astype(bf16)
        high_ref[:, start:stop] = high
        low_ref[:, start:stop] = (total - high.astype(f32)).astype(bf16)


def turn_kernel(factor_ref, earlier_ref, out_ref):
    turned = factor_ref[...].T
    high = turned.astype(jnp.bfloat16)
    out_ref[0, :, :] = high
    out_ref[1, :, :] = (turned - high.astype(jnp.float32)).astype(jnp.bfloat16)


def near_kernel(sizes, earlier, *refs):
    layers, owners, per_owner, block_count, block_rows = sizes
    panels, posts, refs = refs[earlier : earlier + 3], refs[earlier + 3 : earlier + 3 + layers], refs[earlier + 3 + layers :]
    own_ref, other_ref, placed_ref, rows_ref = refs
    f32, bf16 = jnp.float32, jnp.bfloat16
    rows = block_count * block_rows
    group, wide = CAP * block_rows, CAP * rows
    part = rows // 2
    width = rows_ref.shape[1]
    at = 0
    for panel in panels:
        rows_ref[at : at + panel.shape[0], :] = panel[:, :width]
        at += panel.shape[0]
    for u, out_ref in ((1, other_ref), (0, own_ref)):
        for e in range(owners - 1):
            for h in range(layers // 2):
                pair = posts[2 * h : 2 * h + 2]
                pieces = [post[u * part : (u + 1) * part, e * group : (e + 1) * group] for post in pair]
                notes = [row_of(post[rows:, :wide], e) for post in pair]
                start = (e * layers + 2 * h) * rows
                place(placed_ref, slice(start, start + 2 * rows), per_owner, pieces, notes, (block_count, block_rows))
        gram = jnp.dot(placed_ref[...], rows_ref[...], preferred_element_type=f32)
        out_ref[...] = gram.astype(out_ref.dtype)


def join_kernel(sizes, above_ref, below_ref, *refs):
    layers, lane_group, wide = sizes
    posts, out_ref = refs[:layers], refs[-1]
    half, rows = above_ref.shape[0], posts[0].shape[0] - 16
    part, depth = rows // 2, 2 * half
    out_ref[:half, :] = above_ref[...]
    out_ref[half:depth, :] = below_ref[...]
    for k, ref in enumerate(posts):
        for u in range(2):
            piece = ref[u * part : (u + 1) * part, 3 * lane_group : 4 * lane_group]
            at = (u * layers + k) * lane_group
            out_ref[depth : depth + part, at : at + lane_group] = piece
    out_ref[depth + part :, :wide] = rows_from([row_of(ref[rows:, :wide], 3) for ref in posts])


def place_far(sizes, u, ref, placed_ref):
    layers, owners, per_owner, block_count, block_rows = sizes
    rows = block_count * block_rows
    group, wide = CAP * block_rows, CAP * rows
    part, depth = rows // 2, layers * rows
    for h in range(layers // 2):
        pieces, notes = [], []
        for k in (2 * h, 2 * h + 1):
            at = (u * layers + k) * group
            pieces.append(ref[depth : depth + part, at : at + group])
            notes.append(row_of(ref[depth + part :, :wide], k))
        lanes = slice(2 * h * rows, 2 * (h + 1) * rows)
        place(placed_ref, lanes, per_owner, pieces, notes, (block_count, block_rows))


def far_kernel(sizes, joined_ref, turned_ref, out_ref, placed_ref, high_ref, low_ref):
    place_far(sizes, 0, joined_ref, placed_ref)
    inverse_rows(joined_ref, turned_ref, high_ref, low_ref)
    placed = placed_ref[...]
    total = jnp.dot(placed, high_ref[...], preferred_element_type=jnp.float32)
    out_ref[...] = total + jnp.dot(placed, low_ref[...], preferred_element_type=jnp.float32)


def times_inverse(out_ref, terms, turned_ref, added):
    width = out_ref.shape[1]
    for start, stop in ((0, width // 2), (width // 2, width)):
        total = sum(ref[:, start:stop] for ref in added)
        for i, j in ((0, 0), (0, 1), (1, 0))[: len(terms) + 1]:
            total += jnp.dot(terms[i][:, :stop], turned_ref[j, :stop, start:stop], preferred_element_type=jnp.float32)
        out_ref[:, start:stop] = total


def own_kernel(own_ref, turned_ref, out_ref):
    high = own_ref[...].astype(jnp.bfloat16)
    low = (own_ref[...] - high.astype(jnp.float32)).astype(jnp.bfloat16)
    times_inverse(out_ref, (high, low), turned_ref, ())


def middle_kernel(own_ref, other_ref, far_ref, turned_ref, out_ref):
    times_inverse(out_ref, (other_ref[...],), turned_ref, (own_ref, far_ref))


def final_kernel(sizes, middle_ref, joined_ref, turned_ref, out_hbm, sum_ref, placed_ref, high_ref, low_ref, sems):
    f32 = jnp.float32
    place_far(sizes, 1, joined_ref, placed_ref)
    inverse_rows(joined_ref, turned_ref, high_ref, low_ref)
    strips = sems.shape[0]
    height = sum_ref.shape[0] // strips
    copies = []
    for i in range(strips):
        here = pl.ds(i * height, height)
        placed = placed_ref[here, :]
        total = middle_ref[here, :] + jnp.dot(placed, high_ref[...], preferred_element_type=f32)
        sum_ref[here, :] = total + jnp.dot(placed, low_ref[...], preferred_element_type=f32)
        copies.append(pltpu.make_async_copy(sum_ref.at[here, :], out_hbm.at[here, :], sems.at[i]))
        copies[-1].start()
    for copy in copies:
        copy.wait()


def local(jac, panel_jac, weights, tile_lists, tile_masks, tile_order, factor_inverse):
    block_count, slot_count = tile_lists.shape
    rows, panel_width = panel_jac.shape
    block_rows = rows // block_count
    tile_width = jac.shape[1] // slot_count
    slabs, owners = lax.axis_size("rows"), lax.axis_size("cols")
    layers = slabs // 2
    per_owner = tile_order.shape[0] // owners
    slab_width = tile_width // slabs
    f32, bf16 = jnp.float32, jnp.bfloat16
    vmem, anywhere = pl.BlockSpec(memory_space=pltpu.VMEM), pl.BlockSpec(memory_space=pl.ANY)
    params = pltpu.CompilerParams(vmem_limit_bytes=24 << 20)
    shaped = jax.ShapeDtypeStruct

    def in_hbm(value):
        return pltpu.with_memory_space_constraint(value, pltpu.HBM)

    lane_group = CAP * block_rows
    post = layers * lane_group
    wide = CAP * rows
    sizes = (layers, owners, per_owner, block_count, slot_count, block_rows, tile_width)
    weighted, *parcels, factor = pl.pallas_call(
        functools.partial(pack_kernel, sizes),
        out_shape=[shaped((rows, panel_width), bf16)]
        + [shaped((rows, post + wide), bf16)] * owners
        + [shaped(factor_inverse.shape, f32)],
        in_specs=[anywhere] * 7,
        out_specs=[vmem] * (owners + 2),
        scratch_shapes=[
            pltpu.SMEM(tile_lists.shape, jnp.int32),
            pltpu.SMEM(tile_masks.shape, jnp.int32),
            pltpu.SMEM(tile_order.shape, jnp.int32),
            pltpu.VMEM((1, rows), f32),
            pltpu.VMEM(panel_jac.shape, bf16),
            pltpu.VMEM(jac.shape, bf16),
            pltpu.SMEM(tile_order.shape, jnp.int32),
            pltpu.VMEM((block_count * slot_count * tile_width, block_rows), bf16),
            pltpu.SemaphoreType.DMA((7,)),
        ],
        compiler_params=params,
        name="pack",
    )(*map(in_hbm, (tile_lists, tile_masks, tile_order, weights.reshape(1, rows), panel_jac, jac, factor_inverse)))
    line = [shift(weighted, k, 0) for k in range(1, layers)]
    parcels = [parcels[0]] + [shift(parcels[e], 0, e) for e in range(1, owners)]

    column = pl.pallas_call(
        stack_kernel,
        out_shape=shaped((layers * rows, panel_width), bf16),
        in_specs=[vmem] * layers,
        out_specs=vmem,
        compiler_params=params,
        cost_estimate=lasting(10**10),
        name="stack",
    )(*reversed(line), weighted)
    posts = pl.pallas_call(
        functools.partial(sort_kernel, (layers, owners, lane_group)),
        out_shape=[shaped((rows + 16, owners * lane_group), bf16)] * layers,
        in_specs=[vmem] * owners,
        out_specs=[vmem] * layers,
        compiler_params=params,
        cost_estimate=lasting(10**10),
        name="sort",
    )(parcels[0], parcels[3], parcels[2], parcels[1])
    posts = [posts[0]] + [shift(posts[k], k, 0) for k in range(1, layers)]
    by_x, by_y = shift(column, 0, 1), shift(column, 0, 2)


    def cut(kernel, value, name):
        return pl.pallas_call(
            kernel,
            out_shape=shaped((value.shape[0] // 2, panel_width), bf16),
            in_specs=[vmem],
            out_specs=vmem,
            compiler_params=params,
            name=name,
        )(value)

    rows_to_y, rows_to_x = cut(first_kernel, by_x, "first"), cut(last_kernel, by_y, "last")
    across_y, across_x = shift(rows_to_y, 0, 2), shift(rows_to_x, 0, 1)
    count = per_owner * slab_width
    depth = layers * rows
    sizes = (layers, owners, per_owner, block_count, block_rows)
    result = shaped((count, panel_width), f32)
    panels = [column, by_x, by_y]
    own, other = pl.pallas_call(
        functools.partial(near_kernel, sizes, 2),
        out_shape=[result, shaped((count, panel_width), bf16)],
        in_specs=[anywhere] * 2 + [vmem] * (len(panels) + layers),
        out_specs=[vmem] * 2,
        scratch_shapes=[
            pltpu.VMEM((count, (owners - 1) * depth), bf16),
            pltpu.VMEM(((owners - 1) * depth, panel_width), bf16),
        ],
        compiler_params=params,
        cost_estimate=lasting(10**9),
        name="near",
    )(rows_to_y, rows_to_x, *panels, *posts)
    other = shift(other, 0, 0, 1)
    turned = pl.pallas_call(
        turn_kernel,
        out_shape=shaped((2, *factor_inverse.shape), bf16),
        in_specs=[vmem, anywhere],
        out_specs=vmem,
        compiler_params=params,
        name="turn",
    )(factor, own)
    own = pl.pallas_call(
        own_kernel,
        out_shape=result,
        in_specs=[vmem] * 2,
        out_specs=vmem,
        compiler_params=params,
        cost_estimate=lasting(10**9),
        name="own",
    )(own, turned)
    joined = pl.pallas_call(
        functools.partial(join_kernel, (layers, lane_group, wide)),
        out_shape=shaped((depth + rows // 2 + 16, panel_width), bf16),
        in_specs=[vmem] * (2 + layers) + [anywhere],
        out_specs=vmem,
        compiler_params=params,
        cost_estimate=lasting(10**10),
        name="join",
    )(across_y, across_x, *posts, own)
    other_joined = shift(joined, 0, 0, 1)
    far_scratch = [pltpu.VMEM((count, depth), bf16)] + [pltpu.VMEM((depth, panel_width), bf16)] * 2
    far = pl.pallas_call(
        functools.partial(far_kernel, sizes),
        out_shape=result,
        in_specs=[vmem] * 2,
        out_specs=vmem,
        scratch_shapes=far_scratch,
        compiler_params=params,
        name="far",
    )(joined, turned)
    middle = pl.pallas_call(
        middle_kernel,
        out_shape=result,
        in_specs=[vmem] * 4,
        out_specs=vmem,
        compiler_params=params,
        name="middle",
    )(own, other, far, turned)
    out = pl.pallas_call(
        functools.partial(final_kernel, sizes),
        out_shape=result,
        in_specs=[vmem] * 3,
        out_specs=anywhere,
        scratch_shapes=[pltpu.VMEM((count, panel_width), f32)] + far_scratch + [pltpu.SemaphoreType.DMA((4,))],
        compiler_params=params,
        name="final",
    )(middle, other_joined, turned)
    return out.reshape(per_owner, slab_width, panel_width)


def solution(mesh):
    in_specs = (
        P(("rows", "cols"), None),
        P(("rows", "cols"), None),
        P(("rows", "cols")),
        P(("rows", "cols"), None),
        P(("rows", "cols"), None),
        P(),
        P(),
    )
    out_specs = P("cols", "rows", None)
    body = local if (mesh.shape["rows"], mesh.shape["cols"]) == (8, 4) else local_general
    return jax.shard_map(body, mesh=mesh, in_specs=in_specs, out_specs=out_specs, check_vma=False)
```

```python
import functools

import jax
import jax.numpy as jnp
from jax import lax
from jax.experimental import pallas as pl
from jax.experimental.pallas import tpu as pltpu
from jax.sharding import PartitionSpec as P

CAP = 2
GATHERED = 1 << 22


def tile_positions(tile_lists, tile_order):
    tile_count = tile_order.shape[0]
    matches = tile_lists[:, :, None] == tile_order[None, None, :]
    return jnp.sum(jnp.where(matches, jnp.arange(tile_count, dtype=jnp.int32), 0), axis=2)


def apply_inverse(tiles, factor_inverse):
    return jnp.einsum("ntp,qp->ntq", tiles, factor_inverse, precision=lax.Precision.HIGHEST)


def slot_codes(tile_lists, tile_masks, tile_order, owner_ids):
    block_count, slot_count = tile_lists.shape
    per_owner = tile_order.shape[0] // lax.axis_size("cols")
    positions = tile_positions(tile_lists, tile_order).reshape(-1)
    active = tile_masks.reshape(-1) == 1
    owner = positions // per_owner
    same = (owner[:, None] == owner[None, :]) & active[None, :]
    earlier = jnp.tril(jnp.ones(same.shape, bool), -1)
    rank = jnp.sum(same & earlier, axis=1)
    code = (
        (owner[None, None, :] == owner_ids[:, None, None])
        & (rank[None, None, :] == jnp.arange(CAP)[None, :, None])
        & active[None, None, :]
    )
    block = jnp.arange(block_count * slot_count) // slot_count
    place = positions % per_owner + per_owner * block
    return code, jnp.sum(jnp.where(code, place + 1, 0), axis=2) - 1


def local_general(jac, panel_jac, weights, tile_lists, tile_masks, tile_order, factor_inverse):
    block_count, slot_count = tile_lists.shape
    block_rows = jac.shape[0] // block_count
    tile_width = jac.shape[1] // slot_count
    slabs, owners = lax.axis_size("rows"), lax.axis_size("cols")
    devices = slabs * owners
    per_owner = tile_order.shape[0] // owners
    slab_width = tile_width // slabs
    bf16 = jnp.bfloat16
    weighted = (weights[:, None] * panel_jac).astype(bf16)
    code, places = slot_codes(tile_lists, tile_masks, tile_order, jnp.arange(owners))
    columns = jac.reshape(block_count, block_rows, slot_count, slabs, slab_width)
    chosen = code.astype(bf16).reshape(owners, CAP, block_count, slot_count)
    pieces = jnp.einsum("cjbk,bmkrt->rcjmt", chosen, columns, preferred_element_type=jnp.float32).astype(bf16)
    pieces = pieces.reshape(devices, -1)
    note = jnp.broadcast_to(places.astype(bf16)[None], (slabs, owners, CAP)).reshape(devices, CAP)
    note = jnp.pad(note, ((0, 0), (0, 128 - CAP)))
    sent = jnp.concatenate([pieces, note], axis=1)
    got = lax.all_to_all(sent, ("rows", "cols"), split_axis=0, concat_axis=0, tiled=True)
    size = pieces.shape[1]
    data = got[:, :size].reshape(devices, CAP, block_rows, slab_width)
    where = got[:, size : size + CAP].astype(jnp.int32)
    hot = (where[:, :, None] == jnp.arange(block_count * per_owner)).astype(bf16)
    hot = hot.reshape(devices, CAP, block_count, per_owner)
    mixed = jnp.einsum("djbn,djmt->dbmnt", hot, data, preferred_element_type=jnp.float32).astype(bf16)
    strips = max(1, devices * weighted.size * 2 // GATHERED)

    def strip_gram(strip):
        panels = lax.all_gather(strip, ("rows", "cols"), axis=0, tiled=True)
        panels = panels.reshape(devices, block_count, block_rows, -1)
        return jnp.einsum("dbmnt,dbmp->ntp", mixed, panels, preferred_element_type=jnp.float32)

    if strips == 1:
        gram = strip_gram(weighted)
    else:
        narrow = weighted.reshape(weighted.shape[0], strips, -1).swapaxes(0, 1)
        gram = jnp.moveaxis(lax.map(strip_gram, narrow), 0, 2)
        gram = gram.reshape(per_owner, slab_width, -1)
    return apply_inverse(gram, factor_inverse)


def shift(value, steps_z, flip_cols, flip_core=0):
    slabs, owners = lax.axis_size("rows"), lax.axis_size("cols")
    pairs = []
    for r in range(slabs):
        to_r = ((r // 2 + steps_z) % (slabs // 2)) * 2 + ((r % 2) ^ flip_core)
        for c in range(owners):
            pairs.append((r * owners + c, to_r * owners + (c ^ flip_cols)))
    return lax.ppermute(value, ("rows", "cols"), pairs)


def lasting(flops):
    return pl.CostEstimate(flops=flops, bytes_accessed=0, transcendentals=0)


def pack_kernel(sizes, lists_hbm, masks_hbm, order_hbm, weights_hbm, panel_hbm, jac_hbm, factor_hbm, *refs):
    layers, owners, per_owner, block_count, slot_count, block_rows, tile_width = sizes
    weighted_ref, parcels, factor_ref = refs[0], refs[1 : 1 + owners], refs[1 + owners]
    lists_ref, masks_ref, order_ref, weights_ref, panel_ref, jac_ref, places_ref, turned_ref, sems = refs[2 + owners :]
    copies = [
        pltpu.make_async_copy(order_hbm, order_ref, sems.at[0]),
        pltpu.make_async_copy(lists_hbm, lists_ref, sems.at[1]),
        pltpu.make_async_copy(masks_hbm, masks_ref, sems.at[2]),
        pltpu.make_async_copy(weights_hbm, weights_ref, sems.at[3]),
        pltpu.make_async_copy(panel_hbm, panel_ref, sems.at[4]),
        pltpu.make_async_copy(jac_hbm, jac_ref, sems.at[5]),
    ]
    for copy in copies:
        copy.start()
    factor_copy = pltpu.make_async_copy(factor_hbm, factor_ref, sems.at[6])
    factor_copy.start()
    f32, bf16 = jnp.float32, jnp.bfloat16
    rows, width = panel_ref.shape
    lane_group = CAP * block_rows
    post = layers * lane_group
    slab = tile_width // layers
    part = slab // 2
    me_r, me_c = lax.axis_index("rows"), lax.axis_index("cols")
    me_z, me_core = me_r // 2, lax.rem(me_r, 2)
    for copy in copies[:3]:
        copy.wait()
    for i in range(order_ref.shape[0]):
        places_ref[order_ref[i]] = i
    slots = []
    for s in range(block_count * slot_count):
        b, k = divmod(s, slot_count)
        place = places_ref[lists_ref[b, k]]
        owner = jnp.int32(0)
        for c in range(1, owners):
            owner += (place >= c * per_owner).astype(jnp.int32)
        slots.append((place - owner * per_owner, jnp.where(masks_ref[b, k] == 1, owner, -1)))

    found_slots = []
    for e in range(owners):
        wanted = me_c ^ e
        found = jnp.int32(0)
        chosen = [jnp.int32(0)] * CAP
        codes = [jnp.int32(-1)] * CAP
        for s, (place, owner) in enumerate(slots):
            hit = owner == wanted
            for j in range(CAP):
                take = hit & (found == j)
                chosen[j] = jnp.where(take, s, chosen[j])
                codes[j] = jnp.where(take, place, codes[j])
            found += hit.astype(jnp.int32)
        found_slots.append((chosen, codes))

    for copy in copies[3:]:
        copy.wait()

    row_ids = lax.broadcasted_iota(jnp.int32, (rows, rows), 0)
    lane_ids = lax.broadcasted_iota(jnp.int32, (rows, rows), 1)
    column = jnp.sum(jnp.where(row_ids == lane_ids, weights_ref[...], 0.0), axis=1, keepdims=True)
    weighted = (column * panel_ref[...].astype(f32)).astype(bf16)
    weighted_ref[...] = weighted

    for b in range(block_count):
        block = jac_ref[b * block_rows : (b + 1) * block_rows, :].astype(f32)
        start = b * slot_count * tile_width
        turned_ref[start : start + slot_count * tile_width, :] = block.T.astype(bf16)

    shape = (16, CAP * block_count * block_rows)
    lane = lax.broadcasted_iota(jnp.int32, shape, 1)
    for parcel, (chosen, codes) in zip(parcels, found_slots):
        note = jnp.full(shape, -1, jnp.int32)
        for j in range(CAP):
            for b in range(block_count):
                at = (j * block_count + b) * block_rows
                here = (lane >= at) & (lane < at + block_rows)
                code = jnp.where(chosen[j] // slot_count == b, codes[j], -1)
                note = jnp.where(here, code, note)
        parcel[:16, post:] = note.astype(f32).astype(bf16)
        for u in range(2):
            core = me_core ^ u
            for k in range(0, layers, 2):
                pieces = []
                for z in (lax.rem(me_z + k, layers), lax.rem(me_z + k + 1, layers)):
                    for j in range(CAP):
                        first = pl.multiple_of(chosen[j] * tile_width + z * slab + core * part, part)
                        pieces.append(turned_ref[pl.ds(first, part), :])
                lanes = slice(k * lane_group, (k + 2) * lane_group)
                parcel[u * part : (u + 1) * part, lanes] = jnp.concatenate(pieces, axis=1)
    factor_copy.wait()


def row_of(block, i):
    ids = lax.broadcasted_iota(jnp.int32, block.shape, 0)
    return jnp.sum(jnp.where(ids == i, block.astype(jnp.float32), 0.0), axis=0, keepdims=True)


def rows_from(notes):
    ids = lax.broadcasted_iota(jnp.int32, (16, notes[0].shape[1]), 0)
    block = jnp.full(ids.shape, -1.0, jnp.float32)
    for i, note in enumerate(notes):
        block = jnp.where(ids == i, note, block)
    return block.astype(jnp.bfloat16)


def stack_kernel(*refs):
    inputs, out_ref = refs[:-1], refs[-1]
    rows = inputs[0].shape[0]
    for i, ref in enumerate(reversed(inputs)):
        out_ref[i * rows : (i + 1) * rows, :] = ref[...]


def sort_kernel(sizes, *refs):
    layers, owners, lane_group = sizes
    parcels, posts = (refs[0], refs[3], refs[2], refs[1]), refs[owners:]
    rows, codes_at = parcels[0].shape[0], layers * lane_group
    block = rows_from([row_of(parcel[:16, codes_at:], 0) for parcel in parcels])
    for k, out in enumerate(posts):
        for e, parcel in enumerate(parcels):
            piece = parcel[:, k * lane_group : (k + 1) * lane_group]
            out[:rows, e * lane_group : (e + 1) * lane_group] = piece
        out[rows:, : block.shape[1]] = block


def first_kernel(in_ref, out_ref):
    out_ref[...] = in_ref[: out_ref.shape[0], :]


def last_kernel(in_ref, out_ref):
    out_ref[...] = in_ref[in_ref.shape[0] - out_ref.shape[0] :, :]


def place(out_ref, lanes, per_owner, pieces, notes, sizes):
    block_count, block_rows = sizes
    f32, bf16 = jnp.float32, jnp.bfloat16
    part, rows = pieces[0].shape[0], block_count * block_rows
    columns, codes = [], []
    for j in range(CAP):
        parts = []
        for piece in pieces:
            parts += [piece[:, j * block_rows : (j + 1) * block_rows].astype(f32)] * block_count
        columns.append(jnp.concatenate(parts, axis=1).astype(bf16))
        note = jnp.concatenate([note[:, j * rows : (j + 1) * rows] for note in notes], axis=1)
        codes.append(jnp.broadcast_to(note, columns[j].shape).astype(bf16))
    for n in range(per_owner):
        placed = jnp.zeros(columns[0].shape, bf16)
        for j in range(CAP):
            placed = jnp.where(codes[j] == jnp.asarray(n, bf16), columns[j], placed)
        out_ref[n * part : (n + 1) * part, lanes] = placed


def inverse_rows(rows_ref, factor_ref, high_ref, low_ref):
    f32, bf16 = jnp.float32, jnp.bfloat16
    height, width = high_ref.shape
    for start, stop in ((0, width // 2), (width // 2, width)):
        rows = rows_ref[:height, :stop]
        total = jnp.dot(rows, factor_ref[0, :stop, start:stop], preferred_element_type=f32)
        total += jnp.dot(rows, factor_ref[1, :stop, start:stop], preferred_element_type=f32)
        high = total.astype(bf16)
        high_ref[:, start:stop] = high
        low_ref[:, start:stop] = (total - high.astype(f32)).astype(bf16)


def turn_kernel(factor_ref, out_ref):
    turned = factor_ref[...].T
    high = turned.astype(jnp.bfloat16)
    out_ref[0, :, :] = high
    out_ref[1, :, :] = (turned - high.astype(jnp.float32)).astype(jnp.bfloat16)


def near_kernel(sizes, earlier, *refs):
    layers, owners, per_owner, block_count, block_rows = sizes
    panels, posts, refs = refs[earlier : earlier + 3], refs[earlier + 3 : earlier + 3 + layers], refs[earlier + 3 + layers :]
    own_ref, other_ref, placed_ref, rows_ref = refs
    f32, bf16 = jnp.float32, jnp.bfloat16
    rows = block_count * block_rows
    group, wide = CAP * block_rows, CAP * rows
    part = rows // 2
    width = rows_ref.shape[1]
    at = 0
    for panel in panels:
        rows_ref[at : at + panel.shape[0], :] = panel[:, :width]
        at += panel.shape[0]
    for u, out_ref in ((1, other_ref), (0, own_ref)):
        for e in range(owners - 1):
            for h in range(layers // 2):
                pair = posts[2 * h : 2 * h + 2]
                pieces = [post[u * part : (u + 1) * part, e * group : (e + 1) * group] for post in pair]
                notes = [row_of(post[rows:, :wide], e) for post in pair]
                start = (e * layers + 2 * h) * rows
                place(placed_ref, slice(start, start + 2 * rows), per_owner, pieces, notes, (block_count, block_rows))
        gram = jnp.dot(placed_ref[...], rows_ref[...], preferred_element_type=f32)
        out_ref[...] = gram.astype(out_ref.dtype)


def join_kernel(sizes, above_ref, below_ref, *refs):
    layers, lane_group, wide = sizes
    posts, out_ref = refs[:layers], refs[-1]
    half, rows = above_ref.shape[0], posts[0].shape[0] - 16
    part, depth = rows // 2, 2 * half
    out_ref[:half, :] = above_ref[...]
    out_ref[half:depth, :] = below_ref[...]
    for k, ref in enumerate(posts):
        for u in range(2):
            piece = ref[u * part : (u + 1) * part, 3 * lane_group : 4 * lane_group]
            at = (u * layers + k) * lane_group
            out_ref[depth : depth + part, at : at + lane_group] = piece
    out_ref[depth + part :, :wide] = rows_from([row_of(ref[rows:, :wide], 3) for ref in posts])


def place_far(sizes, u, ref, placed_ref):
    layers, owners, per_owner, block_count, block_rows = sizes
    rows = block_count * block_rows
    group, wide = CAP * block_rows, CAP * rows
    part, depth = rows // 2, layers * rows
    for h in range(layers // 2):
        pieces, notes = [], []
        for k in (2 * h, 2 * h + 1):
            at = (u * layers + k) * group
            pieces.append(ref[depth : depth + part, at : at + group])
            notes.append(row_of(ref[depth + part :, :wide], k))
        lanes = slice(2 * h * rows, 2 * (h + 1) * rows)
        place(placed_ref, lanes, per_owner, pieces, notes, (block_count, block_rows))


def far_kernel(sizes, joined_ref, turned_ref, out_ref, placed_ref, high_ref, low_ref):
    place_far(sizes, 0, joined_ref, placed_ref)
    inverse_rows(joined_ref, turned_ref, high_ref, low_ref)
    placed = placed_ref[...]
    total = jnp.dot(placed, high_ref[...], preferred_element_type=jnp.float32)
    out_ref[...] = total + jnp.dot(placed, low_ref[...], preferred_element_type=jnp.float32)


def times_inverse(out_ref, terms, turned_ref, added):
    width = out_ref.shape[1]
    for start, stop in ((0, width // 2), (width // 2, width)):
        total = sum(ref[:, start:stop] for ref in added)
        for i, j in ((0, 0), (0, 1), (1, 0))[: len(terms) + 1]:
            total += jnp.dot(terms[i][:, :stop], turned_ref[j, :stop, start:stop], preferred_element_type=jnp.float32)
        out_ref[:, start:stop] = total


def own_kernel(own_ref, turned_ref, out_ref):
    high = own_ref[...].astype(jnp.bfloat16)
    low = (own_ref[...] - high.astype(jnp.float32)).astype(jnp.bfloat16)
    times_inverse(out_ref, (high, low), turned_ref, ())


def middle_kernel(own_ref, other_ref, far_ref, turned_ref, out_ref):
    times_inverse(out_ref, (other_ref[...],), turned_ref, (own_ref, far_ref))


def final_kernel(sizes, middle_ref, joined_ref, turned_ref, out_hbm, sum_ref, placed_ref, high_ref, low_ref, sems):
    f32 = jnp.float32
    place_far(sizes, 1, joined_ref, placed_ref)
    inverse_rows(joined_ref, turned_ref, high_ref, low_ref)
    strips = sems.shape[0]
    height = sum_ref.shape[0] // strips
    copies = []
    for i in range(strips):
        here = pl.ds(i * height, height)
        placed = placed_ref[here, :]
        total = middle_ref[here, :] + jnp.dot(placed, high_ref[...], preferred_element_type=f32)
        sum_ref[here, :] = total + jnp.dot(placed, low_ref[...], preferred_element_type=f32)
        copies.append(pltpu.make_async_copy(sum_ref.at[here, :], out_hbm.at[here, :], sems.at[i]))
        copies[-1].start()
    for copy in copies:
        copy.wait()


def local(jac, panel_jac, weights, tile_lists, tile_masks, tile_order, factor_inverse):
    block_count, slot_count = tile_lists.shape
    rows, panel_width = panel_jac.shape
    block_rows = rows // block_count
    tile_width = jac.shape[1] // slot_count
    slabs, owners = lax.axis_size("rows"), lax.axis_size("cols")
    layers = slabs // 2
    per_owner = tile_order.shape[0] // owners
    slab_width = tile_width // slabs
    f32, bf16 = jnp.float32, jnp.bfloat16
    vmem, anywhere = pl.BlockSpec(memory_space=pltpu.VMEM), pl.BlockSpec(memory_space=pl.ANY)
    params = pltpu.CompilerParams(vmem_limit_bytes=24 << 20)
    shaped = jax.ShapeDtypeStruct

    def in_hbm(value):
        return pltpu.with_memory_space_constraint(value, pltpu.HBM)

    lane_group = CAP * block_rows
    post = layers * lane_group
    wide = CAP * rows
    sizes = (layers, owners, per_owner, block_count, slot_count, block_rows, tile_width)
    weighted, *parcels, factor = pl.pallas_call(
        functools.partial(pack_kernel, sizes),
        out_shape=[shaped((rows, panel_width), bf16)]
        + [shaped((rows, post + wide), bf16)] * owners
        + [shaped(factor_inverse.shape, f32)],
        in_specs=[anywhere] * 7,
        out_specs=[vmem] * (owners + 2),
        scratch_shapes=[
            pltpu.SMEM(tile_lists.shape, jnp.int32),
            pltpu.SMEM(tile_masks.shape, jnp.int32),
            pltpu.SMEM(tile_order.shape, jnp.int32),
            pltpu.VMEM((1, rows), f32),
            pltpu.VMEM(panel_jac.shape, bf16),
            pltpu.VMEM(jac.shape, bf16),
            pltpu.SMEM(tile_order.shape, jnp.int32),
            pltpu.VMEM((block_count * slot_count * tile_width, block_rows), bf16),
            pltpu.SemaphoreType.DMA((7,)),
        ],
        compiler_params=params,
        name="pack",
    )(*map(in_hbm, (tile_lists, tile_masks, tile_order, weights.reshape(1, rows), panel_jac, jac, factor_inverse)))
    line = [shift(weighted, k, 0) for k in range(1, layers)]
    parcels = [parcels[0]] + [shift(parcels[e], 0, e) for e in range(1, owners)]

    column = pl.pallas_call(
        stack_kernel,
        out_shape=shaped((layers * rows, panel_width), bf16),
        in_specs=[vmem] * layers,
        out_specs=vmem,
        compiler_params=params,
        cost_estimate=lasting(10**10),
        name="stack",
    )(*reversed(line), weighted)
    posts = pl.pallas_call(
        functools.partial(sort_kernel, (layers, owners, lane_group)),
        out_shape=[shaped((rows + 16, owners * lane_group), bf16)] * layers,
        in_specs=[vmem] * owners,
        out_specs=[vmem] * layers,
        compiler_params=params,
        cost_estimate=lasting(10**10),
        name="sort",
    )(parcels[0], parcels[3], parcels[2], parcels[1])
    posts = [posts[0]] + [shift(posts[k], k, 0) for k in range(1, layers)]
    by_x, by_y = shift(column, 0, 1), shift(column, 0, 2)


    def cut(kernel, value, name):
        return pl.pallas_call(
            kernel,
            out_shape=shaped((value.shape[0] // 2, panel_width), bf16),
            in_specs=[vmem],
            out_specs=vmem,
            compiler_params=params,
            name=name,
        )(value)

    rows_to_y, rows_to_x = cut(first_kernel, by_x, "first"), cut(last_kernel, by_y, "last")
    across_y, across_x = shift(rows_to_y, 0, 2), shift(rows_to_x, 0, 1)
    turned = pl.pallas_call(
        turn_kernel,
        out_shape=shaped((2, *factor_inverse.shape), bf16),
        in_specs=[vmem],
        out_specs=vmem,
        compiler_params=params,
        name="turn",
    )(factor)
    count = per_owner * slab_width
    depth = layers * rows
    sizes = (layers, owners, per_owner, block_count, block_rows)
    result = shaped((count, panel_width), f32)
    panels = [column, by_x, by_y]
    own, other = pl.pallas_call(
        functools.partial(near_kernel, sizes, 3),
        out_shape=[result, shaped((count, panel_width), bf16)],
        in_specs=[anywhere] * 3 + [vmem] * (len(panels) + layers),
        out_specs=[vmem] * 2,
        scratch_shapes=[
            pltpu.VMEM((count, (owners - 1) * depth), bf16),
            pltpu.VMEM(((owners - 1) * depth, panel_width), bf16),
        ],
        compiler_params=params,
        cost_estimate=lasting(10**9),
        name="near",
    )(rows_to_y, rows_to_x, turned, *panels, *posts)
    other = shift(other, 0, 0, 1)
    own = pl.pallas_call(
        own_kernel,
        out_shape=result,
        in_specs=[vmem] * 2,
        out_specs=vmem,
        compiler_params=params,
        cost_estimate=lasting(10**9),
        name="own",
    )(own, turned)
    joined = pl.pallas_call(
        functools.partial(join_kernel, (layers, lane_group, wide)),
        out_shape=shaped((depth + rows // 2 + 16, panel_width), bf16),
        in_specs=[vmem] * (2 + layers) + [anywhere],
        out_specs=vmem,
        compiler_params=params,
        cost_estimate=lasting(10**10),
        name="join",
    )(across_y, across_x, *posts, own)
    other_joined = shift(joined, 0, 0, 1)
    far_scratch = [pltpu.VMEM((count, depth), bf16)] + [pltpu.VMEM((depth, panel_width), bf16)] * 2
    far = pl.pallas_call(
        functools.partial(far_kernel, sizes),
        out_shape=result,
        in_specs=[vmem] * 2,
        out_specs=vmem,
        scratch_shapes=far_scratch,
        compiler_params=params,
        name="far",
    )(joined, turned)
    middle = pl.pallas_call(
        middle_kernel,
        out_shape=result,
        in_specs=[vmem] * 4,
        out_specs=vmem,
        compiler_params=params,
        name="middle",
    )(own, other, far, turned)
    out = pl.pallas_call(
        functools.partial(final_kernel, sizes),
        out_shape=result,
        in_specs=[vmem] * 3,
        out_specs=anywhere,
        scratch_shapes=[pltpu.VMEM((count, panel_width), f32)] + far_scratch + [pltpu.SemaphoreType.DMA((6,))],
        compiler_params=params,
        name="final",
    )(middle, other_joined, turned)
    return out.reshape(per_owner, slab_width, panel_width)


def solution(mesh):
    in_specs = (
        P(("rows", "cols"), None),
        P(("rows", "cols"), None),
        P(("rows", "cols")),
        P(("rows", "cols"), None),
        P(("rows", "cols"), None),
        P(),
        P(),
    )
    out_specs = P("cols", "rows", None)
    body = local if (mesh.shape["rows"], mesh.shape["cols"]) == (8, 4) else local_general
    return jax.shard_map(body, mesh=mesh, in_specs=in_specs, out_specs=out_specs, check_vma=False)
```

```python
import functools

import jax
import jax.numpy as jnp
from jax import lax
from jax.experimental import pallas as pl
from jax.experimental.pallas import tpu as pltpu
from jax.sharding import PartitionSpec as P

CAP = 2
GATHERED = 1 << 22


def tile_positions(tile_lists, tile_order):
    tile_count = tile_order.shape[0]
    matches = tile_lists[:, :, None] == tile_order[None, None, :]
    return jnp.sum(jnp.where(matches, jnp.arange(tile_count, dtype=jnp.int32), 0), axis=2)


def apply_inverse(tiles, factor_inverse):
    return jnp.einsum("ntp,qp->ntq", tiles, factor_inverse, precision=lax.Precision.HIGHEST)


def slot_codes(tile_lists, tile_masks, tile_order, owner_ids):
    block_count, slot_count = tile_lists.shape
    per_owner = tile_order.shape[0] // lax.axis_size("cols")
    positions = tile_positions(tile_lists, tile_order).reshape(-1)
    active = tile_masks.reshape(-1) == 1
    owner = positions // per_owner
    same = (owner[:, None] == owner[None, :]) & active[None, :]
    earlier = jnp.tril(jnp.ones(same.shape, bool), -1)
    rank = jnp.sum(same & earlier, axis=1)
    code = (
        (owner[None, None, :] == owner_ids[:, None, None])
        & (rank[None, None, :] == jnp.arange(CAP)[None, :, None])
        & active[None, None, :]
    )
    block = jnp.arange(block_count * slot_count) // slot_count
    place = positions % per_owner + per_owner * block
    return code, jnp.sum(jnp.where(code, place + 1, 0), axis=2) - 1


def local_general(jac, panel_jac, weights, tile_lists, tile_masks, tile_order, factor_inverse):
    block_count, slot_count = tile_lists.shape
    block_rows = jac.shape[0] // block_count
    tile_width = jac.shape[1] // slot_count
    slabs, owners = lax.axis_size("rows"), lax.axis_size("cols")
    devices = slabs * owners
    per_owner = tile_order.shape[0] // owners
    slab_width = tile_width // slabs
    bf16 = jnp.bfloat16
    weighted = (weights[:, None] * panel_jac).astype(bf16)
    code, places = slot_codes(tile_lists, tile_masks, tile_order, jnp.arange(owners))
    columns = jac.reshape(block_count, block_rows, slot_count, slabs, slab_width)
    chosen = code.astype(bf16).reshape(owners, CAP, block_count, slot_count)
    pieces = jnp.einsum("cjbk,bmkrt->rcjmt", chosen, columns, preferred_element_type=jnp.float32).astype(bf16)
    pieces = pieces.reshape(devices, -1)
    note = jnp.broadcast_to(places.astype(bf16)[None], (slabs, owners, CAP)).reshape(devices, CAP)
    note = jnp.pad(note, ((0, 0), (0, 128 - CAP)))
    sent = jnp.concatenate([pieces, note], axis=1)
    got = lax.all_to_all(sent, ("rows", "cols"), split_axis=0, concat_axis=0, tiled=True)
    size = pieces.shape[1]
    data = got[:, :size].reshape(devices, CAP, block_rows, slab_width)
    where = got[:, size : size + CAP].astype(jnp.int32)
    hot = (where[:, :, None] == jnp.arange(block_count * per_owner)).astype(bf16)
    hot = hot.reshape(devices, CAP, block_count, per_owner)
    mixed = jnp.einsum("djbn,djmt->dbmnt", hot, data, preferred_element_type=jnp.float32).astype(bf16)
    strips = max(1, devices * weighted.size * 2 // GATHERED)

    def strip_gram(strip):
        panels = lax.all_gather(strip, ("rows", "cols"), axis=0, tiled=True)
        panels = panels.reshape(devices, block_count, block_rows, -1)
        return jnp.einsum("dbmnt,dbmp->ntp", mixed, panels, preferred_element_type=jnp.float32)

    if strips == 1:
        gram = strip_gram(weighted)
    else:
        narrow = weighted.reshape(weighted.shape[0], strips, -1).swapaxes(0, 1)
        gram = jnp.moveaxis(lax.map(strip_gram, narrow), 0, 2)
        gram = gram.reshape(per_owner, slab_width, -1)
    return apply_inverse(gram, factor_inverse)


def shift(value, steps_z, flip_cols, flip_core=0):
    slabs, owners = lax.axis_size("rows"), lax.axis_size("cols")
    pairs = []
    for r in range(slabs):
        to_r = ((r // 2 + steps_z) % (slabs // 2)) * 2 + ((r % 2) ^ flip_core)
        for c in range(owners):
            pairs.append((r * owners + c, to_r * owners + (c ^ flip_cols)))
    return lax.ppermute(value, ("rows", "cols"), pairs)


def lasting(flops):
    return pl.CostEstimate(flops=flops, bytes_accessed=0, transcendentals=0)


def pack_kernel(sizes, lists_hbm, masks_hbm, order_hbm, weights_hbm, panel_hbm, jac_hbm, factor_hbm, *refs):
    layers, owners, per_owner, block_count, slot_count, block_rows, tile_width = sizes
    weighted_ref, parcels, factor_ref = refs[0], refs[1 : 1 + owners], refs[1 + owners]
    lists_ref, masks_ref, order_ref, weights_ref, panel_ref, jac_ref, places_ref, turned_ref, sems = refs[2 + owners :]
    copies = [
        pltpu.make_async_copy(order_hbm, order_ref, sems.at[0]),
        pltpu.make_async_copy(lists_hbm, lists_ref, sems.at[1]),
        pltpu.make_async_copy(masks_hbm, masks_ref, sems.at[2]),
        pltpu.make_async_copy(weights_hbm, weights_ref, sems.at[3]),
        pltpu.make_async_copy(panel_hbm, panel_ref, sems.at[4]),
        pltpu.make_async_copy(jac_hbm, jac_ref, sems.at[5]),
    ]
    for copy in copies:
        copy.start()
    factor_copy = pltpu.make_async_copy(factor_hbm, factor_ref, sems.at[6])
    factor_copy.start()
    f32, bf16 = jnp.float32, jnp.bfloat16
    rows, width = panel_ref.shape
    lane_group = CAP * block_rows
    post = layers * lane_group
    slab = tile_width // layers
    part = slab // 2
    me_r, me_c = lax.axis_index("rows"), lax.axis_index("cols")
    me_z, me_core = me_r // 2, lax.rem(me_r, 2)
    for copy in copies[:3]:
        copy.wait()
    for i in range(order_ref.shape[0]):
        places_ref[order_ref[i]] = i
    slots = []
    for s in range(block_count * slot_count):
        b, k = divmod(s, slot_count)
        place = places_ref[lists_ref[b, k]]
        owner = jnp.int32(0)
        for c in range(1, owners):
            owner += (place >= c * per_owner).astype(jnp.int32)
        slots.append((place - owner * per_owner, jnp.where(masks_ref[b, k] == 1, owner, -1)))

    found_slots = []
    for e in range(owners):
        wanted = me_c ^ e
        found = jnp.int32(0)
        chosen = [jnp.int32(0)] * CAP
        codes = [jnp.int32(-1)] * CAP
        for s, (place, owner) in enumerate(slots):
            hit = owner == wanted
            for j in range(CAP):
                take = hit & (found == j)
                chosen[j] = jnp.where(take, s, chosen[j])
                codes[j] = jnp.where(take, place, codes[j])
            found += hit.astype(jnp.int32)
        found_slots.append((chosen, codes))

    for copy in copies[3:]:
        copy.wait()

    row_ids = lax.broadcasted_iota(jnp.int32, (rows, rows), 0)
    lane_ids = lax.broadcasted_iota(jnp.int32, (rows, rows), 1)
    column = jnp.sum(jnp.where(row_ids == lane_ids, weights_ref[...], 0.0), axis=1, keepdims=True)
    weighted = (column * panel_ref[...].astype(f32)).astype(bf16)
    weighted_ref[...] = weighted

    for b in range(block_count):
        block = jac_ref[b * block_rows : (b + 1) * block_rows, :].astype(f32)
        start = b * slot_count * tile_width
        turned_ref[start : start + slot_count * tile_width, :] = block.T.astype(bf16)

    shape = (16, CAP * block_count * block_rows)
    lane = lax.broadcasted_iota(jnp.int32, shape, 1)
    for parcel, (chosen, codes) in zip(parcels, found_slots):
        note = jnp.full(shape, -1, jnp.int32)
        for j in range(CAP):
            for b in range(block_count):
                at = (j * block_count + b) * block_rows
                here = (lane >= at) & (lane < at + block_rows)
                code = jnp.where(chosen[j] // slot_count == b, codes[j], -1)
                note = jnp.where(here, code, note)
        parcel[:16, post:] = note.astype(f32).astype(bf16)
        for u in range(2):
            core = me_core ^ u
            for k in range(0, layers, 2):
                pieces = []
                for z in (lax.rem(me_z + k, layers), lax.rem(me_z + k + 1, layers)):
                    for j in range(CAP):
                        first = pl.multiple_of(chosen[j] * tile_width + z * slab + core * part, part)
                        pieces.append(turned_ref[pl.ds(first, part), :])
                lanes = slice(k * lane_group, (k + 2) * lane_group)
                parcel[u * part : (u + 1) * part, lanes] = jnp.concatenate(pieces, axis=1)
    factor_copy.wait()


def row_of(block, i):
    ids = lax.broadcasted_iota(jnp.int32, block.shape, 0)
    return jnp.sum(jnp.where(ids == i, block.astype(jnp.float32), 0.0), axis=0, keepdims=True)


def rows_from(notes):
    ids = lax.broadcasted_iota(jnp.int32, (16, notes[0].shape[1]), 0)
    block = jnp.full(ids.shape, -1.0, jnp.float32)
    for i, note in enumerate(notes):
        block = jnp.where(ids == i, note, block)
    return block.astype(jnp.bfloat16)


def stack_kernel(places, *refs):
    out_ref = refs[-1]
    for place_of, ref in zip(places, refs):
        rows = ref.shape[0]
        out_ref[place_of * rows : (place_of + 1) * rows, :] = ref[...]


def sort_kernel(sizes, *refs):
    layers, owners, lane_group = sizes
    parcels, posts = (refs[0], refs[3], refs[2], refs[1]), refs[owners:]
    rows, codes_at = parcels[0].shape[0], layers * lane_group
    block = rows_from([row_of(parcel[:16, codes_at:], 0) for parcel in parcels])
    for k, out in enumerate(posts):
        for e, parcel in enumerate(parcels):
            piece = parcel[:, k * lane_group : (k + 1) * lane_group]
            out[:rows, e * lane_group : (e + 1) * lane_group] = piece
        out[rows:, : block.shape[1]] = block


def first_kernel(in_ref, out_ref):
    out_ref[...] = in_ref[: out_ref.shape[0], :]


def last_kernel(in_ref, out_ref):
    out_ref[...] = in_ref[in_ref.shape[0] - out_ref.shape[0] :, :]


def place(out_ref, lanes, per_owner, pieces, notes, sizes):
    block_count, block_rows = sizes
    f32, bf16 = jnp.float32, jnp.bfloat16
    part, rows = pieces[0].shape[0], block_count * block_rows
    columns, codes = [], []
    for j in range(CAP):
        parts = []
        for piece in pieces:
            parts += [piece[:, j * block_rows : (j + 1) * block_rows].astype(f32)] * block_count
        columns.append(jnp.concatenate(parts, axis=1).astype(bf16))
        note = jnp.concatenate([note[:, j * rows : (j + 1) * rows] for note in notes], axis=1)
        codes.append(jnp.broadcast_to(note, columns[j].shape).astype(bf16))
    for n in range(per_owner):
        placed = jnp.zeros(columns[0].shape, bf16)
        for j in range(CAP):
            placed = jnp.where(codes[j] == jnp.asarray(n, bf16), columns[j], placed)
        out_ref[n * part : (n + 1) * part, lanes] = placed


def inverse_rows(rows_ref, factor_ref, high_ref, low_ref):
    f32, bf16 = jnp.float32, jnp.bfloat16
    height, width = high_ref.shape
    for start, stop in ((0, width // 2), (width // 2, width)):
        rows = rows_ref[:height, :stop]
        total = jnp.dot(rows, factor_ref[0, :stop, start:stop], preferred_element_type=f32)
        total += jnp.dot(rows, factor_ref[1, :stop, start:stop], preferred_element_type=f32)
        high = total.astype(bf16)
        high_ref[:, start:stop] = high
        low_ref[:, start:stop] = (total - high.astype(f32)).astype(bf16)


def turn_kernel(factor_ref, out_ref):
    turned = factor_ref[...].T
    high = turned.astype(jnp.bfloat16)
    out_ref[0, :, :] = high
    out_ref[1, :, :] = (turned - high.astype(jnp.float32)).astype(jnp.bfloat16)


def near_kernel(sizes, earlier, *refs):
    layers, owners, per_owner, block_count, block_rows = sizes
    panels, posts, refs = refs[earlier : earlier + 3], refs[earlier + 3 : earlier + 3 + layers], refs[earlier + 3 + layers :]
    own_ref, other_ref, placed_ref, rows_ref = refs
    f32, bf16 = jnp.float32, jnp.bfloat16
    rows = block_count * block_rows
    group, wide = CAP * block_rows, CAP * rows
    part = rows // 2
    width = rows_ref.shape[1]
    at = 0
    for panel in panels:
        rows_ref[at : at + panel.shape[0], :] = panel[:, :width]
        at += panel.shape[0]
    for u, out_ref in ((1, other_ref), (0, own_ref)):
        for e in range(owners - 1):
            for h in range(layers // 2):
                pair = posts[2 * h : 2 * h + 2]
                pieces = [post[u * part : (u + 1) * part, e * group : (e + 1) * group] for post in pair]
                notes = [row_of(post[rows:, :wide], e) for post in pair]
                start = (e * layers + 2 * h) * rows
                place(placed_ref, slice(start, start + 2 * rows), per_owner, pieces, notes, (block_count, block_rows))
        gram = jnp.dot(placed_ref[...], rows_ref[...], preferred_element_type=f32)
        out_ref[...] = gram.astype(out_ref.dtype)


def join_kernel(sizes, above_ref, below_ref, *refs):
    layers, lane_group, wide = sizes
    posts, out_ref = refs[:layers], refs[-1]
    half, rows = above_ref.shape[0], posts[0].shape[0] - 16
    part, depth = rows // 2, 2 * half
    out_ref[:half, :] = above_ref[...]
    out_ref[half:depth, :] = below_ref[...]
    for k, ref in enumerate(posts):
        for u in range(2):
            piece = ref[u * part : (u + 1) * part, 3 * lane_group : 4 * lane_group]
            at = (u * layers + k) * lane_group
            out_ref[depth : depth + part, at : at + lane_group] = piece
    out_ref[depth + part :, :wide] = rows_from([row_of(ref[rows:, :wide], 3) for ref in posts])


def place_far(sizes, u, ref, placed_ref):
    layers, owners, per_owner, block_count, block_rows = sizes
    rows = block_count * block_rows
    group, wide = CAP * block_rows, CAP * rows
    part, depth = rows // 2, layers * rows
    for h in range(layers // 2):
        pieces, notes = [], []
        for k in (2 * h, 2 * h + 1):
            at = (u * layers + k) * group
            pieces.append(ref[depth : depth + part, at : at + group])
            notes.append(row_of(ref[depth + part :, :wide], k))
        lanes = slice(2 * h * rows, 2 * (h + 1) * rows)
        place(placed_ref, lanes, per_owner, pieces, notes, (block_count, block_rows))


def far_kernel(sizes, joined_ref, turned_ref, out_ref, placed_ref, high_ref, low_ref):
    place_far(sizes, 0, joined_ref, placed_ref)
    inverse_rows(joined_ref, turned_ref, high_ref, low_ref)
    placed = placed_ref[...]
    total = jnp.dot(placed, high_ref[...], preferred_element_type=jnp.float32)
    out_ref[...] = total + jnp.dot(placed, low_ref[...], preferred_element_type=jnp.float32)


def times_inverse(out_ref, terms, turned_ref, added):
    width = out_ref.shape[1]
    for start, stop in ((0, width // 2), (width // 2, width)):
        total = sum(ref[:, start:stop] for ref in added)
        for i, j in ((0, 0), (0, 1), (1, 0))[: len(terms) + 1]:
            total += jnp.dot(terms[i][:, :stop], turned_ref[j, :stop, start:stop], preferred_element_type=jnp.float32)
        out_ref[:, start:stop] = total


def own_kernel(own_ref, turned_ref, out_ref):
    high = own_ref[...].astype(jnp.bfloat16)
    low = (own_ref[...] - high.astype(jnp.float32)).astype(jnp.bfloat16)
    times_inverse(out_ref, (high, low), turned_ref, ())


def middle_kernel(own_ref, other_ref, far_ref, turned_ref, out_ref):
    times_inverse(out_ref, (other_ref[...],), turned_ref, (own_ref, far_ref))


def final_kernel(sizes, middle_ref, joined_ref, turned_ref, out_hbm, sum_ref, placed_ref, high_ref, low_ref, sems):
    f32 = jnp.float32
    place_far(sizes, 1, joined_ref, placed_ref)
    inverse_rows(joined_ref, turned_ref, high_ref, low_ref)
    strips = sems.shape[0]
    height = sum_ref.shape[0] // strips
    copies = []
    for i in range(strips):
        here = pl.ds(i * height, height)
        placed = placed_ref[here, :]
        total = middle_ref[here, :] + jnp.dot(placed, high_ref[...], preferred_element_type=f32)
        sum_ref[here, :] = total + jnp.dot(placed, low_ref[...], preferred_element_type=f32)
        copies.append(pltpu.make_async_copy(sum_ref.at[here, :], out_hbm.at[here, :], sems.at[i]))
        copies[-1].start()
    for copy in copies:
        copy.wait()


def local(jac, panel_jac, weights, tile_lists, tile_masks, tile_order, factor_inverse):
    block_count, slot_count = tile_lists.shape
    rows, panel_width = panel_jac.shape
    block_rows = rows // block_count
    tile_width = jac.shape[1] // slot_count
    slabs, owners = lax.axis_size("rows"), lax.axis_size("cols")
    layers = slabs // 2
    per_owner = tile_order.shape[0] // owners
    slab_width = tile_width // slabs
    f32, bf16 = jnp.float32, jnp.bfloat16
    vmem, anywhere = pl.BlockSpec(memory_space=pltpu.VMEM), pl.BlockSpec(memory_space=pl.ANY)
    params = pltpu.CompilerParams(vmem_limit_bytes=24 << 20)
    shaped = jax.ShapeDtypeStruct

    def in_hbm(value):
        return pltpu.with_memory_space_constraint(value, pltpu.HBM)

    lane_group = CAP * block_rows
    post = layers * lane_group
    wide = CAP * rows
    sizes = (layers, owners, per_owner, block_count, slot_count, block_rows, tile_width)
    weighted, *parcels, factor = pl.pallas_call(
        functools.partial(pack_kernel, sizes),
        out_shape=[shaped((rows, panel_width), bf16)]
        + [shaped((rows, post + wide), bf16)] * owners
        + [shaped(factor_inverse.shape, f32)],
        in_specs=[anywhere] * 7,
        out_specs=[vmem] * (owners + 2),
        scratch_shapes=[
            pltpu.SMEM(tile_lists.shape, jnp.int32),
            pltpu.SMEM(tile_masks.shape, jnp.int32),
            pltpu.SMEM(tile_order.shape, jnp.int32),
            pltpu.VMEM((1, rows), f32),
            pltpu.VMEM(panel_jac.shape, bf16),
            pltpu.VMEM(jac.shape, bf16),
            pltpu.SMEM(tile_order.shape, jnp.int32),
            pltpu.VMEM((block_count * slot_count * tile_width, block_rows), bf16),
            pltpu.SemaphoreType.DMA((7,)),
        ],
        compiler_params=params,
        name="pack",
    )(*map(in_hbm, (tile_lists, tile_masks, tile_order, weights.reshape(1, rows), panel_jac, jac, factor_inverse)))
    line = [shift(weighted, k, 0) for k in range(1, layers)]
    parcels = [parcels[0]] + [shift(parcels[e], 0, e) for e in range(1, owners)]

    column = pl.pallas_call(
        functools.partial(stack_kernel, (3, 1, 2, 0)),
        out_shape=shaped((layers * rows, panel_width), bf16),
        in_specs=[vmem] * layers,
        out_specs=vmem,
        compiler_params=params,
        cost_estimate=lasting(10**10),
        name="stack",
    )(line[2], line[0], line[1], weighted)
    posts = pl.pallas_call(
        functools.partial(sort_kernel, (layers, owners, lane_group)),
        out_shape=[shaped((rows + 16, owners * lane_group), bf16)] * layers,
        in_specs=[vmem] * owners,
        out_specs=[vmem] * layers,
        compiler_params=params,
        cost_estimate=lasting(10**10),
        name="sort",
    )(parcels[0], parcels[3], parcels[2], parcels[1])
    posts = [posts[0]] + [shift(posts[k], k, 0) for k in range(1, layers)]
    by_x, by_y = shift(column, 0, 1), shift(column, 0, 2)


    def cut(kernel, value, name):
        return pl.pallas_call(
            kernel,
            out_shape=shaped((value.shape[0] // 2, panel_width), bf16),
            in_specs=[vmem],
            out_specs=vmem,
            compiler_params=params,
            name=name,
        )(value)

    rows_to_y, rows_to_x = cut(first_kernel, by_x, "first"), cut(last_kernel, by_y, "last")
    across_y, across_x = shift(rows_to_y, 0, 2), shift(rows_to_x, 0, 1)
    turned = pl.pallas_call(
        turn_kernel,
        out_shape=shaped((2, *factor_inverse.shape), bf16),
        in_specs=[vmem],
        out_specs=vmem,
        compiler_params=params,
        name="turn",
    )(factor)
    count = per_owner * slab_width
    depth = layers * rows
    sizes = (layers, owners, per_owner, block_count, block_rows)
    result = shaped((count, panel_width), f32)
    panels = [column, by_x, by_y]
    own, other = pl.pallas_call(
        functools.partial(near_kernel, sizes, 3),
        out_shape=[result, shaped((count, panel_width), bf16)],
        in_specs=[anywhere] * 3 + [vmem] * (len(panels) + layers),
        out_specs=[vmem] * 2,
        scratch_shapes=[
            pltpu.VMEM((count, (owners - 1) * depth), bf16),
            pltpu.VMEM(((owners - 1) * depth, panel_width), bf16),
        ],
        compiler_params=params,
        cost_estimate=lasting(10**9),
        name="near",
    )(rows_to_y, rows_to_x, turned, *panels, *posts)
    other = shift(other, 0, 0, 1)
    own = pl.pallas_call(
        own_kernel,
        out_shape=result,
        in_specs=[vmem] * 2,
        out_specs=vmem,
        compiler_params=params,
        cost_estimate=lasting(10**9),
        name="own",
    )(own, turned)
    joined = pl.pallas_call(
        functools.partial(join_kernel, (layers, lane_group, wide)),
        out_shape=shaped((depth + rows // 2 + 16, panel_width), bf16),
        in_specs=[vmem] * (2 + layers) + [anywhere],
        out_specs=vmem,
        compiler_params=params,
        cost_estimate=lasting(10**10),
        name="join",
    )(across_y, across_x, *posts, own)
    other_joined = shift(joined, 0, 0, 1)
    far_scratch = [pltpu.VMEM((count, depth), bf16)] + [pltpu.VMEM((depth, panel_width), bf16)] * 2
    far = pl.pallas_call(
        functools.partial(far_kernel, sizes),
        out_shape=result,
        in_specs=[vmem] * 2,
        out_specs=vmem,
        scratch_shapes=far_scratch,
        compiler_params=params,
        name="far",
    )(joined, turned)
    middle = pl.pallas_call(
        middle_kernel,
        out_shape=result,
        in_specs=[vmem] * 4,
        out_specs=vmem,
        compiler_params=params,
        name="middle",
    )(own, other, far, turned)
    out = pl.pallas_call(
        functools.partial(final_kernel, sizes),
        out_shape=result,
        in_specs=[vmem] * 3,
        out_specs=anywhere,
        scratch_shapes=[pltpu.VMEM((count, panel_width), f32)] + far_scratch + [pltpu.SemaphoreType.DMA((4,))],
        compiler_params=params,
        name="final",
    )(middle, other_joined, turned)
    return out.reshape(per_owner, slab_width, panel_width)


def solution(mesh):
    in_specs = (
        P(("rows", "cols"), None),
        P(("rows", "cols"), None),
        P(("rows", "cols")),
        P(("rows", "cols"), None),
        P(("rows", "cols"), None),
        P(),
        P(),
    )
    out_specs = P("cols", "rows", None)
    body = local if (mesh.shape["rows"], mesh.shape["cols"]) == (8, 4) else local_general
    return jax.shard_map(body, mesh=mesh, in_specs=in_specs, out_specs=out_specs, check_vma=False)
```
